32 devices in a mesh: dp: 8 (over z, y), tensor: 4 (over x, core).
Axes of the slice: x: 2, y: 2, z: 4, core: 2. Of those that a mesh axis runs over, the one named last changes fastest.
Arguments:
- tokens: bfloat16 [20480, 1024], P('dp'), may hold values from -6 to 6
- cotangent: bfloat16 [20480, 1024], P('dp'), may hold values from -6 to 6
- seq_extra: int32 [4], replicated, may hold values from 1 to 112, 256 in all
- deal: int32 [320], replicated, may hold values from 0 to 319, as said below
- proj_in: bfloat16 [1024, 4, 768], P('dp', 'tensor'), may hold values from -0.1875 to 0.1875
- decay_down: bfloat16 [1024, 16], P('dp'), may hold values from -0.1875 to 0.1875
- decay_up: bfloat16 [16, 4, 128], P(None, 'tensor'), may hold values from -1.5 to 1.5
- decay_bias: float32 [4, 128], P('tensor'), may hold values from 0.5 to 9
- head_gain: float32 [256], replicated, may hold values from 0.5 to 1.5
- proj_out: bfloat16 [4, 256, 1024], P('tensor', None, 'dp'), may hold values from -0.1875 to 0.1875
- block_gains: float32 [2, 1024], replicated, may hold values from 0.5 to 1.5
- ffn_in: bfloat16 [1024, 2, 2816], P('dp', None, 'tensor'), may hold values from -0.1875 to 0.1875
- ffn_out: bfloat16 [2816, 1024], P('tensor', 'dp'), may hold values from -0.109375 to 0.109375
- first_proj_in: float32 [1024, 4, 768], P('dp', 'tensor'), may hold values from -0.078125 to 0.078125
- second_proj_in: float32 [1024, 4, 768], P('dp', 'tensor'), may hold values from 0.00013 to 0.00053
- first_decay_down: float32 [1024, 16], P('dp'), may hold values from -0.078125 to 0.078125
- second_decay_down: float32 [1024, 16], P('dp'), may hold values from 0.00013 to 0.00053
- first_decay_up: float32 [16, 4, 128], P(None, 'tensor'), may hold values from -0.078125 to 0.078125
- second_decay_up: float32 [16, 4, 128], P(None, 'tensor'), may hold values from 1.5e-05 to 6e-05
- first_decay_bias: float32 [4, 128], P('tensor'), may hold values from -0.078125 to 0.078125
- second_decay_bias: float32 [4, 128], P('tensor'), may hold values from 0.00013 to 0.00053
- first_head_gain: float32 [256], replicated, may hold values from -0.078125 to 0.078125
- second_head_gain: float32 [256], replicated, may hold values from 0.00013 to 0.00053
- first_proj_out: float32 [4, 256, 1024], P('tensor', None, 'dp'), may hold values from -0.078125 to 0.078125
- second_proj_out: float32 [4, 256, 1024], P('tensor', None, 'dp'), may hold values from 0.00013 to 0.00053
- first_block_gains: float32 [2, 1024], replicated, may hold values from -0.078125 to 0.078125
- second_block_gains: float32 [2, 1024], replicated, may hold values from 0.00013 to 0.00053
- first_ffn_in: float32 [1024, 2, 2816], P('dp', None, 'tensor'), may hold values from -0.078125 to 0.078125
- second_ffn_in: float32 [1024, 2, 2816], P('dp', None, 'tensor'), may hold values from 0.00013 to 0.00053
- first_ffn_out: float32 [2816, 1024], P('tensor', 'dp'), may hold values from -0.078125 to 0.078125
- second_ffn_out: float32 [2816, 1024], P('tensor', 'dp'), may hold values from 0.00013 to 0.00053
Outputs:
- block_out: float32 [20480, 1024], P('dp', 'tensor')
- token_grad: float32 [20480, 1024], P('dp')
- grad_norm: float32 [], replicated
- grad_proj_in: float32 [1024, 4, 768], P('dp', 'tensor')
- first_new_proj_in: float32 [1024, 4, 768], P('dp', 'tensor')
- second_new_proj_in: float32 [1024, 4, 768], P('dp', 'tensor')
- step_proj_in: float32 [1024, 4, 768], P('dp', 'tensor')
- grad_decay_down: float32 [1024, 16], P('dp')
- first_new_decay_down: float32 [1024, 16], P('dp')
- second_new_decay_down: float32 [1024, 16], P('dp')
- step_decay_down: float32 [1024, 16], P('dp')
- grad_decay_up: float32 [16, 4, 128], P(None, 'tensor')
- first_new_decay_up: float32 [16, 4, 128], P(None, 'tensor')
- second_new_decay_up: float32 [16, 4, 128], P(None, 'tensor')
- step_decay_up: float32 [16, 4, 128], P(None, 'tensor')
- grad_decay_bias: float32 [4, 128], P('tensor')
- first_new_decay_bias: float32 [4, 128], P('tensor')
- second_new_decay_bias: float32 [4, 128], P('tensor')
- step_decay_bias: float32 [4, 128], P('tensor')
- grad_head_gain: float32 [256], replicated
- first_new_head_gain: float32 [256], replicated
- second_new_head_gain: float32 [256], replicated
- step_head_gain: float32 [256], replicated
- grad_proj_out: float32 [4, 256, 1024], P('tensor', None, 'dp')
- first_new_proj_out: float32 [4, 256, 1024], P('tensor', None, 'dp')
- second_new_proj_out: float32 [4, 256, 1024], P('tensor', None, 'dp')
- step_proj_out: float32 [4, 256, 1024], P('tensor', None, 'dp')
- grad_block_gains: float32 [2, 1024], replicated
- first_new_block_gains: float32 [2, 1024], replicated
- second_new_block_gains: float32 [2, 1024], replicated
- step_block_gains: float32 [2, 1024], replicated
- grad_ffn_in: float32 [1024, 2, 2816], P('dp', None, 'tensor')
- first_new_ffn_in: float32 [1024, 2, 2816], P('dp', None, 'tensor')
- second_new_ffn_in: float32 [1024, 2, 2816], P('dp', None, 'tensor')
- step_ffn_in: float32 [1024, 2, 2816], P('dp', None, 'tensor')
- grad_ffn_out: float32 [2816, 1024], P('tensor', 'dp')
- first_new_ffn_out: float32 [2816, 1024], P('tensor', 'dp')
- second_new_ffn_out: float32 [2816, 1024], P('tensor', 'dp')
- step_ffn_out: float32 [2816, 1024], P('tensor', 'dp')
The draws below stay inside these ranges and needn't reach their ends.
Inputs may be any that keep to these rules, and one draw needn't show every extreme that they name: Sequence i of the dealt layout holds (16 + seq_extra[i]) * 64 tokens; the sequences lie one after another and together fill all 20480 tokens; some sequence has seq_extra equal to 112. deal names every one of the 320 spans once. Span p of the dealt layout lies with index p // 40 of dp, input span deal[p] with index deal[p] // 40. Every index of dp takes exactly 5 spans from each index.
All inputs are finite; a program needn't handle non-finite values.
Results may differ from the reference program's by a relative error of at most 0.02.
Values may be sent and summed in bfloat16 or wider, within the bound.
A program may use at most 256 MiB of HBM per device.

```python
import math
import jax
import jax.numpy as jnp
import numpy as np
from jax import lax

D = 1024
H = 4
DK = 128
DV = 256
FF = 2816
RANK = 16
SPAN = 64
MIN_SPANS = 16
MAX_SPANS = 128
TOK_DEV = 2560
TOKENS = 20480
NCHUNK = 320
NSEQ = 4
QKVG = 768
PARAMS = 12872448
N_TENSOR = 4


def draw_deal(key, part):
    per_dev = TOK_DEV // SPAN
    n_devices = NCHUNK // per_dev
    key_rows = jax.random.fold_in(key, 11)
    key_slots = jax.random.fold_in(key, 12)
    key_local = jax.random.fold_in(key, 13)
    device_order = jax.random.permutation(key_rows, n_devices).astype(jnp.int32)
    slot_order = jax.random.permutation(key_slots, per_dev).astype(jnp.int32)
    source = (device_order[:, None] + slot_order[None, :]) % n_devices
    flat_source = source.reshape(-1).astype(jnp.int32)
    positions = jnp.arange(NCHUNK, dtype=jnp.int32)
    sorted_index = jnp.argsort(flat_source * NCHUNK + positions)
    ranked = jnp.zeros((NCHUNK,), jnp.int32).at[sorted_index].set(positions)
    within = ranked - flat_source * per_dev
    scores = jax.random.randint(key_local, (n_devices, per_dev), 0, 65536) * per_dev + jnp.arange(per_dev, dtype=jnp.int32)[None, :]
    local_order = jnp.argsort(scores, axis=1).astype(jnp.int32)
    local_span = local_order[flat_source, within]
    return (flat_source * per_dev + local_span).astype(jnp.int32)


def levels(own_key, extent, shards, smallest, largest):
    def one(dim, blocks):
        draws = jax.random.uniform(jax.random.fold_in(jax.random.fold_in(own_key, 6), dim), (blocks,), jnp.float32, smallest / len(shards), largest / len(shards))
        return jnp.repeat(jnp.exp(draws), extent[dim] // blocks).reshape((-1,) + (1,) * (len(extent) - dim - 1))

    level = one(*shards[0])
    for cut in shards[1:]:
        level = level * one(*cut)
    return level


def length_profile(amount, total, reach, lean):
    portions = [(1 << 20) // math.isqrt(rank ** lean) + 1 for rank in range(2, amount + 1)]
    spare, given = total - reach - (amount - 1), [1] * (amount - 1)
    while spare > 0:
        movable = [i for i in range(amount - 1) if given[i] < reach]
        whole, remaining = sum([portions[i] for i in movable]), spare
        for i in movable:
            extra = min(reach - given[i], max(1, remaining * portions[i] // whole), spare)
            given[i] = given[i] + extra
            spare = spare - extra
    return np.array([reach] + given)


def uneven_parts(rng, number_of, total, bound, skew):
    if number_of == 2:
        one = jax.random.randint(rng, (), max(1, total - bound), min(bound, total - 1) + 1)
        return jnp.stack([one, total - one])
    tallies = jnp.asarray(length_profile(number_of, total, bound, skew), jnp.int32)
    pairs = (number_of - 1) // 2
    donor, sink = tallies[1:1 + 2 * pairs:2], tallies[2:2 + 2 * pairs:2]
    margin = jnp.minimum(donor - 1, bound - sink)
    shifted = jax.random.randint(jax.random.fold_in(rng, 1), (pairs,), 0, 1 << 20) % (margin + 1)
    tallies = tallies.at[1:1 + 2 * pairs:2].set(donor - shifted).at[2:2 + 2 * pairs:2].set(sink + shifted)
    return tallies[jax.random.permutation(jax.random.fold_in(rng, 2), number_of)]


def normal_values(stream_key, dims, deviation, most, split=(), kind=jnp.bfloat16):
    gain = levels(stream_key, dims, split, -0.22, 0.18) if split else 1.0
    values = jax.random.normal(stream_key, dims, jnp.float32) * deviation * gain
    return jnp.minimum(jnp.maximum(values, -most), most).astype(kind)


def setup_inputs(seed: int = 0) -> dict:
    keys = jax.random.split(jax.random.key(seed), 32)
    tokens = normal_values(keys[0], (TOKENS, D), 1.0, 6.0, ((0, 8),))
    cotangent = normal_values(keys[1], (TOKENS, D), 1.0, 6.0, ((0, 8),))
    seq_extra = uneven_parts(keys[2], NSEQ, NCHUNK - NSEQ * MIN_SPANS, MAX_SPANS - MIN_SPANS, 2).astype(jnp.int32)
    deal = draw_deal(jax.random.fold_in(keys[31], 71), 0)
    proj_in = normal_values(keys[4], (D, H, QKVG), D ** -0.5, 0.1875, ((0, 8), (1, 4)))
    decay_down = normal_values(keys[5], (D, RANK), D ** -0.5, 0.1875, ((0, 8),))
    decay_up = normal_values(keys[6], (RANK, H, DK), RANK ** -0.5, 1.5, ((1, 4),))
    decay_bias = jnp.clip(0.5 + 8.5 * jax.random.uniform(keys[7], (H, DK), jnp.float32) ** levels(keys[7], (H, DK), ((0, 4),), -0.2, 0.2), 0.5, 9.0)
    head_gain = jnp.clip(1.0 + 0.1 * jax.random.normal(keys[8], (DV,), jnp.float32), 0.5, 1.5)
    proj_out = normal_values(keys[9], (H, DV, D), D ** -0.5, 0.1875, ((0, 4), (2, 8)))
    block_gains = jnp.clip(1.0 + 0.1 * jax.random.normal(keys[10], (2, D), jnp.float32), 0.5, 1.5)
    ffn_in = normal_values(keys[11], (D, 2, FF), D ** -0.5, 0.1875, ((0, 8), (2, 4)))
    ffn_out = normal_values(keys[12], (FF, D), FF ** -0.5, 0.109375, ((0, 4), (1, 8)))
    first_proj_in = normal_values(keys[13], (D, H, QKVG), 0.0055, 0.078125, ((0, 8), (1, 4)), jnp.float32)
    second_proj_in = jnp.clip(jnp.exp(math.log(0.00053) - 1.4053426 * jax.random.uniform(keys[14], (D, H, QKVG), jnp.float32) ** levels(keys[14], (D, H, QKVG), ((0, 8), (1, 4)), -0.2, 0.2)), 0.00013, 0.00053)
    first_decay_down = normal_values(keys[15], (D, RANK), 0.0055, 0.078125, ((0, 8),), jnp.float32)
    second_decay_down = jnp.clip(jnp.exp(math.log(0.00053) - 1.4053426 * jax.random.uniform(keys[16], (D, RANK), jnp.float32) ** levels(keys[16], (D, RANK), ((0, 8),), -0.2, 0.2)), 0.00013, 0.00053)
    first_decay_up = normal_values(keys[17], (RANK, H, DK), 0.0055, 0.078125, ((1, 4),), jnp.float32)
    second_decay_up = jnp.clip(jnp.exp(math.log(5.999999848427251e-05) - 1.3862944 * jax.random.uniform(keys[18], (RANK, H, DK), jnp.float32) ** levels(keys[18], (RANK, H, DK), ((1, 4),), -0.2, 0.2)), 1.4999999621068127e-05, 5.999999848427251e-05)
    first_decay_bias = normal_values(keys[19], (H, DK), 0.0055, 0.078125, ((0, 4),), jnp.float32)
    second_decay_bias = jnp.clip(jnp.exp(math.log(0.00053) - 1.4053426 * jax.random.uniform(keys[20], (H, DK), jnp.float32) ** levels(keys[20], (H, DK), ((0, 4),), -0.2, 0.2)), 0.00013, 0.00053)
    first_head_gain = normal_values(keys[21], (DV,), 0.0055, 0.078125, (), jnp.float32)
    second_head_gain = jnp.clip(jnp.exp(jax.random.uniform(keys[22], (DV,), jnp.float32, math.log(0.00013), math.log(0.00053))), 0.00013, 0.00053)
    first_proj_out = normal_values(keys[23], (H, DV, D), 0.0055, 0.078125, ((0, 4), (2, 8)), jnp.float32)
    second_proj_out = jnp.clip(jnp.exp(math.log(0.00053) - 1.4053426 * jax.random.uniform(keys[24], (H, DV, D), jnp.float32) ** levels(keys[24], (H, DV, D), ((0, 4), (2, 8)), -0.2, 0.2)), 0.00013, 0.00053)
    first_block_gains = normal_values(keys[25], (2, D), 0.0055, 0.078125, (), jnp.float32)
    second_block_gains = jnp.clip(jnp.exp(jax.random.uniform(keys[26], (2, D), jnp.float32, math.log(0.00013), math.log(0.00053))), 0.00013, 0.00053)
    first_ffn_in = normal_values(keys[27], (D, 2, FF), 0.0055, 0.078125, ((0, 8), (2, 4)), jnp.float32)
    second_ffn_in = jnp.clip(jnp.exp(math.log(0.00053) - 1.4053426 * jax.random.uniform(keys[28], (D, 2, FF), jnp.float32) ** levels(keys[28], (D, 2, FF), ((0, 8), (2, 4)), -0.2, 0.2)), 0.00013, 0.00053)
    first_ffn_out = normal_values(keys[29], (FF, D), 0.0055, 0.078125, ((0, 4), (1, 8)), jnp.float32)
    second_ffn_out = jnp.clip(jnp.exp(math.log(0.00053) - 1.4053426 * jax.random.uniform(keys[30], (FF, D), jnp.float32) ** levels(keys[30], (FF, D), ((0, 4), (1, 8)), -0.2, 0.2)), 0.00013, 0.00053)
    return {"tokens": tokens, "cotangent": cotangent, "seq_extra": seq_extra, "deal": deal, "proj_in": proj_in, "decay_down": decay_down, "decay_up": decay_up, "decay_bias": decay_bias, "head_gain": head_gain, "proj_out": proj_out, "block_gains": block_gains, "ffn_in": ffn_in, "ffn_out": ffn_out, "first_proj_in": first_proj_in, "second_proj_in": second_proj_in, "first_decay_down": first_decay_down, "second_decay_down": second_decay_down, "first_decay_up": first_decay_up, "second_decay_up": second_decay_up, "first_decay_bias": first_decay_bias, "second_decay_bias": second_decay_bias, "first_head_gain": first_head_gain, "second_head_gain": second_head_gain, "first_proj_out": first_proj_out, "second_proj_out": second_proj_out, "first_block_gains": first_block_gains, "second_block_gains": second_block_gains, "first_ffn_in": first_ffn_in, "second_ffn_in": second_ffn_in, "first_ffn_out": first_ffn_out, "second_ffn_out": second_ffn_out}


norm_eps = 1e-06
highest_precision = lax.Precision.HIGHEST
learn_rate = 0.05
beta_one = 0.9
beta_two = 0.95
adam_eps = 1e-08
weight_decay = 0.1
clip_scale = 0.05
adam_step = 10
decay_scale = 16.0

@jax.custom_vjp
def low(v):
    return lax.optimization_barrier(v.astype(jnp.bfloat16)).astype(jnp.float32)

@jax.custom_vjp
def low_back(v):
    return v

def low_keep(v):
    return (low(v), None)

def low_pass(kept, grad):
    return (grad,)

def back_keep(v):
    return (v, None)

def back_low(kept, grad):
    return (low(grad),)
low.defvjp(low_keep, low_pass)
low_back.defvjp(back_keep, back_low)

def span_starts(seq_extra, span_ids):
    seq_spans = seq_extra + MIN_SPANS
    bounds = jnp.cumsum(seq_spans) - seq_spans
    return jnp.any(bounds[None, :] == span_ids[:, None], axis=1).astype(jnp.float32)

def deal_rows(rows, deal):
    spans = rows.reshape((NCHUNK, SPAN) + rows.shape[1:])
    return spans[deal].reshape(rows.shape)

def undeal_rows(rows, deal):
    spans = rows.reshape((NCHUNK, SPAN) + rows.shape[1:])
    return jnp.zeros_like(spans).at[deal].set(spans).reshape(rows.shape)

def span_step(state, inputs):
    query_rows, key_rows, value_rows, log_decay, start_flag = inputs
    previous_state = state * (1.0 - start_flag)
    running_decay = jnp.cumsum(log_decay, axis=0)
    causal = jnp.tril(jnp.ones((SPAN, SPAN), jnp.float32))
    across_spans = jnp.einsum('cgy,gye->cge', query_rows * jnp.exp(running_decay), previous_state, precision=highest_precision)
    decays = jnp.exp(jnp.minimum(running_decay[:, None] - running_decay[None, :], 0.0)) * causal[:, :, None, None]
    scores = jnp.einsum('thk,shk,tshk->hts', query_rows, key_rows, decays, precision=highest_precision)
    within = jnp.einsum('hts,shv->thv', scores, value_rows, precision=highest_precision)
    final_span_state = running_decay[-1]
    decayed_state = key_rows * jnp.exp(final_span_state[None] - running_decay)
    updated_state = jnp.exp(final_span_state)[:, :, None] * previous_state + jnp.einsum('dnr,dno->nro', decayed_state, value_rows, precision=highest_precision)
    return (updated_state, across_spans + within)

def forward(tokens, proj_in, decay_down, decay_up, decay_bias, head_gain, proj_out, block_gains, ffn_in, ffn_out, starts):
    heads_dev = H // N_TENSOR
    ffn_dev = FF // N_TENSOR
    blocks = tokens.reshape(TOKENS // TOK_DEV, TOK_DEV, D)

    def first_part(row_block):
        inv_first = lax.rsqrt(lax.optimization_barrier(jnp.mean(row_block * row_block, axis=-1, keepdims=True)) + norm_eps)
        normed = low(row_block * inv_first * block_gains[0])
        pieces = []
        for group_index in range(N_TENSOR):
            group_in = low_back(normed)
            weight = proj_in[:, group_index * heads_dev:(group_index + 1) * heads_dev]
            pieces.append(jnp.einsum('td,dhc->thc', group_in, weight, precision=highest_precision))
        project = low_back(jnp.concatenate(pieces, axis=1))
        rank_in = low(low_back(jnp.dot(normed, decay_down, precision=highest_precision)))
        logits = low_back(jnp.einsum('tr,rhk->thk', rank_in, decay_up, precision=highest_precision) + decay_bias)
        log_decay = jax.nn.log_sigmoid(logits) / decay_scale
        return (project, log_decay)
    project, log_decay = lax.map(jax.checkpoint(first_part), blocks)
    project = project.reshape(TOKENS, H, QKVG)
    log_decay = log_decay.reshape(TOKENS, H, DK)
    query_rows = project[..., :DK] * DK ** (-0.5)
    key_rows = project[..., DK:2 * DK]
    value_rows = project[..., 2 * DK:2 * DK + DV]
    gate_raw = project[..., 2 * DK + DV:]

    def by_span(array):
        return array.reshape(NCHUNK, SPAN, H, array.shape[-1])
    initial = jnp.zeros((H, DK, DV), jnp.float32)
    last_state, mixed = lax.scan(jax.checkpoint(span_step), initial, (by_span(query_rows), by_span(key_rows), by_span(value_rows), by_span(log_decay), starts))
    mixed = mixed.reshape(TOKENS // TOK_DEV, TOK_DEV, H, DV)
    gate_blocks = gate_raw.reshape(TOKENS // TOK_DEV, TOK_DEV, H, DV)

    def second_part(inputs):
        row_block, mixed_block, gate_block = inputs
        inv_head = lax.rsqrt(lax.optimization_barrier(jnp.mean(mixed_block * mixed_block, axis=-1, keepdims=True)) + norm_eps)
        gated = low(mixed_block * inv_head * head_gain * gate_block * jax.nn.sigmoid(gate_block))
        hidden = row_block
        for group_index in range(N_TENSOR):
            heads_part = gated[:, group_index * heads_dev:(group_index + 1) * heads_dev].reshape(TOK_DEV, heads_dev * DV)
            weight = proj_out[group_index * heads_dev:(group_index + 1) * heads_dev].reshape(heads_dev * DV, D)
            hidden = hidden + low(low_back(jnp.dot(heads_part, weight, precision=highest_precision)))
        inv_second = lax.rsqrt(lax.optimization_barrier(jnp.mean(hidden * hidden, axis=-1, keepdims=True)) + norm_eps)
        normed = low(hidden * inv_second * block_gains[1])
        output = hidden
        for group_index in range(N_TENSOR):
            group_in = low_back(normed)
            columns = slice(group_index * ffn_dev, (group_index + 1) * ffn_dev)
            gate_up = low_back(jnp.einsum('td,dgf->tgf', group_in, ffn_in[:, :, columns], precision=highest_precision))
            activated = low(jax.nn.silu(gate_up[:, 0]) * gate_up[:, 1])
            output = output + low(low_back(jnp.dot(activated, ffn_out[columns], precision=highest_precision)))
        return output
    output = lax.map(jax.checkpoint(second_part), (blocks, mixed, gate_blocks))
    return output.reshape(TOKENS, D)

def adam_update(weight, grad, first, second, factor, decay_rate):
    clipped = grad * factor
    first_new = beta_one * first + (1.0 - beta_one) * clipped
    second_new = beta_two * second + (1.0 - beta_two) * clipped * clipped
    first_hat = first_new / (1.0 - beta_one ** adam_step)
    second_hat = second_new / (1.0 - beta_two ** adam_step)
    change = -learn_rate * (first_hat / (jnp.sqrt(second_hat) + adam_eps) + decay_rate * weight)
    return (grad, first_new, second_new, change)

def reference(tokens, cotangent, seq_extra, deal, proj_in, decay_down, decay_up, decay_bias, head_gain, proj_out, block_gains, ffn_in, ffn_out, first_proj_in, second_proj_in, first_decay_down, second_decay_down, first_decay_up, second_decay_up, first_decay_bias, second_decay_bias, first_head_gain, second_head_gain, first_proj_out, second_proj_out, first_block_gains, second_block_gains, first_ffn_in, second_ffn_in, first_ffn_out, second_ffn_out):
    starts = span_starts(seq_extra, jnp.arange(NCHUNK, dtype=jnp.int32))
    dealt_tokens = deal_rows(tokens, deal)
    dealt_cotangent = deal_rows(cotangent, deal)
    inputs = [dealt_tokens.astype(jnp.float32), proj_in.astype(jnp.float32), decay_down.astype(jnp.float32), decay_up.astype(jnp.float32), decay_bias.astype(jnp.float32), head_gain.astype(jnp.float32), proj_out.astype(jnp.float32), block_gains.astype(jnp.float32), ffn_in.astype(jnp.float32), ffn_out.astype(jnp.float32)]

    def primal(tokens32, proj_in32, down32, up32, bias32, head32, out32, gains32, ffn_in32, ffn_out32):
        return forward(tokens32, proj_in32, down32, up32, bias32, head32, out32, gains32, ffn_in32, ffn_out32, starts)
    output, pullback = jax.vjp(primal, *inputs)
    grads = pullback(dealt_cotangent.astype(jnp.float32))
    block_out = undeal_rows(output, deal)
    token_grad = undeal_rows(grads[0], deal)
    total = jnp.float32(0.0)
    for index in range(1, 10):
        total = total + jnp.sum(grads[index] * grads[index])
    grad_norm = jnp.sqrt(total)
    clip_norm = clip_scale * math.sqrt(PARAMS)
    factor = jnp.minimum(1.0, clip_norm / (grad_norm + 1e-06))
    update_in = adam_update(inputs[1], grads[1], first_proj_in, second_proj_in, factor, weight_decay)
    update_down = adam_update(inputs[2], grads[2], first_decay_down, second_decay_down, factor, weight_decay)
    update_up = adam_update(inputs[3], grads[3], first_decay_up, second_decay_up, factor, weight_decay)
    update_bias = adam_update(inputs[4], grads[4], first_decay_bias, second_decay_bias, factor, 0.0)
    update_head = adam_update(inputs[5], grads[5], first_head_gain, second_head_gain, factor, 0.0)
    update_out = adam_update(inputs[6], grads[6], first_proj_out, second_proj_out, factor, weight_decay)
    update_gains = adam_update(inputs[7], grads[7], first_block_gains, second_block_gains, factor, 0.0)
    update_ffn_in = adam_update(inputs[8], grads[8], first_ffn_in, second_ffn_in, factor, weight_decay)
    update_ffn_out = adam_update(inputs[9], grads[9], first_ffn_out, second_ffn_out, factor, weight_decay)
    return (block_out, token_grad, grad_norm, update_in[0], update_in[1], update_in[2], update_in[3], update_down[0], update_down[1], update_down[2], update_down[3], update_up[0], update_up[1], update_up[2], update_up[3], update_bias[0], update_bias[1], update_bias[2], update_bias[3], update_head[0], update_head[1], update_head[2], update_head[3], update_out[0], update_out[1], update_out[2], update_out[3], update_gains[0], update_gains[1], update_gains[2], update_gains[3], update_ffn_in[0], update_ffn_in[1], update_ffn_in[2], update_ffn_in[3], update_ffn_out[0], update_ffn_out[1], update_ffn_out[2], update_ffn_out[3])
```

```python
import functools
import math

import jax
import jax.numpy as jnp
from jax import lax
from jax.experimental import pallas as pl
from jax.experimental.pallas import tpu as pltpu
from jax.sharding import Mesh
from jax.sharding import PartitionSpec as P

DK = 128
DV = 256
SPAN = 64
MIN_SPANS = 16
MAX_SPANS = 128
PARAMS = 12872448
TILE = 256
LEVELS = 6
HEAD = 2 * DK + 2 * DV
VMEM_LIMIT = 60 * 1024 * 1024
BF = jnp.bfloat16
F32 = jnp.float32

norm_eps = 1e-06
learn_rate = 0.05
beta_one = 0.9
beta_two = 0.95
adam_eps = 1e-08
weight_decay = 0.1
clip_scale = 0.05
adam_step = 10
decay_scale = 16.0
scaling = DK ** (-0.5)
ANY = pl.BlockSpec(memory_space=pl.ANY)
SMEM = pl.BlockSpec(memory_space=pltpu.SMEM)
VMEM = pl.BlockSpec(memory_space=pltpu.VMEM)


def dot(a, b, ca=1, cb=0):
    return lax.dot_general(a, b, (((ca,), (cb,)), ((), ())), preferred_element_type=F32)


def run(kernel, grid, in_specs, out_specs, out_shape, scratch, name, flops, moved):
    return pl.pallas_call(
        kernel,
        grid=grid,
        in_specs=in_specs,
        out_specs=out_specs,
        out_shape=out_shape,
        scratch_shapes=scratch,
        name=name,
        compiler_params=pltpu.CompilerParams(vmem_limit_bytes=VMEM_LIMIT),
        cost_estimate=pl.CostEstimate(
            flops=int(flops), bytes_accessed=int(moved), transcendentals=0
        ),
    )


def sds(*shape, dtype=F32):
    return jax.ShapeDtypeStruct(shape, dtype)


def rows_spec(cols, order=None):
    if order is None:
        return pl.BlockSpec((TILE, cols), lambda i: (i, 0))
    return pl.BlockSpec((TILE, cols), lambda i: (order - 1 - i, 0))


def whole_spec(*shape):
    zeros = (0,) * len(shape)
    return pl.BlockSpec(shape, lambda i: zeros, pipeline_mode=pl.Buffered(1))


def span_starts(seq_extra, span_ids):
    seq_spans = seq_extra + MIN_SPANS
    n = seq_extra.shape[0]
    earlier = jnp.tril(jnp.ones((n, n), jnp.int32), -1)
    bounds = jnp.sum(earlier * seq_spans[None, :], axis=1)
    return jnp.any(bounds[None, :] == span_ids[:, None], axis=1).astype(jnp.int32)


def deal_tables(deal, n_data, per_dev, capacity, my_index):
    table_grid = deal.reshape(n_data, per_dev)
    src_dev = table_grid // per_dev
    src_local = table_grid % per_dev
    my_source = lax.dynamic_index_in_dim(src_dev, my_index, 0, keepdims=False)
    earlier = jnp.tril(jnp.ones((per_dev, per_dev), jnp.int32), -1)
    same_source = (my_source[:, None] == my_source[None, :]).astype(jnp.int32)
    my_rank = jnp.sum(same_source * earlier, axis=1)
    recv_slot = my_source * capacity + my_rank
    owned_here = (src_dev == my_index).astype(jnp.int32)
    send_rank = jnp.sum(owned_here[:, None, :] * earlier[None], axis=2)
    slot_ids = jnp.arange(capacity, dtype=jnp.int32)
    send_hit = owned_here[:, :, None] * (
        send_rank[:, :, None] == slot_ids[None, None, :]
    ).astype(jnp.int32)
    send_local = jnp.sum(send_hit * src_local[:, :, None], axis=1)
    peer_ids = jnp.arange(n_data, dtype=jnp.int32)
    local_ids = jnp.arange(per_dev, dtype=jnp.int32)
    back_hit = (
        (my_source[None, None, :] == peer_ids[:, None, None])
        & (my_rank[None, None, :] == slot_ids[None, :, None])
    ).astype(jnp.int32)
    back_local = jnp.sum(back_hit * local_ids[None, None, :], axis=2)
    home_hit = owned_here[:, :, None] * (
        src_local[:, :, None] == local_ids[None, None, :]
    ).astype(jnp.int32)
    home_slot = jnp.sum(
        home_hit * (peer_ids[:, None, None] * capacity + send_rank[:, :, None]), axis=(0, 1)
    )
    return recv_slot, send_local.reshape(-1), back_local.reshape(-1), home_slot


def level_matrices():
    t = jnp.arange(TILE, dtype=jnp.int32)[:, None]
    u = jnp.arange(TILE, dtype=jnp.int32)[None, :]
    ups = []
    level = jnp.full((TILE, TILE), LEVELS + 1, jnp.int32)
    for l in range(LEVELS):
        block = SPAN >> l
        half = block // 2
        same = (t // block) == (u // block)
        mid = (t // block) * block + half
        right = (t >= mid) & (u >= mid) & (u <= t)
        left = (t < mid) & (u > t) & (u < mid)
        ups.append(same & (right | left))
        hit = same & (t % block >= half) & (u % block < half)
        level = jnp.where(hit, l, level)
    level = jnp.where(t == u, LEVELS, level)
    same = (t // SPAN) == (u // SPAN)
    ups.append(same & (u <= t))
    ups.append(same & (u > t))
    ups = jnp.stack(ups).astype(BF)
    return ups, jnp.swapaxes(ups, 1, 2), level, level.T


def send_pick_kernel(count, width, table, src, out, sems):
    col = pl.multiple_of(table[count], 128)

    def copy(i):
        return pltpu.make_async_copy(
            src.at[pl.ds(pl.multiple_of(table[i] * SPAN, SPAN), SPAN), pl.ds(col, width)],
            out.at[pl.ds(pl.multiple_of(i * SPAN, SPAN), SPAN), :],
            sems.at[i],
        )

    for i in range(count):
        copy(i).start()
    for i in range(count):
        copy(i).wait()


def send_pick(rows, table, col, width, name):
    count = table.shape[0]
    return pl.pallas_call(
        functools.partial(send_pick_kernel, count, width),
        in_specs=[SMEM, ANY],
        out_specs=VMEM,
        out_shape=sds(count * SPAN, width, dtype=rows.dtype),
        scratch_shapes=[pltpu.SemaphoreType.DMA((count,))],
        name=name,
        cost_estimate=pl.CostEstimate(
            flops=0, bytes_accessed=count * SPAN * width * 4, transcendentals=0
        ),
    )(jnp.concatenate([table, col.reshape(1)]), rows)


def split_pick_kernel(half, table, src, own, other):
    def body(i, _):
        to = pl.multiple_of(i * SPAN, SPAN)
        for out, at in ((own, i), (other, i + half)):
            out[pl.ds(to, SPAN), :] = src[pl.ds(pl.multiple_of(table[at] * SPAN, SPAN), SPAN), :]
        return 0

    lax.fori_loop(0, half, body, 0)


def split_pick(rows, table, name):
    half = table.shape[0] // 2
    out = sds(half * SPAN, rows.shape[1], dtype=rows.dtype)
    return pl.pallas_call(
        functools.partial(split_pick_kernel, half),
        in_specs=[SMEM, VMEM],
        out_specs=[VMEM, VMEM],
        out_shape=[out, out],
        name=name,
        cost_estimate=pl.CostEstimate(
            flops=0, bytes_accessed=rows.size * 4, transcendentals=0
        ),
    )(table, rows)


def join_pick_kernel(count, half, table, own, other, out):
    x = table[count]

    def body(i, _):
        local = table[i]
        low = pl.multiple_of(lax.rem(local, half) * SPAN, SPAN)
        here = (local >= half).astype(jnp.int32) == x
        to = pl.ds(pl.multiple_of(i * SPAN, SPAN), SPAN)

        @pl.when(here)
        def _():
            out[to, :] = own[pl.ds(low, SPAN), :]

        @pl.when(jnp.logical_not(here))
        def _():
            out[to, :] = other[pl.ds(low, SPAN), :]

        return 0

    lax.fori_loop(0, count, body, 0)


def join_pick(own, other, table, x, name):
    count = table.shape[0]
    half = own.shape[0] // SPAN
    return pl.pallas_call(
        functools.partial(join_pick_kernel, count, half),
        in_specs=[SMEM, VMEM, VMEM],
        out_specs=VMEM,
        out_shape=sds(count * SPAN, own.shape[1], dtype=own.dtype),
        name=name,
        cost_estimate=pl.CostEstimate(
            flops=0, bytes_accessed=count * SPAN * own.shape[1] * 4, transcendentals=0
        ),
    )(jnp.concatenate([table, x.reshape(1)]), own, other)


def home_kernel(count, table, *refs):
    srcs, out = refs[:-1], refs[-1]
    width = srcs[0].shape[1]

    def body(i, _):
        row = pl.multiple_of(table[i] * SPAN, SPAN)
        to = pl.multiple_of(i * SPAN, SPAN)
        for k, src in enumerate(srcs):
            col = pl.multiple_of(table[count + k], 128)
            out[pl.ds(to, SPAN), pl.ds(col, width)] = src[pl.ds(row, SPAN), :].astype(F32)
        return 0

    lax.fori_loop(0, count, body, 0)


def home(pieces, table, cols, name):
    count = table.shape[0]
    width = pieces[0].shape[1]
    total = width * len(pieces)
    return pl.pallas_call(
        functools.partial(home_kernel, count),
        in_specs=[SMEM] + [VMEM] * len(pieces),
        out_specs=VMEM,
        out_shape=sds(count * SPAN, total),
        name=name,
        compiler_params=pltpu.CompilerParams(vmem_limit_bytes=VMEM_LIMIT),
        cost_estimate=pl.CostEstimate(
            flops=0, bytes_accessed=count * SPAN * total * 6, transcendentals=0
        ),
    )(jnp.concatenate([table, jnp.stack(cols)]), *pieces)


def rms_scale(x):
    return lax.rsqrt(jnp.mean(x * x, axis=-1, keepdims=True) + norm_eps)


def distances(ups, log_decay):
    high = log_decay.astype(BF)
    lower = (log_decay - high.astype(F32)).astype(BF)
    return dot(ups, high) + dot(ups, lower)


def head_cols(h, part):
    start = h * HEAD + (0, DK, 2 * DK, 2 * DK + DV)[part]
    return slice(start, start + (DK, DK, DV, DV)[part])


def log_sigmoid(v):
    return jnp.minimum(v, 0.0) - jnp.log(1.0 + jnp.exp(-jnp.abs(v)))


def project_kernel(
    spans, n, ints, q0, q1, q2, q3, gain, w_in, w_down, up, bias, ups,
    src, normed, qkvg, log_decay, rank, packet, state, factor,
):
    step = pl.program_id(0)
    quarter = src.shape[1] // 4
    for k, piece in enumerate((q0, q1, q2, q3)):
        src[:, pl.ds(pl.multiple_of(ints[spans + k] * quarter, 128), quarter)] = piece[...]

    @pl.when(step == 0)
    def _():
        state[...] = jnp.zeros_like(state)
        factor[...] = jnp.ones_like(factor)

    x = src[...].astype(F32)
    nf = (x * rms_scale(x) * gain[...]).astype(BF)
    normed[...] = nf
    low = dot(nf, w_down[...], 1, 1).astype(BF)
    rank[...] = low
    logits = dot(low, up[...]) + bias[...]
    ld = log_sigmoid(logits) * (1.0 / decay_scale)
    log_decay[...] = ld
    proj = dot(nf, w_in[...], 1, 1)
    towards = jnp.exp(distances(ups[LEVELS + 1], ld))
    per_tile = TILE // SPAN
    for h in range(2):
        qkvg[:, head_cols(h, 0)] = (proj[:, head_cols(h, 0)] * scaling).astype(BF)
        qkvg[:, h * HEAD + DK : (h + 1) * HEAD] = proj[:, h * HEAD + DK : (h + 1) * HEAD].astype(BF)
    for j in range(per_tile):
        rows = slice(j * SPAN, (j + 1) * SPAN)
        keep = ints[step * per_tile + j].astype(F32)
        total = jnp.exp(jnp.sum(ld[rows], axis=0, keepdims=True)) * keep
        factor[0:1, :] = factor[0:1, :] * total
        for h in range(2):
            lanes = slice(h * DK, (h + 1) * DK)
            kd = (qkvg[rows, head_cols(h, 1)].astype(F32) * towards[rows, lanes]).astype(BF)
            state[h] = state[h] * total[:, lanes] + dot(qkvg[rows, head_cols(h, 2)], kd, 0, 0)

    @pl.when(step == n - 1)
    def _():
        packet[0:DV] = state[0]
        packet[DV : 2 * DV] = state[1]
        packet[2 * DV :] = jnp.zeros((16, DK), F32)
        packet[2 * DV : 2 * DV + 1] = factor[0:1, 0:DK]
        packet[2 * DV + 1 : 2 * DV + 2] = factor[0:1, DK : 2 * DK]


def within_kernel(qkvg, log_decay, ups, level, within):
    ld = log_decay[...]
    high = ld.astype(BF)
    lower = (ld - high.astype(F32)).astype(BF)
    lev = level[...]
    scores = [None, None]
    for l in range(LEVELS + 1):
        if l < LEVELS:
            x = jnp.exp(dot(ups[l], high) + dot(ups[l], lower))
        for h in range(2):
            q, k = qkvg[:, head_cols(h, 0)], qkvg[:, head_cols(h, 1)]
            if l < LEVELS:
                xh = x[:, h * DK : (h + 1) * DK]
                q = (q.astype(F32) * xh).astype(BF)
                k = (k.astype(F32) * xh).astype(BF)
            s = dot(q, k, 1, 1)
            scores[h] = jnp.where(lev == l, s, 0.0 if l == 0 else scores[h])
    for h in range(2):
        within[:, h * DV : (h + 1) * DV] = dot(scores[h].astype(BF), qkvg[:, head_cols(h, 2)])


def mix_kernel(
    spans, ints, qkvg, log_decay, within, entering, ups, head_gain, w_out,
    mixed, gated, attn, before, state,
):
    step = pl.program_id(0)
    per_tile = TILE // SPAN

    @pl.when(step == 0)
    def _():
        state[0] = entering[0:DV]
        state[1] = entering[DV : 2 * DV]

    ld = log_decay[...]
    since = jnp.exp(distances(ups[LEVELS], ld))
    towards = jnp.exp(distances(ups[LEVELS + 1], ld))
    for j in range(per_tile):
        rows = slice(j * SPAN, (j + 1) * SPAN)
        keep = ints[step * per_tile + j].astype(F32)
        for h in range(2):
            lanes = slice(h * DK, (h + 1) * DK)
            values = slice(h * DV, (h + 1) * DV)
            prev = state[h] * keep
            prev_low = prev.astype(BF)
            before[j, h] = prev_low
            qd = (qkvg[rows, head_cols(h, 0)].astype(F32) * since[rows, lanes]).astype(BF)
            kd = (qkvg[rows, head_cols(h, 1)].astype(F32) * towards[rows, lanes]).astype(BF)
            mixed[rows, values] = within[rows, values] + dot(qd, prev_low, 1, 1)
            last = since[j * SPAN + SPAN - 1 : j * SPAN + SPAN, lanes]
            state[h] = prev * last + dot(qkvg[rows, head_cols(h, 2)], kd, 0, 0)
    for h in range(2):
        values = slice(h * DV, (h + 1) * DV)
        m = mixed[:, values]
        g = qkvg[:, head_cols(h, 3)].astype(F32)
        y = m * rms_scale(m) * head_gain[...] * g * jax.nn.sigmoid(g)
        gated[:, values] = y.astype(BF)
    attn[...] = dot(gated[...], w_out[...]).astype(BF)


def ffn_kernel(
    ints, src, attn_a, attn_b, c0, c1, c2, c3, gain, w_gate, w_up, w_out,
    hidden, normed, act, grad_gu, cot, keep_out, send_out, grad_second,
    part,
):
    quarter = cot.shape[1] // 4
    for k, piece in enumerate((c0, c1, c2, c3)):
        cot[:, pl.ds(pl.multiple_of(ints[k] * quarter, 128), quarter)] = piece[...]
    hid = src[...].astype(F32) + (attn_a[...].astype(F32) + attn_b[...].astype(F32))
    hidden[...] = hid
    ns = (hid * rms_scale(hid) * gain[...]).astype(BF)
    normed[...] = ns
    gate = dot(ns, w_gate[...], 1, 1)
    upper = dot(ns, w_up[...], 1, 1)
    sig = jax.nn.sigmoid(gate)
    swish = gate * sig
    low = (swish * upper).astype(BF)
    act[...] = low
    part[...] = dot(low, w_out[...]).astype(BF)
    core = ints[4]
    for h in range(2):
        mine = pl.multiple_of((2 * h + core) * quarter, 128)
        theirs = pl.multiple_of((2 * h + 1 - core) * quarter, 128)
        keep_out[:, h * quarter : (h + 1) * quarter] = part[:, pl.ds(mine, quarter)]
        send_out[:, h * quarter : (h + 1) * quarter] = part[:, pl.ds(theirs, quarter)]
    ga = dot(cot[...], w_out[...], 1, 1)
    f = gate.shape[1]
    gg = (ga * upper * sig * (1.0 + gate * (1.0 - sig))).astype(BF)
    gu = (ga * swish).astype(BF)
    grad_gu[:, :f] = gg
    grad_gu[:, f:] = gu
    grad_second[...] = (dot(gg, w_gate[...]) + dot(gu, w_up[...])).astype(BF)


def ring_dp(p, n):
    p = lax.rem(p + 2 * n, n)
    return jnp.where(p < n // 2, 2 * p, 2 * (n - 1 - p) + 1)


def weight_grad_into(acc, lhs, rhs, chunk):
    def body(i, _):
        at = pl.multiple_of(i * chunk, chunk)
        acc[pl.ds(at, chunk), :] = dot(lhs[:, pl.ds(at, chunk)], rhs[...], 0, 0).astype(BF)
        return 0

    lax.fori_loop(0, acc.shape[0] // chunk, body, 0)


def grad_pair_kernel(n, f, ints, grad_gu, normed, own, *rest):
    others, (acc,) = rest[:n], rest[n:]
    r, x = ints[5], ints[6]
    w = own.shape[2]
    for m in range(2):
        weight_grad_into(acc, grad_gu.at[:, pl.ds(m * 2 * f, 2 * f)], normed, 128)
        for s in range(1, n + 1):
            col = pl.multiple_of(ring_dp(r - s if m == 0 else r + s, n) * w, 128)
            mine = pl.multiple_of(x * f, 16)
            theirs = pl.multiple_of((1 - x) * f, 16)
            own[s - 1, m * f : (m + 1) * f, :] = acc[pl.ds(mine, f), pl.ds(col, w)]
            others[s - 1][m * f : (m + 1) * f, :] = acc[pl.ds(theirs, f), pl.ds(col, w)]


def to_blocks(n, ints, acc, out, f):
    r = ints[5]
    w = out.shape[3]
    for s in range(1, n + 1):
        for h in range(2):
            col = pl.multiple_of(ring_dp(r - s if h == 0 else r + s, n) * w, 128)
            out[s - 1, h] = acc[h * f : (h + 1) * f, pl.ds(col, w)]


def grad_blocks_kernel(n, f, ints, lhs, rhs, out, acc):
    weight_grad_into(acc, lhs, rhs, 128)
    to_blocks(n, ints, acc, out, f)


def grad_plain_kernel(f, ints, lhs, rhs, out):
    weight_grad_into(out, lhs, rhs, 128)


def out_back_kernel(
    spans, n, nd, ints, hidden, cot, gs_a, gs_b, gain, w_out, gated, mixed, qkvg, log_decay, head_gain, ups,
    grad_hidden, grad_mixed, grad_gate, w_grad, gain_grad, head_grad, packet,
    acc, state, gain_sum, head_sum,
):
    step = pl.program_id(0)
    tile = n - 1 - step
    per_tile = TILE // SPAN

    @pl.when(step == 0)
    def _():
        acc[...] = jnp.zeros_like(acc)
        state[...] = jnp.zeros_like(state)
        gain_sum[...] = jnp.zeros_like(gain_sum)
        head_sum[...] = jnp.zeros_like(head_sum)

    gs = gs_a[...].astype(F32) + gs_b[...].astype(F32)
    hid = hidden[...]
    inv = rms_scale(hid)
    normal = hid * inv
    gain_sum[0:1, :] += jnp.sum(gs * normal, axis=0, keepdims=True)
    e = gs * gain[...]
    gh = cot[...].astype(F32) + inv * (e - normal * jnp.mean(e * normal, axis=-1, keepdims=True))
    grad_hidden[...] = gh
    low = gh.astype(BF)
    acc[...] += dot(gated[...], low, 0, 0)
    gg = dot(low, w_out[...], 1, 1)
    for h in range(2):
        values = slice(h * DV, (h + 1) * DV)
        m = mixed[:, values]
        inv_head = rms_scale(m)
        nh = m * inv_head
        g = qkvg[:, head_cols(h, 3)].astype(F32)
        sig = jax.nn.sigmoid(g)
        w = g * sig
        gd = gg[:, values]
        head_sum[0:1, :] += jnp.sum(gd * nh * w, axis=0, keepdims=True)
        gn = gd * head_gain[...]
        grad_gate[:, values] = (gn * nh * sig * (1.0 + g * (1.0 - sig))).astype(BF)
        gn = gn * w
        gm = inv_head * (gn - nh * jnp.mean(gn * nh, axis=-1, keepdims=True))
        grad_mixed[:, values] = gm.astype(BF)
    since = jnp.exp(distances(ups[LEVELS], log_decay[...]))
    for j in reversed(range(per_tile)):
        rows = slice(j * SPAN, (j + 1) * SPAN)
        keep = ints[7 + tile * per_tile + j].astype(F32)
        for h in range(2):
            lanes = slice(h * DK, (h + 1) * DK)
            values = slice(h * DV, (h + 1) * DV)
            qd = (qkvg[rows, head_cols(h, 0)].astype(F32) * since[rows, lanes]).astype(BF)
            last = since[j * SPAN + SPAN - 1 : j * SPAN + SPAN, lanes]
            state[h] = keep * (state[h] * last + dot(grad_mixed[rows, values], qd, 0, 0))

    @pl.when(step == n - 1)
    def _():
        packet[0:DV] = state[0]
        packet[DV : 2 * DV] = state[1]
        gain_grad[...] = gain_sum[...]
        head_grad[...] = head_sum[...]
        low_acc = acc[...].astype(BF)
        if nd is None:
            w_grad[...] = low_acc
        else:
            r = ints[5]
            width = w_grad.shape[3]
            acc[...] = low_acc.astype(F32)
            for s in range(1, nd + 1):
                for h in range(2):
                    col = pl.multiple_of(ring_dp(r - s if h == 0 else r + s, nd) * width, 128)
                    w_grad[s - 1, h] = acc[h * DV : (h + 1) * DV, pl.ds(col, width)].astype(BF)


def within_back_kernel(qkvg, log_decay, grad_mixed, ups, downs, level, level_t, grad_qk, grad_v, grad_ld):
    ld = log_decay[...]
    high = ld.astype(BF)
    lower = (ld - high.astype(F32)).astype(BF)
    lev, lev_t = level[...], level_t[...]
    gd, gd_t = [], []
    for h in range(2):
        v, gm = qkvg[:, head_cols(h, 2)], grad_mixed[:, h * DV : (h + 1) * DV]
        gd.append(dot(gm, v, 1, 1))
        gd_t.append(dot(v, gm, 1, 1))
    scores_t = [None, None]
    grad_q, grad_k = [None, None], [None, None]
    for l in range(LEVELS + 1):
        if l < LEVELS:
            x = jnp.exp(dot(ups[l], high) + dot(ups[l], lower))
        parts = []
        for h in range(2):
            q, k = qkvg[:, head_cols(h, 0)], qkvg[:, head_cols(h, 1)]
            if l < LEVELS:
                xh = x[:, h * DK : (h + 1) * DK]
                qf, kf = q.astype(F32) * xh, k.astype(F32) * xh
                q, k = qf.astype(BF), kf.astype(BF)
            s = dot(k, q, 1, 1)
            scores_t[h] = jnp.where(lev_t == l, s, 0.0 if l == 0 else scores_t[h])
            here = jnp.where(lev == l, gd[h], 0.0).astype(BF)
            here_t = jnp.where(lev_t == l, gd_t[h], 0.0).astype(BF)
            dq, dk = dot(here, k), dot(here_t, q)
            if l < LEVELS:
                parts.append(qf * dq + kf * dk)
                dq, dk = dq * xh, dk * xh
            grad_q[h] = dq if l == 0 else grad_q[h] + dq
            grad_k[h] = dk if l == 0 else grad_k[h] + dk
        if l < LEVELS:
            both = dot(downs[l], jnp.concatenate(parts, axis=1).astype(BF))
            total = both if l == 0 else total + both
    grad_ld[...] = total
    for h in range(2):
        grad_qk[:, 2 * h * DK : (2 * h + 1) * DK] = grad_q[h]
        grad_qk[:, (2 * h + 1) * DK : (2 * h + 2) * DK] = grad_k[h]
        grad_v[:, h * DV : (h + 1) * DV] = dot(
            scores_t[h].astype(BF), grad_mixed[:, h * DV : (h + 1) * DV]
        )


def project_back_kernel(
    n, ints, qkvg, log_decay, grad_mixed, before, leaving, grad_qk, grad_v, grad_ld, grad_gate, rank, up, bias,
    ups, downs, w_in,
    grad_project, grad_first, rank_part, up_grad, bias_grad,
    state, up_sum, bias_sum, d_since, d_towards, ld_sum,
):
    step = pl.program_id(0)
    tile = n - 1 - step
    per_tile = TILE // SPAN

    @pl.when(step == 0)
    def _():
        state[0] = leaving[0:DV]
        state[1] = leaving[DV : 2 * DV]
        up_sum[...] = jnp.zeros_like(up_sum)
        bias_sum[...] = jnp.zeros_like(bias_sum)

    ld = log_decay[...]
    since = jnp.exp(distances(ups[LEVELS], ld))
    towards = jnp.exp(distances(ups[LEVELS + 1], ld))
    for j in reversed(range(per_tile)):
        rows = slice(j * SPAN, (j + 1) * SPAN)
        keep = ints[7 + tile * per_tile + j].astype(F32)
        for h in range(2):
            lanes = slice(h * DK, (h + 1) * DK)
            values = slice(h * DV, (h + 1) * DV)
            gm = grad_mixed[rows, values]
            v = qkvg[rows, head_cols(h, 2)]
            qd = qkvg[rows, head_cols(h, 0)].astype(F32) * since[rows, lanes]
            kd = qkvg[rows, head_cols(h, 1)].astype(F32) * towards[rows, lanes]
            prev = before[j, h]
            after = state[h]
            after_low = after.astype(BF)
            dq = dot(gm, prev)
            dk = dot(v, after_low)
            d_since[rows, lanes] = (qd * dq).astype(BF)
            d_towards[rows, lanes] = (kd * dk).astype(BF)
            dq = grad_qk[rows, 2 * h * DK : (2 * h + 1) * DK] + dq * since[rows, lanes]
            dk = grad_qk[rows, (2 * h + 1) * DK : (2 * h + 2) * DK] + dk * towards[rows, lanes]
            dv = grad_v[rows, values] + dot(kd.astype(BF), after_low, 1, 1)
            grad_project[rows, head_cols(h, 0)] = (dq * scaling).astype(BF)
            grad_project[rows, head_cols(h, 1)] = dk.astype(BF)
            grad_project[rows, head_cols(h, 2)] = dv.astype(BF)
            grad_project[rows, head_cols(h, 3)] = grad_gate[rows, values]
            last = since[j * SPAN + SPAN - 1 : j * SPAN + SPAN, lanes]
            d_last = last * jnp.sum(prev.astype(F32) * after, axis=0, keepdims=True)
            ld_sum[rows, lanes] = grad_ld[rows, lanes] + d_last
            state[h] = keep * (after * last + dot(gm, qd.astype(BF), 0, 0))
    d_log = ld_sum[...] + dot(downs[LEVELS], d_since[...]) + dot(downs[LEVELS + 1], d_towards[...])
    logits = dot(rank[...], up[...]) + bias[...]
    gl = (d_log * (1.0 / decay_scale) * jax.nn.sigmoid(-logits)).astype(BF)
    up_sum[...] += dot(rank[...], gl, 0, 0)
    bias_sum[0:1, :] += jnp.sum(gl.astype(F32), axis=0, keepdims=True)
    rank_part[...] = dot(up[...], gl, 1, 1)
    grad_first[...] = dot(grad_project[...], w_in[...]).astype(BF)

    @pl.when(step == n - 1)
    def _():
        up_grad[...] = up_sum[...]
        bias_grad[...] = bias_sum[...]


def source_back_kernel(
    n, ints, src, normed, gf_a, gf_b, rank_a, rank_b, w_down, gain, grad_hidden,
    own, other, down_grad, gain_grad,
    dealt, down_sum, gain_sum,
):
    step = pl.program_id(0)

    @pl.when(step == 0)
    def _():
        down_sum[...] = jnp.zeros_like(down_sum)
        gain_sum[...] = jnp.zeros_like(gain_sum)

    low = (rank_a[...] + rank_b[...]).astype(BF)
    gf = gf_a[...].astype(F32) + gf_b[...].astype(F32) + dot(low, w_down[...], 0, 0)
    x = src[...].astype(F32)
    inv = rms_scale(x)
    normal = x * inv
    gain_sum[0:1, :] += jnp.sum(gf * normal, axis=0, keepdims=True)
    e = gf * gain[...]
    dealt[...] = (
        grad_hidden[...] + inv * (e - normal * jnp.mean(e * normal, axis=-1, keepdims=True))
    ).astype(BF)
    down_sum[...] += dot(low, normed[...])
    quarter = own.shape[1]
    own[...] = dealt[:, pl.ds(pl.multiple_of(ints[0] * quarter, 128), quarter)]
    other[...] = dealt[:, pl.ds(pl.multiple_of(ints[1] * quarter, 128), quarter)]

    @pl.when(step == n - 1)
    def _():
        down_grad[...] = down_sum[...]
        gain_grad[...] = gain_sum[...]


def block_out_kernel(ints, hidden, keep_out, recv_out, own, other):
    x, core = ints[6], ints[4]
    quarter = own.shape[1]
    for target, half in ((own, x), (other, 1 - x)):
        at = pl.multiple_of((2 * half + core) * quarter, 128)
        pair = pl.multiple_of(half * quarter, 128)
        share = keep_out[:, pl.ds(pair, quarter)].astype(F32) + recv_out[:, pl.ds(pair, quarter)].astype(F32)
        target[...] = (hidden[:, pl.ds(at, quarter)] + share).astype(BF)


def ring_perms(n):
    order = [2 * p for p in range(n // 2)] + [2 * (n - 1 - p) + 1 for p in range(n // 2, n)]
    forward = [(order[p], order[(p + 1) % n]) for p in range(n)]
    return forward, [(b, a) for a, b in forward]


def place_kernel(count, moves, ints, *refs):
    pieces, outs, sems = refs[:count], refs[count:-1], refs[-1]
    copies = []
    for k, (piece, low, rows, out, row_at, col_at) in enumerate(moves):
        w = pieces[piece].shape[1]
        copies.append(
            pltpu.make_async_copy(
                pieces[piece].at[pl.ds(low, rows), :],
                outs[out].at[
                    pl.ds(pl.multiple_of(ints[row_at], 16), rows),
                    pl.ds(pl.multiple_of(ints[col_at], 128), w),
                ],
                sems.at[k],
            )
        )
    for c in copies:
        c.start()
    for c in copies:
        c.wait()


def place(pieces, moves, ints, outs, name):
    return pl.pallas_call(
        functools.partial(place_kernel, len(pieces), moves),
        in_specs=[SMEM] + [ANY] * len(pieces),
        out_specs=[VMEM] * len(outs),
        out_shape=outs,
        scratch_shapes=[pltpu.SemaphoreType.DMA((len(moves),))],
        name=name,
        compiler_params=pltpu.CompilerParams(vmem_limit_bytes=VMEM_LIMIT),
        cost_estimate=pl.CostEstimate(
            flops=0, bytes_accessed=4 * sum(o.size for o in outs), transcendentals=0
        ),
    )(ints, *pieces)


def ring_gather(forward_piece, backward_piece, n):
    forward, backward = ring_perms(n)
    ahead, behind = [forward_piece], [backward_piece]
    for _ in range(n - 1):
        ahead.append(lax.ppermute(ahead[-1], "dp", forward))
        behind.append(lax.ppermute(behind[-1], "dp", backward))
    return ahead, behind


def ring_sum(first, second, n):
    forward, backward = ring_perms(n)
    a, b = first(1).astype(BF), second(1).astype(BF)
    for s in range(1, n):
        a = lax.ppermute(a, "dp", forward).astype(F32) + first(s + 1).astype(F32)
        b = lax.ppermute(b, "dp", backward).astype(F32) + second(s + 1).astype(F32)
        if s < n - 1:
            a, b = a.astype(BF), b.astype(BF)
    return a, b


def combine(earlier, later):
    fe, fl = earlier[2 * DV : 2 * DV + 2], later[2 * DV : 2 * DV + 2]
    se, sl = (a[: 2 * DV].reshape(2, DV, DK) for a in (earlier, later))
    s = fl[:, None, :] * se + sl
    return jnp.concatenate(
        [s.reshape(2 * DV, DK), fl * fe, jnp.zeros((14, DK), F32)], axis=0
    )


def carried(packet, count, reach, ahead):
    def shifted(value, k):
        if ahead:
            perm = [(i, i + k) for i in range(count - k)]
        else:
            perm = [(i + k, i) for i in range(count - k)]
        return lax.ppermute(value.astype(BF), ("dp", "x"), perm).astype(F32)

    width = 1
    while 2 * width < reach:
        packet = combine(shifted(packet, width), packet)
        width *= 2
    return combine(shifted(packet, 1 + width), shifted(packet, 1))


def all_sum(value, axes, sizes):
    for axis, size in zip(axes, sizes):
        bit = 1
        while bit < size:
            value = value + lax.ppermute(value, axis, [(i, i ^ bit) for i in range(size)])
            bit *= 2
    return value


def square_sum(array):
    return jnp.sum(array * array)


def adam_update(weight, grad, first, second, factor, decay_rate):
    clipped = grad * factor
    first_new = beta_one * first + (1.0 - beta_one) * clipped
    second_new = beta_two * second + (1.0 - beta_two) * clipped * clipped
    first_hat = first_new / (1.0 - beta_one**adam_step)
    second_hat = second_new / (1.0 - beta_two**adam_step)
    master = weight.astype(F32)
    change = -learn_rate * (first_hat / (jnp.sqrt(second_hat) + adam_eps) + decay_rate * master)
    return (grad, first_new, second_new, change)


def swap(value, axis):
    return lax.ppermute(value, axis, [(0, 1), (1, 0)])


def on_device(
    tokens, cotangent, seq_extra, deal, proj_in, decay_down, decay_up, decay_bias, head_gain, proj_out, block_gains,
    ffn_in, ffn_out, first_proj_in, second_proj_in, first_decay_down, second_decay_down, first_decay_up,
    second_decay_up, first_decay_bias, second_decay_bias, first_head_gain, second_head_gain, first_proj_out,
    second_proj_out, first_block_gains, second_block_gains, first_ffn_in, second_ffn_in, first_ffn_out, second_ffn_out,
):
    d = tokens.shape[1]
    nd = lax.axis_size("dp")
    dp, x, core = lax.axis_index("dp"), lax.axis_index("x"), lax.axis_index("core")
    tensor = 2 * x + core
    per_dev = tokens.shape[0] // SPAN
    spans = per_dev // 2
    rows = spans * SPAN
    tiles = rows // TILE
    capacity = -(-per_dev // nd)
    quarter = d // 4
    f = ffn_out.shape[0]
    w = d // nd
    ring = w % 128 == 0
    place_in_ring = jnp.where(dp % 2 == 0, dp // 2, nd - 1 - dp // 2)

    recv_slot, send_local, back_local, home_slot = deal_tables(deal, nd, per_dev, capacity, dp)
    mine = lax.dynamic_slice_in_dim(recv_slot, x * spans, spans)
    theirs = lax.dynamic_slice_in_dim(recv_slot, (1 - x) * spans, spans)
    split_table = jnp.concatenate([mine, theirs])
    span_ids = (dp * 2 + x) * spans + jnp.arange(spans, dtype=jnp.int32)
    keep = 1 - span_starts(seq_extra, span_ids)
    other_quarter = 2 * (1 - x) + core
    quarters = jnp.stack([tensor, other_quarter, 2 * x + 1 - core, 2 * (1 - x) + 1 - core])
    ints = jnp.concatenate([quarters, jnp.stack([core, place_in_ring, x]), keep])
    ints = ints.astype(jnp.int32)
    span_ints = jnp.concatenate([keep, quarters]).astype(jnp.int32)
    ups, downs, level, level_t = level_matrices()

    def dealt(array, name):
        picked = send_pick(array, send_local, tensor * quarter, quarter, name + "_send")
        arrived = lax.all_to_all(picked, "dp", split_axis=0, concat_axis=0, tiled=True)
        own, other = split_pick(arrived, split_table, name + "_split")
        across = swap(other, "x")
        return own, across, swap(own, "core"), swap(across, "core")

    down_t = decay_down.T
    shard_p = jnp.concatenate([proj_in.reshape(w, HEAD).T, proj_out.reshape(DV, w), down_t], axis=0)
    shard_f = jnp.concatenate([ffn_in.reshape(w, 2 * f).T, ffn_out], axis=0)

    pieces_t = dealt(tokens, "tokens")
    shard_p_other = swap(shard_p, "x")
    if ring:
        own_p, other_p = ring_gather(shard_p, shard_p_other, nd)
        moves, table = [], [jnp.int32(0), x * HEAD, (1 - x) * HEAD, x * DV, (1 - x) * DV]
        for j in range(nd):
            table.append(ring_dp(place_in_ring - j, nd) * w)
            table.append(ring_dp(place_in_ring + j, nd) * w)
            moves.append((j, 0, HEAD, 0, 1, 5 + 2 * j))
            moves.append((j, HEAD, DV, 1, 3, 5 + 2 * j))
            moves.append((j, HEAD + DV, 16, 2, 0, 5 + 2 * j))
            moves.append((nd + j, 0, HEAD, 0, 2, 6 + 2 * j))
            moves.append((nd + j, HEAD, DV, 1, 4, 6 + 2 * j))
        w_in, w_out, w_down = place(
            own_p + other_p,
            moves,
            jnp.stack(table).astype(jnp.int32),
            [sds(2 * HEAD, d, dtype=BF), sds(2 * DV, d, dtype=BF), sds(16, d, dtype=BF)],
            "place_proj",
        )
        half = (3 * f) // 2
        a, b = ring_gather(shard_f[:half], shard_f[half:], nd)
        ax, bx = [swap(p, "x") for p in a], [swap(p, "x") for p in b]
        moves, table = [], [x * f, (1 - x) * f, x * f + f // 2, (1 - x) * f + f // 2]
        for j in range(nd):
            table.append(ring_dp(place_in_ring - j, nd) * w)
            table.append(ring_dp(place_in_ring + j, nd) * w)
            for side in range(2):
                moves.append((side * 2 * nd + j, 0, f, 0, side, 4 + 2 * j))
                moves.append((side * 2 * nd + j, f, f // 2, 1, side, 4 + 2 * j))
                moves.append((side * 2 * nd + nd + j, 0, f // 2, 1, 2 + side, 5 + 2 * j))
                moves.append((side * 2 * nd + nd + j, f // 2, f, 2, side, 5 + 2 * j))
        f_gate, f_up, f_out = place(
            a + b + ax + bx,
            moves,
            jnp.stack(table).astype(jnp.int32),
            [sds(2 * f, d, dtype=BF)] * 3,
            "place_ffn",
        )
    else:

        def gathered(shard):
            return jnp.swapaxes(lax.all_gather(shard, "dp", axis=0), 0, 1).reshape(shard.shape[0], d)

        own_p, other_p = gathered(shard_p), gathered(shard_p_other)
        low = jnp.where(x == 0, own_p, other_p)
        high = jnp.where(x == 0, other_p, own_p)
        w_in = jnp.concatenate([low[:HEAD], high[:HEAD]])
        w_out = jnp.concatenate([low[HEAD : HEAD + DV], high[HEAD : HEAD + DV]])
        w_down = own_p[HEAD + DV :]
        own_f, other_f = gathered(shard_f), gathered(swap(shard_f, "x"))
        low = jnp.where(x == 0, own_f, other_f)
        high = jnp.where(x == 0, other_f, own_f)
        f_gate, f_up, f_out = (
            jnp.concatenate([low[k * f : (k + 1) * f], high[k * f : (k + 1) * f]]) for k in range(3)
        )

    up_own = decay_up.reshape(16, DK)
    up_other = swap(up_own, "x")
    bias_own = decay_bias.reshape(1, DK)
    bias_other = swap(bias_own, "x")

    def both(own, other):
        return jnp.where(
            x == 0, jnp.concatenate([own, other], axis=1), jnp.concatenate([other, own], axis=1)
        )

    up = both(up_own, up_other)
    bias = both(bias_own, bias_other)
    gain_one, gain_two = block_gains[0:1], block_gains[1:2]
    head_row = head_gain.reshape(1, DV)

    def tall(cols, dtype=BF):
        return sds(rows, cols, dtype=dtype)

    nlev = LEVELS + 2
    src, normed_first, qkvg, log_decay, rank, packet = run(
        functools.partial(project_kernel, spans, tiles),
        (tiles,),
        [SMEM] + [rows_spec(quarter)] * 4
        + [whole_spec(1, d), whole_spec(2 * HEAD, d), whole_spec(16, d), whole_spec(16, 2 * DK),
           whole_spec(1, 2 * DK), whole_spec(nlev, TILE, TILE)],
        [rows_spec(d), rows_spec(d), rows_spec(2 * HEAD), rows_spec(2 * DK), rows_spec(16),
         whole_spec(2 * DV + 16, DK)],
        [tall(d), tall(d), tall(2 * HEAD), tall(2 * DK, F32), tall(16), sds(2 * DV + 16, DK)],
        [pltpu.VMEM((2, DV, DK), F32), pltpu.VMEM((8, 2 * DK), F32)],
        "project", 2 * rows * d * 2 * HEAD, rows * d * 10,
    )(span_ints, *pieces_t, gain_one, w_in, w_down, up, bias, ups)

    sequence = nd * 2
    reach = -(-(MAX_SPANS - 1) // spans)
    entering = carried(packet, sequence, reach, True)

    within = run(
        within_kernel, (tiles,),
        [rows_spec(2 * HEAD), rows_spec(2 * DK), whole_spec(nlev, TILE, TILE), whole_spec(TILE, TILE)],
        rows_spec(2 * DV), tall(2 * DV, F32), [],
        "within", rows * 2 * 8 * 256 * 256, rows * 2 * HEAD * 4,
    )(qkvg, log_decay, ups, level)

    mixed, gated, attn, before = run(
        functools.partial(mix_kernel, spans), (tiles,),
        [SMEM, rows_spec(2 * HEAD), rows_spec(2 * DK), rows_spec(2 * DV), whole_spec(2 * DV + 16, DK),
         whole_spec(nlev, TILE, TILE), whole_spec(1, DV), whole_spec(2 * DV, d)],
        [rows_spec(2 * DV), rows_spec(2 * DV), rows_spec(d),
         pl.BlockSpec((TILE // SPAN, 2, DV, DK), lambda i: (i, 0, 0, 0))],
        [tall(2 * DV, F32), tall(2 * DV), tall(d), sds(spans, 2, DV, DK, dtype=BF)],
        [pltpu.VMEM((2, DV, DK), F32)],
        "mix", 2 * rows * d * 2 * DV, rows * d * 10,
    )(span_ints, qkvg, log_decay, within, entering, ups, head_row, w_out)

    pieces_c = dealt(cotangent, "cotangent")
    attn_other = swap(attn, "core")
    ff = 2 * f
    hidden, normed_second, act, grad_gu, cot, keep_out, send_out, grad_second = run(
        ffn_kernel, (tiles,),
        [SMEM] + [rows_spec(d)] * 3 + [rows_spec(quarter)] * 4
        + [whole_spec(1, d), whole_spec(ff, d), whole_spec(ff, d), whole_spec(ff, d)],
        [rows_spec(d), rows_spec(d), rows_spec(ff), rows_spec(2 * ff), rows_spec(d), rows_spec(2 * quarter),
         rows_spec(2 * quarter), rows_spec(d)],
        [tall(d, F32), tall(d), tall(ff), tall(2 * ff), tall(d), tall(2 * quarter), tall(2 * quarter), tall(d)],
        [pltpu.VMEM((TILE, d), BF)],
        "ffn", 2 * rows * d * ff * 6, rows * d * 20 + 6 * ff * d,
    )(ints, src, attn, attn_other, *pieces_c, gain_two, f_gate, f_up, f_out)

    gs_other = swap(grad_second, "core")
    recv_out = swap(send_out, "core")

    if ring:
        own_gu, *other_gu = pl.pallas_call(
            functools.partial(grad_pair_kernel, nd, f),
            in_specs=[SMEM, VMEM, VMEM],
            out_specs=[VMEM] * (nd + 1),
            out_shape=[sds(nd, ff, w, dtype=BF)] + [sds(ff, w, dtype=BF)] * nd,
            scratch_shapes=[pltpu.VMEM((ff, d), BF)],
            name="grad_ffn_in",
            compiler_params=pltpu.CompilerParams(vmem_limit_bytes=VMEM_LIMIT),
            cost_estimate=pl.CostEstimate(
                flops=2 * rows * d * ff * 2, bytes_accessed=30000000, transcendentals=0
            ),
        )(ints, grad_gu, normed_second)
        across_gu = [swap(o, "x") for o in other_gu]

        def gu_term(m, s):
            at = slice(m * f, (m + 1) * f)
            return own_gu[s - 1, at].astype(F32) + across_gu[s - 1][at].astype(F32)

        shard_gate, shard_up = ring_sum(
            functools.partial(gu_term, 0), functools.partial(gu_term, 1), nd
        )

    def blocks(lhs, rhs, f_rows, name):
        n_out = 2 * f_rows
        flops = 2 * rows * d * n_out
        if ring:
            return pl.pallas_call(
                functools.partial(grad_blocks_kernel, nd, f_rows),
                in_specs=[SMEM, VMEM, VMEM],
                out_specs=VMEM,
                out_shape=sds(nd, 2, f_rows, w, dtype=BF),
                scratch_shapes=[pltpu.VMEM((n_out, d), BF)],
                name=name,
                compiler_params=pltpu.CompilerParams(vmem_limit_bytes=VMEM_LIMIT),
                cost_estimate=pl.CostEstimate(
                    flops=flops, bytes_accessed=15000000, transcendentals=0
                ),
            )(ints, lhs, rhs)
        return pl.pallas_call(
            functools.partial(grad_plain_kernel, f_rows),
            in_specs=[SMEM, VMEM, VMEM],
            out_specs=VMEM,
            out_shape=sds(n_out, d, dtype=BF),
            name=name,
            compiler_params=pltpu.CompilerParams(vmem_limit_bytes=VMEM_LIMIT),
            cost_estimate=pl.CostEstimate(flops=flops, bytes_accessed=15000000, transcendentals=0),
        )(ints, lhs, rhs)

    blocks_o = blocks(act, cot, f, "grad_ffn_out")

    def plain_shard(full, f_rows):
        full = jnp.swapaxes(full.reshape(2 * f_rows, nd, w), 0, 1)
        total = lax.psum_scatter(full, "dp", scatter_dimension=0, tiled=True)[0].astype(F32)
        keep_rows = lax.dynamic_slice_in_dim(total, x * f_rows, f_rows)
        give_rows = lax.dynamic_slice_in_dim(total, (1 - x) * f_rows, f_rows)
        return keep_rows + swap(give_rows, "x")

    def ring_shard(first, second):
        a, b = ring_sum(first, second, nd)
        give = jnp.where(x == 0, b, a).astype(BF)
        return jnp.where(x == 0, a, b) + swap(give, "x").astype(F32)

    if ring:
        shard_fo = ring_shard(lambda s: blocks_o[s - 1, 0], lambda s: blocks_o[s - 1, 1])
    else:
        shard_fo = plain_shard(blocks_o, f)
        shard_gate = plain_shard(blocks(grad_gu[:, :ff], normed_second, f, "grad_gate"), f)
        shard_up = plain_shard(blocks(grad_gu[:, ff:], normed_second, f, "grad_up"), f)

    w_out_shape = sds(nd, 2, DV, w, dtype=BF) if ring else sds(2 * DV, d, dtype=BF)
    grad_hidden, grad_mixed, grad_gate, blocks_po, gain_second, head_part, packet_back = run(
        functools.partial(out_back_kernel, spans, tiles, nd if ring else None), (tiles,),
        [SMEM] + [rows_spec(d, tiles)] * 4
        + [whole_spec(1, d), whole_spec(2 * DV, d), rows_spec(2 * DV, tiles), rows_spec(2 * DV, tiles),
           rows_spec(2 * HEAD, tiles), rows_spec(2 * DK, tiles), whole_spec(1, DV), whole_spec(nlev, TILE, TILE)],
        [rows_spec(d, tiles), rows_spec(2 * DV, tiles), rows_spec(2 * DV, tiles), whole_spec(*w_out_shape.shape),
         whole_spec(8, d), whole_spec(8, DV), whole_spec(2 * DV, DK)],
        [tall(d, F32), tall(2 * DV), tall(2 * DV), w_out_shape, sds(8, d), sds(8, DV), sds(2 * DV, DK)],
        [pltpu.VMEM((2 * DV, d), F32), pltpu.VMEM((2, DV, DK), F32), pltpu.VMEM((8, d), F32), pltpu.VMEM((8, DV), F32)],
        "out_back", 2 * rows * d * 2 * DV * 2, rows * d * 24,
    )(ints, hidden, cot, grad_second, gs_other, gain_two, w_out, gated, mixed, qkvg, log_decay, head_row, ups)

    packet_back = jnp.concatenate([packet_back, packet[2 * DV :]], axis=0)
    leaving = carried(packet_back, sequence, reach, False)

    grad_qk, grad_v, grad_ld = run(
        within_back_kernel, (tiles,),
        [rows_spec(2 * HEAD), rows_spec(2 * DK), rows_spec(2 * DV), whole_spec(nlev, TILE, TILE),
         whole_spec(nlev, TILE, TILE), whole_spec(TILE, TILE), whole_spec(TILE, TILE)],
        [rows_spec(4 * DK), rows_spec(2 * DV), rows_spec(2 * DK)],
        [tall(4 * DK, F32), tall(2 * DV, F32), tall(2 * DK, F32)], [],
        "within_back", rows * 2 * 30 * 256 * 256, rows * 2 * HEAD * 6,
    )(qkvg, log_decay, grad_mixed, ups, downs, level, level_t)

    grad_project, grad_first, rank_part, up_grad, bias_grad = run(
        functools.partial(project_back_kernel, tiles), (tiles,),
        [SMEM, rows_spec(2 * HEAD, tiles), rows_spec(2 * DK, tiles), rows_spec(2 * DV, tiles),
         pl.BlockSpec((TILE // SPAN, 2, DV, DK), lambda i: (tiles - 1 - i, 0, 0, 0)), whole_spec(2 * DV + 16, DK),
         rows_spec(4 * DK, tiles), rows_spec(2 * DV, tiles), rows_spec(2 * DK, tiles), rows_spec(2 * DV, tiles),
         rows_spec(16, tiles), whole_spec(16, 2 * DK), whole_spec(1, 2 * DK), whole_spec(nlev, TILE, TILE),
         whole_spec(nlev, TILE, TILE), whole_spec(2 * HEAD, d)],
        [rows_spec(2 * HEAD, tiles), rows_spec(d, tiles), pl.BlockSpec((16, TILE), lambda i: (0, tiles - 1 - i)),
         whole_spec(16, 2 * DK), whole_spec(8, 2 * DK)],
        [tall(2 * HEAD), tall(d), sds(16, rows), sds(16, 2 * DK), sds(8, 2 * DK)],
        [pltpu.VMEM((2, DV, DK), F32), pltpu.VMEM((16, 2 * DK), F32), pltpu.VMEM((8, 2 * DK), F32),
         pltpu.VMEM((TILE, 2 * DK), BF), pltpu.VMEM((TILE, 2 * DK), BF), pltpu.VMEM((TILE, 2 * DK), F32)],
        "project_back", 2 * rows * d * 2 * HEAD, rows * d * 20,
    )(ints, qkvg, log_decay, grad_mixed, before, leaving, grad_qk, grad_v, grad_ld, grad_gate, rank, up, bias,
      ups, downs, w_in)

    gf_other = swap(grad_first, "core")
    rank_other = swap(rank_part, "core")
    blocks_pi = blocks(grad_project, normed_first, HEAD, "grad_proj_in")
    if ring:

        def p_term(h, s):
            return jnp.concatenate([blocks_pi[s - 1, h], blocks_po[s - 1, h]], axis=0)

        shard_pg = ring_shard(functools.partial(p_term, 0), functools.partial(p_term, 1))
        shard_pi, shard_po = shard_pg[:HEAD], shard_pg[HEAD:]
    else:
        shard_pi = plain_shard(blocks_pi, HEAD)
        shard_po = plain_shard(blocks_po, DV)

    grad_own, grad_cross, down_grad, gain_first = run(
        functools.partial(source_back_kernel, tiles), (tiles,),
        [SMEM] + [rows_spec(d)] * 4 + [pl.BlockSpec((16, TILE), lambda i: (0, i))] * 2
        + [whole_spec(16, d), whole_spec(1, d), rows_spec(d)],
        [rows_spec(quarter), rows_spec(quarter), whole_spec(16, d), whole_spec(8, d)],
        [tall(quarter), tall(quarter), sds(16, d), sds(8, d)],
        [pltpu.VMEM((TILE, d), BF), pltpu.VMEM((16, d), F32), pltpu.VMEM((8, d), F32)],
        "source_back", 2 * rows * d * 64, rows * d * 16,
    )(ints, src, normed_first, grad_first, gf_other, rank_part, rank_other, w_down, gain_one, grad_hidden)

    out_own, out_cross = run(
        block_out_kernel, (tiles,),
        [SMEM, rows_spec(d), rows_spec(2 * quarter), rows_spec(2 * quarter)],
        [rows_spec(quarter)] * 2, [tall(quarter)] * 2, [],
        "block_out", 0, rows * d * 8,
    )(ints, hidden, keep_out, recv_out)

    def undealt(own, cross, name):
        joined = join_pick(own, swap(cross, "x"), back_local, x, name + "_join")
        return lax.all_to_all(joined, "dp", split_axis=0, concat_axis=0, tiled=True)

    back_out = undealt(out_own, out_cross, "block_out")
    block_out = home([back_out], home_slot, [jnp.int32(0)], "block_out_home")
    back_grad = undealt(grad_own, grad_cross, "token_grad")
    back_x = swap(back_grad, "x")
    token_grad = home(
        [back_grad, back_x, swap(back_grad, "core"), swap(back_x, "core")],
        home_slot,
        [quarters[k] * quarter for k in range(4)],
        "token_grad_home",
    )

    small = jnp.concatenate(
        [
            gain_first[0].reshape(-1, 128),
            gain_second[0].reshape(-1, 128),
            down_grad.reshape(-1, 128),
            up_grad.reshape(-1, 128),
            bias_grad[0].reshape(-1, 128),
            head_part[0].reshape(-1, 128),
        ],
        axis=0,
    )
    small = all_sum(small, ("x", "dp"), (2, nd))
    rows_d = d // 128
    cuts = [rows_d, rows_d, 16 * rows_d, 32, 2, 2]
    starts = [sum(cuts[:k]) for k in range(len(cuts) + 1)]
    gain_first, gain_second, down_total, up_total, bias_total, head_total = (
        small[starts[k] : starts[k + 1]].reshape(-1) for k in range(len(cuts))
    )
    head_total = head_total + swap(head_total, "core")
    gains_total = jnp.stack([gain_first, gain_second])
    down_total = down_total.reshape(16, d)
    shard_down = lax.dynamic_slice_in_dim(down_total, dp * w, w, 1).T
    up_total = up_total.reshape(16, 2, DK)
    up_total = jnp.where(x == 0, up_total[:, 0:1], up_total[:, 1:2])
    bias_total = bias_total.reshape(2, DK)
    bias_total = jnp.where(x == 0, bias_total[0:1], bias_total[1:2])

    shard_in = shard_pi.T.reshape(proj_in.shape)
    shard_out = shard_po.reshape(proj_out.shape)
    shard_ffn_in = jnp.stack([shard_gate.T, shard_up.T], axis=1)
    shard_ffn_out = shard_fo
    n_dev = 4 * nd
    local_sq = (
        square_sum(shard_pi)
        + square_sum(shard_po)
        + square_sum(shard_gate)
        + square_sum(shard_up)
        + square_sum(shard_fo)
        + square_sum(shard_down) / 4
        + (square_sum(up_total) + square_sum(bias_total)) / nd
        + (square_sum(head_total) + square_sum(gains_total)) / n_dev
    )
    norm_sq = all_sum(jnp.broadcast_to(local_sq, (8, 128)), ("core", "x", "dp"), (2, 2, nd))
    grad_norm = jnp.sqrt(norm_sq[0, 0])
    clip_norm = clip_scale * math.sqrt(PARAMS)
    factor = jnp.minimum(1.0, clip_norm / (grad_norm + 1e-06))
    update_in = adam_update(proj_in, shard_in, first_proj_in, second_proj_in, factor, weight_decay)
    update_down = adam_update(decay_down, shard_down, first_decay_down, second_decay_down, factor, weight_decay)
    update_up = adam_update(decay_up, up_total, first_decay_up, second_decay_up, factor, weight_decay)
    update_bias = adam_update(decay_bias, bias_total, first_decay_bias, second_decay_bias, factor, 0.0)
    update_head = adam_update(head_gain, head_total, first_head_gain, second_head_gain, factor, 0.0)
    update_out = adam_update(proj_out, shard_out, first_proj_out, second_proj_out, factor, weight_decay)
    update_gains = adam_update(block_gains, gains_total, first_block_gains, second_block_gains, factor, 0.0)
    update_ffn_in = adam_update(ffn_in, shard_ffn_in, first_ffn_in, second_ffn_in, factor, weight_decay)
    update_ffn_out = adam_update(ffn_out, shard_ffn_out, first_ffn_out, second_ffn_out, factor, weight_decay)
    return (
        block_out, token_grad, grad_norm, *update_in, *update_down, *update_up, *update_bias, *update_head,
        *update_out, *update_gains, *update_ffn_in, *update_ffn_out,
    )


def solution(mesh):
    nd, nt = mesh.shape["dp"], mesh.shape["tensor"]
    fine = Mesh(mesh.devices.reshape(nd, nt // 2, 2), ("dp", "x", "core"))
    t = ("x", "core")
    w_specs = {
        "proj_in": P("dp", t, None),
        "decay_down": P("dp", None),
        "decay_up": P(None, t, None),
        "decay_bias": P(t, None),
        "head_gain": P(),
        "proj_out": P(t, None, "dp"),
        "block_gains": P(),
        "ffn_in": P("dp", None, t),
        "ffn_out": P(t, "dp"),
    }
    specs = list(w_specs.values())
    placed = [P("dp", None), P("dp", None), P(), P()] + specs
    results = [P("dp", t), P("dp", None), P()]
    for spec in specs:
        placed += [spec] * 2
        results += [spec] * 4
    return jax.shard_map(
        on_device,
        mesh=fine,
        in_specs=tuple(placed),
        out_specs=tuple(results),
        check_vma=False,
    )
```

```python
import functools
import math

import jax
import jax.numpy as jnp
from jax import lax
from jax.experimental import pallas as pl
from jax.experimental.pallas import tpu as pltpu
from jax.sharding import Mesh
from jax.sharding import PartitionSpec as P

DK = 128
DV = 256
SPAN = 64
MIN_SPANS = 16
MAX_SPANS = 128
PARAMS = 12872448
TILE = 256
LEVELS = 6
HEAD = 2 * DK + 2 * DV
VMEM_LIMIT = 60 * 1024 * 1024
BF = jnp.bfloat16
F32 = jnp.float32

norm_eps = 1e-06
learn_rate = 0.05
beta_one = 0.9
beta_two = 0.95
adam_eps = 1e-08
weight_decay = 0.1
clip_scale = 0.05
adam_step = 10
decay_scale = 16.0
scaling = DK ** (-0.5)
ANY = pl.BlockSpec(memory_space=pl.ANY)
SMEM = pl.BlockSpec(memory_space=pltpu.SMEM)
VMEM = pl.BlockSpec(memory_space=pltpu.VMEM)


def dot(a, b, ca=1, cb=0):
    return lax.dot_general(a, b, (((ca,), (cb,)), ((), ())), preferred_element_type=F32)


def cost(us):
    return pl.CostEstimate(flops=int(us * 1.0e9), bytes_accessed=int(us * 1.0e6), transcendentals=0)


def run(kernel, grid, in_specs, out_specs, out_shape, scratch, name, us):
    return pl.pallas_call(
        kernel,
        grid=grid,
        in_specs=in_specs,
        out_specs=out_specs,
        out_shape=out_shape,
        scratch_shapes=scratch,
        name=name,
        compiler_params=pltpu.CompilerParams(vmem_limit_bytes=VMEM_LIMIT),
        cost_estimate=cost(us),
    )


def sds(*shape, dtype=F32):
    return jax.ShapeDtypeStruct(shape, dtype)


def rows_spec(cols, order=None):
    if order is None:
        return pl.BlockSpec((TILE, cols), lambda i: (i, 0))
    return pl.BlockSpec((TILE, cols), lambda i: (order - 1 - i, 0))


def whole_spec(*shape):
    zeros = (0,) * len(shape)
    return pl.BlockSpec(shape, lambda i: zeros, pipeline_mode=pl.Buffered(1))


def span_starts(seq_extra, span_ids):
    seq_spans = seq_extra + MIN_SPANS
    n = seq_extra.shape[0]
    earlier = jnp.tril(jnp.ones((n, n), jnp.int32), -1)
    bounds = jnp.sum(earlier * seq_spans[None, :], axis=1)
    return jnp.any(bounds[None, :] == span_ids[:, None], axis=1).astype(jnp.int32)


def deal_tables(deal, n_data, per_dev, capacity, my_index):
    table_grid = deal.reshape(n_data, per_dev)
    src_dev = table_grid // per_dev
    src_local = table_grid % per_dev
    my_source = lax.dynamic_index_in_dim(src_dev, my_index, 0, keepdims=False)
    earlier = jnp.tril(jnp.ones((per_dev, per_dev), jnp.int32), -1)
    same_source = (my_source[:, None] == my_source[None, :]).astype(jnp.int32)
    my_rank = jnp.sum(same_source * earlier, axis=1)
    recv_slot = my_source * capacity + my_rank
    owned_here = (src_dev == my_index).astype(jnp.int32)
    send_rank = jnp.sum(owned_here[:, None, :] * earlier[None], axis=2)
    slot_ids = jnp.arange(capacity, dtype=jnp.int32)
    send_hit = owned_here[:, :, None] * (
        send_rank[:, :, None] == slot_ids[None, None, :]
    ).astype(jnp.int32)
    send_local = jnp.sum(send_hit * src_local[:, :, None], axis=1)
    peer_ids = jnp.arange(n_data, dtype=jnp.int32)
    local_ids = jnp.arange(per_dev, dtype=jnp.int32)
    back_hit = (
        (my_source[None, None, :] == peer_ids[:, None, None])
        & (my_rank[None, None, :] == slot_ids[None, :, None])
    ).astype(jnp.int32)
    back_local = jnp.sum(back_hit * local_ids[None, None, :], axis=2)
    home_hit = owned_here[:, :, None] * (
        src_local[:, :, None] == local_ids[None, None, :]
    ).astype(jnp.int32)
    home_slot = jnp.sum(
        home_hit * (peer_ids[:, None, None] * capacity + send_rank[:, :, None]), axis=(0, 1)
    )
    return recv_slot, send_local.reshape(-1), back_local.reshape(-1), home_slot


def level_matrices():
    t = jnp.arange(TILE, dtype=jnp.int32)[:, None]
    u = jnp.arange(TILE, dtype=jnp.int32)[None, :]
    ups = []
    level = jnp.full((TILE, TILE), LEVELS + 1, jnp.int32)
    for l in range(LEVELS):
        block = SPAN >> l
        half = block // 2
        same = (t // block) == (u // block)
        mid = (t // block) * block + half
        right = (t >= mid) & (u >= mid) & (u <= t)
        left = (t < mid) & (u > t) & (u < mid)
        ups.append(same & (right | left))
        hit = same & (t % block >= half) & (u % block < half)
        level = jnp.where(hit, l, level)
    level = jnp.where(t == u, LEVELS, level)
    same = (t // SPAN) == (u // SPAN)
    ups.append(same & (u <= t))
    ups.append(same & (u > t))
    ups = jnp.stack(ups).astype(BF)
    return ups, jnp.swapaxes(ups, 1, 2), level, level.T


def home_kernel(count, table, *refs):
    srcs, out = refs[:-1], refs[-1]
    width = srcs[0].shape[1]

    def body(i, _):
        row = pl.multiple_of(table[i] * SPAN, SPAN)
        to = pl.multiple_of(i * SPAN, SPAN)
        for k, src in enumerate(srcs):
            col = pl.multiple_of(table[count + k], 128)
            out[pl.ds(to, SPAN), pl.ds(col, width)] = src[pl.ds(row, SPAN), :].astype(F32)
        return 0

    lax.fori_loop(0, count, body, 0)


def home(pieces, table, cols, name):
    count = table.shape[0]
    width = pieces[0].shape[1]
    total = width * len(pieces)
    return pl.pallas_call(
        functools.partial(home_kernel, count),
        in_specs=[SMEM] + [VMEM] * len(pieces),
        out_specs=VMEM,
        out_shape=sds(count * SPAN, total),
        name=name,
        compiler_params=pltpu.CompilerParams(vmem_limit_bytes=VMEM_LIMIT),
        cost_estimate=cost(4),
    )(jnp.concatenate([table, jnp.stack(cols)]), *pieces)


def copy_to(src, dst, send_sem, recv_sem, target):
    return pltpu.make_async_remote_copy(
        src_ref=src,
        dst_ref=dst,
        send_sem=send_sem,
        recv_sem=recv_sem,
        device_id=target,
        device_id_type=pl.DeviceIdType.MESH,
    )


def enter(nd, shifts=()):
    dp, x, core = lax.axis_index("dp"), lax.axis_index("x"), lax.axis_index("core")
    peers = [{"dp": lax.rem(dp + k, nd)} for k in range(1, nd)] + [{"x": 1 - x}, {"core": 1 - core}]
    for k in shifts:
        peers += [along_sequence(nd, k), along_sequence(nd, -k)]
    barrier = pltpu.get_barrier_semaphore()
    for peer in peers:
        pl.semaphore_signal(barrier, inc=1, device_id=peer, device_id_type=pl.DeviceIdType.MESH)
    pl.semaphore_wait(barrier, len(peers))


def along_sequence(nd, k):
    q = lax.rem(lax.axis_index("dp") * 2 + lax.axis_index("x") + k + 2 * nd, 2 * nd)
    return {"dp": q // 2, "x": lax.rem(q, 2)}


def carry_widths(reach):
    widths = []
    width = 1
    while 2 * width < reach:
        widths.append(width)
        width *= 2
    return widths, width


class Carry:
    def __init__(self, nd, reach, sign, packet, sent, got, send_sems, recv_sems):
        self.nd, self.sign, self.packet, self.sent, self.got = nd, sign, packet, sent, got
        self.send_sems, self.recv_sems = send_sems, recv_sems
        self.widths, self.last = carry_widths(reach)
        self.q = lax.axis_index("dp") * 2 + lax.axis_index("x")

    def shifts(self):
        return self.widths + [1, 1 + self.last]

    def copy(self, index):
        source = min(index, len(self.widths))
        return copy_to(
            self.sent.at[source],
            self.got.at[index],
            self.send_sems.at[index],
            self.recv_sems.at[index],
            along_sequence(self.nd, self.sign * self.shifts()[index]),
        )

    def send(self, stage):
        self.sent[stage] = self.packet[...].astype(BF)
        self.copy(stage).start()
        if stage == len(self.widths):
            self.copy(stage + 1).start()

    def receive(self, index):
        self.copy(index).wait_recv()
        k = self.shifts()[index]
        there = self.q >= k if self.sign > 0 else self.q + k < 2 * self.nd
        return jnp.where(there, self.got[index].astype(F32), 0.0)

    def step(self, stage):
        if stage < len(self.widths):
            self.join(self.receive(stage), self.packet[...])
            self.send(stage + 1)
        else:
            near, far = self.receive(stage), self.receive(stage + 1)
            self.join(far, near)
            for index in range(stage + 2):
                self.copy(index).wait_send()

    def join(self, earlier, later):
        for h in range(2):
            states = slice(h * DV, (h + 1) * DV)
            f = slice(2 * DV + h, 2 * DV + h + 1)
            self.packet[states] = later[f] * earlier[states] + later[states]
            self.packet[f] = later[f] * earlier[f]

    def run(self):
        return len(self.widths) + 1


class Spread:
    def __init__(self, nd, order, own, window, send_sems, recv_sems):
        self.nz, self.order, self.own, self.window = nd // 2, order, own, window
        self.send_sems, self.recv_sems = send_sems, recv_sems
        dp, self.x = lax.axis_index("dp"), lax.axis_index("x")
        self.z, self.y = dp // 2, lax.rem(dp, 2)
        nz = self.nz
        self.moves = [((0, 0, 0), (k, 0, 0)) for k in range(1, nz)]
        self.moves += [((0, 0, 0), (0, 1, 0)), ((0, 0, 0), (0, 0, 1))]
        for k in range(1, nz):
            self.moves += [((k, 0, 0), (k, 1, 0)), ((k, 0, 0), (k, 0, 1))]
        self.moves += [((k, 1, 0), (k, 1, 1)) for k in range(nz)]

    def place(self, k, first, second):
        fy, fx = (first, second) if self.order == 0 else (second, first)
        y = 1 - self.y if fy else self.y
        x = 1 - self.x if fx else self.x
        return self.window(lax.rem(self.z + self.nz - k, self.nz) * 2 + y, x)

    def copy(self, index):
        here, there = self.moves[index]
        if here[0] != there[0]:
            target = {"dp": lax.rem(self.z + there[0], self.nz) * 2 + self.y}
        elif (here[1] != there[1]) == (self.order == 0):
            target = {"dp": self.z * 2 + 1 - self.y}
        else:
            target = {"x": 1 - self.x}
        k, first, second = there
        return copy_to(
            self.own if here == (0, 0, 0) else self.place(*here),
            self.place(*here),
            self.send_sems.at[index],
            self.recv_sems.at[k + self.nz * (first + 2 * second)],
            target,
        )

    def arrived(self, k, first, second):
        at = self.place(k, first, second)
        sem = self.recv_sems.at[k + self.nz * (first + 2 * second)]
        copy_to(at, at, self.send_sems.at[0], sem, {"x": 1 - self.x}).wait_recv()

    def begin(self):
        for index in range(self.nz + 1):
            self.copy(index).start()

    def relay_z(self, k):
        self.arrived(k, 0, 0)
        for index in range(2):
            self.copy(self.nz + 1 + 2 * (k - 1) + index).start()

    def relay_first(self, k):
        self.arrived(k, 1, 0)
        self.copy(3 * self.nz - 1 + k).start()

    def finish(self):
        for k in range(self.nz):
            self.arrived(k, 0, 1)
            self.arrived(k, 1, 1)
        for index in range(len(self.moves)):
            self.copy(index).wait_send()


CHUNKS = 4


class Deal:
    def __init__(self, nd, spans, table, rows, out, tok, send, recv, other, sems):
        self.nd, self.spans, self.table, self.rows, self.out = nd, spans, table, rows, out
        self.tok, self.sent, self.recv, self.other = tok, send, recv, other
        self.load_sem, self.a2a_send, self.a2a_recv, self.x_send, self.x_recv, self.c_send, self.c_recv = sems
        self.dp, self.x, self.core = lax.axis_index("dp"), lax.axis_index("x"), lax.axis_index("core")
        self.quarter = out.shape[1] // 4
        self.cap = send.shape[1]
        self.mine = pl.multiple_of((2 * self.x + self.core) * self.quarter, 128)
        self.theirs = pl.multiple_of((2 * (1 - self.x) + self.core) * self.quarter, 128)
        self.load = pltpu.make_async_copy(rows.at[:, :, pl.ds(self.mine, self.quarter)], tok, self.load_sem.at[0])
        self.started = []

    def begin(self):
        self.load.start()

    def exchange(self):
        self.load.wait()
        cap, nd = self.cap, self.nd

        def pick(k, out, base):
            d = lax.rem(self.dp + k, nd)
            for j in range(cap):
                out[base + j] = self.tok[self.table[d * cap + j]]

        here = self.dp * cap
        for k in range(1, nd):
            pick(k, self.sent.at[k], 0)
            copy = copy_to(
                self.sent.at[k],
                self.recv.at[pl.ds(here, cap)],
                self.a2a_send.at[k],
                self.a2a_recv.at[k],
                {"dp": lax.rem(self.dp + k, nd)},
            )
            copy.start()
            self.started.append(copy)
        pick(0, self.recv, here)

    def across(self):
        for copy in self.started:
            copy.wait_recv()
        spans, nd = self.spans, self.nd
        count = spans // CHUNKS
        first = nd * self.cap
        self.x_copies, self.c_copies = [], []
        for c in range(CHUNKS):
            rows = pl.ds(c * count * SPAN, count * SPAN)

            def body(i, _, c=c):
                at = c * count + i
                to = pl.ds(pl.multiple_of(at * SPAN, SPAN), SPAN)
                self.other[to, :] = self.recv[self.table[first + spans + at]]
                return 0

            lax.fori_loop(0, count, body, 0)
            copy = copy_to(
                self.other.at[rows, :],
                self.out.at[rows, pl.ds(self.mine, self.quarter)],
                self.x_send.at[c],
                self.x_recv.at[c],
                {"x": 1 - self.x},
            )
            copy.start()
            self.x_copies.append(copy)

        def body(i, _):
            to = pl.ds(pl.multiple_of(i * SPAN, SPAN), SPAN)
            self.out[to, pl.ds(self.mine, self.quarter)] = self.recv[self.table[first + i]]
            return 0

        lax.fori_loop(0, spans, body, 0)
        self.pass_on(slice(None), self.mine, CHUNKS)

    def pass_on(self, rows, col, sem):
        at = self.out.at[rows, pl.ds(col, self.quarter)]
        copy = copy_to(at, at, self.c_send.at[sem], self.c_recv.at[sem], {"core": 1 - self.core})
        copy.start()
        self.c_copies.append(copy)

    def finish(self):
        count = self.spans // CHUNKS
        for c, copy in enumerate(self.x_copies):
            copy.wait_recv()
            self.pass_on(pl.ds(c * count * SPAN, count * SPAN), self.theirs, c)
        for copy in self.c_copies:
            copy.wait_recv()
        for copy in self.x_copies + self.c_copies:
            copy.wait_send()

    def release(self):
        for copy in self.started:
            copy.wait_send()


def deal_buffers(nd, per_dev, spans, quarter, cap):
    return [
        pltpu.VMEM((per_dev, SPAN, quarter), BF),
        pltpu.VMEM((nd, cap, SPAN, quarter), BF),
        pltpu.VMEM((spans * SPAN, quarter), BF),
        pltpu.VMEM((nd * cap, SPAN, quarter), BF),
        pltpu.VMEM((nd * cap, SPAN, quarter), BF),
    ]


def deal_sems(nd):
    dma = pltpu.SemaphoreType.DMA
    return [dma((1,)), dma((nd,)), dma((nd,)), dma((CHUNKS,)), dma((CHUNKS,)), dma((CHUNKS + 1,)), dma((CHUNKS + 1,))]


class Undeal:
    def __init__(self, nd, spans, table, own, cross, joined, sent, gath, sems):
        self.nd, self.spans, self.table, self.own, self.cross = nd, spans, table, own, cross
        self.joined, self.sent, self.gath = joined, sent, gath
        self.x_send, self.x_recv, self.a2a_send, self.a2a_recv, *self.wide_sems = sems
        self.dp, self.x, self.core = lax.axis_index("dp"), lax.axis_index("x"), lax.axis_index("core")
        self.cap = sent.shape[1]
        self.quarter = own.shape[2]
        self.wide = gath.shape[2] != self.quarter
        self.mine, self.theirs = 0, 0
        if self.wide:
            self.mine = pl.multiple_of((2 * self.x + self.core) * self.quarter, 128)
            self.theirs = pl.multiple_of((2 * (1 - self.x) + self.core) * self.quarter, 128)

    def swap(self):
        return copy_to(
            self.cross,
            self.joined.at[pl.ds(self.x * self.spans, self.spans)],
            self.x_send.at[0],
            self.x_recv.at[0],
            {"x": 1 - self.x},
        )

    def begin(self):
        self.swap().start()

        def body(i, _):
            self.joined[self.x * self.spans + i] = self.own[i]
            return 0

        lax.fori_loop(0, self.spans, body, 0)

    def block(self, dp, col):
        return self.gath.at[pl.ds(dp * self.cap, self.cap), :, pl.ds(col, self.quarter)]

    def a2a(self, k):
        return copy_to(
            self.sent.at[k],
            self.block(self.dp, self.mine),
            self.a2a_send.at[k],
            self.a2a_recv.at[k],
            {"dp": lax.rem(self.dp + k, self.nd)},
        )

    def exchange(self):
        self.swap().wait_recv()
        cap = self.cap
        for k in range(1, self.nd):
            d = lax.rem(self.dp + k, self.nd)
            for j in range(cap):
                self.sent[k, j] = self.joined[self.table[d * cap + j]]
            self.a2a(k).start()
        here = self.block(self.dp, self.mine)
        for j in range(cap):
            here[j] = self.joined[self.table[self.dp * cap + j]]
        if self.wide:
            self.widen(0, 0).start()
            self.widen(0, 1).start()

    def widen(self, k, step):
        at = self.block(lax.rem(self.dp + self.nd - k, self.nd), self.theirs if step == 2 else self.mine)
        send, recv = self.wide_sems
        return copy_to(
            at, at, send.at[3 * k + step], recv.at[3 * k + step],
            {"x": 1 - self.x} if step == 0 else {"core": 1 - self.core},
        )

    def arrive(self, k):
        self.a2a(k).wait_recv()
        if self.wide:
            self.widen(k, 0).start()
            self.widen(k, 1).start()

    def finish(self):
        if self.wide:
            for k in range(self.nd):
                self.widen(k, 0).wait_recv()
                self.widen(k, 2).start()
            for k in range(self.nd):
                self.widen(k, 1).wait_recv()
                self.widen(k, 2).wait_recv()
                for step in range(3):
                    self.widen(k, step).wait_send()
        for k in range(1, self.nd):
            self.a2a(k).wait_send()
        self.swap().wait_send()


def undeal_scratch(nd, per_dev, spans, quarter, cap, wide):
    dma = pltpu.SemaphoreType.DMA
    buffers = [
        pltpu.VMEM((spans, SPAN, quarter), BF),
        pltpu.VMEM((spans, SPAN, quarter), BF),
        pltpu.VMEM((per_dev, SPAN, quarter), BF),
        pltpu.VMEM((nd, cap, SPAN, quarter), BF),
        pltpu.VMEM((nd * cap, SPAN, quarter * (4 if wide else 1)), BF),
    ]
    sems = [dma((1,)), dma((1,)), dma((nd,)), dma((nd,))]
    return buffers, sems + ([dma((3 * nd,)), dma((3 * nd,))] if wide else [])


class Collapse:
    def __init__(self, nd, order, acc, pitch, low, rows, got, sems):
        self.nz, self.order, self.acc, self.pitch, self.low, self.rows = nd // 2, order, acc, pitch, low, rows
        self.got = got
        self.send_sems, self.recv_sems = sems
        self.w = got.shape[2]
        dp, self.x = lax.axis_index("dp"), lax.axis_index("x")
        self.z, self.y = dp // 2, lax.rem(dp, 2)

    def window(self, first, second, kz):
        fx, fy = (first, second) if self.order == 0 else (second, first)
        y = 1 - self.y if fy else self.y
        x = 1 - self.x if fx else self.x
        dp = lax.rem(self.z + kz, self.nz) * 2 + y
        return self.acc.at[
            pl.ds(pl.multiple_of(x * self.pitch + self.low, 16), self.rows),
            pl.ds(pl.multiple_of(dp * self.w, 128), self.w),
        ]

    def partner(self, which):
        if (which == 0) == (self.order == 0):
            return {"x": 1 - self.x}
        return {"dp": self.z * 2 + 1 - self.y}

    def slot(self, phase, second, kz):
        nz = self.nz
        return second * nz + kz if phase == 1 else (2 * nz + kz if phase == 2 else 3 * nz + kz - 1)

    def copy(self, phase, second, kz):
        at = self.slot(phase, second, kz)
        if phase == 1:
            src, target = self.window(1, second, kz), self.partner(0)
        elif phase == 2:
            src, target = self.window(0, 1, kz), self.partner(1)
        else:
            src, target = self.window(0, 0, kz), {"dp": lax.rem(self.z + kz, self.nz) * 2 + self.y}
        return copy_to(src, self.got.at[at], self.send_sems.at[at], self.recv_sems.at[at], target)

    def add(self, second, kz, at):
        here = self.window(0, second, kz)
        here[...] = (here[...].astype(F32) + self.got[at].astype(F32)).astype(BF)

    def begin(self):
        for second in (1, 0):
            for kz in range(self.nz):
                self.copy(1, second, (kz + 1) % self.nz).start()

    def second(self, kz):
        self.copy(1, 1, kz).wait_recv()
        self.add(1, kz, self.slot(1, 1, kz))
        self.copy(2, 1, kz).start()

    def third(self, kz):
        self.copy(1, 0, kz).wait_recv()
        self.add(0, kz, self.slot(1, 0, kz))
        self.copy(2, 1, kz).wait_recv()
        self.add(0, kz, self.slot(2, 1, kz))
        if kz:
            self.copy(3, 0, kz).start()

    def finish(self, out):
        total = self.window(0, 0, 0)[...].astype(F32)
        for kz in range(1, self.nz):
            self.copy(3, 0, kz).wait_recv()
            total = total + self.got[self.slot(3, 0, kz)].astype(F32)
        out[...] = total
        for kz in range(self.nz):
            self.copy(1, 0, kz).wait_send()
            self.copy(1, 1, kz).wait_send()
            self.copy(2, 1, kz).wait_send()
            if kz:
                self.copy(3, 0, kz).wait_send()


def collapse_scratch(nd, rows, w):
    count = 4 * (nd // 2) - 1
    dma = pltpu.SemaphoreType.DMA
    return [pltpu.VMEM((count, rows, w), BF), dma((count,)), dma((count,))]


def progress(chains, nz, between=()):
    between = list(between)
    for kz in [k % nz for k in range(1, nz + 1)]:
        for chain in chains:
            chain.second(kz)
        if between:
            between.pop(0)()
    for kz in [k % nz for k in range(1, nz + 1)]:
        for chain in chains:
            chain.third(kz)
        if between:
            between.pop(0)()
    for work in between:
        work()


PROJ_ROWS = 16 + HEAD + DV
PROJ_CUTS = ((0, 528), (528, 512))


FFN_CUTS = 2
PITCH = 768


def up_to(value, step):
    return -(-value // step) * step


def forward_kernel(nd, spans, reach, gather, table, ints, tokens, cotangent, shard_p, shard_f, gain, up, bias, head_gain,
                   ups, level, *rest):
    outs, rest = rest[:13], rest[13:]
    (src_o, cot_o, wp_o, wf_o, normed_o, qkvg_o, log_decay_o, rank_o, mixed_o, gated_o, attn_o, before_o, attn_other) = outs
    (src, cot, wp, wf, normed, qkvg, log_decay, rank, mixed, gated, attn, before), rest = rest[:12], rest[12:]
    (packet, factors, sent_packets, got_packets), rest = rest[:4], rest[4:]
    (tok, sent, other, recv_t, recv_c), rest = rest[:5], rest[5:]
    sems_t, sems_c, rest = rest[:7], rest[7:14], rest[14:]
    carry_send, carry_recv, core_send, core_recv, out_sems, own_sems, *ag_sems = rest
    tiles = spans * SPAN // TILE
    carry = Carry(nd, reach, 1, packet, sent_packets, got_packets, carry_send, carry_recv)
    enter(nd, carry.shifts())
    deal = Deal(nd, spans, table, tokens, src, tok, sent, recv_t, other, sems_t)
    deal_c = Deal(nd, spans, table, cotangent, cot, tok, sent, recv_c, other, sems_c)
    deal.begin()
    local = []
    spreads_p, spreads_f = [], []
    if gather:
        w = shard_p.shape[1]
        f3 = shard_f.shape[0]
        cuts_f = ((0, f3 // 2), (f3 // 2, f3 // 2))

        def window(buffer, pitch, cut, dp, x):
            low, count = cut
            return buffer.at[
                pl.ds(pl.multiple_of(x * pitch + low, 16), count), pl.ds(pl.multiple_of(dp * w, 128), w)
            ]

        for shard, buffer, cuts, spreads in ((shard_p, wp, PROJ_CUTS, spreads_p), (shard_f, wf, cuts_f, spreads_f)):
            for order, cut in enumerate(cuts):
                piece = shard.at[pl.ds(cut[0], cut[1]), :]
                place = functools.partial(window, buffer, shard.shape[0], cut)
                copy = pltpu.make_async_copy(
                    piece, place(lax.axis_index("dp"), lax.axis_index("x")), own_sems.at[len(local)]
                )
                copy.start()
                local.append(copy)
                k = 2 * (len(local) - 1)
                spreads.append(Spread(nd, order, piece, place, ag_sems[k], ag_sems[k + 1]))
    else:
        for shard, buffer in ((shard_p, wp), (shard_f, wf)):
            local.append(pltpu.make_async_copy(shard, buffer, own_sems.at[len(local)]))
            local[-1].start()
    outgoing = []

    def store(value, out):
        outgoing.append(pltpu.make_async_copy(value, out, out_sems.at[len(outgoing)]))
        outgoing[-1].start()

    def relay_z(spreads, k):
        for spread in spreads:
            spread.relay_z(k)

    def relay_first(spreads, k):
        for spread in spreads:
            spread.relay_first(k)

    nz = nd // 2
    last_z = range(1, nz) if gather else ()
    last_first = range(nz) if gather else ()
    for spread in spreads_p:
        spread.begin()
    deal.exchange()
    for spread in spreads_f:
        spread.begin()
    deal_c.begin()
    for k in last_z:
        relay_z(spreads_p, k)
    for k in last_first:
        relay_first(spreads_p, k)
    deal.across()
    deal.release()
    deal_c.exchange()
    for k in last_z[:1]:
        relay_z(spreads_f, k)
    for k in last_first[:1]:
        relay_first(spreads_f, k)
    deal.finish()
    for spread in spreads_p:
        spread.finish()
    for copy in local:
        copy.wait()
    store(src, src_o)
    store(wp, wp_o)

    def at(ref, i):
        return ref.at[pl.ds(pl.multiple_of(i * TILE, TILE), TILE), :]

    packet[...] = jnp.zeros_like(packet)
    packet[2 * DV : 2 * DV + 2] = jnp.ones((2, DK), F32)

    def project(i, _):
        project_kernel(
            i, ints, at(src, i), gain, wp, up, bias, ups,
            at(normed, i), at(qkvg, i), at(log_decay, i), at(rank, i), packet,
        )
        return 0

    lax.fori_loop(0, tiles // 2, project, 0)
    for k in last_z[1:2]:
        relay_z(spreads_f, k)
    for k in last_first[1:2]:
        relay_first(spreads_f, k)
    lax.fori_loop(tiles // 2, tiles, project, 0)
    factors[...] = packet[2 * DV :]
    carry.send(0)
    store(normed, normed_o)
    store(qkvg, qkvg_o)
    store(log_decay, log_decay_o)
    store(rank, rank_o)
    for k in last_z[2:]:
        relay_z(spreads_f, k)
    for k in last_first[2:]:
        relay_first(spreads_f, k)

    def within(i, _):
        within_kernel(at(qkvg, i), at(log_decay, i), ups, level, at(mixed, i))
        return 0

    stages = carry.run()
    for stage in range(stages):
        lax.fori_loop(tiles * stage // stages, tiles * (stage + 1) // stages, within, 0)
        carry.step(stage)
    deal_c.across()
    per_tile = TILE // SPAN

    def mix(i, _):
        mix_kernel(
            i, ints, at(qkvg, i), at(log_decay, i), packet, ups, head_gain, wp,
            at(mixed, i), at(gated, i), at(attn, i), before.at[pl.ds(i * per_tile, per_tile)],
        )
        return 0

    lax.fori_loop(0, tiles, mix, 0)
    swap_attn = copy_to(
        attn, attn_other, core_send.at[0], core_recv.at[0], {"core": 1 - lax.axis_index("core")}
    )
    swap_attn.start()
    store(mixed, mixed_o)
    store(gated, gated_o)
    store(attn, attn_o)
    store(before, before_o)
    deal_c.finish()
    store(cot, cot_o)
    for spread in spreads_f:
        spread.finish()
    store(wf, wf_o)
    deal_c.release()
    swap_attn.wait()
    for copy in outgoing:
        copy.wait()


def forward(table, ints, tokens, cotangent, shard_p, shard_f, gain, up, bias, head_gain, ups, level, nd, spans, reach, gather):
    d = tokens.shape[1]
    per_dev = tokens.shape[0] // SPAN
    cap = -(-per_dev // nd)
    rows = spans * SPAN
    dma = pltpu.SemaphoreType.DMA
    nz = nd // 2
    wf_rows = shard_f.shape[0] * (2 if gather else 1)
    kept = [
        ((rows, d), BF), ((rows, d), BF), ((2 * PROJ_ROWS, d), BF), ((wf_rows, d), BF), ((rows, d), BF),
        ((rows, 2 * HEAD), BF), ((rows, 2 * DK), F32), ((rows, 16), BF), ((rows, 2 * DV), F32), ((rows, 2 * DV), BF),
        ((rows, d), BF), ((spans, 2, DV, DK), BF),
    ]
    widths, _ = carry_widths(reach)
    steps = len(widths) + 2
    scratch = [pltpu.VMEM(shape, dtype) for shape, dtype in kept]
    scratch += [
        pltpu.VMEM((2 * DV + 16, DK), F32),
        pltpu.VMEM((steps - 1, 2 * DV + 16, DK), BF),
        pltpu.VMEM((steps, 2 * DV + 16, DK), BF),
    ]
    scratch += deal_buffers(nd, per_dev, spans, d // 4, cap) + deal_sems(nd) + deal_sems(nd)
    scratch += [dma((steps,)), dma((steps,)), dma((1,)), dma((1,)), dma((12,)), dma((4,))]
    if gather:
        scratch += [dma((4 * nz - 1,)), dma((4 * nz,))] * 4
    outs = [sds(*shape, dtype=dtype) for shape, dtype in kept] + [sds(rows, d, dtype=BF)]
    outs.append(sds(16, DK))
    specs = [ANY] * 13 + [VMEM]

    def kernel(*refs):
        n_in = 12
        ins, rest = refs[:n_in], refs[n_in:]
        results, factors, buffers = rest[:13], rest[13], rest[14:]
        forward_kernel(
            nd, spans, reach, gather, *ins, *results, *buffers[:12], buffers[12], factors, *buffers[13:]
        )

    return pl.pallas_call(
        kernel,
        in_specs=[SMEM, SMEM, ANY, ANY, ANY, ANY] + [VMEM] * 6,
        out_specs=specs,
        out_shape=outs,
        scratch_shapes=scratch,
        name="forward",
        compiler_params=pltpu.CompilerParams(
            vmem_limit_bytes=VMEM_LIMIT, collective_id=0, has_side_effects=True
        ),
        cost_estimate=cost(150),
    )(
        table, ints, tokens.reshape(per_dev, SPAN, d), cotangent.reshape(per_dev, SPAN, d), shard_p, shard_f,
        gain, up, bias, head_gain, ups, level,
    )


def rms_scale(x):
    return lax.rsqrt(jnp.mean(x * x, axis=-1, keepdims=True) + norm_eps)


def distances(ups, log_decay):
    high = log_decay.astype(BF)
    lower = (log_decay - high.astype(F32)).astype(BF)
    return dot(ups, high) + dot(ups, lower)


def head_cols(h, part):
    start = h * HEAD + (0, DK, 2 * DK, 2 * DK + DV)[part]
    return slice(start, start + (DK, DK, DV, DV)[part])


def in_rows(h):
    return slice(h * PROJ_ROWS + 16, h * PROJ_ROWS + 16 + HEAD)


def out_rows(h):
    return slice(h * PROJ_ROWS + 16 + HEAD, (h + 1) * PROJ_ROWS)


def log_sigmoid(v):
    return jnp.minimum(v, 0.0) - jnp.log(1.0 + jnp.exp(-jnp.abs(v)))


def project_kernel(
    step, ints, src, gain, weights, up, bias, ups,
    normed, qkvg, log_decay, rank, packet,
):
    x = src[...].astype(F32)
    nf = (x * rms_scale(x) * gain[...]).astype(BF)
    normed[...] = nf
    low = dot(nf, weights[0:16, :], 1, 1).astype(BF)
    rank[...] = low
    logits = dot(low, up[...]) + bias[...]
    ld = log_sigmoid(logits) * (1.0 / decay_scale)
    log_decay[...] = ld
    towards = jnp.exp(distances(ups[LEVELS + 1], ld))
    per_tile = TILE // SPAN
    for h in range(2):
        proj = dot(nf, weights[in_rows(h), :], 1, 1)
        qkvg[:, head_cols(h, 0)] = (proj[:, :DK] * scaling).astype(BF)
        qkvg[:, h * HEAD + DK : (h + 1) * HEAD] = proj[:, DK:].astype(BF)
    for j in range(per_tile):
        rows = slice(j * SPAN, (j + 1) * SPAN)
        keep = ints[step * per_tile + j].astype(F32)
        total = jnp.exp(jnp.sum(ld[rows], axis=0, keepdims=True)) * keep
        for h in range(2):
            lanes = slice(h * DK, (h + 1) * DK)
            states = slice(h * DV, (h + 1) * DV)
            f = slice(2 * DV + h, 2 * DV + h + 1)
            packet[f] = packet[f] * total[:, lanes]
            kd = (qkvg[rows, head_cols(h, 1)].astype(F32) * towards[rows, lanes]).astype(BF)
            packet[states] = packet[states] * total[:, lanes] + dot(qkvg[rows, head_cols(h, 2)], kd, 0, 0)


def within_kernel(qkvg, log_decay, ups, level, within):
    ld = log_decay[...]
    high = ld.astype(BF)
    lower = (ld - high.astype(F32)).astype(BF)
    lev = level[...]
    scores = [None, None]
    for l in range(LEVELS + 1):
        if l < LEVELS:
            x = jnp.exp(dot(ups[l], high) + dot(ups[l], lower))
        for h in range(2):
            q, k = qkvg[:, head_cols(h, 0)], qkvg[:, head_cols(h, 1)]
            if l < LEVELS:
                xh = x[:, h * DK : (h + 1) * DK]
                q = (q.astype(F32) * xh).astype(BF)
                k = (k.astype(F32) * xh).astype(BF)
            s = dot(q, k, 1, 1)
            scores[h] = jnp.where(lev == l, s, 0.0 if l == 0 else scores[h])
    for h in range(2):
        within[:, h * DV : (h + 1) * DV] = dot(scores[h].astype(BF), qkvg[:, head_cols(h, 2)])


def mix_kernel(
    step, ints, qkvg, log_decay, packet, ups, head_gain, weights,
    mixed, gated, attn, before,
):
    per_tile = TILE // SPAN
    ld = log_decay[...]
    since = jnp.exp(distances(ups[LEVELS], ld))
    towards = jnp.exp(distances(ups[LEVELS + 1], ld))
    for j in range(per_tile):
        rows = slice(j * SPAN, (j + 1) * SPAN)
        keep = ints[step * per_tile + j].astype(F32)
        for h in range(2):
            lanes = slice(h * DK, (h + 1) * DK)
            values = slice(h * DV, (h + 1) * DV)
            prev = packet[values] * keep
            prev_low = prev.astype(BF)
            before[j, h] = prev_low
            qd = (qkvg[rows, head_cols(h, 0)].astype(F32) * since[rows, lanes]).astype(BF)
            kd = (qkvg[rows, head_cols(h, 1)].astype(F32) * towards[rows, lanes]).astype(BF)
            mixed[rows, values] = mixed[rows, values] + dot(qd, prev_low, 1, 1)
            last = since[j * SPAN + SPAN - 1 : j * SPAN + SPAN, lanes]
            packet[values] = prev * last + dot(qkvg[rows, head_cols(h, 2)], kd, 0, 0)
    for h in range(2):
        values = slice(h * DV, (h + 1) * DV)
        m = mixed[:, values]
        g = qkvg[:, head_cols(h, 3)].astype(F32)
        y = m * rms_scale(m) * head_gain[...] * g * jax.nn.sigmoid(g)
        gated[:, values] = y.astype(BF)
    attn[...] = (
        dot(gated[:, :DV], weights[out_rows(0), :]) + dot(gated[:, DV:], weights[out_rows(1), :])
    ).astype(BF)


def ffn_kernel(
    f, ints, src, attn_a, attn_b, cot, gain, weights,
    hidden, normed, act, grad_gu, keep_out, send_out, grad_second,
    part,
):
    quarter = cot.shape[1] // 4
    hid = src[...].astype(F32) + (attn_a[...].astype(F32) + attn_b[...].astype(F32))
    hidden[...] = hid
    ns = (hid * rms_scale(hid) * gain[...]).astype(BF)
    normed[...] = ns
    c = cot[...]
    back, total = None, None
    for g in range(2):
        base = 3 * f * g
        w_gate, w_out, w_up = (slice(base + k * f, base + (k + 1) * f) for k in range(3))
        gate = dot(ns, weights[w_gate, :], 1, 1)
        upper = dot(ns, weights[w_up, :], 1, 1)
        ga = dot(c, weights[w_out, :], 1, 1)
        sig = jax.nn.sigmoid(gate)
        swish = gate * sig
        low = (swish * upper).astype(BF)
        gg = (ga * upper * sig * (1.0 + gate * (1.0 - sig))).astype(BF)
        gu = (ga * swish).astype(BF)
        pitch = act.shape[1] // 2
        act[:, g * pitch : g * pitch + f] = low
        grad_gu[:, g * pitch : g * pitch + f] = gg
        grad_gu[:, (2 + g) * pitch : (2 + g) * pitch + f] = gu
        out = dot(low, weights[w_out, :])
        e = dot(gg, weights[w_gate, :]) + dot(gu, weights[w_up, :])
        total = out if g == 0 else total + out
        back = e if g == 0 else back + e
    part[...] = total.astype(BF)
    grad_second[...] = back.astype(BF)
    core = ints[4]
    for h in range(2):
        mine = pl.multiple_of((2 * h + core) * quarter, 128)
        theirs = pl.multiple_of((2 * h + 1 - core) * quarter, 128)
        keep_out[:, h * quarter : (h + 1) * quarter] = part[:, pl.ds(mine, quarter)]
        send_out[:, h * quarter : (h + 1) * quarter] = part[:, pl.ds(theirs, quarter)]


def weight_grad_into(acc, lhs, rhs, chunk):
    def body(i, _):
        at = pl.multiple_of(i * chunk, chunk)
        acc[pl.ds(at, chunk), :] = dot(lhs[:, pl.ds(at, chunk)], rhs[...], 0, 0).astype(BF)
        return 0

    lax.fori_loop(0, acc.shape[0] // chunk, body, 0)


def out_back_kernel(
    n, ints, hidden, cot, gs_a, gs_b, gain, weights, gated, mixed, qkvg, log_decay, head_gain, ups,
    keep_out, recv_out,
    grad_hidden, grad_mixed, grad_gate, gain_grad, head_grad, packet, out_own, out_cross, *rest,
):
    w_grads, (acc, state, gain_sum, head_sum) = rest[:-4], rest[-4:]
    step = pl.program_id(0)
    tile = n - 1 - step
    per_tile = TILE // SPAN

    @pl.when(step == 0)
    def _():
        acc[...] = jnp.zeros_like(acc)
        state[...] = jnp.zeros_like(state)
        gain_sum[...] = jnp.zeros_like(gain_sum)
        head_sum[...] = jnp.zeros_like(head_sum)

    x, core = ints[7], ints[4]
    quarter = out_own.shape[1]
    for target, half in ((out_own, x), (out_cross, 1 - x)):
        at = pl.multiple_of((2 * half + core) * quarter, 128)
        pair = pl.multiple_of(half * quarter, 128)
        share = keep_out[:, pl.ds(pair, quarter)].astype(F32) + recv_out[:, pl.ds(pair, quarter)].astype(F32)
        target[...] = (hidden[:, pl.ds(at, quarter)] + share).astype(BF)
    gs = gs_a[...].astype(F32) + gs_b[...].astype(F32)
    hid = hidden[...]
    inv = rms_scale(hid)
    normal = hid * inv
    gain_sum[0:1, :] += jnp.sum(gs * normal, axis=0, keepdims=True)
    e = gs * gain[...]
    gh = cot[...].astype(F32) + inv * (e - normal * jnp.mean(e * normal, axis=-1, keepdims=True))
    grad_hidden[...] = gh
    low = gh.astype(BF)
    acc[...] += dot(gated[...], low, 0, 0)
    for h in range(2):
        values = slice(h * DV, (h + 1) * DV)
        m = mixed[:, values]
        inv_head = rms_scale(m)
        nh = m * inv_head
        g = qkvg[:, head_cols(h, 3)].astype(F32)
        sig = jax.nn.sigmoid(g)
        w = g * sig
        gd = dot(low, weights[out_rows(h), :], 1, 1)
        head_sum[0:1, :] += jnp.sum(gd * nh * w, axis=0, keepdims=True)
        gn = gd * head_gain[...]
        grad_gate[:, values] = (gn * nh * sig * (1.0 + g * (1.0 - sig))).astype(BF)
        gn = gn * w
        gm = inv_head * (gn - nh * jnp.mean(gn * nh, axis=-1, keepdims=True))
        grad_mixed[:, values] = gm.astype(BF)
    since = jnp.exp(distances(ups[LEVELS], log_decay[...]))
    for j in reversed(range(per_tile)):
        rows = slice(j * SPAN, (j + 1) * SPAN)
        keep = ints[8 + tile * per_tile + j].astype(F32)
        for h in range(2):
            lanes = slice(h * DK, (h + 1) * DK)
            values = slice(h * DV, (h + 1) * DV)
            qd = (qkvg[rows, head_cols(h, 0)].astype(F32) * since[rows, lanes]).astype(BF)
            last = since[j * SPAN + SPAN - 1 : j * SPAN + SPAN, lanes]
            state[h] = keep * (state[h] * last + dot(grad_mixed[rows, values], qd, 0, 0))

    @pl.when(step == n - 1)
    def _():
        packet[0:DV] = state[0]
        packet[DV : 2 * DV] = state[1]
        gain_grad[...] = gain_sum[...]
        head_grad[...] = head_sum[...]
        w_grads[0][...] = acc[...].astype(BF)


def within_back_kernel(qkvg, log_decay, grad_mixed, ups, downs, level, level_t, grad_qk, grad_v, grad_ld):
    ld = log_decay[...]
    high = ld.astype(BF)
    lower = (ld - high.astype(F32)).astype(BF)
    lev, lev_t = level[...], level_t[...]
    gd, gd_t = [], []
    for h in range(2):
        v, gm = qkvg[:, head_cols(h, 2)], grad_mixed[:, h * DV : (h + 1) * DV]
        gd.append(dot(gm, v, 1, 1))
        gd_t.append(dot(v, gm, 1, 1))
    scores_t = [None, None]
    grad_q, grad_k = [None, None], [None, None]
    for l in range(LEVELS + 1):
        if l < LEVELS:
            x = jnp.exp(dot(ups[l], high) + dot(ups[l], lower))
        parts = []
        for h in range(2):
            q, k = qkvg[:, head_cols(h, 0)], qkvg[:, head_cols(h, 1)]
            if l < LEVELS:
                xh = x[:, h * DK : (h + 1) * DK]
                qf, kf = q.astype(F32) * xh, k.astype(F32) * xh
                q, k = qf.astype(BF), kf.astype(BF)
            s = dot(k, q, 1, 1)
            scores_t[h] = jnp.where(lev_t == l, s, 0.0 if l == 0 else scores_t[h])
            here = jnp.where(lev == l, gd[h], 0.0).astype(BF)
            here_t = jnp.where(lev_t == l, gd_t[h], 0.0).astype(BF)
            dq, dk = dot(here, k), dot(here_t, q)
            if l < LEVELS:
                parts.append(qf * dq + kf * dk)
                dq, dk = dq * xh, dk * xh
            grad_q[h] = dq if l == 0 else grad_q[h] + dq
            grad_k[h] = dk if l == 0 else grad_k[h] + dk
        if l < LEVELS:
            both = dot(downs[l], jnp.concatenate(parts, axis=1).astype(BF))
            total = both if l == 0 else total + both
    grad_ld[...] = total
    for h in range(2):
        grad_qk[:, 2 * h * DK : (2 * h + 1) * DK] = grad_q[h]
        grad_qk[:, (2 * h + 1) * DK : (2 * h + 2) * DK] = grad_k[h]
        grad_v[:, h * DV : (h + 1) * DV] = dot(
            scores_t[h].astype(BF), grad_mixed[:, h * DV : (h + 1) * DV]
        ).astype(BF)


def project_back_kernel(
    tile, ints, qkvg, log_decay, grad_mixed, before, grad_qk, grad_v, grad_ld, grad_gate, rank, up, bias,
    ups, downs, weights,
    grad_project, grad_first, rank_part, packet, up_sum, bias_sum, d_since, d_towards, ld_sum,
):
    per_tile = TILE // SPAN
    ld = log_decay[...]
    since = jnp.exp(distances(ups[0], ld))
    towards = jnp.exp(distances(ups[1], ld))
    for j in reversed(range(per_tile)):
        rows = slice(j * SPAN, (j + 1) * SPAN)
        keep = ints[tile * per_tile + j].astype(F32)
        for h in range(2):
            lanes = slice(h * DK, (h + 1) * DK)
            values = slice(h * DV, (h + 1) * DV)
            gm = grad_mixed[rows, values]
            v = qkvg[rows, head_cols(h, 2)]
            qd = qkvg[rows, head_cols(h, 0)].astype(F32) * since[rows, lanes]
            kd = qkvg[rows, head_cols(h, 1)].astype(F32) * towards[rows, lanes]
            prev = before[j, h]
            after = packet[values]
            after_low = after.astype(BF)
            dq = dot(gm, prev)
            dk = dot(v, after_low)
            d_since[rows, lanes] = (qd * dq).astype(BF)
            d_towards[rows, lanes] = (kd * dk).astype(BF)
            dq = grad_qk[rows, 2 * h * DK : (2 * h + 1) * DK] + dq * since[rows, lanes]
            dk = grad_qk[rows, (2 * h + 1) * DK : (2 * h + 2) * DK] + dk * towards[rows, lanes]
            dv = grad_v[rows, values].astype(F32) + dot(kd.astype(BF), after_low, 1, 1)
            grad_project[rows, head_cols(h, 0)] = (dq * scaling).astype(BF)
            grad_project[rows, head_cols(h, 1)] = dk.astype(BF)
            grad_project[rows, head_cols(h, 2)] = dv.astype(BF)
            grad_project[rows, head_cols(h, 3)] = grad_gate[rows, values]
            last = since[j * SPAN + SPAN - 1 : j * SPAN + SPAN, lanes]
            d_last = last * jnp.sum(prev.astype(F32) * after, axis=0, keepdims=True)
            ld_sum[rows, lanes] = grad_ld[rows, lanes] + d_last
            packet[values] = keep * (after * last + dot(gm, qd.astype(BF), 0, 0))
    d_log = ld_sum[...] + dot(downs[0], d_since[...]) + dot(downs[1], d_towards[...])
    logits = dot(rank[...], up[...]) + bias[...]
    gl = (d_log * (1.0 / decay_scale) * jax.nn.sigmoid(-logits)).astype(BF)
    up_sum[...] += dot(rank[...], gl, 0, 0)
    bias_sum[0:1, :] += jnp.sum(gl.astype(F32), axis=0, keepdims=True)
    rank_part[...] = dot(up[...], gl, 1, 1)
    grad_first[...] = (
        dot(grad_project[:, :HEAD], weights[in_rows(0), :])
        + dot(grad_project[:, HEAD:], weights[in_rows(1), :])
    ).astype(BF)


def source_back_kernel(
    src, normed, gf_a, gf_b, rank_a, rank_b, w_down, gain, grad_hidden,
    own, cross, dealt, down_sum, gain_sum,
):
    low = (rank_a[...] + rank_b[...]).astype(BF)
    gf = gf_a[...].astype(F32) + gf_b[...].astype(F32) + dot(low, w_down[...], 0, 0)
    x = src[...].astype(F32)
    inv = rms_scale(x)
    normal = x * inv
    gain_sum[0:1, :] += jnp.sum(gf * normal, axis=0, keepdims=True)
    e = gf * gain[...]
    dealt[...] = (
        grad_hidden[...] + inv * (e - normal * jnp.mean(e * normal, axis=-1, keepdims=True))
    ).astype(BF)
    down_sum[...] += dot(low, normed[...])
    quarter = own.shape[2]
    at_x, at_core = lax.axis_index("x"), lax.axis_index("core")
    for out, half in ((own, at_x), (cross, 1 - at_x)):
        col = pl.multiple_of((2 * half + at_core) * quarter, 128)
        for j in range(TILE // SPAN):
            out[j] = dealt[j * SPAN : (j + 1) * SPAN, pl.ds(col, quarter)]


def back_kernel(nd, spans, reach, direct, f, table, act, grad_gu, normed, cot, qkvg, log_decay, grad_mixed, packet_in,
                factors, out_own, out_cross, ups, downs, level, level_t, *rest):
    n_sums = 4 if direct else 3
    (leaving, grad_qk_o, grad_v_o, grad_ld_o, gath_o, *sums), rest = rest[: 5 + n_sums], rest[5 + n_sums :]
    (grad_qk, grad_v, grad_ld, sent_packets, got_packets), rest = rest[:5], rest[5:]
    (carry_send, carry_recv, out_sems), rest = rest[:3], rest[3:]
    (joined, sent, gath), rest = rest[:3], rest[3:]
    undeal_sems, rest = rest[:4], rest[4:]
    pitch = act.shape[1] // 2
    tiles = spans * SPAN // TILE
    nz = nd // 2
    carry = Carry(nd, reach, -1, leaving, sent_packets, got_packets, carry_send, carry_recv)
    enter(nd, carry.shifts())
    undeal = Undeal(nd, spans, table, out_own, out_cross, joined, sent, gath, undeal_sems)
    undeal.begin()
    leaving[: 2 * DV] = packet_in[...]
    leaving[2 * DV :] = factors[...]
    carry.send(0)
    outgoing = []

    def store(value, out):
        outgoing.append(pltpu.make_async_copy(value, out, out_sems.at[len(outgoing)]))
        outgoing[-1].start()

    def at(ref, i):
        return ref.at[pl.ds(pl.multiple_of(i * TILE, TILE), TILE), :]

    def tile(i, _):
        within_back_kernel(
            at(qkvg, i), at(log_decay, i), at(grad_mixed, i), ups, downs, level, level_t,
            at(grad_qk, i), at(grad_v, i), at(grad_ld, i),
        )
        return 0

    def some(first, last):
        return lambda: lax.fori_loop(first, last, tile, 0)

    stages = list(range(carry.run()))

    def advance():
        if stages:
            carry.step(stages.pop(0))

    if direct:
        accs, rest = rest[:3], rest[3:]
        chains = [
            Collapse(nd, order, acc, pitch, low, count, rest[3 * k], rest[3 * k + 1 : 3 * k + 3])
            for k, (acc, order, low, count) in enumerate(
                ((accs[0], 0, 0, f), (accs[1], 1, 0, f), (accs[2], 0, 0, f // 2), (accs[2], 1, f // 2, f // 2))
            )
        ]
        weight_grad_into(accs[0], grad_gu.at[:, pl.ds(0, 2 * pitch)], normed, 128)
        chains[0].begin()
        advance()
        weight_grad_into(accs[1], grad_gu.at[:, pl.ds(2 * pitch, 2 * pitch)], normed, 128)
        chains[1].begin()
        advance()
        undeal.exchange()
        for kz in [k % nz for k in range(1, nz + 1)]:
            chains[0].second(kz)
        weight_grad_into(accs[2], act, cot, 128)
        for kz in [k % nz for k in range(1, nz + 1)]:
            chains[1].second(kz)
        chains[2].begin()
        chains[3].begin()
        advance()
        for kz in [k % nz for k in range(1, nz + 1)]:
            chains[0].third(kz)
            chains[1].third(kz)
            some(kz, kz + 1)()
        progress(chains[2:], nz, [some(nz, tiles)])
        for chain, out in zip(chains, sums):
            chain.finish(out)
    else:
        undeal.exchange()
        weight_grad_into(sums[0], grad_gu.at[:, pl.ds(0, 2 * pitch)], normed, 128)
        weight_grad_into(sums[1], grad_gu.at[:, pl.ds(2 * pitch, 2 * pitch)], normed, 128)
        weight_grad_into(sums[2], act, cot, 128)
        some(0, tiles)()
        while stages:
            advance()
    store(grad_qk, grad_qk_o)
    store(grad_v, grad_v_o)
    store(grad_ld, grad_ld_o)
    for k in range(1, nd):
        undeal.arrive(k)
    store(gath, gath_o)
    undeal.finish()
    for copy in outgoing:
        copy.wait()


def last_kernel(nd, spans, direct, table, keep, qkvg, log_decay, grad_mixed, before, leaving, grad_qk, grad_v, grad_ld,
                grad_gate, rank, up, bias, ups, downs, weights, src, normed, grad_hidden, gain, po_in, *rest):
    n_sums = 4 if direct else 1
    (gath_o, down_sum, gain_sum, up_sum, bias_sum, *sums), rest = rest[: 5 + n_sums], rest[5 + n_sums :]
    (packet, grad_project, grad_first, grad_first_other, rank_part, rank_other), rest = rest[:6], rest[6:]
    (d_since, d_towards, ld_sum, dealt), rest = rest[:4], rest[4:]
    (gf_send, gf_recv, rk_send, rk_recv, out_sems), rest = rest[:5], rest[5:]
    (own, cross, joined, sent, gath), rest = rest[:5], rest[5:]
    undeal_sems, rest = rest[:6], rest[6:]
    tiles = spans * SPAN // TILE
    per_tile = TILE // SPAN
    nz = nd // 2
    enter(nd)
    core = lax.axis_index("core")
    undeal = Undeal(nd, spans, table, own, cross, joined, sent, gath, undeal_sems)
    chains = []
    if direct:
        (po_acc, pi_acc), rest = rest[:2], rest[2:]
        halves = ((pi_acc, 0, HEAD), (pi_acc, 1, HEAD), (po_acc, 0, DV), (po_acc, 1, DV))
        chains = [
            Collapse(
                nd, order, acc, size, order * size // 2, size // 2, rest[3 * k], rest[3 * k + 1 : 3 * k + 3]
            )
            for k, (acc, order, size) in enumerate(halves)
        ]
        fill = pltpu.make_async_copy(po_in, po_acc, out_sems.at[0])
        fill.start()
        fill.wait()
        chains[2].begin()
        chains[3].begin()
    packet[...] = leaving[...]
    for ref in (down_sum, gain_sum, up_sum, bias_sum):
        ref[...] = jnp.zeros_like(ref)

    def at(ref, i):
        return ref.at[pl.ds(pl.multiple_of(i * TILE, TILE), TILE), :]

    def swap_first(i):
        return copy_to(at(grad_first, i), at(grad_first_other, i), gf_send.at[i], gf_recv.at[i], {"core": 1 - core})

    def swap_rank(i):
        return copy_to(rank_part.at[i], rank_other.at[i], rk_send.at[i], rk_recv.at[i], {"core": 1 - core})

    def body(step, _):
        i = tiles - 1 - step
        project_back_kernel(
            i, keep, at(qkvg, i), at(log_decay, i), at(grad_mixed, i), before.at[pl.ds(i * per_tile, per_tile)],
            at(grad_qk, i), at(grad_v, i), at(grad_ld, i), at(grad_gate, i), at(rank, i), up, bias, ups, downs, weights,
            at(grad_project, i), at(grad_first, i), rank_part.at[i], packet, up_sum, bias_sum,
            d_since, d_towards, ld_sum,
        )
        swap_first(i).start()
        swap_rank(i).start()
        return 0

    lax.fori_loop(0, tiles, body, 0)
    if direct:
        for kz in [k % nz for k in range(1, nz + 1)]:
            chains[2].second(kz)
            chains[3].second(kz)

    def finish_tile(step, _):
        i = tiles - 1 - step
        swap_first(i).wait()
        swap_rank(i).wait()
        source_back_kernel(
            at(src, i), at(normed, i), at(grad_first, i), at(grad_first_other, i), rank_part.at[i], rank_other.at[i],
            weights.at[pl.ds(0, 16), :], gain, at(grad_hidden, i),
            own.at[pl.ds(i * per_tile, per_tile)], cross.at[pl.ds(i * per_tile, per_tile)],
            dealt, down_sum, gain_sum,
        )
        return 0

    lax.fori_loop(0, tiles, finish_tile, 0)
    undeal.begin()
    if direct:
        weight_grad_into(pi_acc, grad_project, normed, 128)
        chains[0].begin()
        chains[1].begin()
        for kz in [k % nz for k in range(1, nz + 1)]:
            chains[2].third(kz)
            chains[3].third(kz)
    else:
        weight_grad_into(sums[0], grad_project, normed, 128)
    undeal.exchange()
    arrivals = [functools.partial(undeal.arrive, k) for k in range(1, nd)]
    if direct:
        for kz in [k % nz for k in range(1, nz + 1)]:
            chains[0].second(kz)
            chains[1].second(kz)
            if arrivals:
                arrivals.pop(0)()
        for kz in [k % nz for k in range(1, nz + 1)]:
            chains[0].third(kz)
            chains[1].third(kz)
            if arrivals:
                arrivals.pop(0)()
        chains[2].finish(sums[2])
        chains[3].finish(sums[3])
    for arrive in arrivals:
        arrive()
    undeal.finish()
    out = pltpu.make_async_copy(gath, gath_o, out_sems.at[0])
    out.start()
    if direct:
        chains[0].finish(sums[0])
        chains[1].finish(sums[1])
    out.wait()


def remote(kernel, ins, specs, outs, out_specs, scratch, name, number, us):
    return pl.pallas_call(
        kernel,
        in_specs=specs,
        out_specs=out_specs,
        out_shape=outs,
        scratch_shapes=scratch,
        name=name,
        compiler_params=pltpu.CompilerParams(
            vmem_limit_bytes=VMEM_LIMIT, collective_id=number, has_side_effects=True
        ),
        cost_estimate=cost(us),
    )(*ins)


def all_sum(value, axes, sizes):
    for axis, size in zip(axes, sizes):
        bit = 1
        while bit < size:
            value = value + lax.ppermute(value, axis, [(i, i ^ bit) for i in range(size)])
            bit *= 2
    return value


def square_sum(array):
    return jnp.sum(array * array)


def adam_update(weight, grad, first, second, factor, decay_rate):
    clipped = grad * factor
    first_new = beta_one * first + (1.0 - beta_one) * clipped
    second_new = beta_two * second + (1.0 - beta_two) * clipped * clipped
    first_hat = first_new / (1.0 - beta_one**adam_step)
    second_hat = second_new / (1.0 - beta_two**adam_step)
    master = weight.astype(F32)
    change = -learn_rate * (first_hat / (jnp.sqrt(second_hat) + adam_eps) + decay_rate * master)
    return (grad, first_new, second_new, change)


def swap(value, axis):
    return lax.ppermute(value, axis, [(0, 1), (1, 0)])


def on_device(
    tokens, cotangent, seq_extra, deal, proj_in, decay_down, decay_up, decay_bias, head_gain, proj_out, block_gains,
    ffn_in, ffn_out, first_proj_in, second_proj_in, first_decay_down, second_decay_down, first_decay_up,
    second_decay_up, first_decay_bias, second_decay_bias, first_head_gain, second_head_gain, first_proj_out,
    second_proj_out, first_block_gains, second_block_gains, first_ffn_in, second_ffn_in, first_ffn_out, second_ffn_out,
):
    d = tokens.shape[1]
    nd = lax.axis_size("dp")
    nz = nd // 2
    dp, x, core = lax.axis_index("dp"), lax.axis_index("x"), lax.axis_index("core")
    z, y = dp // 2, dp % 2
    tensor = 2 * x + core
    per_dev = tokens.shape[0] // SPAN
    spans = per_dev // 2
    rows = spans * SPAN
    tiles = rows // TILE
    capacity = -(-per_dev // nd)
    quarter = d // 4
    f = ffn_out.shape[0]
    w = d // nd
    direct = w % 128 == 0

    recv_slot, send_local, back_local, home_slot = deal_tables(deal, nd, per_dev, capacity, dp)
    mine = lax.dynamic_slice_in_dim(recv_slot, x * spans, spans)
    theirs = lax.dynamic_slice_in_dim(recv_slot, (1 - x) * spans, spans)
    span_ids = (dp * 2 + x) * spans + jnp.arange(spans, dtype=jnp.int32)
    keep = 1 - span_starts(seq_extra, span_ids)
    other_quarter = 2 * (1 - x) + core
    quarters = jnp.stack([tensor, other_quarter, 2 * x + 1 - core, 2 * (1 - x) + 1 - core])
    ints = jnp.concatenate([quarters, jnp.stack([core, z, y, x]), keep]).astype(jnp.int32)
    ups, downs, level, level_t = level_matrices()

    hh, ho, hf = HEAD // 2, DV // 2, f // 2
    pitch = up_to(f, 128)
    ffn_t = ffn_in.reshape(w, 2 * f).T
    shard_p = jnp.concatenate([decay_down.T, proj_in.reshape(w, HEAD).T, proj_out.reshape(DV, w)], axis=0)
    shard_f = jnp.concatenate([ffn_t[:f], ffn_out, ffn_t[f:]], axis=0)

    def fit(parts):
        return jnp.concatenate(parts, axis=0)

    table = jnp.concatenate([send_local, mine, theirs]).astype(jnp.int32)
    if not direct:

        def gathered(shard):
            return jnp.swapaxes(lax.all_gather(shard, "dp", axis=0), 0, 1).reshape(shard.shape[0], d)

        def halves(shard):
            own, other = gathered(shard), gathered(swap(shard, "x"))
            return jnp.where(x == 0, fit([own, other]), fit([other, own]))

        shard_p, shard_f = halves(shard_p), halves(shard_f)

    up_own = decay_up.reshape(16, DK)
    bias_own = decay_bias.reshape(1, DK)
    small_own = jnp.concatenate([up_own.astype(F32), bias_own, jnp.zeros((7, DK), F32)], axis=0)
    small_other = swap(small_own, "x")
    small_both = jnp.where(
        x == 0,
        jnp.concatenate([small_own, small_other], axis=1),
        jnp.concatenate([small_other, small_own], axis=1),
    )
    up, bias = small_both[:16].astype(BF), small_both[16:17]
    gain_one, gain_two = block_gains[0:1], block_gains[1:2]
    head_row = head_gain.reshape(1, DV)

    def tall(cols, dtype=BF):
        return sds(rows, cols, dtype=dtype)

    nlev = LEVELS + 2
    sequence = nd * 2
    reach = -(-(MAX_SPANS - 1) // spans)
    (src, cot, weights, w_ffn, normed_first, qkvg, log_decay, rank, mixed, gated, attn, before, attn_other,
     factors) = forward(
        table, keep.astype(jnp.int32), tokens, cotangent, shard_p, shard_f, gain_one, up, bias, head_row, ups, level,
        nd, spans, reach, direct,
    )
    ff = 2 * f
    hidden, normed_second, act, grad_gu, keep_out, send_out, grad_second = run(
        functools.partial(ffn_kernel, f), (tiles,),
        [SMEM] + [rows_spec(d)] * 4 + [whole_spec(1, d), whole_spec(3 * ff, d)],
        [rows_spec(d), rows_spec(d), rows_spec(2 * pitch), rows_spec(4 * pitch), rows_spec(2 * quarter),
         rows_spec(2 * quarter), rows_spec(d)],
        [tall(d, F32), tall(d), tall(2 * pitch), tall(4 * pitch), tall(2 * quarter), tall(2 * quarter), tall(d)],
        [pltpu.VMEM((TILE, d), BF)],
        "ffn", 34,
    )(ints, src, attn, attn_other, cot, gain_two, w_ffn)
    gs_other = swap(grad_second, "core")
    recv_out = swap(send_out, "core")

    def plain_shard(full, f_rows):
        full = jnp.swapaxes(full.reshape(2 * f_rows, nd, w), 0, 1)
        total = lax.psum_scatter(full, "dp", scatter_dimension=0, tiled=True)[0].astype(F32)
        keep_rows = lax.dynamic_slice_in_dim(total, x * f_rows, f_rows)
        give_rows = lax.dynamic_slice_in_dim(total, (1 - x) * f_rows, f_rows)
        return keep_rows + swap(give_rows, "x")

    grad_hidden, grad_mixed, grad_gate, gain_second, head_part, packet_back, out_own, out_cross, acc_po = run(
        functools.partial(out_back_kernel, tiles), (tiles,),
        [SMEM] + [rows_spec(d, tiles)] * 4
        + [whole_spec(1, d), whole_spec(2 * PROJ_ROWS, d), rows_spec(2 * DV, tiles), rows_spec(2 * DV, tiles),
           rows_spec(2 * HEAD, tiles), rows_spec(2 * DK, tiles), whole_spec(1, DV), whole_spec(nlev, TILE, TILE),
           rows_spec(2 * quarter, tiles), rows_spec(2 * quarter, tiles)],
        [rows_spec(d, tiles), rows_spec(2 * DV, tiles), rows_spec(2 * DV, tiles), whole_spec(8, d),
         whole_spec(8, DV), whole_spec(2 * DV, DK), rows_spec(quarter, tiles), rows_spec(quarter, tiles),
         whole_spec(2 * DV, d)],
        [tall(d, F32), tall(2 * DV), tall(2 * DV), sds(8, d), sds(8, DV), sds(2 * DV, DK), tall(quarter),
         tall(quarter), sds(2 * DV, d, dtype=BF)],
        [pltpu.VMEM((2 * DV, d), F32), pltpu.VMEM((2, DV, DK), F32), pltpu.VMEM((8, d), F32), pltpu.VMEM((8, DV), F32)],
        "out_back", 19,
    )(ints, hidden, cot, grad_second, gs_other, gain_two, weights, gated, mixed, qkvg, log_decay, head_row, ups,
      keep_out, recv_out)

    dma = pltpu.SemaphoreType.DMA
    steps = len(carry_widths(reach)[0]) + 2
    shape_qk, shape_v, shape_ld = (rows, 4 * DK), (rows, 2 * DV), (rows, 2 * DK)
    buffers, sems = undeal_scratch(nd, per_dev, spans, quarter, capacity, False)
    scratch = [pltpu.VMEM(shape_qk, F32), pltpu.VMEM(shape_v, BF), pltpu.VMEM(shape_ld, F32)]
    scratch += [pltpu.VMEM((steps - 1, 2 * DV + 16, DK), BF), pltpu.VMEM((steps, 2 * DV + 16, DK), BF)]
    scratch += [dma((steps,)), dma((steps,)), dma((4,))] + buffers[2:] + sems
    if direct:
        sums = [sds(f, w), sds(f, w), sds(f // 2, w), sds(f // 2, w)]
        scratch += [pltpu.VMEM((2 * pitch, d), BF)] * 3
        for out in sums:
            scratch += collapse_scratch(nd, out.shape[0], w)
    else:
        sums = [sds(2 * pitch, d, dtype=BF)] * 3
    leaving, grad_qk, grad_v, grad_ld, back_out, *sums_f = remote(
        functools.partial(back_kernel, nd, spans, reach, direct, f),
        (back_local, act, grad_gu, normed_second, cot, qkvg, log_decay, grad_mixed, packet_back, factors,
         out_own.reshape(spans, SPAN, quarter), out_cross.reshape(spans, SPAN, quarter), ups, downs, level, level_t),
        [SMEM] + [VMEM] * 15,
        [sds(2 * DV + 16, DK), sds(*shape_qk), sds(*shape_v, dtype=BF), sds(*shape_ld),
         sds(nd * capacity, SPAN, quarter, dtype=BF)] + sums,
        [VMEM] + [ANY] * 4 + [VMEM] * len(sums),
        scratch, "back_all", 1, 110,
    )
    if direct:
        shard_gate, shard_up, shard_fo = sums_f[0], sums_f[1], fit(sums_f[2:])
    else:
        shard_gate, shard_up, shard_fo = (plain_shard(v, pitch)[:f] for v in sums_f)
    block_out = home([back_out.reshape(-1, quarter)], home_slot, [jnp.int32(0)], "block_out_home")

    buffers, sems = undeal_scratch(nd, per_dev, spans, quarter, capacity, True)
    scratch = [
        pltpu.VMEM((2 * DV + 16, DK), F32), pltpu.VMEM((rows, 2 * HEAD), BF), pltpu.VMEM((rows, d), BF),
        pltpu.VMEM((rows, d), BF), pltpu.VMEM((tiles, 16, TILE), F32), pltpu.VMEM((tiles, 16, TILE), F32),
        pltpu.VMEM((TILE, 2 * DK), BF), pltpu.VMEM((TILE, 2 * DK), BF), pltpu.VMEM((TILE, 2 * DK), F32),
        pltpu.VMEM((TILE, d), BF), dma((tiles,)), dma((tiles,)), dma((tiles,)), dma((tiles,)), dma((1,)),
    ] + buffers + sems
    if direct:
        sums = [sds(hh, w), sds(hh, w), sds(ho, w), sds(ho, w)]
        scratch += [pltpu.VMEM((2 * DV, d), BF), pltpu.VMEM((2 * HEAD, d), BF)]
        for out in sums:
            scratch += collapse_scratch(nd, out.shape[0], w)
    else:
        sums = [sds(2 * HEAD, d, dtype=BF)]
    back_grad, down_grad, gain_first, up_grad, bias_grad, *sums_p = remote(
        functools.partial(last_kernel, nd, spans, direct),
        (back_local, keep.astype(jnp.int32), qkvg, log_decay, grad_mixed, before, leaving, grad_qk, grad_v, grad_ld,
         grad_gate, rank, up, bias, ups[LEVELS:], downs[LEVELS:], weights, src, normed_first, grad_hidden, gain_one,
         acc_po),
        [SMEM, SMEM] + [VMEM] * 19 + [ANY],
        [sds(nd * capacity, SPAN, d, dtype=BF), sds(16, d), sds(8, d), sds(16, 2 * DK), sds(8, 2 * DK)] + sums,
        [ANY] + [VMEM] * (4 + len(sums)),
        scratch, "finish_all", 2, 100,
    )
    if direct:
        shard_pi, shard_po = fit(sums_p[:2]), fit(sums_p[2:])
    else:
        shard_pi, shard_po = plain_shard(sums_p[0], HEAD), plain_shard(acc_po, DV)
    token_grad = home([back_grad.reshape(-1, d)], home_slot, [jnp.int32(0)], "token_grad_home")

    small = jnp.concatenate(
        [
            gain_first[0].reshape(-1, 128),
            gain_second[0].reshape(-1, 128),
            down_grad.reshape(-1, 128),
            up_grad.reshape(-1, 128),
            bias_grad[0].reshape(-1, 128),
            head_part[0].reshape(-1, 128),
        ],
        axis=0,
    )
    small = all_sum(small, ("x", "dp"), (2, nd))
    rows_d = d // 128
    cuts = [rows_d, rows_d, 16 * rows_d, 32, 2, 2]
    starts = [sum(cuts[:k]) for k in range(len(cuts) + 1)]
    gain_first, gain_second, down_total, up_total, bias_total, head_total = (
        small[starts[k] : starts[k + 1]].reshape(-1) for k in range(len(cuts))
    )
    head_total = head_total + swap(head_total, "core")
    gains_total = jnp.stack([gain_first, gain_second])
    down_total = down_total.reshape(16, d)
    shard_down = lax.dynamic_slice_in_dim(down_total, dp * w, w, 1).T
    up_total = up_total.reshape(16, 2, DK)
    up_total = jnp.where(x == 0, up_total[:, 0:1], up_total[:, 1:2])
    bias_total = bias_total.reshape(2, DK)
    bias_total = jnp.where(x == 0, bias_total[0:1], bias_total[1:2])

    shard_in = shard_pi.T.reshape(proj_in.shape)
    shard_out = shard_po.reshape(proj_out.shape)
    shard_ffn_in = jnp.stack([shard_gate.T, shard_up.T], axis=1)
    shard_ffn_out = shard_fo
    n_dev = 4 * nd
    local_sq = (
        square_sum(shard_pi)
        + square_sum(shard_po)
        + square_sum(shard_gate)
        + square_sum(shard_up)
        + square_sum(shard_fo)
        + square_sum(shard_down) / 4
        + (square_sum(up_total) + square_sum(bias_total)) / nd
        + (square_sum(head_total) + square_sum(gains_total)) / n_dev
    )
    norm_sq = all_sum(jnp.broadcast_to(local_sq, (8, 128)), ("core", "x", "dp"), (2, 2, nd))
    grad_norm = jnp.sqrt(norm_sq[0, 0])
    clip_norm = clip_scale * math.sqrt(PARAMS)
    factor = jnp.minimum(1.0, clip_norm / (grad_norm + 1e-06))
    update_in = adam_update(proj_in, shard_in, first_proj_in, second_proj_in, factor, weight_decay)
    update_down = adam_update(decay_down, shard_down, first_decay_down, second_decay_down, factor, weight_decay)
    update_up = adam_update(decay_up, up_total, first_decay_up, second_decay_up, factor, weight_decay)
    update_bias = adam_update(decay_bias, bias_total, first_decay_bias, second_decay_bias, factor, 0.0)
    update_head = adam_update(head_gain, head_total, first_head_gain, second_head_gain, factor, 0.0)
    update_out = adam_update(proj_out, shard_out, first_proj_out, second_proj_out, factor, weight_decay)
    update_gains = adam_update(block_gains, gains_total, first_block_gains, second_block_gains, factor, 0.0)
    update_ffn_in = adam_update(ffn_in, shard_ffn_in, first_ffn_in, second_ffn_in, factor, weight_decay)
    update_ffn_out = adam_update(ffn_out, shard_ffn_out, first_ffn_out, second_ffn_out, factor, weight_decay)
    return (
        block_out, token_grad, grad_norm, *update_in, *update_down, *update_up, *update_bias, *update_head,
        *update_out, *update_gains, *update_ffn_in, *update_ffn_out,
    )


def solution(mesh):
    nd, nt = mesh.shape["dp"], mesh.shape["tensor"]
    fine = Mesh(mesh.devices.reshape(nd, nt // 2, 2), ("dp", "x", "core"))
    t = ("x", "core")
    w_specs = {
        "proj_in": P("dp", t, None),
        "decay_down": P("dp", None),
        "decay_up": P(None, t, None),
        "decay_bias": P(t, None),
        "head_gain": P(),
        "proj_out": P(t, None, "dp"),
        "block_gains": P(),
        "ffn_in": P("dp", None, t),
        "ffn_out": P(t, "dp"),
    }
    specs = list(w_specs.values())
    placed = [P("dp", None), P("dp", None), P(), P()] + specs
    results = [P("dp", t), P("dp", None), P()]
    for spec in specs:
        placed += [spec] * 2
        results += [spec] * 4
    return jax.shard_map(
        on_device,
        mesh=fine,
        in_specs=tuple(placed),
        out_specs=tuple(results),
        check_vma=False,
    )
```

```python
import functools
import math

import jax
import jax.numpy as jnp
import numpy as np
from jax import lax
from jax.experimental import pallas as pl
from jax.experimental.pallas import tpu as pltpu
from jax.sharding import Mesh
from jax.sharding import PartitionSpec as P

DK = 128
DV = 256
SPAN = 64
MIN_SPANS = 16
MAX_SPANS = 128
PARAMS = 12872448
TILE = 256
LEVELS = 6
HEAD = 2 * DK + 2 * DV
VMEM_LIMIT = 61 * 1024 * 1024
BF = jnp.bfloat16
F32 = jnp.float32

norm_eps = 1e-06
learn_rate = 0.05
beta_one = 0.9
beta_two = 0.95
adam_eps = 1e-08
weight_decay = 0.1
clip_scale = 0.05
adam_step = 10
decay_scale = 16.0
scaling = DK ** (-0.5)
ANY = pl.BlockSpec(memory_space=pl.ANY)
SMEM = pl.BlockSpec(memory_space=pltpu.SMEM)
VMEM = pl.BlockSpec(memory_space=pltpu.VMEM)


def dot(a, b, ca=1, cb=0):
    return lax.dot_general(a, b, (((ca,), (cb,)), ((), ())), preferred_element_type=F32)


def cost(us):
    return pl.CostEstimate(flops=int(us * 1.0e9), bytes_accessed=int(us * 1.0e6), transcendentals=0)


def run(kernel, grid, in_specs, out_specs, out_shape, scratch, name, us):
    return pl.pallas_call(
        kernel,
        grid=grid,
        in_specs=in_specs,
        out_specs=out_specs,
        out_shape=out_shape,
        scratch_shapes=scratch,
        name=name,
        compiler_params=pltpu.CompilerParams(vmem_limit_bytes=VMEM_LIMIT),
        cost_estimate=cost(us),
    )


def sds(*shape, dtype=F32):
    return jax.ShapeDtypeStruct(shape, dtype)


def rows_spec(cols, order=None):
    if order is None:
        return pl.BlockSpec((TILE, cols), lambda i: (i, 0))
    return pl.BlockSpec((TILE, cols), lambda i: (order - 1 - i, 0))


def whole_spec(*shape):
    zeros = (0,) * len(shape)
    return pl.BlockSpec(shape, lambda i: zeros, pipeline_mode=pl.Buffered(1))


def span_starts(seq_extra, span_ids):
    seq_spans = seq_extra + MIN_SPANS
    n = seq_extra.shape[0]
    earlier = jnp.tril(jnp.ones((n, n), jnp.int32), -1)
    bounds = jnp.sum(earlier * seq_spans[None, :], axis=1)
    return jnp.any(bounds[None, :] == span_ids[:, None], axis=1).astype(jnp.int32)


def deal_tables(deal, n_data, per_dev, capacity, my_index):
    table_grid = deal.reshape(n_data, per_dev)
    src_dev = table_grid // per_dev
    src_local = table_grid % per_dev
    my_source = lax.dynamic_index_in_dim(src_dev, my_index, 0, keepdims=False)
    earlier = jnp.tril(jnp.ones((per_dev, per_dev), jnp.int32), -1)
    same_source = (my_source[:, None] == my_source[None, :]).astype(jnp.int32)
    my_rank = jnp.sum(same_source * earlier, axis=1)
    recv_slot = my_source * capacity + my_rank
    owned_here = (src_dev == my_index).astype(jnp.int32)
    send_rank = jnp.sum(owned_here[:, None, :] * earlier[None], axis=2)
    slot_ids = jnp.arange(capacity, dtype=jnp.int32)
    send_hit = owned_here[:, :, None] * (
        send_rank[:, :, None] == slot_ids[None, None, :]
    ).astype(jnp.int32)
    send_local = jnp.sum(send_hit * src_local[:, :, None], axis=1)
    peer_ids = jnp.arange(n_data, dtype=jnp.int32)
    local_ids = jnp.arange(per_dev, dtype=jnp.int32)
    back_hit = (
        (my_source[None, None, :] == peer_ids[:, None, None])
        & (my_rank[None, None, :] == slot_ids[None, :, None])
    ).astype(jnp.int32)
    back_local = jnp.sum(back_hit * local_ids[None, None, :], axis=2)
    home_hit = owned_here[:, :, None] * (
        src_local[:, :, None] == local_ids[None, None, :]
    ).astype(jnp.int32)
    home_slot = jnp.sum(
        home_hit * (peer_ids[:, None, None] * capacity + send_rank[:, :, None]), axis=(0, 1)
    )
    return recv_slot, send_local.reshape(-1), back_local.reshape(-1), home_slot


def level_matrices():
    t = np.arange(TILE, dtype=np.int32)[:, None]
    u = np.arange(TILE, dtype=np.int32)[None, :]
    ups = []
    level = np.full((TILE, TILE), LEVELS + 1, np.int32)
    for l in range(LEVELS):
        block = SPAN >> l
        half = block // 2
        same = (t // block) == (u // block)
        mid = (t // block) * block + half
        right = (t >= mid) & (u >= mid) & (u <= t)
        left = (t < mid) & (u > t) & (u < mid)
        ups.append(same & (right | left))
        hit = same & (t % block >= half) & (u % block < half)
        level = np.where(hit, l, level)
    level = np.where(t == u, LEVELS, level)
    same = (t // SPAN) == (u // SPAN)
    ups.append(same & (u <= t))
    ups.append(same & (u > t))
    ups = np.stack(ups).astype(np.float32).astype(BF)
    return ups, np.ascontiguousarray(np.swapaxes(ups, 1, 2)), level, np.ascontiguousarray(level.T)


def home_kernel(count, table, *refs):
    srcs, out = refs[:-1], refs[-1]
    width = srcs[0].shape[1]

    def body(i, _):
        row = pl.multiple_of(table[i] * SPAN, SPAN)
        to = pl.multiple_of(i * SPAN, SPAN)
        for k, src in enumerate(srcs):
            col = pl.multiple_of(table[count + k], 128)
            out[pl.ds(to, SPAN), pl.ds(col, width)] = src[pl.ds(row, SPAN), :].astype(F32)
        return 0

    lax.fori_loop(0, count, body, 0)


def home(pieces, table, cols, name):
    count = table.shape[0]
    width = pieces[0].shape[1]
    total = width * len(pieces)
    return pl.pallas_call(
        functools.partial(home_kernel, count),
        in_specs=[SMEM] + [VMEM] * len(pieces),
        out_specs=VMEM,
        out_shape=sds(count * SPAN, total),
        name=name,
        compiler_params=pltpu.CompilerParams(vmem_limit_bytes=VMEM_LIMIT),
        cost_estimate=cost(4),
    )(jnp.concatenate([table, jnp.stack(cols)]), *pieces)


def copy_to(src, dst, send_sem, recv_sem, target):
    return pltpu.make_async_remote_copy(
        src_ref=src,
        dst_ref=dst,
        send_sem=send_sem,
        recv_sem=recv_sem,
        device_id=target,
        device_id_type=pl.DeviceIdType.MESH,
    )


def enter(nd, shifts=()):
    dp, x, core = lax.axis_index("dp"), lax.axis_index("x"), lax.axis_index("core")
    peers = [{"dp": lax.rem(dp + k, nd)} for k in range(1, nd)] + [{"x": 1 - x}, {"core": 1 - core}]
    for k in shifts:
        peers += [along_sequence(nd, k), along_sequence(nd, -k)]
    barrier = pltpu.get_barrier_semaphore()
    for peer in peers:
        pl.semaphore_signal(barrier, inc=1, device_id=peer, device_id_type=pl.DeviceIdType.MESH)
    pl.semaphore_wait(barrier, len(peers))


def along_sequence(nd, k):
    q = lax.rem(lax.axis_index("dp") * 2 + lax.axis_index("x") + k + 2 * nd, 2 * nd)
    return {"dp": q // 2, "x": lax.rem(q, 2)}


def carry_widths(reach):
    widths = []
    width = 1
    while 2 * width < reach:
        widths.append(width)
        width *= 2
    return widths, width


class Carry:
    def __init__(self, nd, reach, sign, packet, sent, got, send_sems, recv_sems):
        self.nd, self.sign, self.packet, self.sent, self.got = nd, sign, packet, sent, got
        self.send_sems, self.recv_sems = send_sems, recv_sems
        self.widths, self.last = carry_widths(reach)
        self.q = lax.axis_index("dp") * 2 + lax.axis_index("x")

    def shifts(self):
        return self.widths + [1, 1 + self.last]

    def copy(self, index):
        source = min(index, len(self.widths))
        return copy_to(
            self.sent.at[source],
            self.got.at[index],
            self.send_sems.at[index],
            self.recv_sems.at[index],
            along_sequence(self.nd, self.sign * self.shifts()[index]),
        )

    def send(self, stage):
        self.sent[stage] = self.packet[...].astype(BF)
        self.copy(stage).start()
        if stage == len(self.widths):
            self.copy(stage + 1).start()

    def receive(self, index):
        self.copy(index).wait_recv()
        k = self.shifts()[index]
        there = self.q >= k if self.sign > 0 else self.q + k < 2 * self.nd
        return jnp.where(there, self.got[index].astype(F32), 0.0)

    def step(self, stage):
        if stage < len(self.widths):
            self.join(self.receive(stage), self.packet[...])
            self.send(stage + 1)
        else:
            near, far = self.receive(stage), self.receive(stage + 1)
            self.join(far, near)
            for index in range(stage + 2):
                self.copy(index).wait_send()

    def join(self, earlier, later):
        for h in range(2):
            states = slice(h * DV, (h + 1) * DV)
            f = slice(2 * DV + h, 2 * DV + h + 1)
            self.packet[states] = later[f] * earlier[states] + later[states]
            self.packet[f] = later[f] * earlier[f]

    def run(self):
        return len(self.widths) + 1


class Spread:
    def __init__(self, nd, order, own, window, send_sems, recv_sems):
        self.nz, self.order, self.own, self.window = nd // 2, order, own, window
        self.send_sems, self.recv_sems = send_sems, recv_sems
        dp, self.x = lax.axis_index("dp"), lax.axis_index("x")
        self.z, self.y = dp // 2, lax.rem(dp, 2)
        nz = self.nz
        self.moves = [((0, 0, 0), (k, 0, 0)) for k in range(1, nz)]
        self.moves += [((0, 0, 0), (0, 1, 0)), ((0, 0, 0), (0, 0, 1))]
        for k in range(1, nz):
            self.moves += [((k, 0, 0), (k, 1, 0)), ((k, 0, 0), (k, 0, 1))]
        self.moves += [((k, 1, 0), (k, 1, 1)) for k in range(nz)]

    def place(self, k, first, second):
        fy, fx = (first, second) if self.order == 0 else (second, first)
        y = 1 - self.y if fy else self.y
        x = 1 - self.x if fx else self.x
        return self.window(lax.rem(self.z + self.nz - k, self.nz) * 2 + y, x)

    def copy(self, index):
        here, there = self.moves[index]
        if here[0] != there[0]:
            target = {"dp": lax.rem(self.z + there[0], self.nz) * 2 + self.y}
        elif (here[1] != there[1]) == (self.order == 0):
            target = {"dp": self.z * 2 + 1 - self.y}
        else:
            target = {"x": 1 - self.x}
        k, first, second = there
        return copy_to(
            self.own if here == (0, 0, 0) else self.place(*here),
            self.place(*here),
            self.send_sems.at[index],
            self.recv_sems.at[k + self.nz * (first + 2 * second)],
            target,
        )

    def arrived(self, k, first, second):
        at = self.place(k, first, second)
        sem = self.recv_sems.at[k + self.nz * (first + 2 * second)]
        copy_to(at, at, self.send_sems.at[0], sem, {"x": 1 - self.x}).wait_recv()

    def begin(self):
        for index in range(self.nz + 1):
            self.copy(index).start()

    def relay_z(self, k):
        self.arrived(k, 0, 0)
        for index in range(2):
            self.copy(self.nz + 1 + 2 * (k - 1) + index).start()

    def relay_first(self, k):
        self.arrived(k, 1, 0)
        self.copy(3 * self.nz - 1 + k).start()

    def finish(self):
        for k in range(self.nz):
            self.arrived(k, 0, 1)
            self.arrived(k, 1, 1)
        for index in range(len(self.moves)):
            self.copy(index).wait_send()


CHUNKS = 4


class Deal:
    def __init__(self, nd, spans, table, rows, out, tok, send, recv, other, sems):
        self.nd, self.spans, self.table, self.rows, self.out = nd, spans, table, rows, out
        self.tok, self.sent, self.recv, self.other = tok, send, recv, other
        self.load_sem, self.a2a_send, self.a2a_recv, self.x_send, self.x_recv, self.c_send, self.c_recv = sems
        self.dp, self.x, self.core = lax.axis_index("dp"), lax.axis_index("x"), lax.axis_index("core")
        self.quarter = out.shape[1] // 4
        self.cap = send.shape[1]
        self.mine = pl.multiple_of((2 * self.x + self.core) * self.quarter, 128)
        self.theirs = pl.multiple_of((2 * (1 - self.x) + self.core) * self.quarter, 128)
        self.load = pltpu.make_async_copy(rows.at[:, :, pl.ds(self.mine, self.quarter)], tok, self.load_sem.at[0])
        self.started = []

    def begin(self):
        self.load.start()

    def exchange(self):
        self.load.wait()
        cap, nd = self.cap, self.nd

        def pick(k, out, base):
            d = lax.rem(self.dp + k, nd)
            for j in range(cap):
                out[base + j] = self.tok[self.table[d * cap + j]]

        here = self.dp * cap
        for k in range(1, nd):
            pick(k, self.sent.at[k], 0)
            copy = copy_to(
                self.sent.at[k],
                self.recv.at[pl.ds(here, cap)],
                self.a2a_send.at[k],
                self.a2a_recv.at[k],
                {"dp": lax.rem(self.dp + k, nd)},
            )
            copy.start()
            self.started.append(copy)
        pick(0, self.recv, here)

    def across(self):
        for copy in self.started:
            copy.wait_recv()
        spans, nd = self.spans, self.nd
        count = spans // CHUNKS
        first = nd * self.cap
        self.x_copies, self.c_copies = [], []
        for c in range(CHUNKS):
            rows = pl.ds(c * count * SPAN, count * SPAN)

            def body(i, _, c=c):
                at = c * count + i
                to = pl.ds(pl.multiple_of(at * SPAN, SPAN), SPAN)
                self.other[to, :] = self.recv[self.table[first + spans + at]]
                return 0

            lax.fori_loop(0, count, body, 0)
            copy = copy_to(
                self.other.at[rows, :],
                self.out.at[rows, pl.ds(self.mine, self.quarter)],
                self.x_send.at[c],
                self.x_recv.at[c],
                {"x": 1 - self.x},
            )
            copy.start()
            self.x_copies.append(copy)

        def body(i, _):
            to = pl.ds(pl.multiple_of(i * SPAN, SPAN), SPAN)
            self.out[to, pl.ds(self.mine, self.quarter)] = self.recv[self.table[first + i]]
            return 0

        lax.fori_loop(0, spans, body, 0)
        self.pass_on(slice(None), self.mine, CHUNKS)

    def pass_on(self, rows, col, sem):
        at = self.out.at[rows, pl.ds(col, self.quarter)]
        copy = copy_to(at, at, self.c_send.at[sem], self.c_recv.at[sem], {"core": 1 - self.core})
        copy.start()
        self.c_copies.append(copy)

    def finish(self):
        count = self.spans // CHUNKS
        for c, copy in enumerate(self.x_copies):
            copy.wait_recv()
            self.pass_on(pl.ds(c * count * SPAN, count * SPAN), self.theirs, c)
        for copy in self.c_copies:
            copy.wait_recv()
        for copy in self.x_copies + self.c_copies:
            copy.wait_send()

    def release(self):
        for copy in self.started:
            copy.wait_send()


def deal_buffers(nd, per_dev, spans, quarter, cap):
    return [
        pltpu.VMEM((per_dev, SPAN, quarter), BF),
        pltpu.VMEM((nd, cap, SPAN, quarter), BF),
        pltpu.VMEM((spans * SPAN, quarter), BF),
        pltpu.VMEM((nd * cap, SPAN, quarter), BF),
        pltpu.VMEM((nd * cap, SPAN, quarter), BF),
    ]


def deal_sems(nd):
    dma = pltpu.SemaphoreType.DMA
    return [dma((1,)), dma((nd,)), dma((nd,)), dma((CHUNKS,)), dma((CHUNKS,)), dma((CHUNKS + 1,)), dma((CHUNKS + 1,))]


SMALL = 184


class Small:
    def __init__(self, nd, pack, sent, got, norms, sems):
        self.nd, self.pack, self.sent, self.got, self.norms = nd, pack, sent, got, norms
        self.send, self.recv, self.norm_send, self.norm_recv, self.end_send, self.end_recv = sems
        self.dp, self.x, self.core = lax.axis_index("dp"), lax.axis_index("x"), lax.axis_index("core")

    def fill(self, gain_first, gain_second, down, up, bias, head):
        pack = self.pack
        for r in range(8):
            lanes = slice(r * 128, (r + 1) * 128)
            pack[r : r + 1] = gain_first[0:1, lanes]
            pack[8 + r : 9 + r] = gain_second[0:1, lanes]
            pack[16 + 16 * r : 32 + 16 * r] = down[:, lanes]
        for h in range(2):
            lanes = slice(h * 128, (h + 1) * 128)
            pack[144 + 16 * h : 160 + 16 * h] = up[:, lanes]
            pack[176 + h : 177 + h] = bias[0:1, lanes]
            pack[178 + h : 179 + h] = head[0:1, lanes]
        pack[180:] = jnp.zeros((4, 128), F32)

    def copy(self, step):
        if step == 0:
            target = {"x": 1 - self.x}
        else:
            bit = 1 << (step - 1)
            on = lax.rem(self.dp // bit, 2)
            target = {"dp": self.dp + bit - 2 * bit * on}
        return copy_to(self.sent.at[step], self.got.at[step], self.send.at[step], self.recv.at[step], target)

    def steps(self):
        return self.nd.bit_length()

    def begin(self, step):
        self.sent[step] = self.pack[...]
        self.copy(step).start()

    def end(self, step):
        self.copy(step).wait()
        self.pack[...] = self.pack[...] + self.got[step]

    def core_copy(self, step, src, dst, target):
        return copy_to(src, dst, self.end_send.at[step], self.end_recv.at[step], target)

    def head(self):
        at = self.nd + 5
        return self.core_copy(0, self.norms.at[at], self.norms.at[at + 1], {"core": 1 - self.core})

    def begin_head(self):
        self.norms[self.nd + 5] = self.pack[176:184]
        self.head().start()

    def end_head(self):
        self.head().wait()
        self.pack[178:180] = self.pack[178:180] + self.norms[self.nd + 6, 2:4]

    def squares(self):
        nd, v = self.nd, self.pack[...]
        v = v * v
        down = fold(v[16:144])
        up = fold(v[144:176])
        row = lax.broadcasted_iota(jnp.int32, (8, 128), 0)
        tail = v[176:184]
        tail = jnp.where(row < 2, tail / (2 * nd), jnp.where(row < 4, tail / (4 * nd), 0.0))
        return (v[0:8] + v[8:16] + down) / (4 * nd) + up / (2 * nd) + tail

    def norm_copy(self, k):
        return copy_to(
            self.norms.at[self.nd],
            self.norms.at[self.dp],
            self.norm_send.at[k],
            self.norm_recv.at[k],
            {"dp": lax.rem(self.dp + k, self.nd)},
        )

    def begin_norm(self, value):
        self.norms[self.nd] = value
        self.norms[self.dp] = value
        for k in range(1, self.nd):
            self.norm_copy(k).start()

    def end_norm(self, out):
        nd = self.nd
        for k in range(1, nd):
            self.norm_copy(k).wait()
        total = self.norms[0]
        for k in range(1, nd):
            total = total + self.norms[k]
        for step, target in ((1, {"x": 1 - self.x}), (2, {"core": 1 - self.core})):
            at = nd - 1 + 2 * step
            self.norms[at] = total
            copy = self.core_copy(step, self.norms.at[at], self.norms.at[at + 1], target)
            copy.start()
            copy.wait()
            total = total + self.norms[at + 1]
        out[...] = total


def small_scratch(nd):
    dma = pltpu.SemaphoreType.DMA
    steps = nd.bit_length()
    return [
        pltpu.VMEM((steps, SMALL, 128), F32), pltpu.VMEM((steps, SMALL, 128), F32), pltpu.VMEM((nd + 7, 8, 128), F32),
        dma((steps,)), dma((steps,)), dma((nd,)), dma((nd,)), dma((3,)), dma((3,)),
    ]


class Undeal:
    def __init__(self, nd, spans, table, own, cross, joined, sent, gath, sems):
        self.nd, self.spans, self.table, self.own, self.cross = nd, spans, table, own, cross
        self.joined, self.sent, self.gath = joined, sent, gath
        self.x_send, self.x_recv, self.a2a_send, self.a2a_recv, *self.wide_sems = sems
        self.dp, self.x, self.core = lax.axis_index("dp"), lax.axis_index("x"), lax.axis_index("core")
        self.cap = sent.shape[1]
        self.quarter = own.shape[2]
        self.wide = gath.shape[2] != self.quarter
        self.mine, self.theirs = 0, 0
        if self.wide:
            self.mine = pl.multiple_of((2 * self.x + self.core) * self.quarter, 128)
            self.theirs = pl.multiple_of((2 * (1 - self.x) + self.core) * self.quarter, 128)

    def swap(self):
        return copy_to(
            self.cross,
            self.joined.at[pl.ds(self.x * self.spans, self.spans)],
            self.x_send.at[0],
            self.x_recv.at[0],
            {"x": 1 - self.x},
        )

    def begin(self):
        self.swap().start()

        def body(i, _):
            self.joined[self.x * self.spans + i] = self.own[i]
            return 0

        lax.fori_loop(0, self.spans, body, 0)

    def block(self, dp, col):
        return self.gath.at[pl.ds(dp * self.cap, self.cap), :, pl.ds(col, self.quarter)]

    def a2a(self, k):
        return copy_to(
            self.sent.at[k],
            self.block(self.dp, self.mine),
            self.a2a_send.at[k],
            self.a2a_recv.at[k],
            {"dp": lax.rem(self.dp + k, self.nd)},
        )

    def exchange(self):
        self.swap().wait_recv()
        cap = self.cap
        for k in range(1, self.nd):
            d = lax.rem(self.dp + k, self.nd)
            for j in range(cap):
                self.sent[k, j] = self.joined[self.table[d * cap + j]]
            self.a2a(k).start()
        here = self.block(self.dp, self.mine)
        for j in range(cap):
            here[j] = self.joined[self.table[self.dp * cap + j]]
        if self.wide:
            self.widen(0, 0).start()
            self.widen(0, 1).start()

    def widen(self, k, step):
        at = self.block(lax.rem(self.dp + self.nd - k, self.nd), self.theirs if step == 2 else self.mine)
        send, recv = self.wide_sems
        return copy_to(
            at, at, send.at[3 * k + step], recv.at[3 * k + step],
            {"x": 1 - self.x} if step == 0 else {"core": 1 - self.core},
        )

    def arrive(self, k):
        self.a2a(k).wait_recv()
        if self.wide:
            self.widen(k, 0).start()
            self.widen(k, 1).start()

    def finish(self):
        if self.wide:
            for k in range(self.nd):
                self.widen(k, 0).wait_recv()
                self.widen(k, 2).start()
            for k in range(self.nd):
                self.widen(k, 1).wait_recv()
                self.widen(k, 2).wait_recv()
                for step in range(3):
                    self.widen(k, step).wait_send()
        for k in range(1, self.nd):
            self.a2a(k).wait_send()
        self.swap().wait_send()


def undeal_scratch(nd, per_dev, spans, quarter, cap, wide):
    dma = pltpu.SemaphoreType.DMA
    buffers = [
        pltpu.VMEM((spans, SPAN, quarter), BF),
        pltpu.VMEM((spans, SPAN, quarter), BF),
        pltpu.VMEM((per_dev, SPAN, quarter), BF),
        pltpu.VMEM((nd, cap, SPAN, quarter), BF),
        pltpu.VMEM((nd * cap, SPAN, quarter * (4 if wide else 1)), BF),
    ]
    sems = [dma((1,)), dma((1,)), dma((nd,)), dma((nd,))]
    return buffers, sems + ([dma((3 * nd,)), dma((3 * nd,))] if wide else [])


def fold(value):
    return jnp.sum(value.reshape(-1, 8, 128), axis=0)


class Collapse:
    def __init__(self, nd, order, acc, pitch, low, rows, got, sems):
        self.nz, self.order, self.acc, self.pitch, self.low, self.rows = nd // 2, order, acc, pitch, low, rows
        self.got = got
        self.send_sems, self.recv_sems = sems
        self.w = got.shape[2]
        dp, self.x = lax.axis_index("dp"), lax.axis_index("x")
        self.z, self.y = dp // 2, lax.rem(dp, 2)

    def window(self, first, second, kz):
        fx, fy = (first, second) if self.order == 0 else (second, first)
        y = 1 - self.y if fy else self.y
        x = 1 - self.x if fx else self.x
        dp = lax.rem(self.z + kz, self.nz) * 2 + y
        return self.acc.at[
            pl.ds(pl.multiple_of(x * self.pitch + self.low, 16), self.rows),
            pl.ds(pl.multiple_of(dp * self.w, 128), self.w),
        ]

    def partner(self, which):
        if (which == 0) == (self.order == 0):
            return {"x": 1 - self.x}
        return {"dp": self.z * 2 + 1 - self.y}

    def slot(self, phase, second, kz):
        nz = self.nz
        return second * nz + kz if phase == 1 else (2 * nz + kz if phase == 2 else 3 * nz + kz - 1)

    def copy(self, phase, second, kz):
        at = self.slot(phase, second, kz)
        if phase == 1:
            src, target = self.window(1, second, kz), self.partner(0)
        elif phase == 2:
            src, target = self.window(0, 1, kz), self.partner(1)
        else:
            src, target = self.window(0, 0, kz), {"dp": lax.rem(self.z + kz, self.nz) * 2 + self.y}
        return copy_to(src, self.got.at[at], self.send_sems.at[at], self.recv_sems.at[at], target)

    def add(self, second, kz, at):
        here = self.window(0, second, kz)
        here[...] = (here[...].astype(F32) + self.got[at].astype(F32)).astype(BF)

    def begin(self):
        for second in (1, 0):
            for kz in range(self.nz):
                self.copy(1, second, (kz + 1) % self.nz).start()

    def second(self, kz):
        self.copy(1, 1, kz).wait_recv()
        self.add(1, kz, self.slot(1, 1, kz))
        self.copy(2, 1, kz).start()

    def third(self, kz):
        self.copy(1, 0, kz).wait_recv()
        self.add(0, kz, self.slot(1, 0, kz))
        self.copy(2, 1, kz).wait_recv()
        self.add(0, kz, self.slot(2, 1, kz))
        if kz:
            self.copy(3, 0, kz).start()

    def finish(self, out, squares):
        total = self.window(0, 0, 0)[...].astype(F32)
        for kz in range(1, self.nz):
            self.copy(3, 0, kz).wait_recv()
            total = total + self.got[self.slot(3, 0, kz)].astype(F32)
        out[...] = total
        squares[...] += fold(total * total)
        for kz in range(self.nz):
            self.copy(1, 0, kz).wait_send()
            self.copy(1, 1, kz).wait_send()
            self.copy(2, 1, kz).wait_send()
            if kz:
                self.copy(3, 0, kz).wait_send()


def collapse_scratch(nd, rows, w):
    count = 4 * (nd // 2) - 1
    dma = pltpu.SemaphoreType.DMA
    return [pltpu.VMEM((count, rows, w), BF), dma((count,)), dma((count,))]


def progress(chains, nz, between=()):
    between = list(between)
    for kz in [k % nz for k in range(1, nz + 1)]:
        for chain in chains:
            chain.second(kz)
        if between:
            between.pop(0)()
    for kz in [k % nz for k in range(1, nz + 1)]:
        for chain in chains:
            chain.third(kz)
        if between:
            between.pop(0)()
    for work in between:
        work()


PROJ_ROWS = 16 + HEAD + DV
PROJ_CUTS = ((0, 528), (528, 512))


def forward_kernel(nd, spans, reach, gather, table, ints, tokens, cotangent, shard_p, shard_f, gain, up, bias, head_gain,
                   ups, level, *rest):
    outs, rest = rest[:13], rest[13:]
    (src_o, cot_o, wp_o, wf_o, normed_o, qkvg_o, log_decay_o, rank_o, mixed_o, gated_o, attn_o, before_o, attn_other) = outs
    (src, cot, wp, wf, normed, qkvg, log_decay, rank, mixed, gated, attn, before), rest = rest[:12], rest[12:]
    (packet, factors, sent_packets, got_packets), rest = rest[:4], rest[4:]
    (tok, sent, other, recv_t, recv_c), rest = rest[:5], rest[5:]
    sems_t, sems_c, rest = rest[:7], rest[7:14], rest[14:]
    carry_send, carry_recv, core_send, core_recv, out_sems, own_sems, *ag_sems = rest
    tiles = spans * SPAN // TILE
    carry = Carry(nd, reach, 1, packet, sent_packets, got_packets, carry_send, carry_recv)
    enter(nd, carry.shifts())
    deal = Deal(nd, spans, table, tokens, src, tok, sent, recv_t, other, sems_t)
    deal_c = Deal(nd, spans, table, cotangent, cot, tok, sent, recv_c, other, sems_c)
    deal.begin()
    local = []
    spreads_p, spreads_f = [], []
    if gather:
        w = shard_p.shape[1]
        f3 = shard_f.shape[0]
        f = f3 // 3
        cuts_p = [(k, low, count, PROJ_ROWS, low) for k, (low, count) in enumerate(PROJ_CUTS)]
        cuts_f = [
            (0, 0, f, f, 0), (1, 2 * f, f, f, 4 * f), (0, f, f // 2, f, 2 * f), (1, f + f // 2, f // 2, f, 2 * f + f // 2),
        ]

        def window(buffer, count, pitch, base, dp, x):
            return buffer.at[
                pl.ds(pl.multiple_of(x * pitch + base, 16), count), pl.ds(pl.multiple_of(dp * w, 128), w)
            ]

        for shard, buffer, cuts, spreads in ((shard_p, wp, cuts_p, spreads_p), (shard_f, wf, cuts_f, spreads_f)):
            for order, low, count, pitch, base in cuts:
                piece = shard.at[pl.ds(low, count), :]
                place = functools.partial(window, buffer, count, pitch, base)
                copy = pltpu.make_async_copy(
                    piece, place(lax.axis_index("dp"), lax.axis_index("x")), own_sems.at[len(local)]
                )
                copy.start()
                local.append(copy)
                k = 2 * (len(local) - 1)
                spreads.append(Spread(nd, order, piece, place, ag_sems[k], ag_sems[k + 1]))
    else:
        for shard, buffer in ((shard_p, wp), (shard_f, wf)):
            local.append(pltpu.make_async_copy(shard, buffer, own_sems.at[len(local)]))
            local[-1].start()
    outgoing = []

    def store(value, out):
        outgoing.append(pltpu.make_async_copy(value, out, out_sems.at[len(outgoing)]))
        outgoing[-1].start()

    def relay_z(spreads, k):
        for spread in spreads:
            spread.relay_z(k)

    def relay_first(spreads, k):
        for spread in spreads:
            spread.relay_first(k)

    nz = nd // 2
    last_z = range(1, nz) if gather else ()
    last_first = range(nz) if gather else ()
    for spread in spreads_p:
        spread.begin()
    deal.exchange()
    for k in last_first[0:1]:
        relay_first(spreads_p, k)
    deal_c.begin()
    for k in last_z[0:1]:
        relay_z(spreads_p, k)
    for k in last_z[1:2]:
        relay_z(spreads_p, k)
    for k in last_first[1:2]:
        relay_first(spreads_p, k)
    for spread in spreads_f:
        spread.begin()
    for k in last_z[2:3]:
        relay_z(spreads_p, k)
    for k in last_first[2:3]:
        relay_first(spreads_p, k)
    for k in last_first[3:4]:
        relay_first(spreads_p, k)
    for k in last_first[0:1]:
        relay_first(spreads_f, k)
    deal.across()
    deal.release()
    deal_c.exchange()
    for k in last_z[0:1]:
        relay_z(spreads_f, k)
    for k in last_first[1:2]:
        relay_first(spreads_f, k)
    deal.finish()
    for k in last_z[1:2]:
        relay_z(spreads_f, k)
    for spread in spreads_p:
        spread.finish()
    for copy in local:
        copy.wait()
    store(src, src_o)
    store(wp, wp_o)

    def at(ref, i):
        return ref.at[pl.ds(pl.multiple_of(i * TILE, TILE), TILE), :]

    packet[...] = jnp.zeros_like(packet)
    packet[2 * DV : 2 * DV + 2] = jnp.ones((2, DK), F32)

    def project(i, _):
        project_kernel(
            i, ints, at(src, i), gain, wp, up, bias, ups,
            at(normed, i), at(qkvg, i), at(log_decay, i), at(rank, i), packet,
        )
        return 0

    lax.fori_loop(0, tiles // 2, project, 0)
    for k in last_z[2:3]:
        relay_z(spreads_f, k)
    for k in last_first[2:3]:
        relay_first(spreads_f, k)
    lax.fori_loop(tiles // 2, tiles, project, 0)
    factors[...] = packet[2 * DV :]
    carry.send(0)
    store(normed, normed_o)
    store(qkvg, qkvg_o)
    store(log_decay, log_decay_o)
    store(rank, rank_o)
    for k in last_first[3:4]:
        relay_first(spreads_f, k)

    def within(i, _):
        within_kernel(at(qkvg, i), at(log_decay, i), ups, level, at(mixed, i))
        return 0

    stages = carry.run()
    for stage in range(stages):
        lax.fori_loop(tiles * stage // stages, tiles * (stage + 1) // stages, within, 0)
        carry.step(stage)
    deal_c.across()
    per_tile = TILE // SPAN

    def mix(i, _):
        mix_kernel(
            i, ints, at(qkvg, i), at(log_decay, i), packet, ups, head_gain, wp,
            at(mixed, i), at(gated, i), at(attn, i), before.at[pl.ds(i * per_tile, per_tile)],
        )
        return 0

    lax.fori_loop(0, tiles, mix, 0)
    swap_attn = copy_to(
        attn, attn_other, core_send.at[0], core_recv.at[0], {"core": 1 - lax.axis_index("core")}
    )
    swap_attn.start()
    store(mixed, mixed_o)
    store(gated, gated_o)
    store(attn, attn_o)
    store(before, before_o)
    deal_c.finish()
    store(cot, cot_o)
    for spread in spreads_f:
        spread.finish()
    store(wf, wf_o)
    deal_c.release()
    swap_attn.wait()
    for copy in outgoing:
        copy.wait()


def forward(table, ints, tokens, cotangent, shard_p, shard_f, gain, up, bias, head_gain, ups, level, nd, spans, reach, gather):
    d = tokens.shape[1]
    per_dev = tokens.shape[0] // SPAN
    cap = -(-per_dev // nd)
    rows = spans * SPAN
    dma = pltpu.SemaphoreType.DMA
    nz = nd // 2
    wf_rows = shard_f.shape[0] * (2 if gather else 1)
    kept = [
        ((rows, d), BF), ((rows, d), BF), ((2 * PROJ_ROWS, d), BF), ((wf_rows, d), BF), ((rows, d), BF),
        ((rows, 2 * HEAD), BF), ((rows, 2 * DK), F32), ((rows, 16), BF), ((rows, 2 * DV), F32), ((rows, 2 * DV), BF),
        ((rows, d), BF), ((spans, 2, DV, DK), BF),
    ]
    widths, _ = carry_widths(reach)
    steps = len(widths) + 2
    scratch = [pltpu.VMEM(shape, dtype) for shape, dtype in kept]
    scratch += [
        pltpu.VMEM((2 * DV + 16, DK), F32),
        pltpu.VMEM((steps - 1, 2 * DV + 16, DK), BF),
        pltpu.VMEM((steps, 2 * DV + 16, DK), BF),
    ]
    scratch += deal_buffers(nd, per_dev, spans, d // 4, cap) + deal_sems(nd) + deal_sems(nd)
    scratch += [dma((steps,)), dma((steps,)), dma((1,)), dma((1,)), dma((12,)), dma((6,))]
    if gather:
        scratch += [dma((4 * nz - 1,)), dma((4 * nz,))] * 6
    outs = [sds(*shape, dtype=dtype) for shape, dtype in kept] + [sds(rows, d, dtype=BF)]
    outs.append(sds(16, DK))
    specs = [ANY] * 13 + [VMEM]

    def kernel(*refs):
        n_in = 12
        ins, rest = refs[:n_in], refs[n_in:]
        results, factors, buffers = rest[:13], rest[13], rest[14:]
        forward_kernel(
            nd, spans, reach, gather, *ins, *results, *buffers[:12], buffers[12], factors, *buffers[13:]
        )

    return pl.pallas_call(
        kernel,
        in_specs=[SMEM, SMEM, ANY, ANY, ANY, ANY] + [VMEM] * 6,
        out_specs=specs,
        out_shape=outs,
        scratch_shapes=scratch,
        name="forward",
        compiler_params=pltpu.CompilerParams(
            vmem_limit_bytes=VMEM_LIMIT, collective_id=0, has_side_effects=True
        ),
        cost_estimate=cost(150),
    )(
        table, ints, tokens.reshape(per_dev, SPAN, d), cotangent.reshape(per_dev, SPAN, d), shard_p, shard_f,
        gain, up, bias, head_gain, ups, level,
    )


def rms_scale(x):
    return lax.rsqrt(jnp.mean(x * x, axis=-1, keepdims=True) + norm_eps)


def distances(ups, log_decay):
    high = log_decay.astype(BF)
    lower = (log_decay - high.astype(F32)).astype(BF)
    return dot(ups, high) + dot(ups, lower)


def head_cols(h, part):
    start = h * HEAD + (0, DK, 2 * DK, 2 * DK + DV)[part]
    return slice(start, start + (DK, DK, DV, DV)[part])


def in_rows(h):
    return slice(h * PROJ_ROWS + 16, h * PROJ_ROWS + 16 + HEAD)


def out_rows(h):
    return slice(h * PROJ_ROWS + 16 + HEAD, (h + 1) * PROJ_ROWS)


def log_sigmoid(v):
    return jnp.minimum(v, 0.0) - jnp.log(1.0 + jnp.exp(-jnp.abs(v)))


def project_kernel(
    step, ints, src, gain, weights, up, bias, ups,
    normed, qkvg, log_decay, rank, packet,
):
    x = src[...].astype(F32)
    nf = (x * rms_scale(x) * gain[...]).astype(BF)
    normed[...] = nf
    low = dot(nf, weights[0:16, :], 1, 1).astype(BF)
    rank[...] = low
    logits = dot(low, up[...]) + bias[...]
    ld = log_sigmoid(logits) * (1.0 / decay_scale)
    log_decay[...] = ld
    towards = jnp.exp(distances(ups[LEVELS + 1], ld))
    per_tile = TILE // SPAN
    for h in range(2):
        proj = dot(nf, weights[in_rows(h), :], 1, 1)
        qkvg[:, head_cols(h, 0)] = (proj[:, :DK] * scaling).astype(BF)
        qkvg[:, h * HEAD + DK : (h + 1) * HEAD] = proj[:, DK:].astype(BF)
    for j in range(per_tile):
        rows = slice(j * SPAN, (j + 1) * SPAN)
        keep = ints[step * per_tile + j].astype(F32)
        total = jnp.exp(jnp.sum(ld[rows], axis=0, keepdims=True)) * keep
        for h in range(2):
            lanes = slice(h * DK, (h + 1) * DK)
            states = slice(h * DV, (h + 1) * DV)
            f = slice(2 * DV + h, 2 * DV + h + 1)
            packet[f] = packet[f] * total[:, lanes]
            kd = (qkvg[rows, head_cols(h, 1)].astype(F32) * towards[rows, lanes]).astype(BF)
            packet[states] = packet[states] * total[:, lanes] + dot(qkvg[rows, head_cols(h, 2)], kd, 0, 0)


def within_kernel(qkvg, log_decay, ups, level, within):
    ld = log_decay[...]
    high = ld.astype(BF)
    lower = (ld - high.astype(F32)).astype(BF)
    lev = level[...]
    scores = [None, None]
    for l in range(LEVELS + 1):
        if l < LEVELS:
            x = jnp.exp(dot(ups[l], high) + dot(ups[l], lower))
        for h in range(2):
            q, k = qkvg[:, head_cols(h, 0)], qkvg[:, head_cols(h, 1)]
            if l < LEVELS:
                xh = x[:, h * DK : (h + 1) * DK]
                q = (q.astype(F32) * xh).astype(BF)
                k = (k.astype(F32) * xh).astype(BF)
            s = dot(q, k, 1, 1)
            scores[h] = jnp.where(lev == l, s, 0.0 if l == 0 else scores[h])
    for h in range(2):
        within[:, h * DV : (h + 1) * DV] = dot(scores[h].astype(BF), qkvg[:, head_cols(h, 2)])


def mix_kernel(
    step, ints, qkvg, log_decay, packet, ups, head_gain, weights,
    mixed, gated, attn, before,
):
    per_tile = TILE // SPAN
    ld = log_decay[...]
    since = jnp.exp(distances(ups[LEVELS], ld))
    towards = jnp.exp(distances(ups[LEVELS + 1], ld))
    for j in range(per_tile):
        rows = slice(j * SPAN, (j + 1) * SPAN)
        keep = ints[step * per_tile + j].astype(F32)
        for h in range(2):
            lanes = slice(h * DK, (h + 1) * DK)
            values = slice(h * DV, (h + 1) * DV)
            prev = packet[values] * keep
            prev_low = prev.astype(BF)
            before[j, h] = prev_low
            qd = (qkvg[rows, head_cols(h, 0)].astype(F32) * since[rows, lanes]).astype(BF)
            kd = (qkvg[rows, head_cols(h, 1)].astype(F32) * towards[rows, lanes]).astype(BF)
            mixed[rows, values] = mixed[rows, values] + dot(qd, prev_low, 1, 1)
            last = since[j * SPAN + SPAN - 1 : j * SPAN + SPAN, lanes]
            packet[values] = prev * last + dot(qkvg[rows, head_cols(h, 2)], kd, 0, 0)
    for h in range(2):
        values = slice(h * DV, (h + 1) * DV)
        m = mixed[:, values]
        g = qkvg[:, head_cols(h, 3)].astype(F32)
        y = m * rms_scale(m) * head_gain[...] * g * jax.nn.sigmoid(g)
        gated[:, values] = y.astype(BF)
    attn[...] = (
        dot(gated[:, :DV], weights[out_rows(0), :]) + dot(gated[:, DV:], weights[out_rows(1), :])
    ).astype(BF)


def ffn_kernel(
    ints, src, attn_a, attn_b, cot, gain, weights,
    hidden, normed, act, grad_gu, keep_out, send_out, grad_second,
    part,
):
    quarter = cot.shape[1] // 4
    hid = src[...].astype(F32) + (attn_a[...].astype(F32) + attn_b[...].astype(F32))
    hidden[...] = hid
    ns = (hid * rms_scale(hid) * gain[...]).astype(BF)
    normed[...] = ns
    f = act.shape[1]
    w_gate, w_out, w_up = (slice(k * f, (k + 1) * f) for k in range(3))
    gate = dot(ns, weights[w_gate, :], 1, 1)
    upper = dot(ns, weights[w_up, :], 1, 1)
    sig = jax.nn.sigmoid(gate)
    swish = gate * sig
    low = (swish * upper).astype(BF)
    act[...] = low
    ga = dot(cot[...], weights[w_out, :], 1, 1)
    part[...] = dot(low, weights[w_out, :]).astype(BF)
    gg = (ga * upper * sig * (1.0 + gate * (1.0 - sig))).astype(BF)
    gu = (ga * swish).astype(BF)
    grad_gu[:, :f] = gg
    grad_gu[:, f:] = gu
    grad_second[...] = (dot(gg, weights[w_gate, :]) + dot(gu, weights[w_up, :])).astype(BF)
    core = ints[4]
    for h in range(2):
        mine = pl.multiple_of((2 * h + core) * quarter, 128)
        theirs = pl.multiple_of((2 * h + 1 - core) * quarter, 128)
        keep_out[:, h * quarter : (h + 1) * quarter] = part[:, pl.ds(mine, quarter)]
        send_out[:, h * quarter : (h + 1) * quarter] = part[:, pl.ds(theirs, quarter)]


def weight_grad_into(acc, lhs, rhs, chunk):
    def body(i, _):
        at = pl.multiple_of(i * chunk, chunk)
        acc[pl.ds(at, chunk), :] = dot(lhs[:, pl.ds(at, chunk)], rhs[...], 0, 0).astype(BF)
        return 0

    lax.fori_loop(0, acc.shape[0] // chunk, body, 0)


def out_back_kernel(
    n, ints, hidden, cot, gs_a, gs_b, gain, weights, gated, mixed, qkvg, log_decay, head_gain, ups,
    keep_out, recv_out,
    grad_hidden, grad_mixed, grad_gate, gain_grad, head_grad, packet, out_own, out_cross, *rest,
):
    w_grads, (acc, state, gain_sum, head_sum) = rest[:-4], rest[-4:]
    step = pl.program_id(0)
    tile = n - 1 - step
    per_tile = TILE // SPAN

    @pl.when(step == 0)
    def _():
        acc[...] = jnp.zeros_like(acc)
        state[...] = jnp.zeros_like(state)
        gain_sum[...] = jnp.zeros_like(gain_sum)
        head_sum[...] = jnp.zeros_like(head_sum)

    x, core = ints[7], ints[4]
    quarter = out_own.shape[1]
    for target, half in ((out_own, x), (out_cross, 1 - x)):
        at = pl.multiple_of((2 * half + core) * quarter, 128)
        pair = pl.multiple_of(half * quarter, 128)
        share = keep_out[:, pl.ds(pair, quarter)].astype(F32) + recv_out[:, pl.ds(pair, quarter)].astype(F32)
        target[...] = (hidden[:, pl.ds(at, quarter)] + share).astype(BF)
    gs = gs_a[...].astype(F32) + gs_b[...].astype(F32)
    hid = hidden[...]
    inv = rms_scale(hid)
    normal = hid * inv
    gain_sum[0:1, :] += jnp.sum(gs * normal, axis=0, keepdims=True)
    e = gs * gain[...]
    gh = cot[...].astype(F32) + inv * (e - normal * jnp.mean(e * normal, axis=-1, keepdims=True))
    grad_hidden[...] = gh
    low = gh.astype(BF)
    acc[...] += dot(gated[...], low, 0, 0)
    for h in range(2):
        values = slice(h * DV, (h + 1) * DV)
        m = mixed[:, values]
        inv_head = rms_scale(m)
        nh = m * inv_head
        g = qkvg[:, head_cols(h, 3)].astype(F32)
        sig = jax.nn.sigmoid(g)
        w = g * sig
        gd = dot(low, weights[out_rows(h), :], 1, 1)
        head_sum[0:1, :] += jnp.sum(gd * nh * w, axis=0, keepdims=True)
        gn = gd * head_gain[...]
        grad_gate[:, values] = (gn * nh * sig * (1.0 + g * (1.0 - sig))).astype(BF)
        gn = gn * w
        gm = inv_head * (gn - nh * jnp.mean(gn * nh, axis=-1, keepdims=True))
        grad_mixed[:, values] = gm.astype(BF)
    since = jnp.exp(distances(ups[LEVELS], log_decay[...]))
    for j in reversed(range(per_tile)):
        rows = slice(j * SPAN, (j + 1) * SPAN)
        keep = ints[8 + tile * per_tile + j].astype(F32)
        for h in range(2):
            lanes = slice(h * DK, (h + 1) * DK)
            values = slice(h * DV, (h + 1) * DV)
            qd = (qkvg[rows, head_cols(h, 0)].astype(F32) * since[rows, lanes]).astype(BF)
            last = since[j * SPAN + SPAN - 1 : j * SPAN + SPAN, lanes]
            state[h] = keep * (state[h] * last + dot(grad_mixed[rows, values], qd, 0, 0))

    @pl.when(step == n - 1)
    def _():
        packet[0:DV] = state[0]
        packet[DV : 2 * DV] = state[1]
        gain_grad[...] = gain_sum[...]
        head_grad[...] = head_sum[...]
        w_grads[0][...] = acc[...].astype(BF)


def within_back_kernel(qkvg, log_decay, grad_mixed, ups, downs, level, level_t, grad_qk, grad_v, grad_ld):
    ld = log_decay[...]
    high = ld.astype(BF)
    lower = (ld - high.astype(F32)).astype(BF)
    lev, lev_t = level[...], level_t[...]
    gd, gd_t = [], []
    for h in range(2):
        v, gm = qkvg[:, head_cols(h, 2)], grad_mixed[:, h * DV : (h + 1) * DV]
        gd.append(dot(gm, v, 1, 1))
        gd_t.append(dot(v, gm, 1, 1))
    scores_t = [None, None]
    grad_q, grad_k = [None, None], [None, None]
    for l in range(LEVELS + 1):
        if l < LEVELS:
            x = jnp.exp(dot(ups[l], high) + dot(ups[l], lower))
        parts = []
        for h in range(2):
            q, k = qkvg[:, head_cols(h, 0)], qkvg[:, head_cols(h, 1)]
            if l < LEVELS:
                xh = x[:, h * DK : (h + 1) * DK]
                qf, kf = q.astype(F32) * xh, k.astype(F32) * xh
                q, k = qf.astype(BF), kf.astype(BF)
            s = dot(k, q, 1, 1)
            scores_t[h] = jnp.where(lev_t == l, s, 0.0 if l == 0 else scores_t[h])
            here = jnp.where(lev == l, gd[h], 0.0).astype(BF)
            here_t = jnp.where(lev_t == l, gd_t[h], 0.0).astype(BF)
            dq, dk = dot(here, k), dot(here_t, q)
            if l < LEVELS:
                parts.append(qf * dq + kf * dk)
                dq, dk = dq * xh, dk * xh
            grad_q[h] = dq if l == 0 else grad_q[h] + dq
            grad_k[h] = dk if l == 0 else grad_k[h] + dk
        if l < LEVELS:
            both = dot(downs[l], jnp.concatenate(parts, axis=1).astype(BF))
            total = both if l == 0 else total + both
    grad_ld[...] = total
    for h in range(2):
        grad_qk[:, 2 * h * DK : (2 * h + 1) * DK] = grad_q[h]
        grad_qk[:, (2 * h + 1) * DK : (2 * h + 2) * DK] = grad_k[h]
        grad_v[:, h * DV : (h + 1) * DV] = dot(
            scores_t[h].astype(BF), grad_mixed[:, h * DV : (h + 1) * DV]
        ).astype(BF)


def project_back_kernel(
    tile, ints, qkvg, log_decay, grad_mixed, before, grad_qk, grad_v, grad_ld, grad_gate, rank, up, bias,
    ups, downs, weights,
    grad_project, grad_first, rank_part, packet, up_sum, bias_sum, d_since, d_towards, ld_sum,
):
    per_tile = TILE // SPAN
    ld = log_decay[...]
    since = jnp.exp(distances(ups[0], ld))
    towards = jnp.exp(distances(ups[1], ld))
    for j in reversed(range(per_tile)):
        rows = slice(j * SPAN, (j + 1) * SPAN)
        keep = ints[tile * per_tile + j].astype(F32)
        for h in range(2):
            lanes = slice(h * DK, (h + 1) * DK)
            values = slice(h * DV, (h + 1) * DV)
            gm = grad_mixed[rows, values]
            v = qkvg[rows, head_cols(h, 2)]
            qd = qkvg[rows, head_cols(h, 0)].astype(F32) * since[rows, lanes]
            kd = qkvg[rows, head_cols(h, 1)].astype(F32) * towards[rows, lanes]
            prev = before[j, h]
            after = packet[values]
            after_low = after.astype(BF)
            dq = dot(gm, prev)
            dk = dot(v, after_low)
            d_since[rows, lanes] = (qd * dq).astype(BF)
            d_towards[rows, lanes] = (kd * dk).astype(BF)
            dq = grad_qk[rows, 2 * h * DK : (2 * h + 1) * DK] + dq * since[rows, lanes]
            dk = grad_qk[rows, (2 * h + 1) * DK : (2 * h + 2) * DK] + dk * towards[rows, lanes]
            dv = grad_v[rows, values].astype(F32) + dot(kd.astype(BF), after_low, 1, 1)
            grad_project[rows, head_cols(h, 0)] = (dq * scaling).astype(BF)
            grad_project[rows, head_cols(h, 1)] = dk.astype(BF)
            grad_project[rows, head_cols(h, 2)] = dv.astype(BF)
            grad_project[rows, head_cols(h, 3)] = grad_gate[rows, values]
            last = since[j * SPAN + SPAN - 1 : j * SPAN + SPAN, lanes]
            d_last = last * jnp.sum(prev.astype(F32) * after, axis=0, keepdims=True)
            ld_sum[rows, lanes] = grad_ld[rows, lanes] + d_last
            packet[values] = keep * (after * last + dot(gm, qd.astype(BF), 0, 0))
    d_log = ld_sum[...] + dot(downs[0], d_since[...]) + dot(downs[1], d_towards[...])
    logits = dot(rank[...], up[...]) + bias[...]
    gl = (d_log * (1.0 / decay_scale) * jax.nn.sigmoid(-logits)).astype(BF)
    up_sum[...] += dot(rank[...], gl, 0, 0)
    bias_sum[0:1, :] += jnp.sum(gl.astype(F32), axis=0, keepdims=True)
    rank_part[...] = dot(up[...], gl, 1, 1)
    grad_first[...] = (
        dot(grad_project[:, :HEAD], weights[in_rows(0), :])
        + dot(grad_project[:, HEAD:], weights[in_rows(1), :])
    ).astype(BF)


def source_back_kernel(
    src, normed, gf_a, gf_b, rank_a, rank_b, w_down, gain, grad_hidden,
    own, cross, dealt, down_sum, gain_sum,
):
    low = (rank_a[...] + rank_b[...]).astype(BF)
    gf = gf_a[...].astype(F32) + gf_b[...].astype(F32) + dot(low, w_down[...], 0, 0)
    x = src[...].astype(F32)
    inv = rms_scale(x)
    normal = x * inv
    gain_sum[0:1, :] += jnp.sum(gf * normal, axis=0, keepdims=True)
    e = gf * gain[...]
    dealt[...] = (
        grad_hidden[...] + inv * (e - normal * jnp.mean(e * normal, axis=-1, keepdims=True))
    ).astype(BF)
    down_sum[...] += dot(low, normed[...])
    quarter = own.shape[2]
    at_x, at_core = lax.axis_index("x"), lax.axis_index("core")
    for out, half in ((own, at_x), (cross, 1 - at_x)):
        col = pl.multiple_of((2 * half + at_core) * quarter, 128)
        for j in range(TILE // SPAN):
            out[j] = dealt[j * SPAN : (j + 1) * SPAN, pl.ds(col, quarter)]


def back_kernel(nd, spans, reach, direct, f, table, act, grad_gu, normed, cot, qkvg, log_decay, grad_mixed, packet_in,
                factors, out_own, out_cross, ups, downs, level, level_t, *rest):
    n_sums = 5 if direct else 3
    (leaving, grad_qk_o, grad_v_o, grad_ld_o, gath_o, *sums), rest = rest[: 5 + n_sums], rest[5 + n_sums :]
    (grad_qk, grad_v, grad_ld, sent_packets, got_packets), rest = rest[:5], rest[5:]
    (carry_send, carry_recv, out_sems), rest = rest[:3], rest[3:]
    (joined, sent, gath), rest = rest[:3], rest[3:]
    undeal_sems, rest = rest[:4], rest[4:]
    pitch = act.shape[1] // 2
    tiles = spans * SPAN // TILE
    nz = nd // 2
    carry = Carry(nd, reach, -1, leaving, sent_packets, got_packets, carry_send, carry_recv)
    enter(nd, carry.shifts())
    undeal = Undeal(nd, spans, table, out_own, out_cross, joined, sent, gath, undeal_sems)
    undeal.begin()
    leaving[: 2 * DV] = packet_in[...]
    leaving[2 * DV :] = factors[...]
    carry.send(0)
    outgoing = []

    def store(value, out):
        outgoing.append(pltpu.make_async_copy(value, out, out_sems.at[len(outgoing)]))
        outgoing[-1].start()

    def at(ref, i):
        return ref.at[pl.ds(pl.multiple_of(i * TILE, TILE), TILE), :]

    def tile(i, _):
        within_back_kernel(
            at(qkvg, i), at(log_decay, i), at(grad_mixed, i), ups, downs, level, level_t,
            at(grad_qk, i), at(grad_v, i), at(grad_ld, i),
        )
        return 0

    def some(first, last):
        return lambda: lax.fori_loop(first, last, tile, 0)

    stages = list(range(carry.run()))

    def advance():
        if stages:
            carry.step(stages.pop(0))

    if direct:
        accs, rest = rest[:3], rest[3:]
        chains = [
            Collapse(nd, order, acc, pitch, low, count, rest[3 * k], rest[3 * k + 1 : 3 * k + 3])
            for k, (acc, order, low, count) in enumerate(
                ((accs[0], 0, 0, f), (accs[1], 1, 0, f), (accs[2], 0, 0, f // 2), (accs[2], 1, f // 2, f // 2))
            )
        ]
        weight_grad_into(accs[0], grad_gu.at[:, pl.ds(0, 2 * pitch)], normed, 128)
        chains[0].begin()
        advance()
        weight_grad_into(accs[1], grad_gu.at[:, pl.ds(2 * pitch, 2 * pitch)], normed, 128)
        chains[1].begin()
        advance()
        undeal.exchange()
        for kz in [k % nz for k in range(1, nz + 1)]:
            chains[0].second(kz)
        weight_grad_into(accs[2], act, cot, 128)
        for kz in [k % nz for k in range(1, nz + 1)]:
            chains[1].second(kz)
        chains[2].begin()
        chains[3].begin()
        advance()
        for kz in [k % nz for k in range(1, nz + 1)]:
            chains[0].third(kz)
            chains[1].third(kz)
            some(kz, kz + 1)()
        progress(chains[2:], nz, [some(nz, tiles)])
        squares = sums[-1]
        squares[...] = jnp.zeros_like(squares)
        for chain, out in zip(chains, sums):
            chain.finish(out, squares)
    else:
        undeal.exchange()
        weight_grad_into(sums[0], grad_gu.at[:, pl.ds(0, 2 * pitch)], normed, 128)
        weight_grad_into(sums[1], grad_gu.at[:, pl.ds(2 * pitch, 2 * pitch)], normed, 128)
        weight_grad_into(sums[2], act, cot, 128)
        some(0, tiles)()
        while stages:
            advance()
    store(grad_qk, grad_qk_o)
    store(grad_v, grad_v_o)
    store(grad_ld, grad_ld_o)
    for k in range(1, nd):
        undeal.arrive(k)
    store(gath, gath_o)
    undeal.finish()
    for copy in outgoing:
        copy.wait()


def last_kernel(nd, spans, direct, table, keep, qkvg, log_decay, grad_mixed, before, leaving, grad_qk, grad_v, grad_ld,
                grad_gate, rank, up, bias, ups, downs, weights, src, normed, grad_hidden, gain, po_in, gain_second, head_part, squares_in,
                *rest):
    n_sums = 6 if direct else 1
    (gath_o, down_sum, gain_sum, up_sum, bias_sum, *sums), rest = rest[: 5 + n_sums], rest[5 + n_sums :]
    (packet, grad_project, grad_first, grad_first_other, rank_part, rank_other), rest = rest[:6], rest[6:]
    (d_since, d_towards, ld_sum, dealt), rest = rest[:4], rest[4:]
    (gf_send, gf_recv, rk_send, rk_recv, out_sems), rest = rest[:5], rest[5:]
    (own, cross, joined, sent, gath), rest = rest[:5], rest[5:]
    undeal_sems, rest = rest[:6], rest[6:]
    tiles = spans * SPAN // TILE
    per_tile = TILE // SPAN
    nz = nd // 2
    enter(nd)
    core = lax.axis_index("core")
    undeal = Undeal(nd, spans, table, own, cross, joined, sent, gath, undeal_sems)
    chains = []
    if direct:
        (po_acc, pi_acc), rest = rest[:2], rest[2:]
        (small_sent, small_got, small_norms), rest = rest[:3], rest[3:]
        small_sems, rest = rest[:6], rest[6:]
        small = Small(nd, sums[4], small_sent, small_got, small_norms, small_sems)
        squares = sums[5]
        squares[...] = squares_in[...]
        small_left = list(range(small.steps()))

        def advance_small():
            if small_left:
                small.end(small_left.pop(0))
                if small_left:
                    small.begin(small_left[0])

        halves = ((pi_acc, 0, HEAD), (pi_acc, 1, HEAD), (po_acc, 0, DV), (po_acc, 1, DV))
        chains = [
            Collapse(
                nd, order, acc, size, order * size // 2, size // 2, rest[3 * k], rest[3 * k + 1 : 3 * k + 3]
            )
            for k, (acc, order, size) in enumerate(halves)
        ]
        fill = pltpu.make_async_copy(po_in, po_acc, out_sems.at[0])
        fill.start()
        fill.wait()
        chains[2].begin()
        chains[3].begin()
    packet[...] = leaving[...]
    for ref in (down_sum, gain_sum, up_sum, bias_sum):
        ref[...] = jnp.zeros_like(ref)

    def at(ref, i):
        return ref.at[pl.ds(pl.multiple_of(i * TILE, TILE), TILE), :]

    def swap_first(i):
        return copy_to(at(grad_first, i), at(grad_first_other, i), gf_send.at[i], gf_recv.at[i], {"core": 1 - core})

    def swap_rank(i):
        return copy_to(rank_part.at[i], rank_other.at[i], rk_send.at[i], rk_recv.at[i], {"core": 1 - core})

    def body(step, _):
        i = tiles - 1 - step
        project_back_kernel(
            i, keep, at(qkvg, i), at(log_decay, i), at(grad_mixed, i), before.at[pl.ds(i * per_tile, per_tile)],
            at(grad_qk, i), at(grad_v, i), at(grad_ld, i), at(grad_gate, i), at(rank, i), up, bias, ups, downs, weights,
            at(grad_project, i), at(grad_first, i), rank_part.at[i], packet, up_sum, bias_sum,
            d_since, d_towards, ld_sum,
        )
        swap_first(i).start()
        swap_rank(i).start()
        return 0

    lax.fori_loop(0, tiles, body, 0)
    if direct:
        for kz in [k % nz for k in range(1, nz + 1)]:
            chains[2].second(kz)
            chains[3].second(kz)

    def finish_tile(step, _):
        i = tiles - 1 - step
        swap_first(i).wait()
        swap_rank(i).wait()
        source_back_kernel(
            at(src, i), at(normed, i), at(grad_first, i), at(grad_first_other, i), rank_part.at[i], rank_other.at[i],
            weights.at[pl.ds(0, 16), :], gain, at(grad_hidden, i),
            own.at[pl.ds(i * per_tile, per_tile)], cross.at[pl.ds(i * per_tile, per_tile)],
            dealt, down_sum, gain_sum,
        )
        return 0

    lax.fori_loop(0, tiles, finish_tile, 0)
    undeal.begin()
    if direct:
        small.fill(gain_sum, gain_second, down_sum, up_sum, bias_sum, head_part)
        small.begin(0)
        weight_grad_into(pi_acc, grad_project, normed, 128)
        chains[0].begin()
        chains[1].begin()
        advance_small()
        for kz in [k % nz for k in range(1, nz + 1)]:
            chains[2].third(kz)
            chains[3].third(kz)
    else:
        weight_grad_into(sums[0], grad_project, normed, 128)
    undeal.exchange()
    arrivals = [functools.partial(undeal.arrive, k) for k in range(1, nd)]
    if direct:
        for kz in [k % nz for k in range(1, nz + 1)]:
            chains[0].second(kz)
            chains[1].second(kz)
            advance_small()
            if arrivals:
                arrivals.pop(0)()
        while small_left:
            advance_small()
        small.begin_head()
        for kz in [k % nz for k in range(1, nz + 1)]:
            chains[0].third(kz)
            chains[1].third(kz)
            if arrivals:
                arrivals.pop(0)()
        chains[2].finish(sums[2], squares)
        chains[3].finish(sums[3], squares)
        small.end_head()
    for arrive in arrivals:
        arrive()
    if direct:
        chains[0].finish(sums[0], squares)
        chains[1].finish(sums[1], squares)
        small.begin_norm(squares[...] + small.squares())
    undeal.finish()
    out = pltpu.make_async_copy(gath, gath_o, out_sems.at[0])
    out.start()
    if direct:
        small.end_norm(squares)
    out.wait()


def remote(kernel, ins, specs, outs, out_specs, scratch, name, number, us):
    return pl.pallas_call(
        kernel,
        in_specs=specs,
        out_specs=out_specs,
        out_shape=outs,
        scratch_shapes=scratch,
        name=name,
        compiler_params=pltpu.CompilerParams(
            vmem_limit_bytes=VMEM_LIMIT, collective_id=number, has_side_effects=True
        ),
        cost_estimate=cost(us),
    )(*ins)


def all_sum(value, axes, sizes):
    for axis, size in zip(axes, sizes):
        bit = 1
        while bit < size:
            value = value + lax.ppermute(value, axis, [(i, i ^ bit) for i in range(size)])
            bit *= 2
    return value


def square_sum(array):
    return jnp.sum(array * array)


def adam_update(weight, grad, first, second, factor, decay_rate):
    clipped = grad * factor
    first_new = beta_one * first + (1.0 - beta_one) * clipped
    second_new = beta_two * second + (1.0 - beta_two) * clipped * clipped
    first_hat = first_new / (1.0 - beta_one**adam_step)
    second_hat = second_new / (1.0 - beta_two**adam_step)
    master = weight.astype(F32)
    change = -learn_rate * (first_hat / (jnp.sqrt(second_hat) + adam_eps) + decay_rate * master)
    return (grad, first_new, second_new, change)


def swap(value, axis):
    return lax.ppermute(value, axis, [(0, 1), (1, 0)])


def on_device(
    tokens, cotangent, seq_extra, deal, proj_in, decay_down, decay_up, decay_bias, head_gain, proj_out, block_gains,
    ffn_in, ffn_out, first_proj_in, second_proj_in, first_decay_down, second_decay_down, first_decay_up,
    second_decay_up, first_decay_bias, second_decay_bias, first_head_gain, second_head_gain, first_proj_out,
    second_proj_out, first_block_gains, second_block_gains, first_ffn_in, second_ffn_in, first_ffn_out, second_ffn_out,
):
    d = tokens.shape[1]
    nd = lax.axis_size("dp")
    nz = nd // 2
    dp, x, core = lax.axis_index("dp"), lax.axis_index("x"), lax.axis_index("core")
    z, y = dp // 2, dp % 2
    tensor = 2 * x + core
    per_dev = tokens.shape[0] // SPAN
    spans = per_dev // 2
    rows = spans * SPAN
    tiles = rows // TILE
    capacity = -(-per_dev // nd)
    quarter = d // 4
    f = ffn_out.shape[0]
    w = d // nd
    direct = w % 128 == 0

    recv_slot, send_local, back_local, home_slot = deal_tables(deal, nd, per_dev, capacity, dp)
    mine = lax.dynamic_slice_in_dim(recv_slot, x * spans, spans)
    theirs = lax.dynamic_slice_in_dim(recv_slot, (1 - x) * spans, spans)
    span_ids = (dp * 2 + x) * spans + jnp.arange(spans, dtype=jnp.int32)
    keep = 1 - span_starts(seq_extra, span_ids)
    other_quarter = 2 * (1 - x) + core
    quarters = jnp.stack([tensor, other_quarter, 2 * x + 1 - core, 2 * (1 - x) + 1 - core])
    ints = jnp.concatenate([quarters, jnp.stack([core, z, y, x]), keep]).astype(jnp.int32)
    ups, downs, level, level_t = (jnp.asarray(v) for v in level_matrices())
    ups_last, downs_last = (jnp.asarray(v[LEVELS:]) for v in level_matrices()[:2])

    hh, ho, hf = HEAD // 2, DV // 2, f // 2
    pitch = f
    ffn_t = ffn_in.reshape(w, 2 * f).T
    shard_p = jnp.concatenate([decay_down.T, proj_in.reshape(w, HEAD).T, proj_out.reshape(DV, w)], axis=0)
    shard_f = jnp.concatenate([ffn_t[:f], ffn_out, ffn_t[f:]], axis=0)

    def fit(parts):
        return jnp.concatenate(parts, axis=0)

    table = jnp.concatenate([send_local, mine, theirs]).astype(jnp.int32)
    if not direct:

        def gathered(shard):
            return jnp.swapaxes(lax.all_gather(shard, "dp", axis=0), 0, 1).reshape(shard.shape[0], d)

        def halves(shard):
            own, other = gathered(shard), gathered(swap(shard, "x"))
            return jnp.where(x == 0, fit([own, other]), fit([other, own]))

        shard_p = halves(shard_p)
        shard_f = fit([halves(ffn_t[:f]), halves(ffn_out), halves(ffn_t[f:])])

    up_own = decay_up.reshape(16, DK)
    bias_own = decay_bias.reshape(1, DK)
    small_own = jnp.concatenate([up_own.astype(F32), bias_own, jnp.zeros((7, DK), F32)], axis=0)
    small_other = swap(small_own, "x")
    small_both = jnp.where(
        x == 0,
        jnp.concatenate([small_own, small_other], axis=1),
        jnp.concatenate([small_other, small_own], axis=1),
    )
    up, bias = small_both[:16].astype(BF), small_both[16:17]
    gain_one, gain_two = block_gains[0:1], block_gains[1:2]
    head_row = head_gain.reshape(1, DV)

    def tall(cols, dtype=BF):
        return sds(rows, cols, dtype=dtype)

    nlev = LEVELS + 2
    sequence = nd * 2
    reach = -(-(MAX_SPANS - 1) // spans)
    (src, cot, weights, w_ffn, normed_first, qkvg, log_decay, rank, mixed, gated, attn, before, attn_other,
     factors) = forward(
        table, keep.astype(jnp.int32), tokens, cotangent, shard_p, shard_f, gain_one, up, bias, head_row, ups, level,
        nd, spans, reach, direct,
    )
    ff = 2 * f
    hidden, normed_second, act, grad_gu, keep_out, send_out, grad_second = run(
        ffn_kernel, (tiles,),
        [SMEM] + [rows_spec(d)] * 4 + [whole_spec(1, d), whole_spec(3 * ff, d)],
        [rows_spec(d), rows_spec(d), rows_spec(2 * pitch), rows_spec(4 * pitch), rows_spec(2 * quarter),
         rows_spec(2 * quarter), rows_spec(d)],
        [tall(d, F32), tall(d), tall(2 * pitch), tall(4 * pitch), tall(2 * quarter), tall(2 * quarter), tall(d)],
        [pltpu.VMEM((TILE, d), BF)],
        "ffn", 34,
    )(ints, src, attn, attn_other, cot, gain_two, w_ffn)
    gs_other = swap(grad_second, "core")
    recv_out = swap(send_out, "core")

    def plain_shard(full, f_rows):
        full = jnp.swapaxes(full.reshape(2 * f_rows, nd, w), 0, 1)
        total = lax.psum_scatter(full, "dp", scatter_dimension=0, tiled=True)[0].astype(F32)
        keep_rows = lax.dynamic_slice_in_dim(total, x * f_rows, f_rows)
        give_rows = lax.dynamic_slice_in_dim(total, (1 - x) * f_rows, f_rows)
        return keep_rows + swap(give_rows, "x")

    grad_hidden, grad_mixed, grad_gate, gain_second, head_part, packet_back, out_own, out_cross, acc_po = run(
        functools.partial(out_back_kernel, tiles), (tiles,),
        [SMEM] + [rows_spec(d, tiles)] * 4
        + [whole_spec(1, d), whole_spec(2 * PROJ_ROWS, d), rows_spec(2 * DV, tiles), rows_spec(2 * DV, tiles),
           rows_spec(2 * HEAD, tiles), rows_spec(2 * DK, tiles), whole_spec(1, DV), whole_spec(nlev, TILE, TILE),
           rows_spec(2 * quarter, tiles), rows_spec(2 * quarter, tiles)],
        [rows_spec(d, tiles), rows_spec(2 * DV, tiles), rows_spec(2 * DV, tiles), whole_spec(8, d),
         whole_spec(8, DV), whole_spec(2 * DV, DK), rows_spec(quarter, tiles), rows_spec(quarter, tiles),
         whole_spec(2 * DV, d)],
        [tall(d, F32), tall(2 * DV), tall(2 * DV), sds(8, d), sds(8, DV), sds(2 * DV, DK), tall(quarter),
         tall(quarter), sds(2 * DV, d, dtype=BF)],
        [pltpu.VMEM((2 * DV, d), F32), pltpu.VMEM((2, DV, DK), F32), pltpu.VMEM((8, d), F32), pltpu.VMEM((8, DV), F32)],
        "out_back", 19,
    )(ints, hidden, cot, grad_second, gs_other, gain_two, weights, gated, mixed, qkvg, log_decay, head_row, ups,
      keep_out, recv_out)

    dma = pltpu.SemaphoreType.DMA
    steps = len(carry_widths(reach)[0]) + 2
    shape_qk, shape_v, shape_ld = (rows, 4 * DK), (rows, 2 * DV), (rows, 2 * DK)
    buffers, sems = undeal_scratch(nd, per_dev, spans, quarter, capacity, False)
    scratch = [pltpu.VMEM(shape_qk, F32), pltpu.VMEM(shape_v, BF), pltpu.VMEM(shape_ld, F32)]
    scratch += [pltpu.VMEM((steps - 1, 2 * DV + 16, DK), BF), pltpu.VMEM((steps, 2 * DV + 16, DK), BF)]
    scratch += [dma((steps,)), dma((steps,)), dma((4,))] + buffers[2:] + sems
    if direct:
        sums = [sds(f, w), sds(f, w), sds(f // 2, w), sds(f // 2, w), sds(8, 128)]
        scratch += [pltpu.VMEM((2 * pitch, d), BF)] * 3
        for out in sums[:4]:
            scratch += collapse_scratch(nd, out.shape[0], w)
    else:
        sums = [sds(2 * pitch, d, dtype=BF)] * 3
    leaving, grad_qk, grad_v, grad_ld, back_out, *sums_f = remote(
        functools.partial(back_kernel, nd, spans, reach, direct, f),
        (back_local, act, grad_gu, normed_second, cot, qkvg, log_decay, grad_mixed, packet_back, factors,
         out_own.reshape(spans, SPAN, quarter), out_cross.reshape(spans, SPAN, quarter), ups, downs, level, level_t),
        [SMEM] + [VMEM] * 15,
        [sds(2 * DV + 16, DK), sds(*shape_qk), sds(*shape_v, dtype=BF), sds(*shape_ld),
         sds(nd * capacity, SPAN, quarter, dtype=BF)] + sums,
        [VMEM] + [ANY] * 4 + [VMEM] * len(sums),
        scratch, "back_all", 1, 110,
    )
    if direct:
        shard_gate, shard_up, shard_fo = sums_f[0], sums_f[1], fit(sums_f[2:4])
    else:
        shard_gate, shard_up, shard_fo = (plain_shard(v, pitch)[:f] for v in sums_f)
    block_out = home([back_out.reshape(-1, quarter)], home_slot, [jnp.int32(0)], "block_out_home")

    buffers, sems = undeal_scratch(nd, per_dev, spans, quarter, capacity, True)
    scratch = [
        pltpu.VMEM((2 * DV + 16, DK), F32), pltpu.VMEM((rows, 2 * HEAD), BF), pltpu.VMEM((rows, d), BF),
        pltpu.VMEM((rows, d), BF), pltpu.VMEM((tiles, 16, TILE), F32), pltpu.VMEM((tiles, 16, TILE), F32),
        pltpu.VMEM((TILE, 2 * DK), BF), pltpu.VMEM((TILE, 2 * DK), BF), pltpu.VMEM((TILE, 2 * DK), F32),
        pltpu.VMEM((TILE, d), BF), dma((tiles,)), dma((tiles,)), dma((tiles,)), dma((tiles,)), dma((1,)),
    ] + buffers + sems
    if direct:
        sums = [sds(hh, w), sds(hh, w), sds(ho, w), sds(ho, w), sds(SMALL, 128), sds(8, 128)]
        scratch += [pltpu.VMEM((2 * DV, d), BF), pltpu.VMEM((2 * HEAD, d), BF)] + small_scratch(nd)
        for out in sums[:4]:
            scratch += collapse_scratch(nd, out.shape[0], w)
    else:
        sums = [sds(2 * HEAD, d, dtype=BF)]
    back_grad, down_grad, gain_first, up_grad, bias_grad, *sums_p = remote(
        functools.partial(last_kernel, nd, spans, direct),
        (back_local, keep.astype(jnp.int32), qkvg, log_decay, grad_mixed, before, leaving, grad_qk, grad_v, grad_ld,
         grad_gate, rank, up, bias, ups_last, downs_last, weights, src, normed_first, grad_hidden, gain_one,
         acc_po, gain_second, head_part, sums_f[4] if direct else gain_second),
        [SMEM, SMEM] + [VMEM] * 19 + [ANY] + [VMEM] * 3,
        [sds(nd * capacity, SPAN, d, dtype=BF), sds(16, d), sds(8, d), sds(16, 2 * DK), sds(8, 2 * DK)] + sums,
        [ANY] + [VMEM] * (4 + len(sums)),
        scratch, "finish_all", 2, 100,
    )
    if direct:
        shard_pi, shard_po = fit(sums_p[:2]), fit(sums_p[2:4])
    else:
        shard_pi, shard_po = plain_shard(sums_p[0], HEAD), plain_shard(acc_po, DV)
    token_grad = home([back_grad.reshape(-1, d)], home_slot, [jnp.int32(0)], "token_grad_home")

    if direct:
        small, norm_block = sums_p[4], sums_p[5]
        gain_first, gain_second = small[0:8].reshape(d), small[8:16].reshape(d)
        shard_down = lax.dynamic_slice_in_dim(small, 16 + 16 * dp, 16, 0).T
        up_total = lax.dynamic_slice_in_dim(small, 144 + 16 * x, 16, 0)
        bias_total = lax.dynamic_slice_in_dim(small, 176 + x, 1, 0)
        head_total = small[178:180].reshape(DV)
        norm_sq = jnp.sum(norm_block)
    else:
        parts = (gain_first[0], gain_second[0], down_grad, up_grad, bias_grad[0], head_part[0])
        small = jnp.concatenate([v.reshape(-1) for v in parts]).reshape(-1, 128)
        small = all_sum(small, ("x", "dp"), (2, nd)).reshape(-1)
        cuts = [d, d, 16 * d, 32 * DK, 2 * DK, DV]
        starts = [sum(cuts[:k]) for k in range(len(cuts) + 1)]
        gain_first, gain_second, down_total, up_total, bias_total, head_total = (
            small[starts[k] : starts[k + 1]] for k in range(len(cuts))
        )
        head_total = head_total + swap(head_total, "core")
        shard_down = lax.dynamic_slice_in_dim(down_total.reshape(16, d), dp * w, w, 1).T
        up_total = up_total.reshape(16, 2, DK)
        up_total = jnp.where(x == 0, up_total[:, 0], up_total[:, 1])
        bias_total = bias_total.reshape(2, DK)
        bias_total = jnp.where(x == 0, bias_total[0:1], bias_total[1:2])
        local_sq = (
            square_sum(shard_pi) + square_sum(shard_po) + square_sum(shard_gate) + square_sum(shard_up)
            + square_sum(shard_fo) + square_sum(shard_down) / 4
            + (square_sum(up_total) + square_sum(bias_total)) / nd
            + (square_sum(head_total) + square_sum(gain_first) + square_sum(gain_second)) / (4 * nd)
        )
        norm_sq = all_sum(jnp.broadcast_to(local_sq, (8, 128)), ("core", "x", "dp"), (2, 2, nd))[0, 0]
    up_total = up_total.reshape(decay_up.shape)
    bias_total = bias_total.reshape(decay_bias.shape)
    gains_total = jnp.stack([gain_first, gain_second])
    shard_in = shard_pi.T.reshape(proj_in.shape)
    shard_out = shard_po.reshape(proj_out.shape)
    shard_ffn_in = jnp.stack([shard_gate.T, shard_up.T], axis=1)
    shard_ffn_out = shard_fo
    grad_norm = jnp.sqrt(norm_sq)
    clip_norm = clip_scale * math.sqrt(PARAMS)
    factor = jnp.minimum(1.0, clip_norm / (grad_norm + 1e-06))
    update_in = adam_update(proj_in, shard_in, first_proj_in, second_proj_in, factor, weight_decay)
    update_down = adam_update(decay_down, shard_down, first_decay_down, second_decay_down, factor, weight_decay)
    update_up = adam_update(decay_up, up_total, first_decay_up, second_decay_up, factor, weight_decay)
    update_bias = adam_update(decay_bias, bias_total, first_decay_bias, second_decay_bias, factor, 0.0)
    update_head = adam_update(head_gain, head_total, first_head_gain, second_head_gain, factor, 0.0)
    update_out = adam_update(proj_out, shard_out, first_proj_out, second_proj_out, factor, weight_decay)
    update_gains = adam_update(block_gains, gains_total, first_block_gains, second_block_gains, factor, 0.0)
    update_ffn_in = adam_update(ffn_in, shard_ffn_in, first_ffn_in, second_ffn_in, factor, weight_decay)
    update_ffn_out = adam_update(ffn_out, shard_ffn_out, first_ffn_out, second_ffn_out, factor, weight_decay)
    return (
        block_out, token_grad, grad_norm, *update_in, *update_down, *update_up, *update_bias, *update_head,
        *update_out, *update_gains, *update_ffn_in, *update_ffn_out,
    )


def solution(mesh):
    nd, nt = mesh.shape["dp"], mesh.shape["tensor"]
    fine = Mesh(mesh.devices.reshape(nd, nt // 2, 2), ("dp", "x", "core"))
    t = ("x", "core")
    w_specs = {
        "proj_in": P("dp", t, None),
        "decay_down": P("dp", None),
        "decay_up": P(None, t, None),
        "decay_bias": P(t, None),
        "head_gain": P(),
        "proj_out": P(t, None, "dp"),
        "block_gains": P(),
        "ffn_in": P("dp", None, t),
        "ffn_out": P(t, "dp"),
    }
    specs = list(w_specs.values())
    placed = [P("dp", None), P("dp", None), P(), P()] + specs
    results = [P("dp", t), P("dp", None), P()]
    for spec in specs:
        placed += [spec] * 2
        results += [spec] * 4
    return jax.shard_map(
        on_device,
        mesh=fine,
        in_specs=tuple(placed),
        out_specs=tuple(results),
        check_vma=False,
    )
```

```python
import functools
import math

import jax
import jax.numpy as jnp
import numpy as np
from jax import lax
from jax.experimental import pallas as pl
from jax.experimental.pallas import tpu as pltpu
from jax.sharding import Mesh
from jax.sharding import PartitionSpec as P

DK = 128
DV = 256
SPAN = 64
MIN_SPANS = 16
MAX_SPANS = 128
PARAMS = 12872448
TILE = 256
LEVELS = 6
HEAD = 2 * DK + 2 * DV
VMEM_LIMIT = 61 * 1024 * 1024
BF = jnp.bfloat16
F32 = jnp.float32

norm_eps = 1e-06
learn_rate = 0.05
beta_one = 0.9
beta_two = 0.95
adam_eps = 1e-08
weight_decay = 0.1
clip_scale = 0.05
adam_step = 10
decay_scale = 16.0
scaling = DK ** (-0.5)
ANY = pl.BlockSpec(memory_space=pl.ANY)
SMEM = pl.BlockSpec(memory_space=pltpu.SMEM)
VMEM = pl.BlockSpec(memory_space=pltpu.VMEM)


def dot(a, b, ca=1, cb=0):
    return lax.dot_general(a, b, (((ca,), (cb,)), ((), ())), preferred_element_type=F32)


def cost(us):
    return pl.CostEstimate(flops=int(us * 1.0e9), bytes_accessed=int(us * 1.0e6), transcendentals=0)


def run(kernel, grid, in_specs, out_specs, out_shape, scratch, name, us):
    return pl.pallas_call(
        kernel,
        grid=grid,
        in_specs=in_specs,
        out_specs=out_specs,
        out_shape=out_shape,
        scratch_shapes=scratch,
        name=name,
        compiler_params=pltpu.CompilerParams(vmem_limit_bytes=VMEM_LIMIT),
        cost_estimate=cost(us),
    )


def sds(*shape, dtype=F32):
    return jax.ShapeDtypeStruct(shape, dtype)


def rows_spec(cols, order=None):
    if order is None:
        return pl.BlockSpec((TILE, cols), lambda i: (i, 0))
    return pl.BlockSpec((TILE, cols), lambda i: (order - 1 - i, 0))


def whole_spec(*shape):
    zeros = (0,) * len(shape)
    return pl.BlockSpec(shape, lambda i: zeros, pipeline_mode=pl.Buffered(1))


def span_starts(seq_extra, span_ids):
    seq_spans = seq_extra + MIN_SPANS
    n = seq_extra.shape[0]
    earlier = jnp.tril(jnp.ones((n, n), jnp.int32), -1)
    bounds = jnp.sum(earlier * seq_spans[None, :], axis=1)
    return jnp.any(bounds[None, :] == span_ids[:, None], axis=1).astype(jnp.int32)


def deal_tables(deal, n_data, per_dev, capacity, my_index):
    table_grid = deal.reshape(n_data, per_dev)
    src_dev = table_grid // per_dev
    src_local = table_grid % per_dev
    my_source = lax.dynamic_index_in_dim(src_dev, my_index, 0, keepdims=False)
    earlier = jnp.tril(jnp.ones((per_dev, per_dev), jnp.int32), -1)
    same_source = (my_source[:, None] == my_source[None, :]).astype(jnp.int32)
    my_rank = jnp.sum(same_source * earlier, axis=1)
    recv_slot = my_source * capacity + my_rank
    owned_here = (src_dev == my_index).astype(jnp.int32)
    send_rank = jnp.sum(owned_here[:, None, :] * earlier[None], axis=2)
    slot_ids = jnp.arange(capacity, dtype=jnp.int32)
    send_hit = owned_here[:, :, None] * (
        send_rank[:, :, None] == slot_ids[None, None, :]
    ).astype(jnp.int32)
    send_local = jnp.sum(send_hit * src_local[:, :, None], axis=1)
    peer_ids = jnp.arange(n_data, dtype=jnp.int32)
    local_ids = jnp.arange(per_dev, dtype=jnp.int32)
    back_hit = (
        (my_source[None, None, :] == peer_ids[:, None, None])
        & (my_rank[None, None, :] == slot_ids[None, :, None])
    ).astype(jnp.int32)
    back_local = jnp.sum(back_hit * local_ids[None, None, :], axis=2)
    home_hit = owned_here[:, :, None] * (
        src_local[:, :, None] == local_ids[None, None, :]
    ).astype(jnp.int32)
    home_slot = jnp.sum(
        home_hit * (peer_ids[:, None, None] * capacity + send_rank[:, :, None]), axis=(0, 1)
    )
    return recv_slot, send_local.reshape(-1), back_local.reshape(-1), home_slot


def level_matrices():
    t = np.arange(TILE, dtype=np.int32)[:, None]
    u = np.arange(TILE, dtype=np.int32)[None, :]
    ups = []
    level = np.full((TILE, TILE), LEVELS + 1, np.int32)
    for l in range(LEVELS):
        block = SPAN >> l
        half = block // 2
        same = (t // block) == (u // block)
        mid = (t // block) * block + half
        right = (t >= mid) & (u >= mid) & (u <= t)
        left = (t < mid) & (u > t) & (u < mid)
        ups.append(same & (right | left))
        hit = same & (t % block >= half) & (u % block < half)
        level = np.where(hit, l, level)
    level = np.where(t == u, LEVELS, level)
    same = (t // SPAN) == (u // SPAN)
    ups.append(same & (u <= t))
    ups.append(same & (u > t))
    ups = np.stack(ups).astype(np.float32).astype(BF)
    return ups, np.ascontiguousarray(np.swapaxes(ups, 1, 2)), level, np.ascontiguousarray(level.T)


def home_kernel(count, table, src, out):
    step = pl.program_id(0)
    for i in range(count):
        out[i * SPAN : (i + 1) * SPAN, :] = src[table[step * count + i]].astype(F32)


def home(spans, table, name):
    total = table.shape[0]
    count = 5
    d = spans.shape[2]
    return pl.pallas_call(
        functools.partial(home_kernel, count),
        grid=(total // count,),
        in_specs=[SMEM, whole_spec(*spans.shape)],
        out_specs=pl.BlockSpec((count * SPAN, d), lambda i: (i, 0)),
        out_shape=sds(total * SPAN, d),
        name=name,
        compiler_params=pltpu.CompilerParams(vmem_limit_bytes=VMEM_LIMIT),
        cost_estimate=cost(5),
    )(table, spans)


def copy_to(src, dst, send_sem, recv_sem, target):
    return pltpu.make_async_remote_copy(
        src_ref=src,
        dst_ref=dst,
        send_sem=send_sem,
        recv_sem=recv_sem,
        device_id=target,
        device_id_type=pl.DeviceIdType.MESH,
    )


def enter(nd, shifts=()):
    dp, x, core = lax.axis_index("dp"), lax.axis_index("x"), lax.axis_index("core")
    peers = [{"dp": lax.rem(dp + k, nd)} for k in range(1, nd)] + [{"x": 1 - x}, {"core": 1 - core}]
    for k in shifts:
        peers += [along_sequence(nd, k), along_sequence(nd, -k)]
    barrier = pltpu.get_barrier_semaphore()
    for peer in peers:
        pl.semaphore_signal(barrier, inc=1, device_id=peer, device_id_type=pl.DeviceIdType.MESH)
    pl.semaphore_wait(barrier, len(peers))


def along_sequence(nd, k):
    q = lax.rem(lax.axis_index("dp") * 2 + lax.axis_index("x") + k + 2 * nd, 2 * nd)
    return {"dp": q // 2, "x": lax.rem(q, 2)}


def carry_widths(reach):
    widths = []
    width = 1
    while 2 * width < reach:
        widths.append(width)
        width *= 2
    return widths, width


class Carry:
    def __init__(self, nd, reach, sign, packet, sent, got, send_sems, recv_sems):
        self.nd, self.sign, self.packet, self.sent, self.got = nd, sign, packet, sent, got
        self.send_sems, self.recv_sems = send_sems, recv_sems
        self.widths, self.last = carry_widths(reach)
        self.q = lax.axis_index("dp") * 2 + lax.axis_index("x")

    def shifts(self):
        return self.widths + [1, 1 + self.last]

    def copy(self, index):
        source = min(index, len(self.widths))
        return copy_to(
            self.sent.at[source],
            self.got.at[index],
            self.send_sems.at[index],
            self.recv_sems.at[index],
            along_sequence(self.nd, self.sign * self.shifts()[index]),
        )

    def send(self, stage):
        self.sent[stage] = self.packet[...].astype(BF)
        self.copy(stage).start()
        if stage == len(self.widths):
            self.copy(stage + 1).start()

    def receive(self, index):
        self.copy(index).wait_recv()
        k = self.shifts()[index]
        there = self.q >= k if self.sign > 0 else self.q + k < 2 * self.nd
        return jnp.where(there, self.got[index].astype(F32), 0.0)

    def step(self, stage):
        if stage < len(self.widths):
            self.join(self.receive(stage), self.packet[...])
            self.send(stage + 1)
        else:
            near, far = self.receive(stage), self.receive(stage + 1)
            self.join(far, near)
            for index in range(stage + 2):
                self.copy(index).wait_send()

    def join(self, earlier, later):
        for h in range(2):
            states = slice(h * DV, (h + 1) * DV)
            f = slice(2 * DV + h, 2 * DV + h + 1)
            self.packet[states] = later[f] * earlier[states] + later[states]
            self.packet[f] = later[f] * earlier[f]

    def run(self):
        return len(self.widths) + 1


class Spread:
    def __init__(self, nd, order, own, window, send_sems, recv_sems):
        self.nz, self.order, self.own, self.window = nd // 2, order, own, window
        self.send_sems, self.recv_sems = send_sems, recv_sems
        dp, self.x = lax.axis_index("dp"), lax.axis_index("x")
        self.z, self.y = dp // 2, lax.rem(dp, 2)
        nz = self.nz
        self.moves = [((0, 0, 0), (k, 0, 0)) for k in range(1, nz)]
        self.moves += [((0, 0, 0), (0, 1, 0)), ((0, 0, 0), (0, 0, 1))]
        for k in range(1, nz):
            self.moves += [((k, 0, 0), (k, 1, 0)), ((k, 0, 0), (k, 0, 1))]
        self.moves += [((k, 1, 0), (k, 1, 1)) for k in range(nz)]

    def place(self, k, first, second):
        fy, fx = (first, second) if self.order == 0 else (second, first)
        y = 1 - self.y if fy else self.y
        x = 1 - self.x if fx else self.x
        return self.window(lax.rem(self.z + self.nz - k, self.nz) * 2 + y, x)

    def copy(self, index):
        here, there = self.moves[index]
        if here[0] != there[0]:
            target = {"dp": lax.rem(self.z + there[0], self.nz) * 2 + self.y}
        elif (here[1] != there[1]) == (self.order == 0):
            target = {"dp": self.z * 2 + 1 - self.y}
        else:
            target = {"x": 1 - self.x}
        k, first, second = there
        return copy_to(
            self.own if here == (0, 0, 0) else self.place(*here),
            self.place(*here),
            self.send_sems.at[index],
            self.recv_sems.at[k + self.nz * (first + 2 * second)],
            target,
        )

    def arrived(self, k, first, second):
        at = self.place(k, first, second)
        sem = self.recv_sems.at[k + self.nz * (first + 2 * second)]
        copy_to(at, at, self.send_sems.at[0], sem, {"x": 1 - self.x}).wait_recv()

    def begin(self):
        for index in range(self.nz + 1):
            self.copy(index).start()

    def relay_z(self, k):
        self.arrived(k, 0, 0)
        for index in range(2):
            self.copy(self.nz + 1 + 2 * (k - 1) + index).start()

    def relay_first(self, k):
        self.arrived(k, 1, 0)
        self.copy(3 * self.nz - 1 + k).start()

    def finish(self):
        for k in range(self.nz):
            self.arrived(k, 0, 1)
            self.arrived(k, 1, 1)
        for index in range(len(self.moves)):
            self.copy(index).wait_send()


CHUNKS = 4


class Deal:
    def __init__(self, nd, spans, table, rows, out, tok, send, recv, other, sems):
        self.nd, self.spans, self.table, self.rows, self.out = nd, spans, table, rows, out
        self.tok, self.sent, self.recv, self.other = tok, send, recv, other
        self.load_sem, self.a2a_send, self.a2a_recv, self.x_send, self.x_recv, self.c_send, self.c_recv = sems
        self.dp, self.x, self.core = lax.axis_index("dp"), lax.axis_index("x"), lax.axis_index("core")
        self.quarter = out.shape[1] // 4
        self.cap = send.shape[1]
        self.mine = pl.multiple_of((2 * self.x + self.core) * self.quarter, 128)
        self.theirs = pl.multiple_of((2 * (1 - self.x) + self.core) * self.quarter, 128)
        self.load = pltpu.make_async_copy(rows.at[:, :, pl.ds(self.mine, self.quarter)], tok, self.load_sem.at[0])
        self.started = []

    def begin(self):
        self.load.start()

    def exchange(self):
        self.load.wait()
        cap, nd = self.cap, self.nd

        def pick(k, out, base):
            d = lax.rem(self.dp + k, nd)
            for j in range(cap):
                out[base + j] = self.tok[self.table[d * cap + j]]

        here = self.dp * cap
        for k in range(1, nd):
            pick(k, self.sent.at[k], 0)
            copy = copy_to(
                self.sent.at[k],
                self.recv.at[pl.ds(here, cap)],
                self.a2a_send.at[k],
                self.a2a_recv.at[k],
                {"dp": lax.rem(self.dp + k, nd)},
            )
            copy.start()
            self.started.append(copy)
        pick(0, self.recv, here)

    def across(self):
        for copy in self.started:
            copy.wait_recv()
        spans, nd = self.spans, self.nd
        count = spans // CHUNKS
        first = nd * self.cap
        self.x_copies, self.c_copies = [], []
        for c in range(CHUNKS):
            rows = pl.ds(c * count * SPAN, count * SPAN)

            def body(i, _, c=c):
                at = c * count + i
                to = pl.ds(pl.multiple_of(at * SPAN, SPAN), SPAN)
                self.other[to, :] = self.recv[self.table[first + spans + at]]
                return 0

            lax.fori_loop(0, count, body, 0)
            copy = copy_to(
                self.other.at[rows, :],
                self.out.at[rows, pl.ds(self.mine, self.quarter)],
                self.x_send.at[c],
                self.x_recv.at[c],
                {"x": 1 - self.x},
            )
            copy.start()
            self.x_copies.append(copy)

        def body(i, _):
            to = pl.ds(pl.multiple_of(i * SPAN, SPAN), SPAN)
            self.out[to, pl.ds(self.mine, self.quarter)] = self.recv[self.table[first + i]]
            return 0

        lax.fori_loop(0, spans, body, 0)
        self.pass_on(slice(None), self.mine, CHUNKS)

    def pass_on(self, rows, col, sem):
        at = self.out.at[rows, pl.ds(col, self.quarter)]
        copy = copy_to(at, at, self.c_send.at[sem], self.c_recv.at[sem], {"core": 1 - self.core})
        copy.start()
        self.c_copies.append(copy)

    def finish(self):
        count = self.spans // CHUNKS
        for c, copy in enumerate(self.x_copies):
            copy.wait_recv()
            self.pass_on(pl.ds(c * count * SPAN, count * SPAN), self.theirs, c)
        for copy in self.c_copies:
            copy.wait_recv()
        for copy in self.x_copies + self.c_copies:
            copy.wait_send()

    def release(self):
        for copy in self.started:
            copy.wait_send()


def deal_buffers(nd, per_dev, spans, quarter, cap):
    return [
        pltpu.VMEM((per_dev, SPAN, quarter), BF),
        pltpu.VMEM((nd, cap, SPAN, quarter), BF),
        pltpu.VMEM((spans * SPAN, quarter), BF),
        pltpu.VMEM((nd * cap, SPAN, quarter), BF),
        pltpu.VMEM((nd * cap, SPAN, quarter), BF),
    ]


def deal_sems(nd):
    dma = pltpu.SemaphoreType.DMA
    return [dma((1,)), dma((nd,)), dma((nd,)), dma((CHUNKS,)), dma((CHUNKS,)), dma((CHUNKS + 1,)), dma((CHUNKS + 1,))]


SMALL = 184


class Small:
    def __init__(self, nd, pack, sent, got, norms, sems):
        self.nd, self.pack, self.sent, self.got, self.norms = nd, pack, sent, got, norms
        self.send, self.recv, self.norm_send, self.norm_recv, self.end_send, self.end_recv = sems
        self.dp, self.x, self.core = lax.axis_index("dp"), lax.axis_index("x"), lax.axis_index("core")

    def fill(self, gain_first, gain_second, down, up, bias, head):
        pack = self.pack
        for r in range(8):
            lanes = slice(r * 128, (r + 1) * 128)
            pack[r : r + 1] = gain_first[0:1, lanes]
            pack[8 + r : 9 + r] = gain_second[0:1, lanes]
            pack[16 + 16 * r : 32 + 16 * r] = down[:, lanes]
        for h in range(2):
            lanes = slice(h * 128, (h + 1) * 128)
            pack[144 + 16 * h : 160 + 16 * h] = up[:, lanes]
            pack[176 + h : 177 + h] = bias[0:1, lanes]
            pack[178 + h : 179 + h] = head[0:1, lanes]
        pack[180:] = jnp.zeros((4, 128), F32)

    def copy(self, step):
        if step == 0:
            target = {"x": 1 - self.x}
        else:
            bit = 1 << (step - 1)
            on = lax.rem(self.dp // bit, 2)
            target = {"dp": self.dp + bit - 2 * bit * on}
        return copy_to(self.sent.at[step], self.got.at[step], self.send.at[step], self.recv.at[step], target)

    def steps(self):
        return self.nd.bit_length()

    def begin(self, step):
        self.sent[step] = self.pack[...]
        self.copy(step).start()

    def end(self, step):
        self.copy(step).wait()
        self.pack[...] = self.pack[...] + self.got[step]

    def core_copy(self, step, src, dst, target):
        return copy_to(src, dst, self.end_send.at[step], self.end_recv.at[step], target)

    def head(self):
        at = self.nd + 5
        return self.core_copy(0, self.norms.at[at], self.norms.at[at + 1], {"core": 1 - self.core})

    def begin_head(self):
        self.norms[self.nd + 5] = self.pack[176:184]
        self.head().start()

    def end_head(self):
        self.head().wait()
        self.pack[178:180] = self.pack[178:180] + self.norms[self.nd + 6, 2:4]

    def squares(self):
        nd, v = self.nd, self.pack[...]
        v = v * v
        down = fold(v[16:144])
        up = fold(v[144:176])
        row = lax.broadcasted_iota(jnp.int32, (8, 128), 0)
        tail = v[176:184]
        tail = jnp.where(row < 2, tail / (2 * nd), jnp.where(row < 4, tail / (4 * nd), 0.0))
        return (v[0:8] + v[8:16] + down) / (4 * nd) + up / (2 * nd) + tail

    def norm_copy(self, k):
        return copy_to(
            self.norms.at[self.nd],
            self.norms.at[self.dp],
            self.norm_send.at[k],
            self.norm_recv.at[k],
            {"dp": lax.rem(self.dp + k, self.nd)},
        )

    def begin_norm(self, value):
        self.norms[self.nd] = value
        self.norms[self.dp] = value
        for k in range(1, self.nd):
            self.norm_copy(k).start()

    def end_norm(self, out):
        nd = self.nd
        for k in range(1, nd):
            self.norm_copy(k).wait()
        total = self.norms[0]
        for k in range(1, nd):
            total = total + self.norms[k]
        for step, target in ((1, {"x": 1 - self.x}), (2, {"core": 1 - self.core})):
            at = nd - 1 + 2 * step
            self.norms[at] = total
            copy = self.core_copy(step, self.norms.at[at], self.norms.at[at + 1], target)
            copy.start()
            copy.wait()
            total = total + self.norms[at + 1]
        out[...] = total


def small_scratch(nd):
    dma = pltpu.SemaphoreType.DMA
    steps = nd.bit_length()
    return [
        pltpu.VMEM((steps, SMALL, 128), F32), pltpu.VMEM((steps, SMALL, 128), F32), pltpu.VMEM((nd + 7, 8, 128), F32),
        dma((steps,)), dma((steps,)), dma((nd,)), dma((nd,)), dma((3,)), dma((3,)),
    ]


PIECES = 5


def fetch(pairs, sems):
    copies = [pltpu.make_async_copy(src, dst, sems.at[k]) for k, (src, dst) in enumerate(pairs)]
    for copy in copies:
        copy.start()
    return copies


class Undeal:
    def __init__(self, nd, spans, table, own, cross, joined, sent, gath, sems):
        self.nd, self.spans, self.table, self.own, self.cross = nd, spans, table, own, cross
        self.joined, self.sent, self.gath = joined, sent, gath
        self.x_send, self.x_recv, self.a2a_send, self.a2a_recv, *self.wide_sems = sems
        self.dp, self.x, self.core = lax.axis_index("dp"), lax.axis_index("x"), lax.axis_index("core")
        self.cap = sent.shape[1]
        self.quarter = own.shape[2]
        self.wide = gath.shape[2] != self.quarter
        self.mine, self.theirs = 0, 0
        if self.wide:
            self.mine = pl.multiple_of((2 * self.x + self.core) * self.quarter, 128)
            self.theirs = pl.multiple_of((2 * (1 - self.x) + self.core) * self.quarter, 128)

    def swap(self, i):
        count = self.spans // PIECES
        return copy_to(
            self.cross.at[pl.ds(i * count, count)],
            self.joined.at[pl.ds(self.x * self.spans + i * count, count)],
            self.x_send.at[i],
            self.x_recv.at[i],
            {"x": 1 - self.x},
        )

    def begin(self):

        def body(i, _):
            self.joined[self.x * self.spans + i] = self.own[i]
            return 0

        lax.fori_loop(0, self.spans, body, 0)

    def block(self, dp, col):
        return self.gath.at[pl.ds(dp * self.cap, self.cap), :, pl.ds(col, self.quarter)]

    def a2a(self, k):
        return copy_to(
            self.sent.at[k],
            self.block(self.dp, self.mine),
            self.a2a_send.at[k],
            self.a2a_recv.at[k],
            {"dp": lax.rem(self.dp + k, self.nd)},
        )

    def exchange(self):
        for i in range(PIECES):
            self.swap(i).wait_recv()
        cap = self.cap
        for k in range(1, self.nd):
            d = lax.rem(self.dp + k, self.nd)
            for j in range(cap):
                self.sent[k, j] = self.joined[self.table[d * cap + j]]
            self.a2a(k).start()
        here = self.block(self.dp, self.mine)
        for j in range(cap):
            here[j] = self.joined[self.table[self.dp * cap + j]]
        if self.wide:
            self.widen(0, 0).start()
            self.widen(0, 1).start()

    def widen(self, k, step):
        at = self.block(lax.rem(self.dp + self.nd - k, self.nd), self.theirs if step == 2 else self.mine)
        send, recv = self.wide_sems
        return copy_to(
            at, at, send.at[3 * k + step], recv.at[3 * k + step],
            {"x": 1 - self.x} if step == 0 else {"core": 1 - self.core},
        )

    def arrive(self, k):
        self.a2a(k).wait_recv()
        if self.wide:
            self.widen(k, 0).start()
            self.widen(k, 1).start()

    def finish(self):
        if self.wide:
            for k in range(self.nd):
                self.widen(k, 0).wait_recv()
                self.widen(k, 2).start()
            for k in range(self.nd):
                self.widen(k, 1).wait_recv()
                self.widen(k, 2).wait_recv()
                for step in range(3):
                    self.widen(k, step).wait_send()
        for k in range(1, self.nd):
            self.a2a(k).wait_send()
        for i in range(PIECES):
            self.swap(i).wait_send()


def undeal_scratch(nd, per_dev, spans, quarter, cap, wide):
    dma = pltpu.SemaphoreType.DMA
    buffers = [
        pltpu.VMEM((spans, SPAN, quarter), BF),
        pltpu.VMEM((spans, SPAN, quarter), BF),
        pltpu.VMEM((per_dev, SPAN, quarter), BF),
        pltpu.VMEM((nd, cap, SPAN, quarter), BF),
        pltpu.VMEM((nd * cap, SPAN, quarter * (4 if wide else 1)), BF),
    ]
    sems = [dma((PIECES,)), dma((PIECES,)), dma((nd,)), dma((nd,))]
    return buffers, sems + ([dma((3 * nd,)), dma((3 * nd,))] if wide else [])


def fold(value):
    return jnp.sum(value.reshape(-1, 8, 128), axis=0)


class Collapse:
    def __init__(self, nd, order, acc, pitch, low, rows, got, sems):
        self.nz, self.order, self.acc, self.pitch, self.low, self.rows = nd // 2, order, acc, pitch, low, rows
        self.got = got
        self.send_sems, self.recv_sems = sems
        self.w = got.shape[2]
        dp, self.x = lax.axis_index("dp"), lax.axis_index("x")
        self.z, self.y = dp // 2, lax.rem(dp, 2)

    def window(self, first, second, kz):
        fx, fy = (first, second) if self.order == 0 else (second, first)
        y = 1 - self.y if fy else self.y
        x = 1 - self.x if fx else self.x
        dp = lax.rem(self.z + kz, self.nz) * 2 + y
        return self.acc.at[
            pl.ds(pl.multiple_of(x * self.pitch + self.low, 16), self.rows),
            pl.ds(pl.multiple_of(dp * self.w, 128), self.w),
        ]

    def partner(self, which):
        if (which == 0) == (self.order == 0):
            return {"x": 1 - self.x}
        return {"dp": self.z * 2 + 1 - self.y}

    def slot(self, phase, second, kz):
        nz = self.nz
        return second * nz + kz if phase == 1 else (2 * nz + kz if phase == 2 else 3 * nz + kz - 1)

    def copy(self, phase, second, kz):
        at = self.slot(phase, second, kz)
        if phase == 1:
            src, target = self.window(1, second, kz), self.partner(0)
        elif phase == 2:
            src, target = self.window(0, 1, kz), self.partner(1)
        else:
            src, target = self.window(0, 0, kz), {"dp": lax.rem(self.z + kz, self.nz) * 2 + self.y}
        return copy_to(src, self.got.at[at], self.send_sems.at[at], self.recv_sems.at[at], target)

    def add(self, second, kz, at):
        here = self.window(0, second, kz)
        here[...] = (here[...].astype(F32) + self.got[at].astype(F32)).astype(BF)

    def begin(self):
        for second in (1, 0):
            for kz in range(self.nz):
                self.copy(1, second, (kz + 1) % self.nz).start()

    def second(self, kz):
        self.copy(1, 1, kz).wait_recv()
        self.add(1, kz, self.slot(1, 1, kz))
        self.copy(2, 1, kz).start()

    def third(self, kz):
        self.copy(1, 0, kz).wait_recv()
        self.add(0, kz, self.slot(1, 0, kz))
        self.copy(2, 1, kz).wait_recv()
        self.add(0, kz, self.slot(2, 1, kz))
        if kz:
            self.copy(3, 0, kz).start()

    def finish(self, out, squares):
        total = self.window(0, 0, 0)[...].astype(F32)
        for kz in range(1, self.nz):
            self.copy(3, 0, kz).wait_recv()
            total = total + self.got[self.slot(3, 0, kz)].astype(F32)
        out[...] = total
        squares[...] += fold(total * total)
        for kz in range(self.nz):
            self.copy(1, 0, kz).wait_send()
            self.copy(1, 1, kz).wait_send()
            self.copy(2, 1, kz).wait_send()
            if kz:
                self.copy(3, 0, kz).wait_send()


def collapse_scratch(nd, rows, w):
    count = 4 * (nd // 2) - 1
    dma = pltpu.SemaphoreType.DMA
    return [pltpu.VMEM((count, rows, w), BF), dma((count,)), dma((count,))]


def progress(chains, nz, between=()):
    between = list(between)
    for kz in [k % nz for k in range(1, nz + 1)]:
        for chain in chains:
            chain.second(kz)
        if between:
            between.pop(0)()
    for kz in [k % nz for k in range(1, nz + 1)]:
        for chain in chains:
            chain.third(kz)
        if between:
            between.pop(0)()
    for work in between:
        work()


PROJ_ROWS = 16 + HEAD + DV
PROJ_CUTS = ((0, 528), (528, 512))


def forward_kernel(nd, spans, reach, gather, table, ints, tokens, cotangent, shard_p, shard_f, gain, up, bias, head_gain,
                   ups, level, *rest):
    outs, rest = rest[:13], rest[13:]
    (src_o, cot_o, wp_o, wf_o, normed_o, qkvg_o, log_decay_o, rank_o, mixed_o, gated_o, attn_o, before_o, attn_other) = outs
    (src, cot, wp, wf, normed, qkvg, log_decay, rank, mixed, gated, attn, before), rest = rest[:12], rest[12:]
    (packet, factors, sent_packets, got_packets), rest = rest[:4], rest[4:]
    (tok, sent, other, recv_t, recv_c), rest = rest[:5], rest[5:]
    sems_t, sems_c, rest = rest[:7], rest[7:14], rest[14:]
    carry_send, carry_recv, core_send, core_recv, out_sems, own_sems, *ag_sems = rest
    tiles = spans * SPAN // TILE
    carry = Carry(nd, reach, 1, packet, sent_packets, got_packets, carry_send, carry_recv)
    enter(nd, carry.shifts())
    deal = Deal(nd, spans, table, tokens, src, tok, sent, recv_t, other, sems_t)
    deal_c = Deal(nd, spans, table, cotangent, cot, tok, sent, recv_c, other, sems_c)
    deal.begin()
    local = []
    spreads_p, spreads_f = [], []
    if gather:
        w = shard_p.shape[1]
        f3 = shard_f.shape[0]
        f = f3 // 3
        cuts_p = [(k, low, count, PROJ_ROWS, low) for k, (low, count) in enumerate(PROJ_CUTS)]
        cuts_f = [
            (0, 0, f, f, 0), (1, 2 * f, f, f, 4 * f), (0, f, f // 2, f, 2 * f), (1, f + f // 2, f // 2, f, 2 * f + f // 2),
        ]

        def window(buffer, count, pitch, base, dp, x):
            return buffer.at[
                pl.ds(pl.multiple_of(x * pitch + base, 16), count), pl.ds(pl.multiple_of(dp * w, 128), w)
            ]

        for shard, buffer, cuts, spreads in ((shard_p, wp, cuts_p, spreads_p), (shard_f, wf, cuts_f, spreads_f)):
            for order, low, count, pitch, base in cuts:
                piece = shard.at[pl.ds(low, count), :]
                place = functools.partial(window, buffer, count, pitch, base)
                copy = pltpu.make_async_copy(
                    piece, place(lax.axis_index("dp"), lax.axis_index("x")), own_sems.at[len(local)]
                )
                copy.start()
                local.append(copy)
                k = 2 * (len(local) - 1)
                spreads.append(Spread(nd, order, piece, place, ag_sems[k], ag_sems[k + 1]))
    else:
        for shard, buffer in ((shard_p, wp), (shard_f, wf)):
            local.append(pltpu.make_async_copy(shard, buffer, own_sems.at[len(local)]))
            local[-1].start()
    outgoing = []

    def store(value, out):
        outgoing.append(pltpu.make_async_copy(value, out, out_sems.at[len(outgoing)]))
        outgoing[-1].start()

    def relay_z(spreads, k):
        for spread in spreads:
            spread.relay_z(k)

    def relay_first(spreads, k):
        for spread in spreads:
            spread.relay_first(k)

    nz = nd // 2
    last_z = range(1, nz) if gather else ()
    last_first = range(nz) if gather else ()
    for spread in spreads_p:
        spread.begin()
    deal.exchange()
    for k in last_first[0:1]:
        relay_first(spreads_p, k)
    deal_c.begin()
    for k in last_z[0:1]:
        relay_z(spreads_p, k)
    for k in last_z[1:2]:
        relay_z(spreads_p, k)
    for k in last_first[1:2]:
        relay_first(spreads_p, k)
    for spread in spreads_f:
        spread.begin()
    for k in last_z[2:3]:
        relay_z(spreads_p, k)
    for k in last_first[2:3]:
        relay_first(spreads_p, k)
    for k in last_first[3:4]:
        relay_first(spreads_p, k)
    for k in last_first[0:1]:
        relay_first(spreads_f, k)
    deal.across()
    deal.release()
    deal_c.exchange()
    for k in last_z[0:1]:
        relay_z(spreads_f, k)
    for k in last_first[1:2]:
        relay_first(spreads_f, k)
    deal.finish()
    for k in last_z[1:2]:
        relay_z(spreads_f, k)
    for spread in spreads_p:
        spread.finish()
    for copy in local:
        copy.wait()
    store(src, src_o)
    store(wp, wp_o)

    def at(ref, i):
        return ref.at[pl.ds(pl.multiple_of(i * TILE, TILE), TILE), :]

    packet[...] = jnp.zeros_like(packet)
    packet[2 * DV : 2 * DV + 2] = jnp.ones((2, DK), F32)

    def project(i, _):
        project_kernel(
            i, ints, at(src, i), gain, wp, up, bias, ups,
            at(normed, i), at(qkvg, i), at(log_decay, i), at(rank, i), packet,
        )
        return 0

    lax.fori_loop(0, tiles // 2, project, 0)
    for k in last_z[2:3]:
        relay_z(spreads_f, k)
    for k in last_first[2:3]:
        relay_first(spreads_f, k)
    lax.fori_loop(tiles // 2, tiles, project, 0)
    factors[...] = packet[2 * DV :]
    carry.send(0)
    store(normed, normed_o)
    store(qkvg, qkvg_o)
    store(log_decay, log_decay_o)
    store(rank, rank_o)
    for k in last_first[3:4]:
        relay_first(spreads_f, k)

    def within(i, _):
        within_kernel(at(qkvg, i), at(log_decay, i), ups, level, at(mixed, i))
        return 0

    stages = carry.run()
    for stage in range(stages):
        lax.fori_loop(tiles * stage // stages, tiles * (stage + 1) // stages, within, 0)
        carry.step(stage)
    deal_c.across()
    per_tile = TILE // SPAN

    def mix(i, _):
        mix_kernel(
            i, ints, at(qkvg, i), at(log_decay, i), packet, ups, head_gain, wp,
            at(mixed, i), at(gated, i), at(attn, i), before.at[pl.ds(i * per_tile, per_tile)],
        )
        return 0

    lax.fori_loop(0, tiles, mix, 0)
    swap_attn = copy_to(
        attn, attn_other, core_send.at[0], core_recv.at[0], {"core": 1 - lax.axis_index("core")}
    )
    swap_attn.start()
    store(mixed, mixed_o)
    store(gated, gated_o)
    store(attn, attn_o)
    store(before, before_o)
    deal_c.finish()
    store(cot, cot_o)
    for spread in spreads_f:
        spread.finish()
    store(wf, wf_o)
    deal_c.release()
    swap_attn.wait()
    for copy in outgoing:
        copy.wait()


def forward(table, ints, tokens, cotangent, shard_p, shard_f, gain, up, bias, head_gain, ups, level, nd, spans, reach, gather):
    d = tokens.shape[1]
    per_dev = tokens.shape[0] // SPAN
    cap = -(-per_dev // nd)
    rows = spans * SPAN
    dma = pltpu.SemaphoreType.DMA
    nz = nd // 2
    wf_rows = shard_f.shape[0] * (2 if gather else 1)
    kept = [
        ((rows, d), BF), ((rows, d), BF), ((2 * PROJ_ROWS, d), BF), ((wf_rows, d), BF), ((rows, d), BF),
        ((rows, 2 * HEAD), BF), ((rows, 2 * DK), F32), ((rows, 16), BF), ((rows, 2 * DV), F32), ((rows, 2 * DV), BF),
        ((rows, d), BF), ((spans, 2, DV, DK), BF),
    ]
    widths, _ = carry_widths(reach)
    steps = len(widths) + 2
    scratch = [pltpu.VMEM(shape, dtype) for shape, dtype in kept]
    scratch += [
        pltpu.VMEM((2 * DV + 16, DK), F32),
        pltpu.VMEM((steps - 1, 2 * DV + 16, DK), BF),
        pltpu.VMEM((steps, 2 * DV + 16, DK), BF),
    ]
    scratch += deal_buffers(nd, per_dev, spans, d // 4, cap) + deal_sems(nd) + deal_sems(nd)
    scratch += [dma((steps,)), dma((steps,)), dma((1,)), dma((1,)), dma((12,)), dma((6,))]
    if gather:
        scratch += [dma((4 * nz - 1,)), dma((4 * nz,))] * 6
    outs = [sds(*shape, dtype=dtype) for shape, dtype in kept] + [sds(rows, d, dtype=BF)]
    outs.append(sds(16, DK))
    specs = [ANY] * 13 + [VMEM]

    def kernel(*refs):
        n_in = 12
        ins, rest = refs[:n_in], refs[n_in:]
        results, factors, buffers = rest[:13], rest[13], rest[14:]
        forward_kernel(
            nd, spans, reach, gather, *ins, *results, *buffers[:12], buffers[12], factors, *buffers[13:]
        )

    return pl.pallas_call(
        kernel,
        in_specs=[SMEM, SMEM, ANY, ANY, ANY, ANY] + [VMEM] * 6,
        out_specs=specs,
        out_shape=outs,
        scratch_shapes=scratch,
        name="forward",
        compiler_params=pltpu.CompilerParams(
            vmem_limit_bytes=VMEM_LIMIT, collective_id=0, has_side_effects=True
        ),
        cost_estimate=cost(150),
    )(
        table, ints, tokens.reshape(per_dev, SPAN, d), cotangent.reshape(per_dev, SPAN, d), shard_p, shard_f,
        gain, up, bias, head_gain, ups, level,
    )


def rms_scale(x):
    return lax.rsqrt(jnp.mean(x * x, axis=-1, keepdims=True) + norm_eps)


def distances(ups, log_decay):
    high = log_decay.astype(BF)
    lower = (log_decay - high.astype(F32)).astype(BF)
    return dot(ups, high) + dot(ups, lower)


def head_cols(h, part):
    start = h * HEAD + (0, DK, 2 * DK, 2 * DK + DV)[part]
    return slice(start, start + (DK, DK, DV, DV)[part])


def in_rows(h):
    return slice(h * PROJ_ROWS + 16, h * PROJ_ROWS + 16 + HEAD)


def out_rows(h):
    return slice(h * PROJ_ROWS + 16 + HEAD, (h + 1) * PROJ_ROWS)


def log_sigmoid(v):
    return jnp.minimum(v, 0.0) - jnp.log(1.0 + jnp.exp(-jnp.abs(v)))


def project_kernel(
    step, ints, src, gain, weights, up, bias, ups,
    normed, qkvg, log_decay, rank, packet,
):
    x = src[...].astype(F32)
    nf = (x * rms_scale(x) * gain[...]).astype(BF)
    normed[...] = nf
    low = dot(nf, weights[0:16, :], 1, 1).astype(BF)
    rank[...] = low
    logits = dot(low, up[...]) + bias[...]
    ld = log_sigmoid(logits) * (1.0 / decay_scale)
    log_decay[...] = ld
    towards = jnp.exp(distances(ups[LEVELS + 1], ld))
    per_tile = TILE // SPAN
    for h in range(2):
        proj = dot(nf, weights[in_rows(h), :], 1, 1)
        qkvg[:, head_cols(h, 0)] = (proj[:, :DK] * scaling).astype(BF)
        qkvg[:, h * HEAD + DK : (h + 1) * HEAD] = proj[:, DK:].astype(BF)
    for j in range(per_tile):
        rows = slice(j * SPAN, (j + 1) * SPAN)
        keep = ints[step * per_tile + j].astype(F32)
        total = jnp.exp(jnp.sum(ld[rows], axis=0, keepdims=True)) * keep
        for h in range(2):
            lanes = slice(h * DK, (h + 1) * DK)
            states = slice(h * DV, (h + 1) * DV)
            f = slice(2 * DV + h, 2 * DV + h + 1)
            packet[f] = packet[f] * total[:, lanes]
            kd = (qkvg[rows, head_cols(h, 1)].astype(F32) * towards[rows, lanes]).astype(BF)
            packet[states] = packet[states] * total[:, lanes] + dot(qkvg[rows, head_cols(h, 2)], kd, 0, 0)


def within_kernel(qkvg, log_decay, ups, level, within):
    ld = log_decay[...]
    high = ld.astype(BF)
    lower = (ld - high.astype(F32)).astype(BF)
    lev = level[...]
    scores = [None, None]
    for l in range(LEVELS + 1):
        if l < LEVELS:
            x = jnp.exp(dot(ups[l], high) + dot(ups[l], lower))
        for h in range(2):
            q, k = qkvg[:, head_cols(h, 0)], qkvg[:, head_cols(h, 1)]
            if l < LEVELS:
                xh = x[:, h * DK : (h + 1) * DK]
                q = (q.astype(F32) * xh).astype(BF)
                k = (k.astype(F32) * xh).astype(BF)
            s = dot(q, k, 1, 1)
            scores[h] = jnp.where(lev == l, s, 0.0 if l == 0 else scores[h])
    for h in range(2):
        within[:, h * DV : (h + 1) * DV] = dot(scores[h].astype(BF), qkvg[:, head_cols(h, 2)])


def mix_kernel(
    step, ints, qkvg, log_decay, packet, ups, head_gain, weights,
    mixed, gated, attn, before,
):
    per_tile = TILE // SPAN
    ld = log_decay[...]
    since = jnp.exp(distances(ups[LEVELS], ld))
    towards = jnp.exp(distances(ups[LEVELS + 1], ld))
    for j in range(per_tile):
        rows = slice(j * SPAN, (j + 1) * SPAN)
        keep = ints[step * per_tile + j].astype(F32)
        for h in range(2):
            lanes = slice(h * DK, (h + 1) * DK)
            values = slice(h * DV, (h + 1) * DV)
            prev = packet[values] * keep
            prev_low = prev.astype(BF)
            before[j, h] = prev_low
            qd = (qkvg[rows, head_cols(h, 0)].astype(F32) * since[rows, lanes]).astype(BF)
            kd = (qkvg[rows, head_cols(h, 1)].astype(F32) * towards[rows, lanes]).astype(BF)
            mixed[rows, values] = mixed[rows, values] + dot(qd, prev_low, 1, 1)
            last = since[j * SPAN + SPAN - 1 : j * SPAN + SPAN, lanes]
            packet[values] = prev * last + dot(qkvg[rows, head_cols(h, 2)], kd, 0, 0)
    for h in range(2):
        values = slice(h * DV, (h + 1) * DV)
        m = mixed[:, values]
        g = qkvg[:, head_cols(h, 3)].astype(F32)
        y = m * rms_scale(m) * head_gain[...] * g * jax.nn.sigmoid(g)
        gated[:, values] = y.astype(BF)
    attn[...] = (
        dot(gated[:, :DV], weights[out_rows(0), :]) + dot(gated[:, DV:], weights[out_rows(1), :])
    ).astype(BF)


def ffn_kernel(
    ints, src, attn_a, attn_b, cot, gain, weights,
    hidden, normed, act, grad_gu, keep_out, send_out, grad_second,
    part,
):
    quarter = cot.shape[1] // 4
    hid = src[...].astype(F32) + (attn_a[...].astype(F32) + attn_b[...].astype(F32))
    hidden[...] = hid
    ns = (hid * rms_scale(hid) * gain[...]).astype(BF)
    normed[...] = ns
    f = act.shape[1]
    w_gate, w_out, w_up = (slice(k * f, (k + 1) * f) for k in range(3))
    gate = dot(ns, weights[w_gate, :], 1, 1)
    upper = dot(ns, weights[w_up, :], 1, 1)
    sig = jax.nn.sigmoid(gate)
    swish = gate * sig
    low = (swish * upper).astype(BF)
    act[...] = low
    ga = dot(cot[...], weights[w_out, :], 1, 1)
    part[...] = dot(low, weights[w_out, :]).astype(BF)
    gg = (ga * upper * sig * (1.0 + gate * (1.0 - sig))).astype(BF)
    gu = (ga * swish).astype(BF)
    grad_gu[:, :f] = gg
    grad_gu[:, f:] = gu
    grad_second[...] = (dot(gg, weights[w_gate, :]) + dot(gu, weights[w_up, :])).astype(BF)
    core = ints[4]
    for h in range(2):
        mine = pl.multiple_of((2 * h + core) * quarter, 128)
        theirs = pl.multiple_of((2 * h + 1 - core) * quarter, 128)
        keep_out[:, h * quarter : (h + 1) * quarter] = part[:, pl.ds(mine, quarter)]
        send_out[:, h * quarter : (h + 1) * quarter] = part[:, pl.ds(theirs, quarter)]


def weight_grad_into(acc, lhs, rhs, first=0, count=None):
    def body(i, _):
        at = pl.multiple_of(i * 128, 128)
        acc[pl.ds(at, 128), :] = dot(lhs[:, pl.ds(at, 128)], rhs[...], 0, 0).astype(BF)
        return 0

    last = acc.shape[0] // 128 if count is None else first + count
    lax.fori_loop(first, last, body, 0)


def out_back_kernel(
    n, ints, hidden, cot, gs_a, gs_b, gain, weights, gated, mixed, qkvg, log_decay, head_gain, ups,
    keep_out, recv_out,
    grad_hidden, grad_mixed, grad_gate, gain_grad, head_grad, packet, out_own, out_cross, *rest,
):
    w_grads, (acc, state, gain_sum, head_sum) = rest[:-4], rest[-4:]
    step = pl.program_id(0)
    tile = n - 1 - step
    per_tile = TILE // SPAN

    @pl.when(step == 0)
    def _():
        acc[...] = jnp.zeros_like(acc)
        state[...] = jnp.zeros_like(state)
        gain_sum[...] = jnp.zeros_like(gain_sum)
        head_sum[...] = jnp.zeros_like(head_sum)

    x, core = ints[7], ints[4]
    quarter = out_own.shape[1]
    for target, half in ((out_own, x), (out_cross, 1 - x)):
        at = pl.multiple_of((2 * half + core) * quarter, 128)
        pair = pl.multiple_of(half * quarter, 128)
        share = keep_out[:, pl.ds(pair, quarter)].astype(F32) + recv_out[:, pl.ds(pair, quarter)].astype(F32)
        target[...] = (hidden[:, pl.ds(at, quarter)] + share).astype(BF)
    gs = gs_a[...].astype(F32) + gs_b[...].astype(F32)
    hid = hidden[...]
    inv = rms_scale(hid)
    normal = hid * inv
    gain_sum[0:1, :] += jnp.sum(gs * normal, axis=0, keepdims=True)
    e = gs * gain[...]
    gh = cot[...].astype(F32) + inv * (e - normal * jnp.mean(e * normal, axis=-1, keepdims=True))
    grad_hidden[...] = gh
    low = gh.astype(BF)
    acc[...] += dot(gated[...], low, 0, 0)
    for h in range(2):
        values = slice(h * DV, (h + 1) * DV)
        m = mixed[:, values]
        inv_head = rms_scale(m)
        nh = m * inv_head
        g = qkvg[:, head_cols(h, 3)].astype(F32)
        sig = jax.nn.sigmoid(g)
        w = g * sig
        gd = dot(low, weights[out_rows(h), :], 1, 1)
        head_sum[0:1, :] += jnp.sum(gd * nh * w, axis=0, keepdims=True)
        gn = gd * head_gain[...]
        grad_gate[:, values] = (gn * nh * sig * (1.0 + g * (1.0 - sig))).astype(BF)
        gn = gn * w
        gm = inv_head * (gn - nh * jnp.mean(gn * nh, axis=-1, keepdims=True))
        grad_mixed[:, values] = gm.astype(BF)
    since = jnp.exp(distances(ups[LEVELS], log_decay[...]))
    for j in reversed(range(per_tile)):
        rows = slice(j * SPAN, (j + 1) * SPAN)
        keep = ints[8 + tile * per_tile + j].astype(F32)
        for h in range(2):
            lanes = slice(h * DK, (h + 1) * DK)
            values = slice(h * DV, (h + 1) * DV)
            qd = (qkvg[rows, head_cols(h, 0)].astype(F32) * since[rows, lanes]).astype(BF)
            last = since[j * SPAN + SPAN - 1 : j * SPAN + SPAN, lanes]
            state[h] = keep * (state[h] * last + dot(grad_mixed[rows, values], qd, 0, 0))

    @pl.when(step == n - 1)
    def _():
        packet[0:DV] = state[0]
        packet[DV : 2 * DV] = state[1]
        gain_grad[...] = gain_sum[...]
        head_grad[...] = head_sum[...]
        w_grads[0][...] = acc[...].astype(BF)


def within_back_kernel(qkvg, log_decay, grad_mixed, ups, downs, level, level_t, grad_qk, grad_v, grad_ld):
    ld = log_decay[...]
    high = ld.astype(BF)
    lower = (ld - high.astype(F32)).astype(BF)
    lev, lev_t = level[...], level_t[...]
    gd, gd_t = [], []
    for h in range(2):
        v, gm = qkvg[:, head_cols(h, 2)], grad_mixed[:, h * DV : (h + 1) * DV]
        gd.append(dot(gm, v, 1, 1))
        gd_t.append(dot(v, gm, 1, 1))
    scores_t = [None, None]
    grad_q, grad_k = [None, None], [None, None]
    for l in range(LEVELS + 1):
        if l < LEVELS:
            x = jnp.exp(dot(ups[l], high) + dot(ups[l], lower))
        parts = []
        for h in range(2):
            q, k = qkvg[:, head_cols(h, 0)], qkvg[:, head_cols(h, 1)]
            if l < LEVELS:
                xh = x[:, h * DK : (h + 1) * DK]
                qf, kf = q.astype(F32) * xh, k.astype(F32) * xh
                q, k = qf.astype(BF), kf.astype(BF)
            s = dot(k, q, 1, 1)
            scores_t[h] = jnp.where(lev_t == l, s, 0.0 if l == 0 else scores_t[h])
            here = jnp.where(lev == l, gd[h], 0.0).astype(BF)
            here_t = jnp.where(lev_t == l, gd_t[h], 0.0).astype(BF)
            dq, dk = dot(here, k), dot(here_t, q)
            if l < LEVELS:
                parts.append(qf * dq + kf * dk)
                dq, dk = dq * xh, dk * xh
            grad_q[h] = dq if l == 0 else grad_q[h] + dq
            grad_k[h] = dk if l == 0 else grad_k[h] + dk
        if l < LEVELS:
            both = dot(downs[l], jnp.concatenate(parts, axis=1).astype(BF))
            total = both if l == 0 else total + both
    grad_ld[...] = total
    for h in range(2):
        grad_qk[:, 2 * h * DK : (2 * h + 1) * DK] = grad_q[h]
        grad_qk[:, (2 * h + 1) * DK : (2 * h + 2) * DK] = grad_k[h]
        grad_v[:, h * DV : (h + 1) * DV] = dot(
            scores_t[h].astype(BF), grad_mixed[:, h * DV : (h + 1) * DV]
        ).astype(BF)


def project_back_kernel(
    tile, ints, qkvg, log_decay, grad_mixed, before, grad_qk, grad_v, grad_ld, grad_gate, rank, up, bias,
    ups, downs, weights,
    grad_project, grad_first, rank_part, packet, up_sum, bias_sum, d_since, d_towards, ld_sum,
):
    per_tile = TILE // SPAN
    ld = log_decay[...]
    since = jnp.exp(distances(ups[0], ld))
    towards = jnp.exp(distances(ups[1], ld))
    for j in reversed(range(per_tile)):
        rows = slice(j * SPAN, (j + 1) * SPAN)
        keep = ints[tile * per_tile + j].astype(F32)
        for h in range(2):
            lanes = slice(h * DK, (h + 1) * DK)
            values = slice(h * DV, (h + 1) * DV)
            gm = grad_mixed[rows, values]
            v = qkvg[rows, head_cols(h, 2)]
            qd = qkvg[rows, head_cols(h, 0)].astype(F32) * since[rows, lanes]
            kd = qkvg[rows, head_cols(h, 1)].astype(F32) * towards[rows, lanes]
            prev = before[j, h]
            after = packet[values]
            after_low = after.astype(BF)
            dq = dot(gm, prev)
            dk = dot(v, after_low)
            d_since[rows, lanes] = (qd * dq).astype(BF)
            d_towards[rows, lanes] = (kd * dk).astype(BF)
            dq = grad_qk[rows, 2 * h * DK : (2 * h + 1) * DK] + dq * since[rows, lanes]
            dk = grad_qk[rows, (2 * h + 1) * DK : (2 * h + 2) * DK] + dk * towards[rows, lanes]
            dv = grad_v[rows, values].astype(F32) + dot(kd.astype(BF), after_low, 1, 1)
            grad_project[rows, head_cols(h, 0)] = (dq * scaling).astype(BF)
            grad_project[rows, head_cols(h, 1)] = dk.astype(BF)
            grad_project[rows, head_cols(h, 2)] = dv.astype(BF)
            grad_project[rows, head_cols(h, 3)] = grad_gate[rows, values]
            last = since[j * SPAN + SPAN - 1 : j * SPAN + SPAN, lanes]
            d_last = last * jnp.sum(prev.astype(F32) * after, axis=0, keepdims=True)
            ld_sum[rows, lanes] = grad_ld[rows, lanes] + d_last
            packet[values] = keep * (after * last + dot(gm, qd.astype(BF), 0, 0))
    d_log = ld_sum[...] + dot(downs[0], d_since[...]) + dot(downs[1], d_towards[...])
    logits = dot(rank[...], up[...]) + bias[...]
    gl = (d_log * (1.0 / decay_scale) * jax.nn.sigmoid(-logits)).astype(BF)
    up_sum[...] += dot(rank[...], gl, 0, 0)
    bias_sum[0:1, :] += jnp.sum(gl.astype(F32), axis=0, keepdims=True)
    rank_part[...] = dot(up[...], gl, 1, 1)
    grad_first[...] = (
        dot(grad_project[:, :HEAD], weights[in_rows(0), :])
        + dot(grad_project[:, HEAD:], weights[in_rows(1), :])
    ).astype(BF)


def source_back_kernel(
    src, normed, gf_a, gf_b, rank_a, rank_b, w_down, gain, grad_hidden,
    own, cross, dealt, down_sum, gain_sum,
):
    low = (rank_a[...] + rank_b[...]).astype(BF)
    gf = gf_a[...].astype(F32) + gf_b[...].astype(F32) + dot(low, w_down[...], 0, 0)
    x = src[...].astype(F32)
    inv = rms_scale(x)
    normal = x * inv
    gain_sum[0:1, :] += jnp.sum(gf * normal, axis=0, keepdims=True)
    e = gf * gain[...]
    dealt[...] = (
        grad_hidden[...] + inv * (e - normal * jnp.mean(e * normal, axis=-1, keepdims=True))
    ).astype(BF)
    down_sum[...] += dot(low, normed[...])
    quarter = own.shape[2]
    at_x, at_core = lax.axis_index("x"), lax.axis_index("core")
    for out, half in ((own, at_x), (cross, 1 - at_x)):
        col = pl.multiple_of((2 * half + at_core) * quarter, 128)
        for j in range(TILE // SPAN):
            out[j] = dealt[j * SPAN : (j + 1) * SPAN, pl.ds(col, quarter)]


def back_kernel(nd, spans, reach, direct, f, table, act_in, grad_gu, normed, cot_in, qkvg_in, log_decay_in, mixed_in, packet_in,
                factors, out_own, out_cross, ups, downs, level, level_t, *rest):
    n_sums = 5 if direct else 3
    (leaving, grad_qk_o, grad_v_o, grad_ld_o, gath_o, *sums), rest = rest[: 5 + n_sums], rest[5 + n_sums :]
    (grad_qk, grad_v, grad_ld, sent_packets, got_packets), rest = rest[:5], rest[5:]
    (carry_send, carry_recv, out_sems), rest = rest[:3], rest[3:]
    (joined, sent, gath), rest = rest[:3], rest[3:]
    undeal_sems, rest = rest[:4], rest[4:]
    (act, cot, qkvg, log_decay, grad_mixed, late_sems), rest = rest[:6], rest[6:]
    late = fetch(
        ((act_in, act), (cot_in, cot), (qkvg_in, qkvg), (log_decay_in, log_decay), (mixed_in, grad_mixed)), late_sems
    )
    pitch = act.shape[1] // 2
    tiles = spans * SPAN // TILE
    nz = nd // 2
    carry = Carry(nd, reach, -1, leaving, sent_packets, got_packets, carry_send, carry_recv)
    enter(nd, carry.shifts())
    undeal = Undeal(nd, spans, table, out_own, out_cross, joined, sent, gath, undeal_sems)
    for i in range(PIECES):
        undeal.swap(i).start()
    undeal.begin()
    leaving[: 2 * DV] = packet_in[...]
    leaving[2 * DV :] = factors[...]
    carry.send(0)
    outgoing = []

    def store(value, out):
        outgoing.append(pltpu.make_async_copy(value, out, out_sems.at[len(outgoing)]))
        outgoing[-1].start()

    def at(ref, i):
        return ref.at[pl.ds(pl.multiple_of(i * TILE, TILE), TILE), :]

    def tile(i, _):
        within_back_kernel(
            at(qkvg, i), at(log_decay, i), at(grad_mixed, i), ups, downs, level, level_t,
            at(grad_qk, i), at(grad_v, i), at(grad_ld, i),
        )
        return 0

    def some(first, last):
        return lambda: lax.fori_loop(first, last, tile, 0)

    stages = list(range(carry.run()))

    def advance():
        if stages:
            carry.step(stages.pop(0))

    if direct:
        accs, rest = rest[:3], rest[3:]
        chains = [
            Collapse(nd, order, acc, pitch, low, count, rest[3 * k], rest[3 * k + 1 : 3 * k + 3])
            for k, (acc, order, low, count) in enumerate(
                ((accs[0], 0, 0, f), (accs[1], 1, 0, f), (accs[2], 0, 0, f // 2), (accs[2], 1, f // 2, f // 2))
            )
        ]
        at_x = lax.axis_index("x")
        chunks = 2 * pitch // 128
        part = -(-pitch // 128)
        gate = grad_gu.at[:, pl.ds(0, 2 * pitch)]
        weight_grad_into(accs[0], gate, normed, (chunks - part) * (1 - at_x), part)
        chains[0].begin()
        weight_grad_into(accs[0], gate, normed, part * at_x, chunks - part)
        advance()
        weight_grad_into(accs[1], grad_gu.at[:, pl.ds(2 * pitch, 2 * pitch)], normed)
        chains[1].begin()
        advance()
        for copy in late:
            copy.wait()
        third = -(-chunks // nz)
        for i in range(nz):
            chains[0].second((i + 1) % nz)
            weight_grad_into(accs[2], act, cot, third * i, max(0, min(third, chunks - third * i)))
        for i in range(nz):
            chains[1].second((i + 1) % nz)
        chains[2].begin()
        chains[3].begin()
        undeal.exchange()
        advance()
        for kz in [k % nz for k in range(1, nz + 1)]:
            chains[0].third(kz)
            chains[1].third(kz)
            some(kz, kz + 1)()
        progress(chains[2:], nz, [some(nz, tiles)])
        squares = sums[-1]
        squares[...] = jnp.zeros_like(squares)
        for chain, out in zip(chains, sums):
            chain.finish(out, squares)
    else:
        undeal.exchange()
        weight_grad_into(sums[0], grad_gu.at[:, pl.ds(0, 2 * pitch)], normed)
        weight_grad_into(sums[1], grad_gu.at[:, pl.ds(2 * pitch, 2 * pitch)], normed)
        for copy in late:
            copy.wait()
        weight_grad_into(sums[2], act, cot)
        some(0, tiles)()
        while stages:
            advance()
    store(grad_qk, grad_qk_o)
    store(grad_v, grad_v_o)
    store(grad_ld, grad_ld_o)
    for k in range(1, nd):
        undeal.arrive(k)
    store(gath, gath_o)
    undeal.finish()
    for copy in outgoing:
        copy.wait()


def last_kernel(nd, spans, direct, table, keep, qkvg, log_decay, grad_mixed, before, leaving, grad_qk, grad_v, grad_ld,
                grad_gate, rank, up, bias, ups, downs, weights, src_in, normed_in, hidden_in, gain, po_in, gain_second, head_part, squares_in,
                *rest):
    n_sums = 6 if direct else 1
    (gath_o, down_sum, gain_sum, up_sum, bias_sum, *sums), rest = rest[: 5 + n_sums], rest[5 + n_sums :]
    (packet, grad_project, grad_first, grad_first_other, rank_part, rank_other), rest = rest[:6], rest[6:]
    (d_since, d_towards, ld_sum, dealt), rest = rest[:4], rest[4:]
    (gf_send, gf_recv, rk_send, rk_recv, out_sems), rest = rest[:5], rest[5:]
    (own, cross, joined, sent, gath), rest = rest[:5], rest[5:]
    undeal_sems, rest = rest[:6], rest[6:]
    (src, normed, grad_hidden, late_sems), rest = rest[:4], rest[4:]
    late = fetch(((src_in, src), (normed_in, normed), (hidden_in, grad_hidden)), late_sems)
    tiles = spans * SPAN // TILE
    per_tile = TILE // SPAN
    nz = nd // 2
    enter(nd)
    core = lax.axis_index("core")
    undeal = Undeal(nd, spans, table, own, cross, joined, sent, gath, undeal_sems)
    chains = []
    if direct:
        (po_acc, pi_acc), rest = rest[:2], rest[2:]
        (small_sent, small_got, small_norms), rest = rest[:3], rest[3:]
        small_sems, rest = rest[:6], rest[6:]
        small = Small(nd, sums[4], small_sent, small_got, small_norms, small_sems)
        squares = sums[5]
        squares[...] = squares_in[...]
        small_left = list(range(small.steps()))

        def advance_small():
            if small_left:
                small.end(small_left.pop(0))
                if small_left:
                    small.begin(small_left[0])

        halves = ((pi_acc, 0, HEAD), (pi_acc, 1, HEAD), (po_acc, 0, DV), (po_acc, 1, DV))
        chains = [
            Collapse(
                nd, order, acc, size, order * size // 2, size // 2, rest[3 * k], rest[3 * k + 1 : 3 * k + 3]
            )
            for k, (acc, order, size) in enumerate(halves)
        ]
        fill = pltpu.make_async_copy(po_in, po_acc, out_sems.at[0])
        fill.start()
        fill.wait()
        chains[2].begin()
        chains[3].begin()
    packet[...] = leaving[...]
    for ref in (down_sum, gain_sum, up_sum, bias_sum):
        ref[...] = jnp.zeros_like(ref)

    def at(ref, i):
        return ref.at[pl.ds(pl.multiple_of(i * TILE, TILE), TILE), :]

    def swap_first(i):
        return copy_to(at(grad_first, i), at(grad_first_other, i), gf_send.at[i], gf_recv.at[i], {"core": 1 - core})

    def swap_rank(i):
        return copy_to(rank_part.at[i], rank_other.at[i], rk_send.at[i], rk_recv.at[i], {"core": 1 - core})

    def body(step, _):
        i = tiles - 1 - step
        project_back_kernel(
            i, keep, at(qkvg, i), at(log_decay, i), at(grad_mixed, i), before.at[pl.ds(i * per_tile, per_tile)],
            at(grad_qk, i), at(grad_v, i), at(grad_ld, i), at(grad_gate, i), at(rank, i), up, bias, ups, downs, weights,
            at(grad_project, i), at(grad_first, i), rank_part.at[i], packet, up_sum, bias_sum,
            d_since, d_towards, ld_sum,
        )
        swap_first(i).start()
        swap_rank(i).start()
        return 0

    lax.fori_loop(0, tiles, body, 0)
    if direct:
        for kz in [k % nz for k in range(1, nz + 1)]:
            chains[2].second(kz)
            chains[3].second(kz)

    def finish_tile(step, _):
        i = tiles - 1 - step
        swap_first(i).wait()
        swap_rank(i).wait()
        source_back_kernel(
            at(src, i), at(normed, i), at(grad_first, i), at(grad_first_other, i), rank_part.at[i], rank_other.at[i],
            weights.at[pl.ds(0, 16), :], gain, at(grad_hidden, i),
            own.at[pl.ds(i * per_tile, per_tile)], cross.at[pl.ds(i * per_tile, per_tile)],
            dealt, down_sum, gain_sum,
        )
        undeal.swap(i).start()
        return 0

    for copy in late:
        copy.wait()
    lax.fori_loop(0, tiles, finish_tile, 0)
    undeal.begin()
    if direct:
        small.fill(gain_sum, gain_second, down_sum, up_sum, bias_sum, head_part)
        small.begin(0)
        at_x = lax.axis_index("x")
        part = HEAD // 256
        weight_grad_into(pi_acc, grad_project, normed, 2 * part * (1 - at_x), part)
        chains[0].begin()
        weight_grad_into(pi_acc, grad_project, normed, part, part)
        weight_grad_into(pi_acc, grad_project, normed, 3 * part, part)
        chains[1].begin()
        weight_grad_into(pi_acc, grad_project, normed, 2 * part * at_x, part)
        advance_small()
        for kz in [k % nz for k in range(1, nz + 1)]:
            chains[2].third(kz)
            chains[3].third(kz)
    else:
        weight_grad_into(sums[0], grad_project, normed)
    undeal.exchange()
    arrivals = [functools.partial(undeal.arrive, k) for k in range(1, nd)]
    if direct:
        for kz in [k % nz for k in range(1, nz + 1)]:
            chains[0].second(kz)
            chains[1].second(kz)
            advance_small()
            if arrivals:
                arrivals.pop(0)()
        while small_left:
            advance_small()
        small.begin_head()
        for kz in [k % nz for k in range(1, nz + 1)]:
            chains[0].third(kz)
            chains[1].third(kz)
            if arrivals:
                arrivals.pop(0)()
        chains[2].finish(sums[2], squares)
        chains[3].finish(sums[3], squares)
        small.end_head()
    for arrive in arrivals:
        arrive()
    if direct:
        chains[0].finish(sums[0], squares)
        chains[1].finish(sums[1], squares)
        small.begin_norm(squares[...] + small.squares())
    undeal.finish()
    out = pltpu.make_async_copy(gath, gath_o, out_sems.at[0])
    out.start()
    if direct:
        small.end_norm(squares)
    out.wait()


def remote(kernel, ins, specs, outs, out_specs, scratch, name, number, us):
    return pl.pallas_call(
        kernel,
        in_specs=specs,
        out_specs=out_specs,
        out_shape=outs,
        scratch_shapes=scratch,
        name=name,
        compiler_params=pltpu.CompilerParams(
            vmem_limit_bytes=VMEM_LIMIT, collective_id=number, has_side_effects=True
        ),
        cost_estimate=cost(us),
    )(*ins)


def all_sum(value, axes, sizes):
    for axis, size in zip(axes, sizes):
        bit = 1
        while bit < size:
            value = value + lax.ppermute(value, axis, [(i, i ^ bit) for i in range(size)])
            bit *= 2
    return value


def square_sum(array):
    return jnp.sum(array * array)


def adam_update(weight, grad, first, second, factor, decay_rate):
    clipped = grad * factor
    first_new = beta_one * first + (1.0 - beta_one) * clipped
    second_new = beta_two * second + (1.0 - beta_two) * clipped * clipped
    first_hat = first_new / (1.0 - beta_one**adam_step)
    second_hat = second_new / (1.0 - beta_two**adam_step)
    master = weight.astype(F32)
    change = -learn_rate * (first_hat / (jnp.sqrt(second_hat) + adam_eps) + decay_rate * master)
    return (grad, first_new, second_new, change)


def swap(value, axis):
    return lax.ppermute(value, axis, [(0, 1), (1, 0)])


def on_device(
    tokens, cotangent, seq_extra, deal, proj_in, decay_down, decay_up, decay_bias, head_gain, proj_out, block_gains,
    ffn_in, ffn_out, first_proj_in, second_proj_in, first_decay_down, second_decay_down, first_decay_up,
    second_decay_up, first_decay_bias, second_decay_bias, first_head_gain, second_head_gain, first_proj_out,
    second_proj_out, first_block_gains, second_block_gains, first_ffn_in, second_ffn_in, first_ffn_out, second_ffn_out,
):
    d = tokens.shape[1]
    nd = lax.axis_size("dp")
    nz = nd // 2
    dp, x, core = lax.axis_index("dp"), lax.axis_index("x"), lax.axis_index("core")
    z, y = dp // 2, dp % 2
    tensor = 2 * x + core
    per_dev = tokens.shape[0] // SPAN
    spans = per_dev // 2
    rows = spans * SPAN
    tiles = rows // TILE
    capacity = -(-per_dev // nd)
    quarter = d // 4
    f = ffn_out.shape[0]
    w = d // nd
    direct = w % 128 == 0

    recv_slot, send_local, back_local, home_slot = deal_tables(deal, nd, per_dev, capacity, dp)
    mine = lax.dynamic_slice_in_dim(recv_slot, x * spans, spans)
    theirs = lax.dynamic_slice_in_dim(recv_slot, (1 - x) * spans, spans)
    span_ids = (dp * 2 + x) * spans + jnp.arange(spans, dtype=jnp.int32)
    keep = 1 - span_starts(seq_extra, span_ids)
    other_quarter = 2 * (1 - x) + core
    quarters = jnp.stack([tensor, other_quarter, 2 * x + 1 - core, 2 * (1 - x) + 1 - core])
    ints = jnp.concatenate([quarters, jnp.stack([core, z, y, x]), keep]).astype(jnp.int32)
    ups, downs, level, level_t = (jnp.asarray(v) for v in level_matrices())
    ups_last, downs_last = (jnp.asarray(v[LEVELS:]) for v in level_matrices()[:2])

    hh, ho, hf = HEAD // 2, DV // 2, f // 2
    pitch = f
    ffn_t = ffn_in.reshape(w, 2 * f).T
    shard_p = jnp.concatenate([decay_down.T, proj_in.reshape(w, HEAD).T, proj_out.reshape(DV, w)], axis=0)
    shard_f = jnp.concatenate([ffn_t[:f], ffn_out, ffn_t[f:]], axis=0)

    def fit(parts):
        return jnp.concatenate(parts, axis=0)

    table = jnp.concatenate([send_local, mine, theirs]).astype(jnp.int32)
    if not direct:

        def gathered(shard):
            return jnp.swapaxes(lax.all_gather(shard, "dp", axis=0), 0, 1).reshape(shard.shape[0], d)

        def halves(shard):
            own, other = gathered(shard), gathered(swap(shard, "x"))
            return jnp.where(x == 0, fit([own, other]), fit([other, own]))

        shard_p = halves(shard_p)
        shard_f = fit([halves(ffn_t[:f]), halves(ffn_out), halves(ffn_t[f:])])

    up_own = decay_up.reshape(16, DK)
    bias_own = decay_bias.reshape(1, DK)
    small_own = jnp.concatenate([up_own.astype(F32), bias_own, jnp.zeros((7, DK), F32)], axis=0)
    small_other = swap(small_own, "x")
    small_both = jnp.where(
        x == 0,
        jnp.concatenate([small_own, small_other], axis=1),
        jnp.concatenate([small_other, small_own], axis=1),
    )
    up, bias = small_both[:16].astype(BF), small_both[16:17]
    gain_one, gain_two = block_gains[0:1], block_gains[1:2]
    head_row = head_gain.reshape(1, DV)

    def tall(cols, dtype=BF):
        return sds(rows, cols, dtype=dtype)

    nlev = LEVELS + 2
    sequence = nd * 2
    reach = -(-(MAX_SPANS - 1) // spans)
    (src, cot, weights, w_ffn, normed_first, qkvg, log_decay, rank, mixed, gated, attn, before, attn_other,
     factors) = forward(
        table, keep.astype(jnp.int32), tokens, cotangent, shard_p, shard_f, gain_one, up, bias, head_row, ups, level,
        nd, spans, reach, direct,
    )
    ff = 2 * f
    hidden, normed_second, act, grad_gu, keep_out, send_out, grad_second = run(
        ffn_kernel, (tiles,),
        [SMEM] + [rows_spec(d)] * 4 + [whole_spec(1, d), whole_spec(3 * ff, d)],
        [rows_spec(d), rows_spec(d), rows_spec(2 * pitch), rows_spec(4 * pitch), rows_spec(2 * quarter),
         rows_spec(2 * quarter), rows_spec(d)],
        [tall(d, F32), tall(d), tall(2 * pitch), tall(4 * pitch), tall(2 * quarter), tall(2 * quarter), tall(d)],
        [pltpu.VMEM((TILE, d), BF)],
        "ffn", 34,
    )(ints, src, attn, attn_other, cot, gain_two, w_ffn)
    gs_other = swap(grad_second, "core")
    recv_out = swap(send_out, "core")

    def plain_shard(full, f_rows):
        full = jnp.swapaxes(full.reshape(2 * f_rows, nd, w), 0, 1)
        total = lax.psum_scatter(full, "dp", scatter_dimension=0, tiled=True)[0].astype(F32)
        keep_rows = lax.dynamic_slice_in_dim(total, x * f_rows, f_rows)
        give_rows = lax.dynamic_slice_in_dim(total, (1 - x) * f_rows, f_rows)
        return keep_rows + swap(give_rows, "x")

    grad_hidden, grad_mixed, grad_gate, gain_second, head_part, packet_back, out_own, out_cross, acc_po = run(
        functools.partial(out_back_kernel, tiles), (tiles,),
        [SMEM] + [rows_spec(d, tiles)] * 4
        + [whole_spec(1, d), whole_spec(2 * PROJ_ROWS, d), rows_spec(2 * DV, tiles), rows_spec(2 * DV, tiles),
           rows_spec(2 * HEAD, tiles), rows_spec(2 * DK, tiles), whole_spec(1, DV), whole_spec(nlev, TILE, TILE),
           rows_spec(2 * quarter, tiles), rows_spec(2 * quarter, tiles)],
        [rows_spec(d, tiles), rows_spec(2 * DV, tiles), rows_spec(2 * DV, tiles), whole_spec(8, d),
         whole_spec(8, DV), whole_spec(2 * DV, DK), rows_spec(quarter, tiles), rows_spec(quarter, tiles),
         whole_spec(2 * DV, d)],
        [tall(d, F32), tall(2 * DV), tall(2 * DV), sds(8, d), sds(8, DV), sds(2 * DV, DK), tall(quarter),
         tall(quarter), sds(2 * DV, d, dtype=BF)],
        [pltpu.VMEM((2 * DV, d), F32), pltpu.VMEM((2, DV, DK), F32), pltpu.VMEM((8, d), F32), pltpu.VMEM((8, DV), F32)],
        "out_back", 19,
    )(ints, hidden, cot, grad_second, gs_other, gain_two, weights, gated, mixed, qkvg, log_decay, head_row, ups,
      keep_out, recv_out)

    dma = pltpu.SemaphoreType.DMA
    steps = len(carry_widths(reach)[0]) + 2
    shape_qk, shape_v, shape_ld = (rows, 4 * DK), (rows, 2 * DV), (rows, 2 * DK)
    buffers, sems = undeal_scratch(nd, per_dev, spans, quarter, capacity, False)
    scratch = [pltpu.VMEM(shape_qk, F32), pltpu.VMEM(shape_v, BF), pltpu.VMEM(shape_ld, F32)]
    scratch += [pltpu.VMEM((steps - 1, 2 * DV + 16, DK), BF), pltpu.VMEM((steps, 2 * DV + 16, DK), BF)]
    scratch += [dma((steps,)), dma((steps,)), dma((4,))] + buffers[2:] + sems
    scratch += [pltpu.VMEM(v.shape, v.dtype) for v in (act, cot, qkvg, log_decay, grad_mixed)] + [dma((5,))]
    if direct:
        sums = [sds(f, w), sds(f, w), sds(f // 2, w), sds(f // 2, w), sds(8, 128)]
        scratch += [pltpu.VMEM((2 * pitch, d), BF)] * 3
        for out in sums[:4]:
            scratch += collapse_scratch(nd, out.shape[0], w)
    else:
        sums = [sds(2 * pitch, d, dtype=BF)] * 3
    leaving, grad_qk, grad_v, grad_ld, back_out, *sums_f = remote(
        functools.partial(back_kernel, nd, spans, reach, direct, f),
        (back_local, act, grad_gu, normed_second, cot, qkvg, log_decay, grad_mixed, packet_back, factors,
         out_own.reshape(spans, SPAN, quarter), out_cross.reshape(spans, SPAN, quarter), ups, downs, level, level_t),
        [SMEM, ANY, VMEM, VMEM, ANY, ANY, ANY, ANY] + [VMEM] * 8,
        [sds(2 * DV + 16, DK), sds(*shape_qk), sds(*shape_v, dtype=BF), sds(*shape_ld),
         sds(nd * capacity, SPAN, quarter, dtype=BF)] + sums,
        [VMEM] + [ANY] * 4 + [VMEM] * len(sums),
        scratch, "back_all", 1, 110,
    )
    if direct:
        shard_gate, shard_up, shard_fo = sums_f[0], sums_f[1], fit(sums_f[2:4])
    else:
        shard_gate, shard_up, shard_fo = (plain_shard(v, pitch)[:f] for v in sums_f)
    block_out = home(back_out, home_slot, "block_out_home")

    buffers, sems = undeal_scratch(nd, per_dev, spans, quarter, capacity, True)
    scratch = [
        pltpu.VMEM((2 * DV + 16, DK), F32), pltpu.VMEM((rows, 2 * HEAD), BF), pltpu.VMEM((rows, d), BF),
        pltpu.VMEM((rows, d), BF), pltpu.VMEM((tiles, 16, TILE), F32), pltpu.VMEM((tiles, 16, TILE), F32),
        pltpu.VMEM((TILE, 2 * DK), BF), pltpu.VMEM((TILE, 2 * DK), BF), pltpu.VMEM((TILE, 2 * DK), F32),
        pltpu.VMEM((TILE, d), BF), dma((tiles,)), dma((tiles,)), dma((tiles,)), dma((tiles,)), dma((1,)),
    ] + buffers + sems
    scratch += [pltpu.VMEM(v.shape, v.dtype) for v in (src, normed_first, grad_hidden)] + [dma((3,))]
    if direct:
        sums = [sds(hh, w), sds(hh, w), sds(ho, w), sds(ho, w), sds(SMALL, 128), sds(8, 128)]
        scratch += [pltpu.VMEM((2 * DV, d), BF), pltpu.VMEM((2 * HEAD, d), BF)] + small_scratch(nd)
        for out in sums[:4]:
            scratch += collapse_scratch(nd, out.shape[0], w)
    else:
        sums = [sds(2 * HEAD, d, dtype=BF)]
    back_grad, down_grad, gain_first, up_grad, bias_grad, *sums_p = remote(
        functools.partial(last_kernel, nd, spans, direct),
        (back_local, keep.astype(jnp.int32), qkvg, log_decay, grad_mixed, before, leaving, grad_qk, grad_v, grad_ld,
         grad_gate, rank, up, bias, ups_last, downs_last, weights, src, normed_first, grad_hidden, gain_one,
         acc_po, gain_second, head_part, sums_f[4] if direct else gain_second),
        [SMEM, SMEM] + [VMEM] * 15 + [ANY] * 3 + [VMEM, ANY] + [VMEM] * 3,
        [sds(nd * capacity, SPAN, d, dtype=BF), sds(16, d), sds(8, d), sds(16, 2 * DK), sds(8, 2 * DK)] + sums,
        [ANY] + [VMEM] * (4 + len(sums)),
        scratch, "finish_all", 2, 100,
    )
    if direct:
        shard_pi, shard_po = fit(sums_p[:2]), fit(sums_p[2:4])
    else:
        shard_pi, shard_po = plain_shard(sums_p[0], HEAD), plain_shard(acc_po, DV)
    token_grad = home(back_grad, home_slot, "token_grad_home")

    if direct:
        small, norm_block = sums_p[4], sums_p[5]
        gain_first, gain_second = small[0:8].reshape(d), small[8:16].reshape(d)
        shard_down = lax.dynamic_slice_in_dim(small, 16 + 16 * dp, 16, 0).T
        up_total = lax.dynamic_slice_in_dim(small, 144 + 16 * x, 16, 0)
        bias_total = lax.dynamic_slice_in_dim(small, 176 + x, 1, 0)
        head_total = small[178:180].reshape(DV)
        norm_sq = jnp.sum(norm_block)
    else:
        parts = (gain_first[0], gain_second[0], down_grad, up_grad, bias_grad[0], head_part[0])
        small = jnp.concatenate([v.reshape(-1) for v in parts]).reshape(-1, 128)
        small = all_sum(small, ("x", "dp"), (2, nd)).reshape(-1)
        cuts = [d, d, 16 * d, 32 * DK, 2 * DK, DV]
        starts = [sum(cuts[:k]) for k in range(len(cuts) + 1)]
        gain_first, gain_second, down_total, up_total, bias_total, head_total = (
            small[starts[k] : starts[k + 1]] for k in range(len(cuts))
        )
        head_total = head_total + swap(head_total, "core")
        shard_down = lax.dynamic_slice_in_dim(down_total.reshape(16, d), dp * w, w, 1).T
        up_total = up_total.reshape(16, 2, DK)
        up_total = jnp.where(x == 0, up_total[:, 0], up_total[:, 1])
        bias_total = bias_total.reshape(2, DK)
        bias_total = jnp.where(x == 0, bias_total[0:1], bias_total[1:2])
        local_sq = (
            square_sum(shard_pi) + square_sum(shard_po) + square_sum(shard_gate) + square_sum(shard_up)
            + square_sum(shard_fo) + square_sum(shard_down) / 4
            + (square_sum(up_total) + square_sum(bias_total)) / nd
            + (square_sum(head_total) + square_sum(gain_first) + square_sum(gain_second)) / (4 * nd)
        )
        norm_sq = all_sum(jnp.broadcast_to(local_sq, (8, 128)), ("core", "x", "dp"), (2, 2, nd))[0, 0]
    up_total = up_total.reshape(decay_up.shape)
    bias_total = bias_total.reshape(decay_bias.shape)
    gains_total = jnp.stack([gain_first, gain_second])
    shard_in = shard_pi.T.reshape(proj_in.shape)
    shard_out = shard_po.reshape(proj_out.shape)
    shard_ffn_in = jnp.stack([shard_gate.T, shard_up.T], axis=1)
    shard_ffn_out = shard_fo
    grad_norm = jnp.sqrt(norm_sq)
    clip_norm = clip_scale * math.sqrt(PARAMS)
    factor = jnp.minimum(1.0, clip_norm / (grad_norm + 1e-06))
    update_in = adam_update(proj_in, shard_in, first_proj_in, second_proj_in, factor, weight_decay)
    update_down = adam_update(decay_down, shard_down, first_decay_down, second_decay_down, factor, weight_decay)
    update_up = adam_update(decay_up, up_total, first_decay_up, second_decay_up, factor, weight_decay)
    update_bias = adam_update(decay_bias, bias_total, first_decay_bias, second_decay_bias, factor, 0.0)
    update_head = adam_update(head_gain, head_total, first_head_gain, second_head_gain, factor, 0.0)
    update_out = adam_update(proj_out, shard_out, first_proj_out, second_proj_out, factor, weight_decay)
    update_gains = adam_update(block_gains, gains_total, first_block_gains, second_block_gains, factor, 0.0)
    update_ffn_in = adam_update(ffn_in, shard_ffn_in, first_ffn_in, second_ffn_in, factor, weight_decay)
    update_ffn_out = adam_update(ffn_out, shard_ffn_out, first_ffn_out, second_ffn_out, factor, weight_decay)
    return (
        block_out, token_grad, grad_norm, *update_in, *update_down, *update_up, *update_bias, *update_head,
        *update_out, *update_gains, *update_ffn_in, *update_ffn_out,
    )


def solution(mesh):
    nd, nt = mesh.shape["dp"], mesh.shape["tensor"]
    fine = Mesh(mesh.devices.reshape(nd, nt // 2, 2), ("dp", "x", "core"))
    t = ("x", "core")
    w_specs = {
        "proj_in": P("dp", t, None),
        "decay_down": P("dp", None),
        "decay_up": P(None, t, None),
        "decay_bias": P(t, None),
        "head_gain": P(),
        "proj_out": P(t, None, "dp"),
        "block_gains": P(),
        "ffn_in": P("dp", None, t),
        "ffn_out": P(t, "dp"),
    }
    specs = list(w_specs.values())
    placed = [P("dp", None), P("dp", None), P(), P()] + specs
    results = [P("dp", t), P("dp", None), P()]
    for spec in specs:
        placed += [spec] * 2
        results += [spec] * 4
    return jax.shard_map(
        on_device,
        mesh=fine,
        in_specs=tuple(placed),
        out_specs=tuple(results),
        check_vma=False,
    )
```

```python
import functools
import math

import jax
import jax.numpy as jnp
import numpy as np
from jax import lax
from jax.experimental import pallas as pl
from jax.experimental.pallas import tpu as pltpu
from jax.sharding import Mesh
from jax.sharding import PartitionSpec as P

DK = 128
DV = 256
SPAN = 64
MIN_SPANS = 16
MAX_SPANS = 128
PARAMS = 12872448
TILE = 256
LEVELS = 6
HEAD = 2 * DK + 2 * DV
VMEM_LIMIT = 61 * 1024 * 1024
BF = jnp.bfloat16
F32 = jnp.float32

norm_eps = 1e-06
learn_rate = 0.05
beta_one = 0.9
beta_two = 0.95
adam_eps = 1e-08
weight_decay = 0.1
clip_scale = 0.05
adam_step = 10
decay_scale = 16.0
scaling = DK ** (-0.5)
ANY = pl.BlockSpec(memory_space=pl.ANY)
SMEM = pl.BlockSpec(memory_space=pltpu.SMEM)
VMEM = pl.BlockSpec(memory_space=pltpu.VMEM)


def dot(a, b, ca=1, cb=0):
    return lax.dot_general(a, b, (((ca,), (cb,)), ((), ())), preferred_element_type=F32)


def cost(us):
    return pl.CostEstimate(flops=int(us * 1.0e9), bytes_accessed=int(us * 1.0e6), transcendentals=0)


def run(kernel, grid, in_specs, out_specs, out_shape, scratch, name, us):
    return pl.pallas_call(
        kernel,
        grid=grid,
        in_specs=in_specs,
        out_specs=out_specs,
        out_shape=out_shape,
        scratch_shapes=scratch,
        name=name,
        compiler_params=pltpu.CompilerParams(vmem_limit_bytes=VMEM_LIMIT),
        cost_estimate=cost(us),
    )


def sds(*shape, dtype=F32):
    return jax.ShapeDtypeStruct(shape, dtype)


def rows_spec(cols, order=None):
    if order is None:
        return pl.BlockSpec((TILE, cols), lambda i: (i, 0))
    return pl.BlockSpec((TILE, cols), lambda i: (order - 1 - i, 0))


def whole_spec(*shape):
    zeros = (0,) * len(shape)
    return pl.BlockSpec(shape, lambda i: zeros, pipeline_mode=pl.Buffered(1))


def span_starts(seq_extra, span_ids):
    seq_spans = seq_extra + MIN_SPANS
    n = seq_extra.shape[0]
    earlier = jnp.tril(jnp.ones((n, n), jnp.int32), -1)
    bounds = jnp.sum(earlier * seq_spans[None, :], axis=1)
    return jnp.any(bounds[None, :] == span_ids[:, None], axis=1).astype(jnp.int32)


def deal_tables(deal, n_data, per_dev, capacity, my_index):
    table_grid = deal.reshape(n_data, per_dev)
    src_dev = table_grid // per_dev
    src_local = table_grid % per_dev
    my_source = lax.dynamic_index_in_dim(src_dev, my_index, 0, keepdims=False)
    earlier = jnp.tril(jnp.ones((per_dev, per_dev), jnp.int32), -1)
    same_source = (my_source[:, None] == my_source[None, :]).astype(jnp.int32)
    my_rank = jnp.sum(same_source * earlier, axis=1)
    recv_slot = my_source * capacity + my_rank
    owned_here = (src_dev == my_index).astype(jnp.int32)
    send_rank = jnp.sum(owned_here[:, None, :] * earlier[None], axis=2)
    slot_ids = jnp.arange(capacity, dtype=jnp.int32)
    send_hit = owned_here[:, :, None] * (
        send_rank[:, :, None] == slot_ids[None, None, :]
    ).astype(jnp.int32)
    send_local = jnp.sum(send_hit * src_local[:, :, None], axis=1)
    peer_ids = jnp.arange(n_data, dtype=jnp.int32)
    local_ids = jnp.arange(per_dev, dtype=jnp.int32)
    back_hit = (
        (my_source[None, None, :] == peer_ids[:, None, None])
        & (my_rank[None, None, :] == slot_ids[None, :, None])
    ).astype(jnp.int32)
    back_local = jnp.sum(back_hit * local_ids[None, None, :], axis=2)
    home_hit = owned_here[:, :, None] * (
        src_local[:, :, None] == local_ids[None, None, :]
    ).astype(jnp.int32)
    home_slot = jnp.sum(
        home_hit * (peer_ids[:, None, None] * capacity + send_rank[:, :, None]), axis=(0, 1)
    )
    return recv_slot, send_local.reshape(-1), back_local.reshape(-1), home_slot


def level_matrices():
    t = np.arange(TILE, dtype=np.int32)[:, None]
    u = np.arange(TILE, dtype=np.int32)[None, :]
    ups = []
    level = np.full((TILE, TILE), LEVELS + 1, np.int32)
    for l in range(LEVELS):
        block = SPAN >> l
        half = block // 2
        same = (t // block) == (u // block)
        mid = (t // block) * block + half
        right = (t >= mid) & (u >= mid) & (u <= t)
        left = (t < mid) & (u > t) & (u < mid)
        ups.append(same & (right | left))
        hit = same & (t % block >= half) & (u % block < half)
        level = np.where(hit, l, level)
    level = np.where(t == u, LEVELS, level)
    same = (t // SPAN) == (u // SPAN)
    ups.append(same & (u <= t))
    ups.append(same & (u > t))
    ups = np.stack(ups).astype(np.float32).astype(BF)
    return ups, np.ascontiguousarray(np.swapaxes(ups, 1, 2)), level, np.ascontiguousarray(level.T)


def home_kernel(count, table, src, out):
    step = pl.program_id(0)
    for i in range(count):
        out[i * SPAN : (i + 1) * SPAN, :] = src[table[step * count + i]].astype(F32)


def home(spans, table, name):
    total = table.shape[0]
    count = 5
    d = spans.shape[2]
    return pl.pallas_call(
        functools.partial(home_kernel, count),
        grid=(total // count,),
        in_specs=[SMEM, whole_spec(*spans.shape)],
        out_specs=pl.BlockSpec((count * SPAN, d), lambda i: (i, 0)),
        out_shape=sds(total * SPAN, d),
        name=name,
        compiler_params=pltpu.CompilerParams(vmem_limit_bytes=VMEM_LIMIT),
        cost_estimate=cost(5),
    )(table, spans)


def copy_to(src, dst, send_sem, recv_sem, target):
    return pltpu.make_async_remote_copy(
        src_ref=src,
        dst_ref=dst,
        send_sem=send_sem,
        recv_sem=recv_sem,
        device_id=target,
        device_id_type=pl.DeviceIdType.MESH,
    )


def enter(nd, shifts=()):
    dp, x, core = lax.axis_index("dp"), lax.axis_index("x"), lax.axis_index("core")
    peers = [{"dp": lax.rem(dp + k, nd)} for k in range(1, nd)] + [{"x": 1 - x}, {"core": 1 - core}]
    for k in shifts:
        peers += [along_sequence(nd, k), along_sequence(nd, -k)]
    barrier = pltpu.get_barrier_semaphore()
    for peer in peers:
        pl.semaphore_signal(barrier, inc=1, device_id=peer, device_id_type=pl.DeviceIdType.MESH)
    pl.semaphore_wait(barrier, len(peers))


def along_sequence(nd, k):
    q = lax.rem(lax.axis_index("dp") * 2 + lax.axis_index("x") + k + 2 * nd, 2 * nd)
    return {"dp": q // 2, "x": lax.rem(q, 2)}


def carry_widths(reach):
    widths = []
    width = 1
    while 2 * width < reach:
        widths.append(width)
        width *= 2
    return widths, width


class Carry:
    def __init__(self, nd, reach, sign, packet, sent, got, send_sems, recv_sems):
        self.nd, self.sign, self.packet, self.sent, self.got = nd, sign, packet, sent, got
        self.send_sems, self.recv_sems = send_sems, recv_sems
        self.widths, self.last = carry_widths(reach)
        self.q = lax.axis_index("dp") * 2 + lax.axis_index("x")

    def shifts(self):
        return self.widths + [1, 1 + self.last]

    def copy(self, index):
        source = min(index, len(self.widths))
        return copy_to(
            self.sent.at[source],
            self.got.at[index],
            self.send_sems.at[index],
            self.recv_sems.at[index],
            along_sequence(self.nd, self.sign * self.shifts()[index]),
        )

    def send(self, stage):
        self.sent[stage] = self.packet[...].astype(BF)
        self.copy(stage).start()
        if stage == len(self.widths):
            self.copy(stage + 1).start()

    def receive(self, index):
        self.copy(index).wait_recv()
        k = self.shifts()[index]
        there = self.q >= k if self.sign > 0 else self.q + k < 2 * self.nd
        return jnp.where(there, self.got[index].astype(F32), 0.0)

    def step(self, stage):
        if stage < len(self.widths):
            self.join(self.receive(stage), self.packet[...])
            self.send(stage + 1)
        else:
            near, far = self.receive(stage), self.receive(stage + 1)
            self.join(far, near)
            for index in range(stage + 2):
                self.copy(index).wait_send()

    def join(self, earlier, later):
        for h in range(2):
            states = slice(h * DV, (h + 1) * DV)
            f = slice(2 * DV + h, 2 * DV + h + 1)
            self.packet[states] = later[f] * earlier[states] + later[states]
            self.packet[f] = later[f] * earlier[f]

    def run(self):
        return len(self.widths) + 1


class Spread:
    def __init__(self, nd, order, own, window, send_sems, recv_sems):
        self.nz, self.order, self.own, self.window = nd // 2, order, own, window
        self.send_sems, self.recv_sems = send_sems, recv_sems
        dp, self.x = lax.axis_index("dp"), lax.axis_index("x")
        self.z, self.y = dp // 2, lax.rem(dp, 2)
        nz = self.nz
        self.moves = [((0, 0, 0), (k, 0, 0)) for k in range(1, nz)]
        self.moves += [((0, 0, 0), (0, 1, 0)), ((0, 0, 0), (0, 0, 1))]
        for k in range(1, nz):
            self.moves += [((k, 0, 0), (k, 1, 0)), ((k, 0, 0), (k, 0, 1))]
        self.moves += [((k, 1, 0), (k, 1, 1)) for k in range(nz)]

    def place(self, k, first, second):
        fy, fx = (first, second) if self.order == 0 else (second, first)
        y = 1 - self.y if fy else self.y
        x = 1 - self.x if fx else self.x
        return self.window(lax.rem(self.z + self.nz - k, self.nz) * 2 + y, x)

    def copy(self, index):
        here, there = self.moves[index]
        if here[0] != there[0]:
            target = {"dp": lax.rem(self.z + there[0], self.nz) * 2 + self.y}
        elif (here[1] != there[1]) == (self.order == 0):
            target = {"dp": self.z * 2 + 1 - self.y}
        else:
            target = {"x": 1 - self.x}
        k, first, second = there
        return copy_to(
            self.own if here == (0, 0, 0) else self.place(*here),
            self.place(*here),
            self.send_sems.at[index],
            self.recv_sems.at[k + self.nz * (first + 2 * second)],
            target,
        )

    def arrived(self, k, first, second):
        at = self.place(k, first, second)
        sem = self.recv_sems.at[k + self.nz * (first + 2 * second)]
        copy_to(at, at, self.send_sems.at[0], sem, {"x": 1 - self.x}).wait_recv()

    def begin(self):
        for index in range(self.nz + 1):
            self.copy(index).start()

    def relay_z(self, k):
        self.arrived(k, 0, 0)
        for index in range(2):
            self.copy(self.nz + 1 + 2 * (k - 1) + index).start()

    def relay_first(self, k):
        self.arrived(k, 1, 0)
        self.copy(3 * self.nz - 1 + k).start()

    def finish(self):
        for k in range(self.nz):
            self.arrived(k, 0, 1)
            self.arrived(k, 1, 1)
        for index in range(len(self.moves)):
            self.copy(index).wait_send()


CHUNKS = 4


class Deal:
    def __init__(self, nd, spans, table, rows, out, tok, send, recv, other, sems):
        self.nd, self.spans, self.table, self.rows, self.out = nd, spans, table, rows, out
        self.tok, self.sent, self.recv, self.other = tok, send, recv, other
        self.load_sem, self.a2a_send, self.a2a_recv, self.x_send, self.x_recv, self.c_send, self.c_recv = sems
        self.dp, self.x, self.core = lax.axis_index("dp"), lax.axis_index("x"), lax.axis_index("core")
        self.quarter = out.shape[1] // 4
        self.cap = send.shape[1]
        self.mine = pl.multiple_of((2 * self.x + self.core) * self.quarter, 128)
        self.theirs = pl.multiple_of((2 * (1 - self.x) + self.core) * self.quarter, 128)
        self.load = pltpu.make_async_copy(rows.at[:, :, pl.ds(self.mine, self.quarter)], tok, self.load_sem.at[0])
        self.started = []

    def begin(self):
        self.load.start()

    def exchange(self):
        self.load.wait()
        cap, nd = self.cap, self.nd

        def pick(k, out, base):
            d = lax.rem(self.dp + k, nd)
            for j in range(cap):
                out[base + j] = self.tok[self.table[d * cap + j]]

        here = self.dp * cap
        for k in range(1, nd):
            pick(k, self.sent.at[k], 0)
            copy = copy_to(
                self.sent.at[k],
                self.recv.at[pl.ds(here, cap)],
                self.a2a_send.at[k],
                self.a2a_recv.at[k],
                {"dp": lax.rem(self.dp + k, nd)},
            )
            copy.start()
            self.started.append(copy)
        pick(0, self.recv, here)

    def across(self):
        for copy in self.started:
            copy.wait_recv()
        spans, nd = self.spans, self.nd
        count = spans // CHUNKS
        first = nd * self.cap
        self.x_copies, self.c_copies = [], []
        for c in range(CHUNKS):
            rows = pl.ds(c * count * SPAN, count * SPAN)

            def body(i, _, c=c):
                at = c * count + i
                to = pl.ds(pl.multiple_of(at * SPAN, SPAN), SPAN)
                self.other[to, :] = self.recv[self.table[first + spans + at]]
                return 0

            lax.fori_loop(0, count, body, 0)
            copy = copy_to(
                self.other.at[rows, :],
                self.out.at[rows, pl.ds(self.mine, self.quarter)],
                self.x_send.at[c],
                self.x_recv.at[c],
                {"x": 1 - self.x},
            )
            copy.start()
            self.x_copies.append(copy)

        def body(i, _):
            to = pl.ds(pl.multiple_of(i * SPAN, SPAN), SPAN)
            self.out[to, pl.ds(self.mine, self.quarter)] = self.recv[self.table[first + i]]
            return 0

        lax.fori_loop(0, spans, body, 0)
        self.pass_on(slice(None), self.mine, CHUNKS)

    def pass_on(self, rows, col, sem):
        at = self.out.at[rows, pl.ds(col, self.quarter)]
        copy = copy_to(at, at, self.c_send.at[sem], self.c_recv.at[sem], {"core": 1 - self.core})
        copy.start()
        self.c_copies.append(copy)

    def finish(self):
        count = self.spans // CHUNKS
        for c, copy in enumerate(self.x_copies):
            copy.wait_recv()
            self.pass_on(pl.ds(c * count * SPAN, count * SPAN), self.theirs, c)
        for copy in self.c_copies:
            copy.wait_recv()
        for copy in self.x_copies + self.c_copies:
            copy.wait_send()

    def release(self):
        for copy in self.started:
            copy.wait_send()


def deal_buffers(nd, per_dev, spans, quarter, cap):
    return [
        pltpu.VMEM((per_dev, SPAN, quarter), BF),
        pltpu.VMEM((nd, cap, SPAN, quarter), BF),
        pltpu.VMEM((spans * SPAN, quarter), BF),
        pltpu.VMEM((nd * cap, SPAN, quarter), BF),
        pltpu.VMEM((nd * cap, SPAN, quarter), BF),
    ]


def deal_sems(nd):
    dma = pltpu.SemaphoreType.DMA
    return [dma((1,)), dma((nd,)), dma((nd,)), dma((CHUNKS,)), dma((CHUNKS,)), dma((CHUNKS + 1,)), dma((CHUNKS + 1,))]


SMALL = 184


class Small:
    def __init__(self, nd, pack, sent, got, norms, sems):
        self.nd, self.pack, self.sent, self.got, self.norms = nd, pack, sent, got, norms
        self.send, self.recv, self.norm_send, self.norm_recv, self.end_send, self.end_recv = sems
        self.dp, self.x, self.core = lax.axis_index("dp"), lax.axis_index("x"), lax.axis_index("core")

    def fill(self, gain_first, gain_second, down, up, bias, head):
        pack = self.pack
        for r in range(8):
            lanes = slice(r * 128, (r + 1) * 128)
            pack[r : r + 1] = gain_first[0:1, lanes]
            pack[8 + r : 9 + r] = gain_second[0:1, lanes]
            pack[16 + 16 * r : 32 + 16 * r] = down[:, lanes]
        for h in range(2):
            lanes = slice(h * 128, (h + 1) * 128)
            pack[144 + 16 * h : 160 + 16 * h] = up[:, lanes]
            pack[176 + h : 177 + h] = bias[0:1, lanes]
            pack[178 + h : 179 + h] = head[0:1, lanes]
        pack[180:] = jnp.zeros((4, 128), F32)

    def copy(self, step):
        if step == 0:
            target = {"x": 1 - self.x}
        else:
            bit = 1 << (step - 1)
            on = lax.rem(self.dp // bit, 2)
            target = {"dp": self.dp + bit - 2 * bit * on}
        return copy_to(self.sent.at[step], self.got.at[step], self.send.at[step], self.recv.at[step], target)

    def steps(self):
        return self.nd.bit_length()

    def begin(self, step):
        self.sent[step] = self.pack[...]
        self.copy(step).start()

    def end(self, step):
        self.copy(step).wait()
        self.pack[...] = self.pack[...] + self.got[step]

    def core_copy(self, step, src, dst, target):
        return copy_to(src, dst, self.end_send.at[step], self.end_recv.at[step], target)

    def head(self):
        at = self.nd + 5
        return self.core_copy(0, self.norms.at[at], self.norms.at[at + 1], {"core": 1 - self.core})

    def begin_head(self):
        self.norms[self.nd + 5] = self.pack[176:184]
        self.head().start()

    def end_head(self):
        self.head().wait()
        self.pack[178:180] = self.pack[178:180] + self.norms[self.nd + 6, 2:4]

    def squares(self):
        nd, v = self.nd, self.pack[...]
        v = v * v
        down = fold(v[16:144])
        up = fold(v[144:176])
        row = lax.broadcasted_iota(jnp.int32, (8, 128), 0)
        tail = v[176:184]
        tail = jnp.where(row < 2, tail / (2 * nd), jnp.where(row < 4, tail / (4 * nd), 0.0))
        return (v[0:8] + v[8:16] + down) / (4 * nd) + up / (2 * nd) + tail

    def norm_copy(self, k):
        return copy_to(
            self.norms.at[self.nd],
            self.norms.at[self.dp],
            self.norm_send.at[k],
            self.norm_recv.at[k],
            {"dp": lax.rem(self.dp + k, self.nd)},
        )

    def begin_norm(self, value):
        self.norms[self.nd] = value
        self.norms[self.dp] = value
        for k in range(1, self.nd):
            self.norm_copy(k).start()

    def end_norm(self, out):
        nd = self.nd
        for k in range(1, nd):
            self.norm_copy(k).wait()
        total = self.norms[0]
        for k in range(1, nd):
            total = total + self.norms[k]
        for step, target in ((1, {"x": 1 - self.x}), (2, {"core": 1 - self.core})):
            at = nd - 1 + 2 * step
            self.norms[at] = total
            copy = self.core_copy(step, self.norms.at[at], self.norms.at[at + 1], target)
            copy.start()
            copy.wait()
            total = total + self.norms[at + 1]
        out[...] = total


def small_scratch(nd):
    dma = pltpu.SemaphoreType.DMA
    steps = nd.bit_length()
    return [
        pltpu.VMEM((steps, SMALL, 128), F32), pltpu.VMEM((steps, SMALL, 128), F32), pltpu.VMEM((nd + 7, 8, 128), F32),
        dma((steps,)), dma((steps,)), dma((nd,)), dma((nd,)), dma((3,)), dma((3,)),
    ]


PIECES = 5


def fetch(pairs, sems):
    copies = [pltpu.make_async_copy(src, dst, sems.at[k]) for k, (src, dst) in enumerate(pairs)]
    for copy in copies:
        copy.start()
    return copies


class Undeal:
    def __init__(self, nd, spans, table, own, cross, joined, sent, gath, sems):
        self.nd, self.spans, self.table, self.own, self.cross = nd, spans, table, own, cross
        self.joined, self.sent, self.gath = joined, sent, gath
        self.x_send, self.x_recv, self.a2a_send, self.a2a_recv, *self.wide_sems = sems
        self.dp, self.x, self.core = lax.axis_index("dp"), lax.axis_index("x"), lax.axis_index("core")
        self.cap = sent.shape[1]
        self.quarter = own.shape[2]
        self.wide = gath.shape[2] != self.quarter
        self.mine, self.theirs = 0, 0
        if self.wide:
            self.mine = pl.multiple_of((2 * self.x + self.core) * self.quarter, 128)
            self.theirs = pl.multiple_of((2 * (1 - self.x) + self.core) * self.quarter, 128)

    def swap(self, i):
        count = self.spans // PIECES
        return copy_to(
            self.cross.at[pl.ds(i * count, count)],
            self.joined.at[pl.ds(self.x * self.spans + i * count, count)],
            self.x_send.at[i],
            self.x_recv.at[i],
            {"x": 1 - self.x},
        )

    def begin(self):

        def body(i, _):
            self.joined[self.x * self.spans + i] = self.own[i]
            return 0

        lax.fori_loop(0, self.spans, body, 0)

    def block(self, dp, col):
        return self.gath.at[pl.ds(dp * self.cap, self.cap), :, pl.ds(col, self.quarter)]

    def a2a(self, k):
        return copy_to(
            self.sent.at[k],
            self.block(self.dp, self.mine),
            self.a2a_send.at[k],
            self.a2a_recv.at[k],
            {"dp": lax.rem(self.dp + k, self.nd)},
        )

    def exchange(self):
        for i in range(PIECES):
            self.swap(i).wait_recv()
        cap = self.cap
        for k in range(1, self.nd):
            d = lax.rem(self.dp + k, self.nd)
            for j in range(cap):
                self.sent[k, j] = self.joined[self.table[d * cap + j]]
            self.a2a(k).start()
        here = self.block(self.dp, self.mine)
        for j in range(cap):
            here[j] = self.joined[self.table[self.dp * cap + j]]
        if self.wide:
            self.widen(0, 0).start()
            self.widen(0, 1).start()

    def widen(self, k, step):
        at = self.block(lax.rem(self.dp + self.nd - k, self.nd), self.theirs if step == 2 else self.mine)
        send, recv = self.wide_sems
        return copy_to(
            at, at, send.at[3 * k + step], recv.at[3 * k + step],
            {"x": 1 - self.x} if step == 0 else {"core": 1 - self.core},
        )

    def arrive(self, k):
        self.a2a(k).wait_recv()
        if self.wide:
            self.widen(k, 0).start()
            self.widen(k, 1).start()

    def finish(self):
        if self.wide:
            for k in range(self.nd):
                self.widen(k, 0).wait_recv()
                self.widen(k, 2).start()
            for k in range(self.nd):
                self.widen(k, 1).wait_recv()
                self.widen(k, 2).wait_recv()
                for step in range(3):
                    self.widen(k, step).wait_send()
        for k in range(1, self.nd):
            self.a2a(k).wait_send()
        for i in range(PIECES):
            self.swap(i).wait_send()


def undeal_scratch(nd, per_dev, spans, quarter, cap, wide):
    dma = pltpu.SemaphoreType.DMA
    buffers = [
        pltpu.VMEM((spans, SPAN, quarter), BF),
        pltpu.VMEM((spans, SPAN, quarter), BF),
        pltpu.VMEM((per_dev, SPAN, quarter), BF),
        pltpu.VMEM((nd, cap, SPAN, quarter), BF),
        pltpu.VMEM((nd * cap, SPAN, quarter * (4 if wide else 1)), BF),
    ]
    sems = [dma((PIECES,)), dma((PIECES,)), dma((nd,)), dma((nd,))]
    return buffers, sems + ([dma((3 * nd,)), dma((3 * nd,))] if wide else [])


def fold(value):
    return jnp.sum(value.reshape(-1, 8, 128), axis=0)


class Collapse:
    def __init__(self, nd, order, acc, pitch, low, rows, got, sems):
        self.nz, self.order, self.acc, self.pitch, self.low, self.rows = nd // 2, order, acc, pitch, low, rows
        self.got = got
        self.send_sems, self.recv_sems = sems
        self.w = got.shape[2]
        dp, self.x = lax.axis_index("dp"), lax.axis_index("x")
        self.z, self.y = dp // 2, lax.rem(dp, 2)

    def window(self, first, second, kz):
        fx, fy = (first, second) if self.order == 0 else (second, first)
        y = 1 - self.y if fy else self.y
        x = 1 - self.x if fx else self.x
        dp = lax.rem(self.z + kz, self.nz) * 2 + y
        return self.acc.at[
            pl.ds(pl.multiple_of(x * self.pitch + self.low, 16), self.rows),
            pl.ds(pl.multiple_of(dp * self.w, 128), self.w),
        ]

    def partner(self, which):
        if (which == 0) == (self.order == 0):
            return {"x": 1 - self.x}
        return {"dp": self.z * 2 + 1 - self.y}

    def slot(self, phase, second, kz):
        nz = self.nz
        return second * nz + kz if phase == 1 else (2 * nz + kz if phase == 2 else 3 * nz + kz - 1)

    def copy(self, phase, second, kz):
        at = self.slot(phase, second, kz)
        if phase == 1:
            src, target = self.window(1, second, kz), self.partner(0)
        elif phase == 2:
            src, target = self.window(0, 1, kz), self.partner(1)
        else:
            src, target = self.window(0, 0, kz), {"dp": lax.rem(self.z + kz, self.nz) * 2 + self.y}
        return copy_to(src, self.got.at[at], self.send_sems.at[at], self.recv_sems.at[at], target)

    def add(self, second, kz, at):
        here = self.window(0, second, kz)
        here[...] = (here[...].astype(F32) + self.got[at].astype(F32)).astype(BF)

    def begin(self):
        for second in (1, 0):
            for kz in range(self.nz):
                self.copy(1, second, (kz + 1) % self.nz).start()

    def second(self, kz):
        self.copy(1, 1, kz).wait_recv()
        self.add(1, kz, self.slot(1, 1, kz))
        self.copy(2, 1, kz).start()

    def third(self, kz):
        self.copy(1, 0, kz).wait_recv()
        self.add(0, kz, self.slot(1, 0, kz))
        self.copy(2, 1, kz).wait_recv()
        self.add(0, kz, self.slot(2, 1, kz))
        if kz:
            self.copy(3, 0, kz).start()

    def finish(self, out, squares):
        total = self.window(0, 0, 0)[...].astype(F32)
        for kz in range(1, self.nz):
            self.copy(3, 0, kz).wait_recv()
            total = total + self.got[self.slot(3, 0, kz)].astype(F32)
        out[...] = total
        squares[...] += fold(total * total)
        for kz in range(self.nz):
            self.copy(1, 0, kz).wait_send()
            self.copy(1, 1, kz).wait_send()
            self.copy(2, 1, kz).wait_send()
            if kz:
                self.copy(3, 0, kz).wait_send()


def collapse_scratch(nd, rows, w):
    count = 4 * (nd // 2) - 1
    dma = pltpu.SemaphoreType.DMA
    return [pltpu.VMEM((count, rows, w), BF), dma((count,)), dma((count,))]


def progress(chains, nz, between=()):
    between = list(between)
    for kz in [k % nz for k in range(1, nz + 1)]:
        for chain in chains:
            chain.second(kz)
        if between:
            between.pop(0)()
    for kz in [k % nz for k in range(1, nz + 1)]:
        for chain in chains:
            chain.third(kz)
        if between:
            between.pop(0)()
    for work in between:
        work()


PROJ_ROWS = 16 + HEAD + DV
PROJ_CUTS = ((0, 528), (528, 512))


def forward_kernel(nd, spans, reach, gather, table, ints, tokens, cotangent, shard_p, shard_f, gain, up, bias, head_gain,
                   ups, level, *rest):
    outs, rest = rest[:13], rest[13:]
    (src_o, cot_o, wp_o, wf_o, normed_o, qkvg_o, log_decay_o, rank_o, mixed_o, gated_o, attn_o, before_o, attn_other) = outs
    (src, cot, wp, wf, normed, qkvg, log_decay, rank, mixed, gated, attn, before), rest = rest[:12], rest[12:]
    (packet, factors, sent_packets, got_packets), rest = rest[:4], rest[4:]
    (tok, sent, other, recv_t, recv_c), rest = rest[:5], rest[5:]
    sems_t, sems_c, rest = rest[:7], rest[7:14], rest[14:]
    carry_send, carry_recv, core_send, core_recv, out_sems, own_sems, *ag_sems = rest
    tiles = spans * SPAN // TILE
    carry = Carry(nd, reach, 1, packet, sent_packets, got_packets, carry_send, carry_recv)
    enter(nd, carry.shifts())
    deal = Deal(nd, spans, table, tokens, src, tok, sent, recv_t, other, sems_t)
    deal_c = Deal(nd, spans, table, cotangent, cot, tok, sent, recv_c, other, sems_c)
    deal.begin()
    local = []
    spreads_p, spreads_f = [], []
    if gather:
        w = shard_p.shape[1]
        f3 = shard_f.shape[0]
        f = f3 // 3
        cuts_p = [(k, low, count, PROJ_ROWS, low) for k, (low, count) in enumerate(PROJ_CUTS)]
        cuts_f = [
            (0, 0, f, f, 0), (1, 2 * f, f, f, 4 * f), (0, f, f // 2, f, 2 * f), (1, f + f // 2, f // 2, f, 2 * f + f // 2),
        ]

        def window(buffer, count, pitch, base, dp, x):
            return buffer.at[
                pl.ds(pl.multiple_of(x * pitch + base, 16), count), pl.ds(pl.multiple_of(dp * w, 128), w)
            ]

        for shard, buffer, cuts, spreads in ((shard_p, wp, cuts_p, spreads_p), (shard_f, wf, cuts_f, spreads_f)):
            for order, low, count, pitch, base in cuts:
                piece = shard.at[pl.ds(low, count), :]
                place = functools.partial(window, buffer, count, pitch, base)
                copy = pltpu.make_async_copy(
                    piece, place(lax.axis_index("dp"), lax.axis_index("x")), own_sems.at[len(local)]
                )
                copy.start()
                local.append(copy)
                k = 2 * (len(local) - 1)
                spreads.append(Spread(nd, order, piece, place, ag_sems[k], ag_sems[k + 1]))
    else:
        for shard, buffer in ((shard_p, wp), (shard_f, wf)):
            local.append(pltpu.make_async_copy(shard, buffer, own_sems.at[len(local)]))
            local[-1].start()
    outgoing = []

    def store(value, out):
        outgoing.append(pltpu.make_async_copy(value, out, out_sems.at[len(outgoing)]))
        outgoing[-1].start()

    def relay_z(spreads, k):
        for spread in spreads:
            spread.relay_z(k)

    def relay_first(spreads, k):
        for spread in spreads:
            spread.relay_first(k)

    nz = nd // 2
    last_z = range(1, nz) if gather else ()
    last_first = range(nz) if gather else ()
    for spread in spreads_p:
        spread.begin()
    deal.exchange()
    for k in last_first[0:1]:
        relay_first(spreads_p, k)
    deal_c.begin()
    for k in last_z[0:1]:
        relay_z(spreads_p, k)
    for k in last_z[1:2]:
        relay_z(spreads_p, k)
    for k in last_first[1:2]:
        relay_first(spreads_p, k)
    for spread in spreads_f:
        spread.begin()
    for k in last_z[2:3]:
        relay_z(spreads_p, k)
    for k in last_first[2:3]:
        relay_first(spreads_p, k)
    for k in last_first[3:4]:
        relay_first(spreads_p, k)
    for k in last_first[0:1]:
        relay_first(spreads_f, k)
    deal.across()
    deal.release()
    deal_c.exchange()
    for k in last_z[0:1]:
        relay_z(spreads_f, k)
    for k in last_first[1:2]:
        relay_first(spreads_f, k)
    deal.finish()
    for k in last_z[1:2]:
        relay_z(spreads_f, k)
    for spread in spreads_p:
        spread.finish()
    for copy in local:
        copy.wait()
    store(src, src_o)
    store(wp, wp_o)

    def at(ref, i):
        return ref.at[pl.ds(pl.multiple_of(i * TILE, TILE), TILE), :]

    packet[...] = jnp.zeros_like(packet)
    packet[2 * DV : 2 * DV + 2] = jnp.ones((2, DK), F32)

    def project(i, _):
        project_kernel(
            i, ints, at(src, i), gain, wp, up, bias, ups,
            at(normed, i), at(qkvg, i), at(log_decay, i), at(rank, i), packet,
        )
        return 0

    lax.fori_loop(0, tiles // 2, project, 0)
    for k in last_z[2:3]:
        relay_z(spreads_f, k)
    for k in last_first[2:3]:
        relay_first(spreads_f, k)
    lax.fori_loop(tiles // 2, tiles, project, 0)
    factors[...] = packet[2 * DV :]
    carry.send(0)
    store(normed, normed_o)
    store(qkvg, qkvg_o)
    store(log_decay, log_decay_o)
    store(rank, rank_o)
    for k in last_first[3:4]:
        relay_first(spreads_f, k)

    def within(i, _):
        within_kernel(at(qkvg, i), at(log_decay, i), ups, level, at(mixed, i))
        return 0

    stages = carry.run()
    for stage in range(stages):
        lax.fori_loop(tiles * stage // stages, tiles * (stage + 1) // stages, within, 0)
        carry.step(stage)
    deal_c.across()
    per_tile = TILE // SPAN

    def mix(i, _):
        mix_kernel(
            i, ints, at(qkvg, i), at(log_decay, i), packet, ups, head_gain, wp,
            at(mixed, i), at(gated, i), at(attn, i), before.at[pl.ds(i * per_tile, per_tile)],
        )
        return 0

    lax.fori_loop(0, tiles, mix, 0)
    swap_attn = copy_to(
        attn, attn_other, core_send.at[0], core_recv.at[0], {"core": 1 - lax.axis_index("core")}
    )
    swap_attn.start()
    store(mixed, mixed_o)
    store(gated, gated_o)
    store(attn, attn_o)
    store(before, before_o)
    deal_c.finish()
    store(cot, cot_o)
    for spread in spreads_f:
        spread.finish()
    store(wf, wf_o)
    deal_c.release()
    swap_attn.wait()
    for copy in outgoing:
        copy.wait()


def forward(table, ints, tokens, cotangent, shard_p, shard_f, gain, up, bias, head_gain, ups, level, nd, spans, reach, gather):
    d = tokens.shape[1]
    per_dev = tokens.shape[0] // SPAN
    cap = -(-per_dev // nd)
    rows = spans * SPAN
    dma = pltpu.SemaphoreType.DMA
    nz = nd // 2
    wf_rows = shard_f.shape[0] * (2 if gather else 1)
    kept = [
        ((rows, d), BF), ((rows, d), BF), ((2 * PROJ_ROWS, d), BF), ((wf_rows, d), BF), ((rows, d), BF),
        ((rows, 2 * HEAD), BF), ((rows, 2 * DK), F32), ((rows, 16), BF), ((rows, 2 * DV), F32), ((rows, 2 * DV), BF),
        ((rows, d), BF), ((spans, 2, DV, DK), BF),
    ]
    widths, _ = carry_widths(reach)
    steps = len(widths) + 2
    scratch = [pltpu.VMEM(shape, dtype) for shape, dtype in kept]
    scratch += [
        pltpu.VMEM((2 * DV + 16, DK), F32),
        pltpu.VMEM((steps - 1, 2 * DV + 16, DK), BF),
        pltpu.VMEM((steps, 2 * DV + 16, DK), BF),
    ]
    scratch += deal_buffers(nd, per_dev, spans, d // 4, cap) + deal_sems(nd) + deal_sems(nd)
    scratch += [dma((steps,)), dma((steps,)), dma((1,)), dma((1,)), dma((12,)), dma((6,))]
    if gather:
        scratch += [dma((4 * nz - 1,)), dma((4 * nz,))] * 6
    outs = [sds(*shape, dtype=dtype) for shape, dtype in kept] + [sds(rows, d, dtype=BF)]
    outs.append(sds(16, DK))
    specs = [ANY] * 13 + [VMEM]

    def kernel(*refs):
        n_in = 12
        ins, rest = refs[:n_in], refs[n_in:]
        results, factors, buffers = rest[:13], rest[13], rest[14:]
        forward_kernel(
            nd, spans, reach, gather, *ins, *results, *buffers[:12], buffers[12], factors, *buffers[13:]
        )

    return pl.pallas_call(
        kernel,
        in_specs=[SMEM, SMEM, ANY, ANY, ANY, ANY] + [VMEM] * 6,
        out_specs=specs,
        out_shape=outs,
        scratch_shapes=scratch,
        name="forward",
        compiler_params=pltpu.CompilerParams(
            vmem_limit_bytes=VMEM_LIMIT, collective_id=0, has_side_effects=True
        ),
        cost_estimate=cost(150),
    )(
        table, ints, tokens.reshape(per_dev, SPAN, d), cotangent.reshape(per_dev, SPAN, d), shard_p, shard_f,
        gain, up, bias, head_gain, ups, level,
    )


def rms_scale(x):
    return lax.rsqrt(jnp.mean(x * x, axis=-1, keepdims=True) + norm_eps)


def distances(ups, log_decay):
    high = log_decay.astype(BF)
    lower = (log_decay - high.astype(F32)).astype(BF)
    return dot(ups, high) + dot(ups, lower)


def head_cols(h, part):
    start = h * HEAD + (0, DK, 2 * DK, 2 * DK + DV)[part]
    return slice(start, start + (DK, DK, DV, DV)[part])


def in_rows(h):
    return slice(h * PROJ_ROWS + 16, h * PROJ_ROWS + 16 + HEAD)


def out_rows(h):
    return slice(h * PROJ_ROWS + 16 + HEAD, (h + 1) * PROJ_ROWS)


def log_sigmoid(v):
    return jnp.minimum(v, 0.0) - jnp.log(1.0 + jnp.exp(-jnp.abs(v)))


def project_kernel(
    step, ints, src, gain, weights, up, bias, ups,
    normed, qkvg, log_decay, rank, packet,
):
    x = src[...].astype(F32)
    nf = (x * rms_scale(x) * gain[...]).astype(BF)
    normed[...] = nf
    low = dot(nf, weights[0:16, :], 1, 1).astype(BF)
    rank[...] = low
    logits = dot(low, up[...]) + bias[...]
    ld = log_sigmoid(logits) * (1.0 / decay_scale)
    log_decay[...] = ld
    towards = jnp.exp(distances(ups[LEVELS + 1], ld))
    per_tile = TILE // SPAN
    for h in range(2):
        proj = dot(nf, weights[in_rows(h), :], 1, 1)
        qkvg[:, head_cols(h, 0)] = (proj[:, :DK] * scaling).astype(BF)
        qkvg[:, h * HEAD + DK : (h + 1) * HEAD] = proj[:, DK:].astype(BF)
    for j in range(per_tile):
        rows = slice(j * SPAN, (j + 1) * SPAN)
        keep = ints[step * per_tile + j].astype(F32)
        total = jnp.exp(jnp.sum(ld[rows], axis=0, keepdims=True)) * keep
        for h in range(2):
            lanes = slice(h * DK, (h + 1) * DK)
            states = slice(h * DV, (h + 1) * DV)
            f = slice(2 * DV + h, 2 * DV + h + 1)
            packet[f] = packet[f] * total[:, lanes]
            kd = (qkvg[rows, head_cols(h, 1)].astype(F32) * towards[rows, lanes]).astype(BF)
            packet[states] = packet[states] * total[:, lanes] + dot(qkvg[rows, head_cols(h, 2)], kd, 0, 0)


def within_kernel(qkvg, log_decay, ups, level, within):
    ld = log_decay[...]
    high = ld.astype(BF)
    lower = (ld - high.astype(F32)).astype(BF)
    lev = level[...]
    scores = [None, None]
    for l in range(LEVELS + 1):
        if l < LEVELS:
            x = jnp.exp(dot(ups[l], high) + dot(ups[l], lower))
        for h in range(2):
            q, k = qkvg[:, head_cols(h, 0)], qkvg[:, head_cols(h, 1)]
            if l < LEVELS:
                xh = x[:, h * DK : (h + 1) * DK]
                q = (q.astype(F32) * xh).astype(BF)
                k = (k.astype(F32) * xh).astype(BF)
            s = dot(q, k, 1, 1)
            scores[h] = jnp.where(lev == l, s, 0.0 if l == 0 else scores[h])
    for h in range(2):
        within[:, h * DV : (h + 1) * DV] = dot(scores[h].astype(BF), qkvg[:, head_cols(h, 2)])


def mix_kernel(
    step, ints, qkvg, log_decay, packet, ups, head_gain, weights,
    mixed, gated, attn, before,
):
    per_tile = TILE // SPAN
    ld = log_decay[...]
    since = jnp.exp(distances(ups[LEVELS], ld))
    towards = jnp.exp(distances(ups[LEVELS + 1], ld))
    for j in range(per_tile):
        rows = slice(j * SPAN, (j + 1) * SPAN)
        keep = ints[step * per_tile + j].astype(F32)
        for h in range(2):
            lanes = slice(h * DK, (h + 1) * DK)
            values = slice(h * DV, (h + 1) * DV)
            prev = packet[values] * keep
            prev_low = prev.astype(BF)
            before[j, h] = prev_low
            qd = (qkvg[rows, head_cols(h, 0)].astype(F32) * since[rows, lanes]).astype(BF)
            kd = (qkvg[rows, head_cols(h, 1)].astype(F32) * towards[rows, lanes]).astype(BF)
            mixed[rows, values] = mixed[rows, values] + dot(qd, prev_low, 1, 1)
            last = since[j * SPAN + SPAN - 1 : j * SPAN + SPAN, lanes]
            packet[values] = prev * last + dot(qkvg[rows, head_cols(h, 2)], kd, 0, 0)
    for h in range(2):
        values = slice(h * DV, (h + 1) * DV)
        m = mixed[:, values]
        g = qkvg[:, head_cols(h, 3)].astype(F32)
        y = m * rms_scale(m) * head_gain[...] * g * jax.nn.sigmoid(g)
        gated[:, values] = y.astype(BF)
    attn[...] = (
        dot(gated[:, :DV], weights[out_rows(0), :]) + dot(gated[:, DV:], weights[out_rows(1), :])
    ).astype(BF)


def ffn_kernel(
    ints, src, attn_a, attn_b, cot, gain, weights,
    hidden, normed, act, grad_gu, keep_out, send_out, grad_second,
    part,
):
    quarter = cot.shape[1] // 4
    hid = src[...].astype(F32) + (attn_a[...].astype(F32) + attn_b[...].astype(F32))
    hidden[...] = hid
    ns = (hid * rms_scale(hid) * gain[...]).astype(BF)
    normed[...] = ns
    f = act.shape[1]
    w_gate, w_out, w_up = (slice(k * f, (k + 1) * f) for k in range(3))
    gate = dot(ns, weights[w_gate, :], 1, 1)
    upper = dot(ns, weights[w_up, :], 1, 1)
    sig = jax.nn.sigmoid(gate)
    swish = gate * sig
    low = (swish * upper).astype(BF)
    act[...] = low
    ga = dot(cot[...], weights[w_out, :], 1, 1)
    part[...] = dot(low, weights[w_out, :]).astype(BF)
    gg = (ga * upper * sig * (1.0 + gate * (1.0 - sig))).astype(BF)
    gu = (ga * swish).astype(BF)
    grad_gu[:, :f] = gg
    grad_gu[:, f:] = gu
    grad_second[...] = (dot(gg, weights[w_gate, :]) + dot(gu, weights[w_up, :])).astype(BF)
    core = ints[4]
    for h in range(2):
        mine = pl.multiple_of((2 * h + core) * quarter, 128)
        theirs = pl.multiple_of((2 * h + 1 - core) * quarter, 128)
        keep_out[:, h * quarter : (h + 1) * quarter] = part[:, pl.ds(mine, quarter)]
        send_out[:, h * quarter : (h + 1) * quarter] = part[:, pl.ds(theirs, quarter)]


def weight_grad_into(acc, lhs, rhs, first=0, count=None):
    def body(i, _):
        at = pl.multiple_of(i * 128, 128)
        acc[pl.ds(at, 128), :] = dot(lhs[:, pl.ds(at, 128)], rhs[...], 0, 0).astype(BF)
        return 0

    last = acc.shape[0] // 128 if count is None else first + count
    lax.fori_loop(first, last, body, 0)


def out_back_kernel(
    n, ints, hidden, cot, gs_a, gs_b, gain, weights, gated, mixed, qkvg, log_decay, head_gain, ups,
    keep_out, recv_out,
    grad_hidden, grad_mixed, grad_gate, gain_grad, head_grad, packet, out_own, out_cross, *rest,
):
    w_grads, (acc, state, gain_sum, head_sum) = rest[:-4], rest[-4:]
    step = pl.program_id(0)
    tile = n - 1 - step
    per_tile = TILE // SPAN

    @pl.when(step == 0)
    def _():
        acc[...] = jnp.zeros_like(acc)
        state[...] = jnp.zeros_like(state)
        gain_sum[...] = jnp.zeros_like(gain_sum)
        head_sum[...] = jnp.zeros_like(head_sum)

    x, core = ints[7], ints[4]
    quarter = out_own.shape[1]
    for target, half in ((out_own, x), (out_cross, 1 - x)):
        at = pl.multiple_of((2 * half + core) * quarter, 128)
        pair = pl.multiple_of(half * quarter, 128)
        share = keep_out[:, pl.ds(pair, quarter)].astype(F32) + recv_out[:, pl.ds(pair, quarter)].astype(F32)
        target[...] = (hidden[:, pl.ds(at, quarter)] + share).astype(BF)
    gs = gs_a[...].astype(F32) + gs_b[...].astype(F32)
    hid = hidden[...]
    inv = rms_scale(hid)
    normal = hid * inv
    gain_sum[0:1, :] += jnp.sum(gs * normal, axis=0, keepdims=True)
    e = gs * gain[...]
    gh = cot[...].astype(F32) + inv * (e - normal * jnp.mean(e * normal, axis=-1, keepdims=True))
    grad_hidden[...] = gh
    low = gh.astype(BF)
    acc[...] += dot(gated[...], low, 0, 0)
    for h in range(2):
        values = slice(h * DV, (h + 1) * DV)
        m = mixed[:, values]
        inv_head = rms_scale(m)
        nh = m * inv_head
        g = qkvg[:, head_cols(h, 3)].astype(F32)
        sig = jax.nn.sigmoid(g)
        w = g * sig
        gd = dot(low, weights[out_rows(h), :], 1, 1)
        head_sum[0:1, :] += jnp.sum(gd * nh * w, axis=0, keepdims=True)
        gn = gd * head_gain[...]
        grad_gate[:, values] = (gn * nh * sig * (1.0 + g * (1.0 - sig))).astype(BF)
        gn = gn * w
        gm = inv_head * (gn - nh * jnp.mean(gn * nh, axis=-1, keepdims=True))
        grad_mixed[:, values] = gm.astype(BF)
    since = jnp.exp(distances(ups[LEVELS], log_decay[...]))
    for j in reversed(range(per_tile)):
        rows = slice(j * SPAN, (j + 1) * SPAN)
        keep = ints[8 + tile * per_tile + j].astype(F32)
        for h in range(2):
            lanes = slice(h * DK, (h + 1) * DK)
            values = slice(h * DV, (h + 1) * DV)
            qd = (qkvg[rows, head_cols(h, 0)].astype(F32) * since[rows, lanes]).astype(BF)
            last = since[j * SPAN + SPAN - 1 : j * SPAN + SPAN, lanes]
            state[h] = keep * (state[h] * last + dot(grad_mixed[rows, values], qd, 0, 0))

    @pl.when(step == n - 1)
    def _():
        packet[0:DV] = state[0]
        packet[DV : 2 * DV] = state[1]
        gain_grad[...] = gain_sum[...]
        head_grad[...] = head_sum[...]
        w_grads[0][...] = acc[...].astype(BF)


def within_back_kernel(qkvg, log_decay, grad_mixed, ups, downs, level, level_t, grad_qk, grad_v, grad_ld):
    ld = log_decay[...]
    high = ld.astype(BF)
    lower = (ld - high.astype(F32)).astype(BF)
    lev, lev_t = level[...], level_t[...]
    gd, gd_t = [], []
    for h in range(2):
        v, gm = qkvg[:, head_cols(h, 2)], grad_mixed[:, h * DV : (h + 1) * DV]
        gd.append(dot(gm, v, 1, 1))
        gd_t.append(dot(v, gm, 1, 1))
    scores_t = [None, None]
    grad_q, grad_k = [None, None], [None, None]
    for l in range(LEVELS + 1):
        if l < LEVELS:
            x = jnp.exp(dot(ups[l], high) + dot(ups[l], lower))
        parts = []
        for h in range(2):
            q, k = qkvg[:, head_cols(h, 0)], qkvg[:, head_cols(h, 1)]
            if l < LEVELS:
                xh = x[:, h * DK : (h + 1) * DK]
                qf, kf = q.astype(F32) * xh, k.astype(F32) * xh
                q, k = qf.astype(BF), kf.astype(BF)
            s = dot(k, q, 1, 1)
            scores_t[h] = jnp.where(lev_t == l, s, 0.0 if l == 0 else scores_t[h])
            here = jnp.where(lev == l, gd[h], 0.0).astype(BF)
            here_t = jnp.where(lev_t == l, gd_t[h], 0.0).astype(BF)
            dq, dk = dot(here, k), dot(here_t, q)
            if l < LEVELS:
                parts.append(qf * dq + kf * dk)
                dq, dk = dq * xh, dk * xh
            grad_q[h] = dq if l == 0 else grad_q[h] + dq
            grad_k[h] = dk if l == 0 else grad_k[h] + dk
        if l < LEVELS:
            both = dot(downs[l], jnp.concatenate(parts, axis=1).astype(BF))
            total = both if l == 0 else total + both
    grad_ld[...] = total
    for h in range(2):
        grad_qk[:, 2 * h * DK : (2 * h + 1) * DK] = grad_q[h]
        grad_qk[:, (2 * h + 1) * DK : (2 * h + 2) * DK] = grad_k[h]
        grad_v[:, h * DV : (h + 1) * DV] = dot(
            scores_t[h].astype(BF), grad_mixed[:, h * DV : (h + 1) * DV]
        ).astype(BF)


def project_back_kernel(
    tile, ints, qkvg, log_decay, grad_mixed, before, grad_qk, grad_v, grad_ld, grad_gate, rank, up, bias,
    ups, downs, weights,
    grad_project, grad_first, rank_part, packet, up_sum, bias_sum, d_since, d_towards, ld_sum,
):
    per_tile = TILE // SPAN
    ld = log_decay[...]
    since = jnp.exp(distances(ups[0], ld))
    towards = jnp.exp(distances(ups[1], ld))
    for j in reversed(range(per_tile)):
        rows = slice(j * SPAN, (j + 1) * SPAN)
        keep = ints[tile * per_tile + j].astype(F32)
        for h in range(2):
            lanes = slice(h * DK, (h + 1) * DK)
            values = slice(h * DV, (h + 1) * DV)
            gm = grad_mixed[rows, values]
            v = qkvg[rows, head_cols(h, 2)]
            qd = qkvg[rows, head_cols(h, 0)].astype(F32) * since[rows, lanes]
            kd = qkvg[rows, head_cols(h, 1)].astype(F32) * towards[rows, lanes]
            prev = before[j, h]
            after = packet[values]
            after_low = after.astype(BF)
            dq = dot(gm, prev)
            dk = dot(v, after_low)
            d_since[rows, lanes] = (qd * dq).astype(BF)
            d_towards[rows, lanes] = (kd * dk).astype(BF)
            dq = grad_qk[rows, 2 * h * DK : (2 * h + 1) * DK] + dq * since[rows, lanes]
            dk = grad_qk[rows, (2 * h + 1) * DK : (2 * h + 2) * DK] + dk * towards[rows, lanes]
            dv = grad_v[rows, values].astype(F32) + dot(kd.astype(BF), after_low, 1, 1)
            grad_project[rows, head_cols(h, 0)] = (dq * scaling).astype(BF)
            grad_project[rows, head_cols(h, 1)] = dk.astype(BF)
            grad_project[rows, head_cols(h, 2)] = dv.astype(BF)
            grad_project[rows, head_cols(h, 3)] = grad_gate[rows, values]
            last = since[j * SPAN + SPAN - 1 : j * SPAN + SPAN, lanes]
            d_last = last * jnp.sum(prev.astype(F32) * after, axis=0, keepdims=True)
            ld_sum[rows, lanes] = grad_ld[rows, lanes] + d_last
            packet[values] = keep * (after * last + dot(gm, qd.astype(BF), 0, 0))
    d_log = ld_sum[...] + dot(downs[0], d_since[...]) + dot(downs[1], d_towards[...])
    logits = dot(rank[...], up[...]) + bias[...]
    gl = (d_log * (1.0 / decay_scale) * jax.nn.sigmoid(-logits)).astype(BF)
    up_sum[...] += dot(rank[...], gl, 0, 0)
    bias_sum[0:1, :] += jnp.sum(gl.astype(F32), axis=0, keepdims=True)
    rank_part[...] = dot(up[...], gl, 1, 1)
    grad_first[...] = (
        dot(grad_project[:, :HEAD], weights[in_rows(0), :])
        + dot(grad_project[:, HEAD:], weights[in_rows(1), :])
    ).astype(BF)


def source_back_kernel(
    src, normed, gf_a, gf_b, rank_a, rank_b, w_down, gain, grad_hidden,
    own, cross, dealt, down_sum, gain_sum,
):
    low = (rank_a[...] + rank_b[...]).astype(BF)
    gf = gf_a[...].astype(F32) + gf_b[...].astype(F32) + dot(low, w_down[...], 0, 0)
    x = src[...].astype(F32)
    inv = rms_scale(x)
    normal = x * inv
    gain_sum[0:1, :] += jnp.sum(gf * normal, axis=0, keepdims=True)
    e = gf * gain[...]
    dealt[...] = (
        grad_hidden[...] + inv * (e - normal * jnp.mean(e * normal, axis=-1, keepdims=True))
    ).astype(BF)
    down_sum[...] += dot(low, normed[...])
    quarter = own.shape[2]
    at_x, at_core = lax.axis_index("x"), lax.axis_index("core")
    for out, half in ((own, at_x), (cross, 1 - at_x)):
        col = pl.multiple_of((2 * half + at_core) * quarter, 128)
        for j in range(TILE // SPAN):
            out[j] = dealt[j * SPAN : (j + 1) * SPAN, pl.ds(col, quarter)]


def back_kernel(nd, spans, reach, direct, f, table, act_in, grad_gu, normed, cot_in, qkvg_in, log_decay_in, mixed_in, packet_in,
                factors, out_own, out_cross, ups, downs, level, level_t, *rest):
    n_sums = 5 if direct else 3
    (leaving, grad_qk_o, grad_v_o, grad_ld_o, gath_o, *sums), rest = rest[: 5 + n_sums], rest[5 + n_sums :]
    (grad_qk, grad_v, grad_ld, sent_packets, got_packets), rest = rest[:5], rest[5:]
    (carry_send, carry_recv, out_sems), rest = rest[:3], rest[3:]
    (joined, sent, gath), rest = rest[:3], rest[3:]
    undeal_sems, rest = rest[:4], rest[4:]
    (act, cot, qkvg, log_decay, grad_mixed, late_sems), rest = rest[:6], rest[6:]
    late = fetch(
        ((act_in, act), (cot_in, cot), (qkvg_in, qkvg), (log_decay_in, log_decay), (mixed_in, grad_mixed)), late_sems
    )
    pitch = act.shape[1] // 2
    tiles = spans * SPAN // TILE
    nz = nd // 2
    carry = Carry(nd, reach, -1, leaving, sent_packets, got_packets, carry_send, carry_recv)
    enter(nd, carry.shifts())
    undeal = Undeal(nd, spans, table, out_own, out_cross, joined, sent, gath, undeal_sems)
    for i in range(PIECES):
        undeal.swap(i).start()
    undeal.begin()
    leaving[: 2 * DV] = packet_in[...]
    leaving[2 * DV :] = factors[...]
    carry.send(0)
    outgoing = []

    def store(value, out):
        outgoing.append(pltpu.make_async_copy(value, out, out_sems.at[len(outgoing)]))
        outgoing[-1].start()

    def at(ref, i):
        return ref.at[pl.ds(pl.multiple_of(i * TILE, TILE), TILE), :]

    def tile(i, _):
        within_back_kernel(
            at(qkvg, i), at(log_decay, i), at(grad_mixed, i), ups, downs, level, level_t,
            at(grad_qk, i), at(grad_v, i), at(grad_ld, i),
        )
        return 0

    def some(first, last):
        return lambda: lax.fori_loop(first, last, tile, 0)

    stages = list(range(carry.run()))

    def advance():
        if stages:
            carry.step(stages.pop(0))

    if direct:
        accs, rest = rest[:3], rest[3:]
        chains = [
            Collapse(nd, order, acc, pitch, low, count, rest[3 * k], rest[3 * k + 1 : 3 * k + 3])
            for k, (acc, order, low, count) in enumerate(
                ((accs[0], 0, 0, f), (accs[1], 1, 0, f), (accs[2], 0, 0, f // 2), (accs[2], 1, f // 2, f // 2))
            )
        ]
        at_x = lax.axis_index("x")
        chunks = 2 * pitch // 128
        part = -(-pitch // 128)
        gate = grad_gu.at[:, pl.ds(0, 2 * pitch)]
        weight_grad_into(accs[0], gate, normed, (chunks - part) * (1 - at_x), part)
        chains[0].begin()
        weight_grad_into(accs[0], gate, normed, part * at_x, chunks - part)
        advance()
        weight_grad_into(accs[1], grad_gu.at[:, pl.ds(2 * pitch, 2 * pitch)], normed)
        chains[1].begin()
        advance()
        for copy in late:
            copy.wait()
        third = -(-chunks // nz)
        for i in range(nz):
            chains[0].second((i + 1) % nz)
            weight_grad_into(accs[2], act, cot, third * i, max(0, min(third, chunks - third * i)))
        for i in range(nz):
            chains[1].second((i + 1) % nz)
        chains[2].begin()
        chains[3].begin()
        undeal.exchange()
        advance()
        for kz in [k % nz for k in range(1, nz + 1)]:
            chains[0].third(kz)
            chains[1].third(kz)
            some(kz, kz + 1)()
        progress(chains[2:], nz, [some(nz, tiles)])
        squares = sums[-1]
        squares[...] = jnp.zeros_like(squares)
        for chain, out in zip(chains, sums):
            chain.finish(out, squares)
    else:
        undeal.exchange()
        weight_grad_into(sums[0], grad_gu.at[:, pl.ds(0, 2 * pitch)], normed)
        weight_grad_into(sums[1], grad_gu.at[:, pl.ds(2 * pitch, 2 * pitch)], normed)
        for copy in late:
            copy.wait()
        weight_grad_into(sums[2], act, cot)
        some(0, tiles)()
        while stages:
            advance()
    store(grad_qk, grad_qk_o)
    store(grad_v, grad_v_o)
    store(grad_ld, grad_ld_o)
    for k in range(1, nd):
        undeal.arrive(k)
    store(gath, gath_o)
    undeal.finish()
    for copy in outgoing:
        copy.wait()


def last_kernel(nd, spans, direct, table, keep, qkvg, log_decay, grad_mixed, before, leaving, grad_qk, grad_v, grad_ld,
                grad_gate, rank, up, bias, ups, downs, weights, src_in, normed_in, hidden_in, gain, po_in, gain_second, head_part, squares_in,
                *rest):
    n_sums = 6 if direct else 1
    (gath_o, down_sum, gain_sum, up_sum, bias_sum, *sums), rest = rest[: 5 + n_sums], rest[5 + n_sums :]
    (packet, grad_project, grad_first, grad_first_other, rank_part, rank_other), rest = rest[:6], rest[6:]
    (d_since, d_towards, ld_sum, dealt), rest = rest[:4], rest[4:]
    (gf_send, gf_recv, rk_send, rk_recv, out_sems), rest = rest[:5], rest[5:]
    (own, cross, joined, sent, gath), rest = rest[:5], rest[5:]
    undeal_sems, rest = rest[:6], rest[6:]
    (src, normed, grad_hidden, late_sems), rest = rest[:4], rest[4:]
    late = fetch(((src_in, src), (normed_in, normed), (hidden_in, grad_hidden)), late_sems)
    tiles = spans * SPAN // TILE
    per_tile = TILE // SPAN
    nz = nd // 2
    enter(nd)
    core = lax.axis_index("core")
    undeal = Undeal(nd, spans, table, own, cross, joined, sent, gath, undeal_sems)
    chains = []
    if direct:
        (po_acc, pi_acc), rest = rest[:2], rest[2:]
        (small_sent, small_got, small_norms), rest = rest[:3], rest[3:]
        small_sems, rest = rest[:6], rest[6:]
        small = Small(nd, sums[4], small_sent, small_got, small_norms, small_sems)
        squares = sums[5]
        squares[...] = squares_in[...]
        small_left = list(range(small.steps()))

        def advance_small():
            if small_left:
                small.end(small_left.pop(0))
                if small_left:
                    small.begin(small_left[0])

        halves = ((pi_acc, 0, HEAD), (pi_acc, 1, HEAD), (po_acc, 0, DV), (po_acc, 1, DV))
        chains = [
            Collapse(
                nd, order, acc, size, order * size // 2, size // 2, rest[3 * k], rest[3 * k + 1 : 3 * k + 3]
            )
            for k, (acc, order, size) in enumerate(halves)
        ]
        fill = pltpu.make_async_copy(po_in, po_acc, out_sems.at[0])
        fill.start()
        fill.wait()
        chains[2].begin()
        chains[3].begin()
    packet[...] = leaving[...]
    for ref in (down_sum, gain_sum, up_sum, bias_sum):
        ref[...] = jnp.zeros_like(ref)

    def at(ref, i):
        return ref.at[pl.ds(pl.multiple_of(i * TILE, TILE), TILE), :]

    def swap_first(i):
        return copy_to(at(grad_first, i), at(grad_first_other, i), gf_send.at[i], gf_recv.at[i], {"core": 1 - core})

    def swap_rank(i):
        return copy_to(rank_part.at[i], rank_other.at[i], rk_send.at[i], rk_recv.at[i], {"core": 1 - core})

    def body(step, _):
        i = tiles - 1 - step
        project_back_kernel(
            i, keep, at(qkvg, i), at(log_decay, i), at(grad_mixed, i), before.at[pl.ds(i * per_tile, per_tile)],
            at(grad_qk, i), at(grad_v, i), at(grad_ld, i), at(grad_gate, i), at(rank, i), up, bias, ups, downs, weights,
            at(grad_project, i), at(grad_first, i), rank_part.at[i], packet, up_sum, bias_sum,
            d_since, d_towards, ld_sum,
        )
        swap_first(i).start()
        swap_rank(i).start()
        return 0

    lax.fori_loop(0, tiles, body, 0)
    if direct:
        for kz in [k % nz for k in range(1, nz + 1)]:
            chains[2].second(kz)
            chains[3].second(kz)

    def finish_tile(step, _):
        i = tiles - 1 - step
        swap_first(i).wait()
        swap_rank(i).wait()
        source_back_kernel(
            at(src, i), at(normed, i), at(grad_first, i), at(grad_first_other, i), rank_part.at[i], rank_other.at[i],
            weights.at[pl.ds(0, 16), :], gain, at(grad_hidden, i),
            own.at[pl.ds(i * per_tile, per_tile)], cross.at[pl.ds(i * per_tile, per_tile)],
            dealt, down_sum, gain_sum,
        )
        undeal.swap(i).start()
        return 0

    for copy in late:
        copy.wait()
    lax.fori_loop(0, tiles, finish_tile, 0)
    undeal.begin()
    if direct:
        small.fill(gain_sum, gain_second, down_sum, up_sum, bias_sum, head_part)
        small.begin(0)
        at_x = lax.axis_index("x")
        part = HEAD // 256
        weight_grad_into(pi_acc, grad_project, normed, 2 * part * (1 - at_x), part)
        chains[0].begin()
        weight_grad_into(pi_acc, grad_project, normed, part, part)
        weight_grad_into(pi_acc, grad_project, normed, 3 * part, part)
        chains[1].begin()
        undeal.exchange()
        weight_grad_into(pi_acc, grad_project, normed, 2 * part * at_x, part)
        advance_small()
        for kz in [k % nz for k in range(1, nz + 1)]:
            chains[2].third(kz)
            chains[3].third(kz)
    else:
        undeal.exchange()
        weight_grad_into(sums[0], grad_project, normed)
    arrivals = [functools.partial(undeal.arrive, k) for k in range(1, nd)]
    if direct:
        for kz in [k % nz for k in range(1, nz + 1)]:
            chains[0].second(kz)
            chains[1].second(kz)
            advance_small()
            if arrivals:
                arrivals.pop(0)()
        while small_left:
            advance_small()
        small.begin_head()
        for kz in [k % nz for k in range(1, nz + 1)]:
            chains[0].third(kz)
            chains[1].third(kz)
            if arrivals:
                arrivals.pop(0)()
        chains[2].finish(sums[2], squares)
        chains[3].finish(sums[3], squares)
        small.end_head()
    for arrive in arrivals:
        arrive()
    if direct:
        chains[0].finish(sums[0], squares)
        chains[1].finish(sums[1], squares)
        small.begin_norm(squares[...] + small.squares())
    undeal.finish()
    out = pltpu.make_async_copy(gath, gath_o, out_sems.at[0])
    out.start()
    if direct:
        small.end_norm(squares)
    out.wait()


def remote(kernel, ins, specs, outs, out_specs, scratch, name, number, us):
    return pl.pallas_call(
        kernel,
        in_specs=specs,
        out_specs=out_specs,
        out_shape=outs,
        scratch_shapes=scratch,
        name=name,
        compiler_params=pltpu.CompilerParams(
            vmem_limit_bytes=VMEM_LIMIT, collective_id=number, has_side_effects=True
        ),
        cost_estimate=cost(us),
    )(*ins)


def all_sum(value, axes, sizes):
    for axis, size in zip(axes, sizes):
        bit = 1
        while bit < size:
            value = value + lax.ppermute(value, axis, [(i, i ^ bit) for i in range(size)])
            bit *= 2
    return value


def square_sum(array):
    return jnp.sum(array * array)


def adam_update(weight, grad, first, second, factor, decay_rate):
    clipped = grad * factor
    first_new = beta_one * first + (1.0 - beta_one) * clipped
    second_new = beta_two * second + (1.0 - beta_two) * clipped * clipped
    first_hat = first_new / (1.0 - beta_one**adam_step)
    second_hat = second_new / (1.0 - beta_two**adam_step)
    master = weight.astype(F32)
    change = -learn_rate * (first_hat / (jnp.sqrt(second_hat) + adam_eps) + decay_rate * master)
    return (grad, first_new, second_new, change)


def swap(value, axis):
    return lax.ppermute(value, axis, [(0, 1), (1, 0)])


def on_device(
    tokens, cotangent, seq_extra, deal, proj_in, decay_down, decay_up, decay_bias, head_gain, proj_out, block_gains,
    ffn_in, ffn_out, first_proj_in, second_proj_in, first_decay_down, second_decay_down, first_decay_up,
    second_decay_up, first_decay_bias, second_decay_bias, first_head_gain, second_head_gain, first_proj_out,
    second_proj_out, first_block_gains, second_block_gains, first_ffn_in, second_ffn_in, first_ffn_out, second_ffn_out,
):
    d = tokens.shape[1]
    nd = lax.axis_size("dp")
    nz = nd // 2
    dp, x, core = lax.axis_index("dp"), lax.axis_index("x"), lax.axis_index("core")
    z, y = dp // 2, dp % 2
    tensor = 2 * x + core
    per_dev = tokens.shape[0] // SPAN
    spans = per_dev // 2
    rows = spans * SPAN
    tiles = rows // TILE
    capacity = -(-per_dev // nd)
    quarter = d // 4
    f = ffn_out.shape[0]
    w = d // nd
    direct = w % 128 == 0

    recv_slot, send_local, back_local, home_slot = deal_tables(deal, nd, per_dev, capacity, dp)
    mine = lax.dynamic_slice_in_dim(recv_slot, x * spans, spans)
    theirs = lax.dynamic_slice_in_dim(recv_slot, (1 - x) * spans, spans)
    span_ids = (dp * 2 + x) * spans + jnp.arange(spans, dtype=jnp.int32)
    keep = 1 - span_starts(seq_extra, span_ids)
    other_quarter = 2 * (1 - x) + core
    quarters = jnp.stack([tensor, other_quarter, 2 * x + 1 - core, 2 * (1 - x) + 1 - core])
    ints = jnp.concatenate([quarters, jnp.stack([core, z, y, x]), keep]).astype(jnp.int32)
    ups, downs, level, level_t = (jnp.asarray(v) for v in level_matrices())
    ups_last, downs_last = (jnp.asarray(v[LEVELS:]) for v in level_matrices()[:2])

    hh, ho, hf = HEAD // 2, DV // 2, f // 2
    pitch = f
    ffn_t = ffn_in.reshape(w, 2 * f).T
    shard_p = jnp.concatenate([decay_down.T, proj_in.reshape(w, HEAD).T, proj_out.reshape(DV, w)], axis=0)
    shard_f = jnp.concatenate([ffn_t[:f], ffn_out, ffn_t[f:]], axis=0)

    def fit(parts):
        return jnp.concatenate(parts, axis=0)

    table = jnp.concatenate([send_local, mine, theirs]).astype(jnp.int32)
    if not direct:

        def gathered(shard):
            return jnp.swapaxes(lax.all_gather(shard, "dp", axis=0), 0, 1).reshape(shard.shape[0], d)

        def halves(shard):
            own, other = gathered(shard), gathered(swap(shard, "x"))
            return jnp.where(x == 0, fit([own, other]), fit([other, own]))

        shard_p = halves(shard_p)
        shard_f = fit([halves(ffn_t[:f]), halves(ffn_out), halves(ffn_t[f:])])

    up_own = decay_up.reshape(16, DK)
    bias_own = decay_bias.reshape(1, DK)
    small_own = jnp.concatenate([up_own.astype(F32), bias_own, jnp.zeros((7, DK), F32)], axis=0)
    small_other = swap(small_own, "x")
    small_both = jnp.where(
        x == 0,
        jnp.concatenate([small_own, small_other], axis=1),
        jnp.concatenate([small_other, small_own], axis=1),
    )
    up, bias = small_both[:16].astype(BF), small_both[16:17]
    gain_one, gain_two = block_gains[0:1], block_gains[1:2]
    head_row = head_gain.reshape(1, DV)

    def tall(cols, dtype=BF):
        return sds(rows, cols, dtype=dtype)

    nlev = LEVELS + 2
    sequence = nd * 2
    reach = -(-(MAX_SPANS - 1) // spans)
    (src, cot, weights, w_ffn, normed_first, qkvg, log_decay, rank, mixed, gated, attn, before, attn_other,
     factors) = forward(
        table, keep.astype(jnp.int32), tokens, cotangent, shard_p, shard_f, gain_one, up, bias, head_row, ups, level,
        nd, spans, reach, direct,
    )
    ff = 2 * f
    hidden, normed_second, act, grad_gu, keep_out, send_out, grad_second = run(
        ffn_kernel, (tiles,),
        [SMEM] + [rows_spec(d)] * 4 + [whole_spec(1, d), whole_spec(3 * ff, d)],
        [rows_spec(d), rows_spec(d), rows_spec(2 * pitch), rows_spec(4 * pitch), rows_spec(2 * quarter),
         rows_spec(2 * quarter), rows_spec(d)],
        [tall(d, F32), tall(d), tall(2 * pitch), tall(4 * pitch), tall(2 * quarter), tall(2 * quarter), tall(d)],
        [pltpu.VMEM((TILE, d), BF)],
        "ffn", 34,
    )(ints, src, attn, attn_other, cot, gain_two, w_ffn)
    gs_other = swap(grad_second, "core")
    recv_out = swap(send_out, "core")

    def plain_shard(full, f_rows):
        full = jnp.swapaxes(full.reshape(2 * f_rows, nd, w), 0, 1)
        total = lax.psum_scatter(full, "dp", scatter_dimension=0, tiled=True)[0].astype(F32)
        keep_rows = lax.dynamic_slice_in_dim(total, x * f_rows, f_rows)
        give_rows = lax.dynamic_slice_in_dim(total, (1 - x) * f_rows, f_rows)
        return keep_rows + swap(give_rows, "x")

    grad_hidden, grad_mixed, grad_gate, gain_second, head_part, packet_back, out_own, out_cross, acc_po = run(
        functools.partial(out_back_kernel, tiles), (tiles,),
        [SMEM] + [rows_spec(d, tiles)] * 4
        + [whole_spec(1, d), whole_spec(2 * PROJ_ROWS, d), rows_spec(2 * DV, tiles), rows_spec(2 * DV, tiles),
           rows_spec(2 * HEAD, tiles), rows_spec(2 * DK, tiles), whole_spec(1, DV), whole_spec(nlev, TILE, TILE),
           rows_spec(2 * quarter, tiles), rows_spec(2 * quarter, tiles)],
        [rows_spec(d, tiles), rows_spec(2 * DV, tiles), rows_spec(2 * DV, tiles), whole_spec(8, d),
         whole_spec(8, DV), whole_spec(2 * DV, DK), rows_spec(quarter, tiles), rows_spec(quarter, tiles),
         whole_spec(2 * DV, d)],
        [tall(d, F32), tall(2 * DV), tall(2 * DV), sds(8, d), sds(8, DV), sds(2 * DV, DK), tall(quarter),
         tall(quarter), sds(2 * DV, d, dtype=BF)],
        [pltpu.VMEM((2 * DV, d), F32), pltpu.VMEM((2, DV, DK), F32), pltpu.VMEM((8, d), F32), pltpu.VMEM((8, DV), F32)],
        "out_back", 19,
    )(ints, hidden, cot, grad_second, gs_other, gain_two, weights, gated, mixed, qkvg, log_decay, head_row, ups,
      keep_out, recv_out)

    dma = pltpu.SemaphoreType.DMA
    steps = len(carry_widths(reach)[0]) + 2
    shape_qk, shape_v, shape_ld = (rows, 4 * DK), (rows, 2 * DV), (rows, 2 * DK)
    buffers, sems = undeal_scratch(nd, per_dev, spans, quarter, capacity, False)
    scratch = [pltpu.VMEM(shape_qk, F32), pltpu.VMEM(shape_v, BF), pltpu.VMEM(shape_ld, F32)]
    scratch += [pltpu.VMEM((steps - 1, 2 * DV + 16, DK), BF), pltpu.VMEM((steps, 2 * DV + 16, DK), BF)]
    scratch += [dma((steps,)), dma((steps,)), dma((4,))] + buffers[2:] + sems
    scratch += [pltpu.VMEM(v.shape, v.dtype) for v in (act, cot, qkvg, log_decay, grad_mixed)] + [dma((5,))]
    if direct:
        sums = [sds(f, w), sds(f, w), sds(f // 2, w), sds(f // 2, w), sds(8, 128)]
        scratch += [pltpu.VMEM((2 * pitch, d), BF)] * 3
        for out in sums[:4]:
            scratch += collapse_scratch(nd, out.shape[0], w)
    else:
        sums = [sds(2 * pitch, d, dtype=BF)] * 3
    leaving, grad_qk, grad_v, grad_ld, back_out, *sums_f = remote(
        functools.partial(back_kernel, nd, spans, reach, direct, f),
        (back_local, act, grad_gu, normed_second, cot, qkvg, log_decay, grad_mixed, packet_back, factors,
         out_own.reshape(spans, SPAN, quarter), out_cross.reshape(spans, SPAN, quarter), ups, downs, level, level_t),
        [SMEM, ANY, VMEM, VMEM, ANY, ANY, ANY, ANY] + [VMEM] * 8,
        [sds(2 * DV + 16, DK), sds(*shape_qk), sds(*shape_v, dtype=BF), sds(*shape_ld),
         sds(nd * capacity, SPAN, quarter, dtype=BF)] + sums,
        [VMEM] + [ANY] * 4 + [VMEM] * len(sums),
        scratch, "back_all", 1, 110,
    )
    if direct:
        shard_gate, shard_up, shard_fo = sums_f[0], sums_f[1], fit(sums_f[2:4])
    else:
        shard_gate, shard_up, shard_fo = (plain_shard(v, pitch)[:f] for v in sums_f)
    block_out = home(back_out, home_slot, "block_out_home")

    buffers, sems = undeal_scratch(nd, per_dev, spans, quarter, capacity, True)
    scratch = [
        pltpu.VMEM((2 * DV + 16, DK), F32), pltpu.VMEM((rows, 2 * HEAD), BF), pltpu.VMEM((rows, d), BF),
        pltpu.VMEM((rows, d), BF), pltpu.VMEM((tiles, 16, TILE), F32), pltpu.VMEM((tiles, 16, TILE), F32),
        pltpu.VMEM((TILE, 2 * DK), BF), pltpu.VMEM((TILE, 2 * DK), BF), pltpu.VMEM((TILE, 2 * DK), F32),
        pltpu.VMEM((TILE, d), BF), dma((tiles,)), dma((tiles,)), dma((tiles,)), dma((tiles,)), dma((1,)),
    ] + buffers + sems
    scratch += [pltpu.VMEM(v.shape, v.dtype) for v in (src, normed_first, grad_hidden)] + [dma((3,))]
    if direct:
        sums = [sds(hh, w), sds(hh, w), sds(ho, w), sds(ho, w), sds(SMALL, 128), sds(8, 128)]
        scratch += [pltpu.VMEM((2 * DV, d), BF), pltpu.VMEM((2 * HEAD, d), BF)] + small_scratch(nd)
        for out in sums[:4]:
            scratch += collapse_scratch(nd, out.shape[0], w)
    else:
        sums = [sds(2 * HEAD, d, dtype=BF)]
    back_grad, down_grad, gain_first, up_grad, bias_grad, *sums_p = remote(
        functools.partial(last_kernel, nd, spans, direct),
        (back_local, keep.astype(jnp.int32), qkvg, log_decay, grad_mixed, before, leaving, grad_qk, grad_v, grad_ld,
         grad_gate, rank, up, bias, ups_last, downs_last, weights, src, normed_first, grad_hidden, gain_one,
         acc_po, gain_second, head_part, sums_f[4] if direct else gain_second),
        [SMEM, SMEM] + [VMEM] * 15 + [ANY] * 3 + [VMEM, ANY] + [VMEM] * 3,
        [sds(nd * capacity, SPAN, d, dtype=BF), sds(16, d), sds(8, d), sds(16, 2 * DK), sds(8, 2 * DK)] + sums,
        [ANY] + [VMEM] * (4 + len(sums)),
        scratch, "finish_all", 2, 100,
    )
    if direct:
        shard_pi, shard_po = fit(sums_p[:2]), fit(sums_p[2:4])
    else:
        shard_pi, shard_po = plain_shard(sums_p[0], HEAD), plain_shard(acc_po, DV)
    token_grad = home(back_grad, home_slot, "token_grad_home")

    if direct:
        small, norm_block = sums_p[4], sums_p[5]
        gain_first, gain_second = small[0:8].reshape(d), small[8:16].reshape(d)
        shard_down = lax.dynamic_slice_in_dim(small, 16 + 16 * dp, 16, 0).T
        up_total = lax.dynamic_slice_in_dim(small, 144 + 16 * x, 16, 0)
        bias_total = lax.dynamic_slice_in_dim(small, 176 + x, 1, 0)
        head_total = small[178:180].reshape(DV)
        norm_sq = jnp.sum(norm_block)
    else:
        parts = (gain_first[0], gain_second[0], down_grad, up_grad, bias_grad[0], head_part[0])
        small = jnp.concatenate([v.reshape(-1) for v in parts]).reshape(-1, 128)
        small = all_sum(small, ("x", "dp"), (2, nd)).reshape(-1)
        cuts = [d, d, 16 * d, 32 * DK, 2 * DK, DV]
        starts = [sum(cuts[:k]) for k in range(len(cuts) + 1)]
        gain_first, gain_second, down_total, up_total, bias_total, head_total = (
            small[starts[k] : starts[k + 1]] for k in range(len(cuts))
        )
        head_total = head_total + swap(head_total, "core")
        shard_down = lax.dynamic_slice_in_dim(down_total.reshape(16, d), dp * w, w, 1).T
        up_total = up_total.reshape(16, 2, DK)
        up_total = jnp.where(x == 0, up_total[:, 0], up_total[:, 1])
        bias_total = bias_total.reshape(2, DK)
        bias_total = jnp.where(x == 0, bias_total[0:1], bias_total[1:2])
        local_sq = (
            square_sum(shard_pi) + square_sum(shard_po) + square_sum(shard_gate) + square_sum(shard_up)
            + square_sum(shard_fo) + square_sum(shard_down) / 4
            + (square_sum(up_total) + square_sum(bias_total)) / nd
            + (square_sum(head_total) + square_sum(gain_first) + square_sum(gain_second)) / (4 * nd)
        )
        norm_sq = all_sum(jnp.broadcast_to(local_sq, (8, 128)), ("core", "x", "dp"), (2, 2, nd))[0, 0]
    up_total = up_total.reshape(decay_up.shape)
    bias_total = bias_total.reshape(decay_bias.shape)
    gains_total = jnp.stack([gain_first, gain_second])
    shard_in = shard_pi.T.reshape(proj_in.shape)
    shard_out = shard_po.reshape(proj_out.shape)
    shard_ffn_in = jnp.stack([shard_gate.T, shard_up.T], axis=1)
    shard_ffn_out = shard_fo
    grad_norm = jnp.sqrt(norm_sq)
    clip_norm = clip_scale * math.sqrt(PARAMS)
    factor = jnp.minimum(1.0, clip_norm / (grad_norm + 1e-06))
    update_in = adam_update(proj_in, shard_in, first_proj_in, second_proj_in, factor, weight_decay)
    update_down = adam_update(decay_down, shard_down, first_decay_down, second_decay_down, factor, weight_decay)
    update_up = adam_update(decay_up, up_total, first_decay_up, second_decay_up, factor, weight_decay)
    update_bias = adam_update(decay_bias, bias_total, first_decay_bias, second_decay_bias, factor, 0.0)
    update_head = adam_update(head_gain, head_total, first_head_gain, second_head_gain, factor, 0.0)
    update_out = adam_update(proj_out, shard_out, first_proj_out, second_proj_out, factor, weight_decay)
    update_gains = adam_update(block_gains, gains_total, first_block_gains, second_block_gains, factor, 0.0)
    update_ffn_in = adam_update(ffn_in, shard_ffn_in, first_ffn_in, second_ffn_in, factor, weight_decay)
    update_ffn_out = adam_update(ffn_out, shard_ffn_out, first_ffn_out, second_ffn_out, factor, weight_decay)
    return (
        block_out, token_grad, grad_norm, *update_in, *update_down, *update_up, *update_bias, *update_head,
        *update_out, *update_gains, *update_ffn_in, *update_ffn_out,
    )


def solution(mesh):
    nd, nt = mesh.shape["dp"], mesh.shape["tensor"]
    fine = Mesh(mesh.devices.reshape(nd, nt // 2, 2), ("dp", "x", "core"))
    t = ("x", "core")
    w_specs = {
        "proj_in": P("dp", t, None),
        "decay_down": P("dp", None),
        "decay_up": P(None, t, None),
        "decay_bias": P(t, None),
        "head_gain": P(),
        "proj_out": P(t, None, "dp"),
        "block_gains": P(),
        "ffn_in": P("dp", None, t),
        "ffn_out": P(t, "dp"),
    }
    specs = list(w_specs.values())
    placed = [P("dp", None), P("dp", None), P(), P()] + specs
    results = [P("dp", t), P("dp", None), P()]
    for spec in specs:
        placed += [spec] * 2
        results += [spec] * 4
    return jax.shard_map(
        on_device,
        mesh=fine,
        in_specs=tuple(placed),
        out_specs=tuple(results),
        check_vma=False,
    )
```
